32 devices in a mesh: sample: 8 (over y, x, core), depth: 4 (over z).
Axes of the slice: x: 2, y: 2, z: 4, core: 2. Of those that a mesh axis runs over, the one named last changes fastest.
Arguments:
- volume: bfloat16 [8, 16, 8, 2048], P('sample', 'depth'), may hold values from -6 to 6
- kernels: bfloat16 [3, 27, 1024], replicated, may hold values from -0.21875 to 0.21875
- partner: int32 [8], replicated, may hold values from 0 to 7, each once
- cotangent: bfloat16 [8, 16, 8, 2048], P('sample', 'depth'), may hold values from -6 to 6
Outputs:
- grad_volume: bfloat16 [8, 16, 8, 2048], P('sample', 'depth')
- kernel_grads: float32 [8, 3, 27, 1024], P('sample')
The draws below stay inside these ranges and needn't reach their ends.
Inputs may be any that keep to these rules, and one draw needn't show every extreme that they name: partner is a permutation of the 8 crops: every crop is the partner of exactly one crop, and a crop may be its own partner.
All inputs are finite; a program needn't handle non-finite values.
Results may differ from the reference program's by a relative error of at most 0.014.
Values may be sent and summed in bfloat16 or wider, within the bound.
No kernel may reach another device: no remote copies, remote signals or barrier semaphores. Data moves between devices by JAX's collectives and lax.ppermute only.
A program may use at most 64 MiB of HBM per device.

```python
import jax
import jax.numpy as jnp
from jax import lax

CH = 32
HEIGHT = 8
WIDTH = 64
LAYERS = 3
TAPS = 27
CROPS = 8
DEPTH = 16


def steps_of(key, dims, split, least, largest):
    factor_of, own = 1.0, jax.random.fold_in(key, 6)
    for dim, shards_of in split:
        draws = jnp.exp(jax.random.uniform(jax.random.fold_in(own, dim), (shards_of,), jnp.float32, least / len(split), largest / len(split)))
        factor_of = factor_of * jnp.repeat(draws, dims[dim] // shards_of).reshape([-1 if axis == dim else 1 for axis in range(len(dims))])
    return factor_of


def bell_draw(key, extent, spread, reach, cuts=(), held_as=jnp.bfloat16):
    entries = spread * jax.random.normal(key, extent, jnp.float32)
    if cuts:
        entries = entries * steps_of(key, extent, cuts, -0.22, 0.18)
    return jnp.clip(entries, -reach, reach).astype(held_as)


def setup_inputs(seed: int = 0) -> dict:
    keys = jax.random.split(jax.random.key(seed), 5)
    return {
        "volume": bell_draw(keys[0], (CROPS, DEPTH, HEIGHT, WIDTH * CH), 1.0, 6.0, ((0, 8), (1, 4))),
        "kernels": bell_draw(keys[1], (LAYERS, TAPS, CH * CH), (TAPS * CH) ** -0.5, 0.21875),
        "partner": jax.random.permutation(keys[2], CROPS).astype(jnp.int32),
        "cotangent": bell_draw(keys[3], (CROPS, DEPTH, HEIGHT, WIDTH * CH), 1.0, 6.0, ((0, 8), (1, 4))),
    }


OWN_SHARE = 0.6
PARTNER_SHARE = 0.4

def swish_value(values):
    return values * jax.nn.sigmoid(values)

def swish_slope(values):
    logistic = jax.nn.sigmoid(values)
    return logistic * (1.0 + values * (1.0 - logistic))

def rounded(values):
    return lax.optimization_barrier(values.astype(jnp.bfloat16)).astype(jnp.float32)

def conv_grid(values, kernel):
    weights = kernel.reshape(3, 3, 3, CH, CH)
    result = lax.conv_general_dilated(values[None], weights, (1, 1, 1), [(1, 1), (1, 1), (1, 1)], dimension_numbers=('NDHWC', 'DHWIO', 'NDHWC'), precision=lax.Precision.HIGHEST)
    return result[0]

def reference(volume, kernels, partner, cotangent):
    grid_shape = (DEPTH, HEIGHT, WIDTH, CH)
    weights = kernels.astype(jnp.float32)

    def first_layer(crop_cells):
        return swish_value(conv_grid(crop_cells.reshape(grid_shape).astype(jnp.float32), weights[0])).astype(jnp.bfloat16)
    hidden = lax.map(first_layer, volume)
    blended = (OWN_SHARE * hidden.astype(jnp.float32) + PARTNER_SHARE * hidden[partner].astype(jnp.float32)).astype(jnp.bfloat16)

    def middle_layers(crop_pair):
        blended_crop, cot_crop = crop_pair
        pre_two, pull_two = jax.vjp(conv_grid, blended_crop.astype(jnp.float32), weights[1])
        second = rounded(swish_value(pre_two))
        pre_three, pull_three = jax.vjp(conv_grid, second, weights[2])
        grad_three = rounded(cot_crop.reshape(grid_shape).astype(jnp.float32) * swish_slope(pre_three))
        grad_second, kernel_three = pull_three(grad_three)
        grad_two = rounded(grad_second * swish_slope(pre_two))
        grad_blended, kernel_two = pull_two(grad_two)
        return (grad_blended.astype(jnp.bfloat16), kernel_two, kernel_three)
    grad_blended, kernel_two, kernel_three = lax.map(middle_layers, (blended, cotangent))
    grad_partner = grad_blended[jnp.argsort(partner)]

    def first_backward(triple):
        crop_cells, own_grad, other_grad = triple
        pre_one, pull_one = jax.vjp(conv_grid, crop_cells.reshape(grid_shape).astype(jnp.float32), weights[0])
        grad_hidden = OWN_SHARE * own_grad.astype(jnp.float32) + PARTNER_SHARE * other_grad.astype(jnp.float32)
        grad_one = rounded(grad_hidden * swish_slope(pre_one))
        grad_crop, kernel_one = pull_one(grad_one)
        return (grad_crop.astype(jnp.bfloat16).reshape(DEPTH, HEIGHT, WIDTH * CH), kernel_one)
    grad_volume, kernel_one = lax.map(first_backward, (volume, grad_blended, grad_partner))
    kernel_grads = jnp.stack([kernel_one, kernel_two, kernel_three], axis=1)
    return (grad_volume, kernel_grads)
```

```python
import functools

import jax
import jax.numpy as jnp
from jax import lax
from jax.experimental import pallas as pl
from jax.experimental.pallas import tpu as pltpu
from jax.sharding import PartitionSpec as P

CH = 32
OWN_SHARE = 0.6
PARTNER_SHARE = 0.4
LANES = 128
CELLS = LANES // CH
TILE = 2 * LANES
WIDE = 3 * TILE

SLOTS = (
    [(1 + h, 1 + w) for h in range(2) for w in range(CELLS)]
    + [(0, 1 + w) for w in range(CELLS)]
    + [(3, 1 + w) for w in range(CELLS)]
    + [(1, 5), (0, 0), (0, 5), (1, 0)]
    + [(2, 5), (3, 0), (3, 5), (2, 0)]
)
SLOT_OF = {cell: at for at, cell in enumerate(SLOTS)}

H_VOL, H_BLEND, H_SECOND, H_G3, H_G2, H_G1 = 6, 5, 4, 3, 2, 1


def chunks_of(rows):
    count = max(1, (rows + 2) // 5)
    base, extra = divmod(rows, count)
    start, result = 0, []
    for index in range(count):
        size = base + (index < extra)
        result.append((start, size))
        start += size
    return result


def sigmoid(v):
    return 0.5 + 0.5 * jnp.tanh(0.5 * v)


def build_weights(kt_ref, t_ref):
    cell = lax.broadcasted_iota(jnp.int32, (CH, LANES), 1) // CH

    def one(index, carry):
        layer, a = index // 3, index % 3
        bands = {}
        for b in range(3):
            taps = [kt_ref[layer, a * 9 + b * 3 + c].astype(jnp.float32) for c in range(3)]
            for ww in range(CELLS + 2):
                band = jnp.zeros((CH, LANES), jnp.float32)
                for c in range(3):
                    if 0 <= ww - c < CELLS:
                        band = jnp.where(cell == ww - c, taps[c], band)
                bands[b, ww] = band.astype(jnp.bfloat16)
        zero = jnp.zeros((CH, LANES), jnp.bfloat16)
        for at, (hh, ww) in enumerate(SLOTS):
            for h in range(2):
                t_ref[layer, a, at * CH : (at + 1) * CH, h * LANES : (h + 1) * LANES] = bands.get(
                    (hh - h, ww), zero
                )
        return carry

    lax.fori_loop(0, t_ref.shape[0] * 3, one, 0)


def expand(x, out_ref, lead, pairs, tiles):
    x = x.reshape(pairs, tiles, TILE)
    lane = lax.broadcasted_iota(jnp.int32, x.shape, 2)
    cell = (lane % LANES) // CH
    row = lax.broadcasted_iota(jnp.int32, x.shape, 1)
    before = pltpu.roll(x, 1, 1)
    after = pltpu.roll(x, tiles - 1, 1)
    edge = jnp.where(
        (cell == CELLS - 1) & (row > 0),
        before,
        jnp.where((cell == 0) & (row < tiles - 1), after, 0.0),
    )
    e0, e1 = edge[..., :LANES], edge[..., LANES:]
    r0, r1 = pltpu.roll(e0, LANES // 2, 2), pltpu.roll(e1, LANES // 2, 2)
    zero = jnp.zeros((1, tiles, LANES), jnp.float32)
    low = jnp.concatenate([zero, x[:-1, :, LANES:]], 0)
    high = jnp.concatenate([x[1:, :, :LANES], zero], 0)
    e0 = e0 + jnp.concatenate([zero, r1[:-1]], 0)
    e1 = e1 + jnp.concatenate([r0[1:], zero], 0)
    flat = lambda v: v.reshape(pairs * tiles, v.shape[-1]).astype(jnp.bfloat16)
    out_ref[(*lead, slice(None), slice(0, TILE))] = flat(x)
    out_ref[(*lead, slice(None), slice(TILE, TILE + LANES))] = flat(low)
    out_ref[(*lead, slice(None), slice(TILE + LANES, 2 * TILE))] = flat(high)
    out_ref[(*lead, slice(None), slice(2 * TILE, 2 * TILE + LANES))] = flat(e0)
    out_ref[(*lead, slice(None), slice(2 * TILE + LANES, WIDE))] = flat(e1)


def conv_rows(x_ref, lead, start, rows, t_ref, layer):
    total = None
    for a in range(3):
        block = x_ref[(*lead, pl.ds(start + a, rows))].reshape(-1, WIDE)
        part = jnp.dot(block, t_ref[layer, a], preferred_element_type=jnp.float32)
        total = part if total is None else total + part
    return total


def rounded(v):
    return v.astype(jnp.bfloat16).astype(jnp.float32)


def body(
    depth, pairs, tiles,
    idx_ref, vol_ref, cot_ref, kt_ref,
    gv_ref, kg_ref,
    t_ref, xv, hid, sl1, xb, sl2, xs, xg3, xg2, gb, xg1, rw,
):
    rows = gv_ref.shape[0]
    cells = pairs * tiles
    first = idx_ref[0] * rows
    grow = functools.partial(expand, pairs=pairs, tiles=tiles)

    def inside(v, row):
        at = first + row
        return jnp.where((at >= 0) & (at < depth), v, 0.0)

    build_weights(kt_ref, t_ref)

    def widen(index, carry):
        crop, d = index // (rows + 2 * H_VOL), index % (rows + 2 * H_VOL)
        grow(vol_ref[crop, d].astype(jnp.float32), xv, (crop, d))
        return carry

    lax.fori_loop(0, 3 * (rows + 2 * H_VOL), widen, 0)

    def layer_one(crop, slopes):
        for start, count in chunks_of(rows + 2 * H_BLEND):
            pre = conv_rows(xv, (crop,), start, count, t_ref, 0)
            gate = sigmoid(pre)
            hid[crop, pl.ds(start, count)] = (
                (pre * gate).astype(jnp.bfloat16).reshape(count, cells, TILE)
            )
            if slopes:
                slope = (gate * (1.0 + pre * (1.0 - gate))).reshape(count, cells, TILE)
                for d in range(count):
                    to = start + d - (H_BLEND - H_G1)
                    if 0 <= to < rows + 2 * H_G1:
                        sl1[to] = slope[d]

    layer_one(0, True)

    def others(crop, carry):
        layer_one(crop, False)
        return carry

    lax.fori_loop(1, 3, others, 0)

    def blend(index, carry):
        j, d = index // (rows + 2 * H_BLEND), index % (rows + 2 * H_BLEND)
        mixed = OWN_SHARE * hid[2 * j, d].astype(jnp.float32) + PARTNER_SHARE * hid[
            1 - j, d
        ].astype(jnp.float32)
        grow(rounded(inside(mixed, d - H_BLEND)), xb, (j, d))
        return carry

    lax.fori_loop(0, 2 * (rows + 2 * H_BLEND), blend, 0)

    def middle(j, carry):
        for start, count in chunks_of(rows + 2 * H_SECOND):
            pre = conv_rows(xb, (j,), start, count, t_ref, 1)
            gate = sigmoid(pre)
            value = (pre * gate).reshape(count, cells, TILE)
            slope = (gate * (1.0 + pre * (1.0 - gate))).reshape(count, cells, TILE)
            for d in range(count):
                grow(rounded(inside(value[d], start + d - H_SECOND)), xs, (j, start + d))
                to = start + d - (H_SECOND - H_G2)
                if 0 <= to < rows + 2 * H_G2:
                    sl2[j, to] = slope[d]
        for start, count in chunks_of(rows + 2 * H_G3):
            pre = conv_rows(xs, (j,), start, count, t_ref, 2)
            gate = sigmoid(pre)
            slope = (gate * (1.0 + pre * (1.0 - gate))).reshape(count, cells, TILE)
            for d in range(count):
                grad = cot_ref[j, start + d].astype(jnp.float32) * slope[d]
                grow(rounded(grad), xg3, (j, start + d))
        for start, count in chunks_of(rows + 2 * H_G2):
            back = conv_rows(xg3, (j,), start, count, t_ref, 5).reshape(count, cells, TILE)
            for d in range(count):
                grad = inside(back[d] * sl2[j, start + d], start + d - H_G2)
                grow(rounded(grad), xg2, (j, start + d))
        for start, count in chunks_of(rows + 2 * H_G1):
            back = conv_rows(xg2, (j,), start, count, t_ref, 4).reshape(count, cells, TILE)
            gb[j, pl.ds(start, count)] = back.astype(jnp.bfloat16)
        return carry

    lax.fori_loop(0, 2, middle, 0)

    def first_grad(d, carry):
        mixed = OWN_SHARE * gb[0, d].astype(jnp.float32) + PARTNER_SHARE * gb[1, d].astype(
            jnp.float32
        )
        grow(rounded(inside(mixed * sl1[d], d - H_G1)), xg1, (d,))
        return carry

    lax.fori_loop(0, rows + 2 * H_G1, first_grad, 0)

    for start, count in chunks_of(rows):
        back = conv_rows(xg1, (), start, count, t_ref, 3).reshape(count, cells, TILE)
        gv_ref[pl.ds(start, count)] = back.astype(jnp.bfloat16)

    cell = lax.broadcasted_iota(jnp.int32, (kg_ref.shape[1], LANES), 1) // CH
    grads = (
        (xv, (0,), H_VOL, xg1, (), H_G1),
        (xb, (0,), H_BLEND, xg2, (0,), H_G2),
        (xs, (0,), H_SECOND, xg3, (0,), H_G3),
    )
    for layer, (u, u_lead, u_halo, g, g_lead, g_halo) in enumerate(grads):
        gradient = g[(*g_lead, pl.ds(g_halo, rows), slice(None), slice(0, TILE))].reshape(-1, TILE)
        for a in range(3):
            values = u[(*u_lead, pl.ds(u_halo - 1 + a, rows))].reshape(-1, WIDE)
            terms = lax.dot_general(
                values, gradient, (((0,), (0,)), ((), ())), preferred_element_type=jnp.float32
            )
            for b in range(3):
                for c in range(3):
                    at = (a * 9 + b * 3 + c) * CH
                    for w in range(CELLS):
                        s0, s1 = SLOT_OF[b, w + c] * CH, SLOT_OF[b + 1, w + c] * CH
                        rw[w, at : at + CH] = (
                            terms[s0 : s0 + CH, :LANES] + terms[s1 : s1 + CH, LANES:]
                        )
        dense = jnp.zeros((kg_ref.shape[1], LANES), jnp.float32)
        for q in range(CELLS):
            part = None
            for w in range(CELLS):
                piece = rw[w, pl.ds(q, kg_ref.shape[1], stride=CELLS), :]
                if q != w:
                    piece = pltpu.roll(piece, (q - w) % CELLS * CH, 1)
                part = piece if part is None else part + piece
            dense = jnp.where(cell == q, part, dense)
        kg_ref[layer] = dense.astype(kg_ref.dtype)


def window(depth, pairs, tiles, index, vol, cot, kt):
    rows = vol.shape[1] - 2 * H_VOL
    cells = pairs * tiles
    taps = kt.shape[1]
    bf16, f32 = jnp.bfloat16, jnp.float32
    wide = lambda *lead: pltpu.VMEM((*lead, cells, WIDE), bf16)
    vmem = pl.BlockSpec(memory_space=pltpu.VMEM)
    macs = 9 * (3 * (rows + 10) + 2 * (rows + 8 + rows + 6 + rows + 4 + rows + 2) + 4 * rows)
    return pl.pallas_call(
        functools.partial(body, depth, pairs, tiles),
        out_shape=(
            jax.ShapeDtypeStruct((rows, cells, TILE), bf16),
            jax.ShapeDtypeStruct((3, taps * CH // CELLS, LANES), bf16),
        ),
        in_specs=[pl.BlockSpec(memory_space=pltpu.SMEM), vmem, vmem, vmem],
        out_specs=(vmem, vmem),
        scratch_shapes=[
            pltpu.VMEM((6, 3, WIDE, TILE), bf16),
            wide(3, rows + 2 * H_VOL),
            pltpu.VMEM((3, rows + 2 * H_BLEND, cells, TILE), bf16),
            pltpu.VMEM((rows + 2 * H_G1, cells, TILE), f32),
            wide(2, rows + 2 * H_BLEND),
            pltpu.VMEM((2, rows + 2 * H_G2, cells, TILE), f32),
            wide(2, rows + 2 * H_SECOND),
            wide(2, rows + 2 * H_G3),
            wide(2, rows + 2 * H_G2),
            pltpu.VMEM((2, rows + 2 * H_G1, cells, TILE), bf16),
            wide(rows + 2 * H_G1),
            pltpu.VMEM((CELLS, taps * CH, LANES), f32),
        ],
        compiler_params=pltpu.CompilerParams(vmem_limit_bytes=48 * 2**20),
        cost_estimate=pl.CostEstimate(
            flops=2 * macs * cells * TILE * TILE, bytes_accessed=4 * 2**20, transcendentals=0
        ),
    )(index, vol, cot, kt)


def halo(values, width, dim):
    rows = values.shape[dim]
    count = lax.axis_size("depth")
    low, high = [], []
    hop = 1
    while width > 0:
        take = min(rows, width)
        up = [(i, i + hop) for i in range(count - hop)]
        down = [(target, source) for source, target in up]
        low.insert(
            0, lax.ppermute(lax.slice_in_dim(values, rows - take, rows, axis=dim), "depth", up)
        )
        high.append(lax.ppermute(lax.slice_in_dim(values, 0, take, axis=dim), "depth", down))
        width -= take
        hop += 1
    return jnp.concatenate([*low, values, *high], axis=dim)


def per_device(volume, kernels, partner, cotangent):
    _, rows, height, lanes = volume.shape
    pairs, tiles = height // 2, lanes // LANES
    cells = pairs * tiles
    groups = lax.axis_size("sample")
    depth = rows * lax.axis_size("depth")

    def tiled(values):
        split = values.reshape(rows, pairs, 2, tiles, LANES)
        return jnp.transpose(split, (0, 1, 3, 2, 4)).reshape(rows * cells, TILE)

    own = jnp.stack([tiled(volume), tiled(cotangent)])
    ids = jnp.arange(groups, dtype=jnp.int32)
    inverse = jnp.sum(jnp.where(partner[:, None] == ids[None, :], ids[:, None], 0), axis=0)
    wanted = jnp.stack([2 * partner, 2 * inverse, 2 * inverse + 1], axis=1)

    pieces = jnp.swapaxes(own.reshape(2, groups, -1, TILE), 0, 1)
    spread = lax.all_to_all(pieces, "sample", split_axis=0, concat_axis=0, tiled=True)
    chosen = jnp.take(spread.reshape(2 * groups, -1, TILE), wanted, axis=0)
    joined = lax.all_to_all(chosen, "sample", split_axis=0, concat_axis=0, tiled=True)
    others = jnp.swapaxes(joined, 0, 1).reshape(3, rows, cells, TILE)
    own = own.reshape(2, rows, cells, TILE)

    vol = halo(jnp.concatenate([own[:1], others[:2]]), H_VOL, 1)
    cot = halo(jnp.concatenate([own[1:], others[2:]]), H_G3, 1)

    taps = kernels.reshape(*kernels.shape[:2], CH, CH)
    both = jnp.concatenate([taps, jnp.swapaxes(taps[:, ::-1], 2, 3)])
    kt = jnp.tile(both, (1, 1, 1, CELLS))
    index = lax.axis_index("depth").astype(jnp.int32).reshape(1)
    grad, terms = window(depth, pairs, tiles, index, vol, cot, kt)

    split = grad.reshape(rows, pairs, tiles, 2, LANES)
    grad_volume = jnp.transpose(split, (0, 1, 3, 2, 4)).reshape(volume.shape)
    count = lax.axis_size("depth")
    copies = jnp.broadcast_to(terms[None], (count, *terms.shape))
    every = lax.all_to_all(copies, "depth", split_axis=0, concat_axis=0, tiled=True)
    total = jnp.sum(every.astype(jnp.float32), axis=0)
    return (grad_volume, total.reshape(1, *kernels.shape))


def solution(mesh):
    in_specs = (P("sample", "depth", None, None), P(), P(), P("sample", "depth", None, None))
    out_specs = (P("sample", "depth", None, None), P("sample", None, None, None))
    return jax.shard_map(
        per_device, mesh=mesh, in_specs=in_specs, out_specs=out_specs, check_vma=False
    )
```

```python
import functools

import jax
import jax.numpy as jnp
from jax import lax
from jax.experimental import pallas as pl
from jax.experimental.pallas import tpu as pltpu
from jax.sharding import PartitionSpec as P

CH = 32
OWN_SHARE = 0.6
PARTNER_SHARE = 0.4
LANES = 128
CELLS = LANES // CH
TILE = 2 * LANES
WIDE = 3 * TILE
VMEM_LIMIT = 40 * 2**20

SLOTS = (
    [(1 + h, 1 + w) for h in range(2) for w in range(CELLS)]
    + [(0, 1 + w) for w in range(CELLS)]
    + [(3, 1 + w) for w in range(CELLS)]
    + [(1, 5), (0, 0), (0, 5), (1, 0)]
    + [(2, 5), (3, 0), (3, 5), (2, 0)]
)
SLOT_OF = {cell: at for at, cell in enumerate(SLOTS)}

H_HIDDEN, H_TWO, H_G3, H_G2, H_G1 = 3, 2, 3, 2, 1


def chunks_of(rows):
    count = max(1, (rows + 2) // 5)
    base, extra = divmod(rows, count)
    start, result = 0, []
    for index in range(count):
        size = base + (index < extra)
        result.append((start, size))
        start += size
    return result


def sigmoid(v):
    return 0.5 + 0.5 * jnp.tanh(0.5 * v)


def spread_group(x, group):
    cell = lax.broadcasted_iota(jnp.int32, x.shape, 1) // CH
    x = jnp.where(cell == group, x, 0.0)
    x = x + pltpu.roll(x, CH, 1)
    return x + pltpu.roll(x, 2 * CH, 1)


def weights_body(taps, kr_ref, fwd_ref, bwd_ref, kf, kb):
    cell = lax.broadcasted_iota(jnp.int32, (CH, LANES), 1) // CH
    rows = kr_ref.shape[1]

    def layer_taps(layer, carry):
        packed = kr_ref[layer].astype(jnp.float32)
        for q in range(CELLS):
            kf[layer, pl.ds(q, rows, stride=CELLS), :] = spread_group(packed, q)
        for group in range((taps + CELLS - 1) // CELLS):
            turned = kf[layer, group * LANES : (group + 1) * LANES, :].T[:CH]
            for tap in range(CELLS):
                at = taps - 1 - (group * CELLS + tap)
                if at >= 0:
                    kb[layer, at * CH : (at + 1) * CH, :] = spread_group(turned, tap)
        return carry

    kf[:, taps * CH :, :] = jnp.zeros_like(kf[:, taps * CH :, :])
    lax.fori_loop(0, kr_ref.shape[0], layer_taps, 0)

    def one(index, carry):
        layer, a = index // 3, index % 3
        for source, t_ref in ((kf, fwd_ref), (kb, bwd_ref)):
            bands = {}
            for b in range(3):
                values = [
                    source[layer, pl.ds(pl.multiple_of((a * 9 + b * 3 + c) * CH, CH), CH), :]
                    for c in range(3)
                ]
                for ww in range(CELLS + 2):
                    band = jnp.zeros((CH, LANES), jnp.float32)
                    for c in range(3):
                        if 0 <= ww - c < CELLS:
                            band = jnp.where(cell == ww - c, values[c], band)
                    bands[b, ww] = band.astype(jnp.bfloat16)
            zero = jnp.zeros((CH, LANES), jnp.bfloat16)
            for at, (hh, ww) in enumerate(SLOTS):
                for h in range(2):
                    t_ref[layer, a, at * CH : (at + 1) * CH, h * LANES : (h + 1) * LANES] = (
                        bands.get((hh - h, ww), zero)
                    )
        return carry

    lax.fori_loop(0, kr_ref.shape[0] * 3, one, 0)


def banded_weights(kernels):
    layers, taps, _ = kernels.shape
    packed = kernels.reshape(layers, taps * CH // CELLS, LANES)
    vmem = pl.BlockSpec(memory_space=pltpu.VMEM)
    shape = jax.ShapeDtypeStruct((layers, 3, WIDE, TILE), jnp.bfloat16)
    room = (taps + CELLS - 1) // CELLS * LANES
    return pl.pallas_call(
        functools.partial(weights_body, taps),
        out_shape=(shape, shape),
        in_specs=[vmem],
        out_specs=(vmem, vmem),
        scratch_shapes=[pltpu.VMEM((layers, room, LANES), jnp.float32)] * 2,
        compiler_params=pltpu.CompilerParams(vmem_limit_bytes=VMEM_LIMIT),
        cost_estimate=pl.CostEstimate(flops=0, bytes_accessed=8 * 2**20, transcendentals=0),
    )(packed)


def expand(x, out_ref, lead, pairs, tiles):
    x = x.reshape(pairs, tiles, TILE)
    lane = lax.broadcasted_iota(jnp.int32, x.shape, 2)
    cell = (lane % LANES) // CH
    row = lax.broadcasted_iota(jnp.int32, x.shape, 1)
    before = pltpu.roll(x, 1, 1)
    after = pltpu.roll(x, tiles - 1, 1)
    edge = jnp.where(
        (cell == CELLS - 1) & (row > 0),
        before,
        jnp.where((cell == 0) & (row < tiles - 1), after, 0.0),
    )
    e0, e1 = edge[..., :LANES], edge[..., LANES:]
    r0, r1 = pltpu.roll(e0, LANES // 2, 2), pltpu.roll(e1, LANES // 2, 2)
    zero = jnp.zeros((1, tiles, LANES), jnp.float32)
    low = jnp.concatenate([zero, x[:-1, :, LANES:]], 0)
    high = jnp.concatenate([x[1:, :, :LANES], zero], 0)
    e0 = e0 + jnp.concatenate([zero, r1[:-1]], 0)
    e1 = e1 + jnp.concatenate([r0[1:], zero], 0)
    flat = lambda v: v.reshape(pairs * tiles, v.shape[-1]).astype(jnp.bfloat16)
    out_ref[(*lead, slice(None), slice(0, TILE))] = flat(x)
    out_ref[(*lead, slice(None), slice(TILE, TILE + LANES))] = flat(low)
    out_ref[(*lead, slice(None), slice(TILE + LANES, 2 * TILE))] = flat(high)
    out_ref[(*lead, slice(None), slice(2 * TILE, 2 * TILE + LANES))] = flat(e0)
    out_ref[(*lead, slice(None), slice(2 * TILE + LANES, WIDE))] = flat(e1)


def conv_rows(x_ref, lead, start, rows, t_ref, layer):
    total = None
    for a in range(3):
        block = x_ref[(*lead, pl.ds(start + a, rows))].reshape(-1, WIDE)
        part = jnp.dot(block, t_ref[layer, a], preferred_element_type=jnp.float32)
        total = part if total is None else total + part
    return total


def slope_of(pre, gate):
    return gate * (1.0 + pre * (1.0 - gate))


def fetch(source, target, sems, order):
    copies = {}
    for layer in order:
        copies[layer] = pltpu.make_async_copy(source.at[layer], target.at[layer], sems.at[layer])
        copies[layer].start()
    return copies


def rounded(v):
    return v.astype(jnp.bfloat16).astype(jnp.float32)


def inside(v, row, depth):
    return jnp.where((row >= 0) & (row < depth), v, 0.0)


def widen(parts, lead, x_ref, x_lead, grow):
    base = 0
    for part in parts:
        rows = part.shape[len(lead)]

        def step(d, carry, part=part, base=base):
            grow(part[(*lead, d)].astype(jnp.float32), x_ref, (*x_lead, base + d))
            return carry

        lax.fori_loop(0, rows, step, 0)
        base += rows


def layer_one(xv, lead, out_ref, t_ref, slopes_ref=None):
    rows, cells = out_ref.shape[len(lead)], out_ref.shape[-2]
    for start, count in chunks_of(rows):
        pre = conv_rows(xv, lead, start, count, t_ref, 0)
        gate = sigmoid(pre)
        value = (pre * gate).astype(jnp.bfloat16).reshape(count, cells, TILE)
        out_ref[(*lead, pl.ds(start, count))] = value
        if slopes_ref is not None:
            slope = slope_of(pre, gate).reshape(count, cells, TILE)
            for d in range(count):
                to = start + d - (H_HIDDEN - H_G1)
                if 0 <= to < slopes_ref.shape[0]:
                    slopes_ref[to] = slope[d]


def own_body(pairs, tiles, low, mid, high, t_hbm, hid, sl1, xv_own, t_ref, sems, xv):
    grow = functools.partial(expand, pairs=pairs, tiles=tiles)
    copies = fetch(t_hbm, t_ref, sems, (0,))
    widen((low, mid, high), (), xv, (), grow)
    copies[0].wait()
    layer_one(xv, (), hid, t_ref, sl1)
    rows = mid.shape[0]
    xv_own[...] = xv[rows - 1 : 2 * rows + 1]


def forward_body(
    depth, pairs, tiles,
    idx, low, mid, high, hid_own, cot_own, cot_other, t_hbm,
    g3, g3_up, g3_down, sl2, xb_own, xs_own,
    t_ref, sems, xv, hid, xb, xs,
):
    rows = mid.shape[1]
    cells = pairs * tiles
    first = idx[0] * rows
    grow = functools.partial(expand, pairs=pairs, tiles=tiles)
    copies = fetch(t_hbm, t_ref, sems, (0, 1, 2))

    def others(crop, carry):
        widen((low, mid, high), (crop,), xv, (crop,), grow)
        return carry

    lax.fori_loop(0, 2, others, 0)
    copies[0].wait()

    def first_layer(crop, carry):
        layer_one(xv, (crop,), hid, t_ref)
        return carry

    lax.fori_loop(0, 2, first_layer, 0)

    def blend(d, carry):
        own = hid_own[d].astype(jnp.float32)
        partner, other = hid[0, d].astype(jnp.float32), hid[1, d].astype(jnp.float32)
        row = first + d - H_HIDDEN
        for j, (a, b) in enumerate(((own, partner), (other, own))):
            mixed = OWN_SHARE * a + PARTNER_SHARE * b
            grow(rounded(inside(mixed, row, depth)), xb, (j, d))
        return carry

    lax.fori_loop(0, rows + 2 * H_HIDDEN, blend, 0)
    copies[1].wait()
    copies[2].wait()

    def middle(j, cot):
        for start, count in chunks_of(rows + 2 * H_TWO):
            pre = conv_rows(xb, (j,), start, count, t_ref, 1)
            gate = sigmoid(pre)
            value = (pre * gate).reshape(count, cells, TILE)
            slope = slope_of(pre, gate).reshape(count, cells, TILE)
            for d in range(count):
                sl2[j, start + d] = slope[d]
                to = start + d - (H_TWO - 1)
                if 0 <= to < rows + 2:
                    grow(rounded(inside(value[d], first + to - 1, depth)), xs, (j, to))
        for start, count in chunks_of(rows):
            pre = conv_rows(xs, (j,), start, count, t_ref, 2)
            slope = slope_of(pre, sigmoid(pre)).reshape(count, cells, TILE)
            for d in range(count):
                at = start + d
                grad = (cot[at].astype(jnp.float32) * slope[d]).astype(jnp.bfloat16)
                g3[j, at] = grad
                if at >= rows - H_G3:
                    g3_up[j, at - (rows - H_G3)] = grad
                if at < H_G3:
                    g3_down[j, at] = grad

    middle(0, cot_own)
    middle(1, cot_other)
    xb_own[...] = xb[0, H_HIDDEN - 1 : H_HIDDEN + rows + 1]
    xs_own[...] = xs[0]


def kernel_terms(values, gradient, rw, kg_ref, layer):
    rows = gradient.shape[0]
    gradient = gradient.reshape(-1, TILE)
    for a in range(3):
        block = values[a : a + rows].reshape(-1, WIDE)
        terms = lax.dot_general(
            block, gradient, (((0,), (0,)), ((), ())), preferred_element_type=jnp.float32
        )
        for b in range(3):
            for c in range(3):
                at = (a * 9 + b * 3 + c) * CH
                for w in range(CELLS):
                    s0, s1 = SLOT_OF[b, w + c] * CH, SLOT_OF[b + 1, w + c] * CH
                    rw[w, at : at + CH] = (
                        terms[s0 : s0 + CH, :LANES] + terms[s1 : s1 + CH, LANES:]
                    )
    count = kg_ref.shape[1]
    cell = lax.broadcasted_iota(jnp.int32, (count, LANES), 1) // CH
    dense = jnp.zeros((count, LANES), jnp.float32)
    for q in range(CELLS):
        part = None
        for w in range(CELLS):
            piece = rw[w, pl.ds(q, count, stride=CELLS), :]
            if q != w:
                piece = pltpu.roll(piece, (q - w) % CELLS * CH, 1)
            part = piece if part is None else part + piece
        dense = jnp.where(cell == q, part, dense)
    kg_ref[layer] = dense.astype(kg_ref.dtype)


def backward_body(
    depth, pairs, tiles,
    idx, low, mid, high, sl1, sl2, xv_own, xb_own, xs_own, t_hbm,
    gv, kg,
    t_ref, sems, xg3, xg2, gb, xg1, rw,
):
    rows = mid.shape[1]
    cells = pairs * tiles
    first = idx[0] * rows
    grow = functools.partial(expand, pairs=pairs, tiles=tiles)
    copies = fetch(t_hbm, t_ref, sems, (2, 1, 0))

    def crops(j, carry):
        widen((low, mid, high), (j,), xg3, (j,), grow)
        return carry

    lax.fori_loop(0, 2, crops, 0)
    copies[2].wait()
    copies[1].wait()

    def middle(j, carry):
        for start, count in chunks_of(rows + 2 * H_G2):
            back = conv_rows(xg3, (j,), start, count, t_ref, 2).reshape(count, cells, TILE)
            for d in range(count):
                at = start + d
                grad = inside(back[d] * sl2[j, at], first + at - H_G2, depth)
                grow(rounded(grad), xg2, (j, at))
        for start, count in chunks_of(rows + 2 * H_G1):
            back = conv_rows(xg2, (j,), start, count, t_ref, 1).reshape(count, cells, TILE)
            gb[j, pl.ds(start, count)] = back.astype(jnp.bfloat16)
        return carry

    lax.fori_loop(0, 2, middle, 0)

    def first_grad(d, carry):
        mixed = OWN_SHARE * gb[0, d].astype(jnp.float32) + PARTNER_SHARE * gb[1, d].astype(
            jnp.float32
        )
        grow(rounded(inside(mixed * sl1[d], first + d - H_G1, depth)), xg1, (d,))
        return carry

    lax.fori_loop(0, rows + 2 * H_G1, first_grad, 0)
    copies[0].wait()

    for start, count in chunks_of(rows):
        back = conv_rows(xg1, (), start, count, t_ref, 0).reshape(count, cells, TILE)
        gv[pl.ds(start, count)] = back.astype(jnp.bfloat16)

    kernel_terms(xv_own[...], xg1[H_G1 : H_G1 + rows, :, :TILE], rw, kg, 0)
    kernel_terms(xb_own[...], xg2[0, H_G2 : H_G2 + rows, :, :TILE], rw, kg, 1)
    kernel_terms(xs_own[...], xg3[0, H_G3 : H_G3 + rows, :, :TILE], rw, kg, 2)


def neighbours(up, down):
    count = lax.axis_size("depth")
    forward = [(i, i + 1) for i in range(count - 1)]
    backward = [(target, source) for source, target in forward]
    return lax.ppermute(up, "depth", forward), lax.ppermute(down, "depth", backward)


def call(kernel, outs, scratch, inputs, macs):
    vmem, smem, hbm = (
        pl.BlockSpec(memory_space=space) for space in (pltpu.VMEM, pltpu.SMEM, pl.ANY)
    )
    specs = [smem if x.dtype == jnp.int32 else hbm if x.shape[-2] == WIDE else vmem for x in inputs]
    return pl.pallas_call(
        kernel,
        out_shape=tuple(jax.ShapeDtypeStruct(shape, dtype) for shape, dtype in outs),
        in_specs=specs,
        out_specs=(vmem,) * len(outs),
        scratch_shapes=scratch,
        compiler_params=pltpu.CompilerParams(vmem_limit_bytes=VMEM_LIMIT),
        cost_estimate=pl.CostEstimate(
            flops=2 * macs, bytes_accessed=4 * 2**20, transcendentals=0
        ),
    )(*inputs)


def per_device(volume, kernels, partner, cotangent):
    _, rows, height, lanes = volume.shape
    pairs, tiles = height // 2, lanes // LANES
    cells = pairs * tiles
    groups = lax.axis_size("sample")
    depth = rows * lax.axis_size("depth")
    taps = kernels.shape[1]
    bf16, f32 = jnp.bfloat16, jnp.float32
    row_macs = 3 * cells * WIDE * TILE

    def tiled(values):
        split = values.reshape(rows, pairs, 2, tiles, LANES)
        return jnp.transpose(split, (0, 1, 3, 2, 4)).reshape(rows, cells, TILE)

    own = jnp.stack([tiled(volume), tiled(cotangent)])
    ids = jnp.arange(groups, dtype=jnp.int32)
    inverse = jnp.sum(jnp.where(partner[:, None] == ids[None, :], ids[:, None], 0), axis=0)
    wanted = jnp.stack([2 * partner, 2 * inverse, 2 * inverse + 1], axis=1)
    index = lax.axis_index("depth").astype(jnp.int32).reshape(1)

    pieces = jnp.swapaxes(own.reshape(2, groups, -1, TILE), 0, 1)
    spread = lax.all_to_all(pieces, "sample", split_axis=0, concat_axis=0, tiled=True)
    low, high = neighbours(own[0], own[0])
    fwd, bwd = banded_weights(kernels)
    wide = lambda *lead: pltpu.VMEM((*lead, cells, WIDE), bf16)
    weights = [pltpu.VMEM(fwd.shape, bf16), pltpu.SemaphoreType.DMA((3,))]
    hid_rows = rows + 2 * H_HIDDEN
    hid_own, sl1, xv_own = call(
        functools.partial(own_body, pairs, tiles),
        [
            ((hid_rows, cells, TILE), bf16),
            ((rows + 2 * H_G1, cells, TILE), f32),
            ((rows + 2, cells, WIDE), bf16),
        ],
        [*weights, wide(3 * rows)],
        [low, own[0], high, fwd],
        hid_rows * row_macs,
    )

    chosen = jnp.take(spread.reshape(2 * groups, -1, TILE), wanted, axis=0)
    joined = lax.all_to_all(chosen, "sample", split_axis=0, concat_axis=0, tiled=True)
    others = jnp.swapaxes(joined, 0, 1).reshape(3, rows, cells, TILE)
    vol = others[:2]
    low, high = neighbours(vol, vol)
    g3, g3_up, g3_down, sl2, xb_own, xs_own = call(
        functools.partial(forward_body, depth, pairs, tiles),
        [
            ((2, rows, cells, TILE), bf16),
            ((2, H_G3, cells, TILE), bf16),
            ((2, H_G3, cells, TILE), bf16),
            ((2, rows + 2 * H_TWO, cells, TILE), f32),
            ((rows + 2, cells, WIDE), bf16),
            ((rows + 2, cells, WIDE), bf16),
        ],
        [
            *weights,
            wide(2, 3 * rows),
            pltpu.VMEM((2, hid_rows, cells, TILE), bf16),
            wide(2, hid_rows),
            wide(2, rows + 2),
        ],
        [index, low, vol, high, hid_own, own[1], others[2], fwd],
        (2 * hid_rows + 2 * (rows + 4) + 2 * rows) * row_macs,
    )

    low, high = neighbours(g3_up, g3_down)
    grad, terms = call(
        functools.partial(backward_body, depth, pairs, tiles),
        [((rows, cells, TILE), bf16), ((3, taps * CH // CELLS, LANES), bf16)],
        [
            *weights,
            wide(2, rows + 2 * H_G3),
            wide(2, rows + 2 * H_G2),
            pltpu.VMEM((2, rows + 2 * H_G1, cells, TILE), bf16),
            wide(rows + 2 * H_G1),
            pltpu.VMEM((CELLS, taps * CH, LANES), f32),
        ],
        [index, low, g3, high, sl1, sl2, xv_own, xb_own, xs_own, bwd],
        (2 * (rows + 4) + 2 * (rows + 2) + 4 * rows) * row_macs,
    )

    split = grad.reshape(rows, pairs, tiles, 2, LANES)
    grad_volume = jnp.transpose(split, (0, 1, 3, 2, 4)).reshape(volume.shape)
    count = lax.axis_size("depth")
    copies = jnp.broadcast_to(terms[None], (count, *terms.shape))
    every = lax.all_to_all(copies, "depth", split_axis=0, concat_axis=0, tiled=True)
    total = jnp.sum(every.astype(jnp.float32), axis=0)
    return (grad_volume, total.reshape(1, *kernels.shape))


def solution(mesh):
    in_specs = (P("sample", "depth", None, None), P(), P(), P("sample", "depth", None, None))
    out_specs = (P("sample", "depth", None, None), P("sample", None, None, None))
    return jax.shard_map(
        per_device, mesh=mesh, in_specs=in_specs, out_specs=out_specs, check_vma=False
    )
```

```python
import functools

import jax
import jax.numpy as jnp
from jax import lax
from jax.experimental import pallas as pl
from jax.experimental.pallas import tpu as pltpu
from jax.sharding import PartitionSpec as P

CH = 32
OWN_SHARE = 0.6
PARTNER_SHARE = 0.4
LANES = 128
CELLS = LANES // CH
TILE = 2 * LANES
WIDE = 3 * TILE
VMEM_LIMIT = 40 * 2**20

SLOTS = (
    [(1 + h, 1 + w) for h in range(2) for w in range(CELLS)]
    + [(0, 1 + w) for w in range(CELLS)]
    + [(3, 1 + w) for w in range(CELLS)]
    + [(1, 5), (0, 0), (0, 5), (1, 0)]
    + [(2, 5), (3, 0), (3, 5), (2, 0)]
)
SLOT_OF = {cell: at for at, cell in enumerate(SLOTS)}

H_HIDDEN, H_TWO, H_G3, H_G2, H_G1 = 3, 2, 3, 2, 1


def chunks_of(rows):
    count = max(1, (rows + 2) // 5)
    base, extra = divmod(rows, count)
    start, result = 0, []
    for index in range(count):
        size = base + (index < extra)
        result.append((start, size))
        start += size
    return result


def sigmoid(v):
    return 0.5 + 0.5 * jnp.tanh(0.5 * v)


def spread_group(x, group):
    cell = lax.broadcasted_iota(jnp.int32, x.shape, 1) // CH
    x = jnp.where(cell == group, x, 0.0)
    x = x + pltpu.roll(x, CH, 1)
    return x + pltpu.roll(x, 2 * CH, 1)


def fill_weights(taps, kr_ref, t_ref, kf, kb=None):
    cell = lax.broadcasted_iota(jnp.int32, (CH, LANES), 1) // CH
    layers, rows = kr_ref.shape[:2]

    def layer_taps(layer, carry):
        packed = kr_ref[layer].astype(jnp.float32)
        for q in range(CELLS):
            kf[layer, pl.ds(q, rows, stride=CELLS), :] = spread_group(packed, q)
        if kb is not None:
            for group in range((taps + CELLS - 1) // CELLS):
                turned = kf[layer, group * LANES : (group + 1) * LANES, :].T[:CH]
                for tap in range(CELLS):
                    at = taps - 1 - (group * CELLS + tap)
                    if at >= 0:
                        kb[layer, at * CH : (at + 1) * CH, :] = spread_group(turned, tap)
        return carry

    kf[:, taps * CH :, :] = jnp.zeros_like(kf[:, taps * CH :, :])
    lax.fori_loop(0, layers, layer_taps, 0)
    source = kf if kb is None else kb

    def one(index, carry):
        layer, a = index // 3, index % 3
        bands = {}
        for b in range(3):
            values = [
                source[layer, pl.ds(pl.multiple_of((a * 9 + b * 3 + c) * CH, CH), CH), :]
                for c in range(3)
            ]
            for ww in range(CELLS + 2):
                band = jnp.zeros((CH, LANES), jnp.float32)
                for c in range(3):
                    if 0 <= ww - c < CELLS:
                        band = jnp.where(cell == ww - c, values[c], band)
                bands[b, ww] = band.astype(jnp.bfloat16)
        zero = jnp.zeros((CH, LANES), jnp.bfloat16)
        for at, (hh, ww) in enumerate(SLOTS):
            for h in range(2):
                t_ref[layer, a, at * CH : (at + 1) * CH, h * LANES : (h + 1) * LANES] = bands.get(
                    (hh - h, ww), zero
                )
        return carry

    lax.fori_loop(0, layers * 3, one, 0)


def weights_body(taps, kr_ref, t_ref, kf):
    fill_weights(taps, kr_ref, t_ref, kf)


def edge_masks(tiles):
    shape = (1, tiles, TILE)
    cell = lax.broadcasted_iota(jnp.int32, shape, 2) % LANES // CH
    row = lax.broadcasted_iota(jnp.int32, shape, 1)
    from_before = (cell == CELLS - 1) & (row > 0)
    from_after = (cell == 0) & (row < tiles - 1)
    return tuple(
        jnp.where(mask, 1.0, 0.0).astype(jnp.bfloat16) for mask in (from_before, from_after)
    )


def expand(x, out_ref, lead, pairs, tiles, masks):
    x = x.reshape(pairs, tiles, TILE)
    edge = pltpu.roll(x, 1, 1) * masks[0] + pltpu.roll(x, tiles - 1, 1) * masks[1]
    e0, e1 = edge[..., :LANES], edge[..., LANES:]
    r0, r1 = pltpu.roll(e0, LANES // 2, 2), pltpu.roll(e1, LANES // 2, 2)
    zero = jnp.zeros((1, tiles, LANES), x.dtype)
    low = jnp.concatenate([zero, x[:-1, :, LANES:]], 0)
    high = jnp.concatenate([x[1:, :, :LANES], zero], 0)
    e0 = e0 + jnp.concatenate([zero, r1[:-1]], 0)
    e1 = e1 + jnp.concatenate([r0[1:], zero], 0)
    flat = lambda v: v.reshape(pairs * tiles, v.shape[-1])
    out_ref[(*lead, slice(None), slice(0, TILE))] = flat(x)
    out_ref[(*lead, slice(None), slice(TILE, TILE + LANES))] = flat(low)
    out_ref[(*lead, slice(None), slice(TILE + LANES, 2 * TILE))] = flat(high)
    out_ref[(*lead, slice(None), slice(2 * TILE, 2 * TILE + LANES))] = flat(e0)
    out_ref[(*lead, slice(None), slice(2 * TILE + LANES, WIDE))] = flat(e1)


def conv_rows(x_ref, lead, start, rows, t_ref, layer):
    total = None
    for a in range(3):
        block = x_ref[(*lead, pl.ds(start + a, rows))].reshape(-1, WIDE)
        part = jnp.dot(block, t_ref[layer, a], preferred_element_type=jnp.float32)
        total = part if total is None else total + part
    return total


def slope_of(pre, gate):
    return gate * (1.0 + pre * (1.0 - gate))


def rounded(v):
    return v.astype(jnp.bfloat16)


def inside(v, row, depth):
    return jnp.where((row >= 0) & (row < depth), v, 0.0)


def widen(parts, lead, x_ref, x_lead, grow):
    base = 0
    for part in parts:
        rows = part.shape[len(lead)]

        def step(d, carry, part=part, base=base):
            grow(part[(*lead, d)], x_ref, (*x_lead, base + d))
            return carry

        lax.fori_loop(0, rows, step, 0)
        base += rows


def layer_one(xv, lead, out_ref, t_ref, slopes_ref=None):
    rows, cells = out_ref.shape[len(lead)], out_ref.shape[-2]
    for start, count in chunks_of(rows):
        pre = conv_rows(xv, lead, start, count, t_ref, 0)
        gate = sigmoid(pre)
        value = (pre * gate).astype(jnp.bfloat16).reshape(count, cells, TILE)
        out_ref[(*lead, pl.ds(start, count))] = value
        if slopes_ref is not None:
            slope = slope_of(pre, gate).reshape(count, cells, TILE)
            for d in range(count):
                to = start + d - (H_HIDDEN - H_G1)
                if 0 <= to < slopes_ref.shape[0]:
                    slopes_ref[to] = slope[d]


def tile_body(groups, vol, cot, *refs):
    *outs, scratch = refs
    rows, height, lanes = vol.shape
    tiles = lanes // LANES
    for at, source in enumerate((vol, cot)):
        for d in range(rows):
            for t in range(tiles):
                piece = source[d, :, t * LANES : (t + 1) * LANES].astype(jnp.float32)
                scratch[at, d, t * height : (t + 1) * height, :] = piece
            for h in range(height):
                piece = scratch[at, d, pl.ds(h, tiles, stride=height), :].astype(jnp.bfloat16)
                row, side = h // 2 * tiles, slice(h % 2 * LANES, (h % 2 + 1) * LANES)
                outs[at][d, row : row + tiles, side] = piece
                if len(outs) > 2:
                    size = outs[2].shape[2]
                    flat = d * (height // 2 * tiles) + row
                    to = flat % size
                    outs[2][flat // size, at, to : to + tiles, side] = piece


def choose_body(partner, spread, low, high, chosen, inverse):
    del low, high
    groups = spread.shape[0]

    def invert(n, carry):
        inverse[partner[n]] = n
        return carry

    lax.fori_loop(0, groups, invert, 0)

    def pick(n, carry):
        chosen[n, 0] = spread[partner[n], 0]
        chosen[n, 1:] = spread[inverse[n]]
        return carry

    lax.fori_loop(0, groups, pick, 0)


def split_body(joined, done, vol, cot):
    del done

    def part(k, carry):
        vol[0, k] = joined[k, 0]
        vol[1, k] = joined[k, 1]
        cot[k] = joined[k, 2]
        return carry

    lax.fori_loop(0, joined.shape[0], part, 0)


def own_body(pairs, tiles, low, mid, high, t_ref, hid, sl1, xv_own, xv):
    grow = functools.partial(expand, pairs=pairs, tiles=tiles, masks=edge_masks(tiles))
    rows = mid.shape[0]
    widen((low, mid, high), (), xv, (), grow)
    layer_one(xv, (), hid, t_ref, sl1)
    xv_own[...] = xv[rows - 1 : 2 * rows + 1]


def forward_body(
    depth, pairs, tiles,
    idx, low, mid, high, hid_own, cot_own, cot_other, t_ref,
    g3, g3_up, g3_down, sl2, xb_own, xs_own,
    xv, hid, xb, xs,
):
    rows = mid.shape[1]
    cells = pairs * tiles
    first = idx[0] * rows
    grow = functools.partial(expand, pairs=pairs, tiles=tiles, masks=edge_masks(tiles))

    def others(crop, carry):
        widen((low, mid, high), (crop,), xv, (crop,), grow)
        return carry

    lax.fori_loop(0, 2, others, 0)

    def first_layer(crop, carry):
        layer_one(xv, (crop,), hid, t_ref)
        return carry

    lax.fori_loop(0, 2, first_layer, 0)

    def blend(d, carry):
        own = hid_own[d].astype(jnp.float32)
        partner, other = hid[0, d].astype(jnp.float32), hid[1, d].astype(jnp.float32)
        row = first + d - H_HIDDEN
        for j, (a, b) in enumerate(((own, partner), (other, own))):
            mixed = OWN_SHARE * a + PARTNER_SHARE * b
            grow(rounded(inside(mixed, row, depth)), xb, (j, d))
        return carry

    lax.fori_loop(0, rows + 2 * H_HIDDEN, blend, 0)

    def middle(j, cot):
        for start, count in chunks_of(rows + 2 * H_TWO):
            pre = conv_rows(xb, (j,), start, count, t_ref, 1)
            gate = sigmoid(pre)
            value = (pre * gate).reshape(count, cells, TILE)
            slope = slope_of(pre, gate).reshape(count, cells, TILE)
            for d in range(count):
                sl2[j, start + d] = slope[d]
                to = start + d - (H_TWO - 1)
                if 0 <= to < rows + 2:
                    grow(rounded(inside(value[d], first + to - 1, depth)), xs, (j, to))
        for start, count in chunks_of(rows):
            pre = conv_rows(xs, (j,), start, count, t_ref, 2)
            slope = slope_of(pre, sigmoid(pre)).reshape(count, cells, TILE)
            for d in range(count):
                at = start + d
                grad = rounded(cot[at].astype(jnp.float32) * slope[d])
                g3[j, at] = grad
                if at >= rows - H_G3:
                    g3_up[j, at - (rows - H_G3)] = grad
                if at < H_G3:
                    g3_down[j, at] = grad

    middle(0, cot_own)
    middle(1, cot_other)
    xb_own[...] = xb[0, H_HIDDEN - 1 : H_HIDDEN + rows + 1]
    xs_own[...] = xs[0]


def kernel_terms(values, gradient, rw):
    rows = gradient.shape[0]
    gradient = gradient.reshape(-1, TILE)
    for a in range(3):
        block = values[a : a + rows].reshape(-1, WIDE)
        terms = lax.dot_general(
            block, gradient, (((0,), (0,)), ((), ())), preferred_element_type=jnp.float32
        )
        for b in range(3):
            for c in range(3):
                at = (a * 9 + b * 3 + c) * CH
                for w in range(CELLS):
                    s0, s1 = SLOT_OF[b, w + c] * CH, SLOT_OF[b + 1, w + c] * CH
                    rw[w, at : at + CH] = (
                        terms[s0 : s0 + CH, :LANES] + terms[s1 : s1 + CH, LANES:]
                    )
    count = rw.shape[1] // CELLS
    cell = lax.broadcasted_iota(jnp.int32, (count, LANES), 1) // CH
    dense = jnp.zeros((count, LANES), jnp.float32)
    for q in range(CELLS):
        part = None
        for w in range(CELLS):
            piece = rw[w, pl.ds(q, count, stride=CELLS), :]
            if q != w:
                piece = pltpu.roll(piece, (q - w) % CELLS * CH, 1)
            part = piece if part is None else part + piece
        dense = jnp.where(cell == q, part, dense)
    return dense.astype(jnp.bfloat16)


def between_body(taps, kr_ref, xs_own, g3, t_ref, terms, kf, kb, rw):
    fill_weights(taps, kr_ref, t_ref, kf, kb)
    terms[...] = kernel_terms(xs_own[...], g3[0], rw)


def back_two(j, x_ref, sl2, x2_ref, t_ref, first, depth, grow):
    rows, cells = x2_ref.shape[-3:-1]
    for start, count in chunks_of(rows):
        back = conv_rows(x_ref, (), start, count, t_ref, 2).reshape(count, cells, TILE)
        for d in range(count):
            at = start + d
            grad = inside(back[d] * sl2[j, at], first + at - H_G2, depth)
            grow(rounded(grad), x2_ref, (at,))


def own_back_body(
    depth, pairs, tiles,
    idx, low, mid, high, sl2, xb_own, terms_three, t_ref,
    xg2, terms,
    xg3, rw,
):
    rows = mid.shape[1]
    grow = functools.partial(expand, pairs=pairs, tiles=tiles, masks=edge_masks(tiles))
    widen((low, mid, high), (0,), xg3, (), grow)
    back_two(0, xg3, sl2, xg2, t_ref, idx[0] * rows, depth, grow)
    two = kernel_terms(xb_own[...], xg2[H_G2 : H_G2 + rows, :, :TILE], rw)
    for to in range(terms.shape[0]):
        terms[to, 0] = two
        terms[to, 1] = terms_three[...]


def back_body(
    depth, pairs, tiles,
    idx, low, mid, high, sl1, sl2, xv_own, xg2_own, t_ref,
    xg1, terms,
    xg3, xg2, rw,
):
    rows = mid.shape[1]
    cells = pairs * tiles
    first = idx[0] * rows
    grow = functools.partial(expand, pairs=pairs, tiles=tiles, masks=edge_masks(tiles))
    widen((low, mid, high), (1,), xg3, (), grow)
    back_two(1, xg3, sl2, xg2, t_ref, first, depth, grow)
    for start, count in chunks_of(rows + 2 * H_G1):
        own = rounded(conv_rows(xg2_own, (), start, count, t_ref, 1)).astype(jnp.float32)
        other = rounded(conv_rows(xg2, (), start, count, t_ref, 1)).astype(jnp.float32)
        mixed = (OWN_SHARE * own + PARTNER_SHARE * other).reshape(count, cells, TILE)
        for d in range(count):
            at = start + d
            grad = inside(mixed[d] * sl1[at], first + at - H_G1, depth)
            grow(rounded(grad), xg1, (at,))
    one = kernel_terms(xv_own[...], xg1[H_G1 : H_G1 + rows, :, :TILE], rw)
    for to in range(terms.shape[0]):
        terms[to] = one


def last_body(pairs, tiles, xg1, t_ref, gv, scratch):
    rows, height, _ = gv.shape
    cells = pairs * tiles
    for start, count in chunks_of(rows):
        back = conv_rows(xg1, (), start, count, t_ref, 0).reshape(count, cells, TILE)
        for d in range(count):
            for h in range(height):
                row, side = h // 2 * tiles, slice(h % 2 * LANES, (h % 2 + 1) * LANES)
                scratch[start + d, pl.ds(h, tiles, stride=height), :] = back[
                    d, row : row + tiles, side
                ]
            for t in range(tiles):
                gv[start + d, :, t * LANES : (t + 1) * LANES] = scratch[
                    start + d, t * height : (t + 1) * height, :
                ].astype(jnp.bfloat16)


def total_body(ones, others, out):
    add = lambda parts: functools.reduce(lambda a, b: a + b, parts)
    count = ones.shape[0]
    out[0] = add([ones[i].astype(jnp.float32) for i in range(count)])
    for layer in range(others.shape[1]):
        out[1 + layer] = add([others[i, layer].astype(jnp.float32) for i in range(count)])


def neighbours(up, down):
    count = lax.axis_size("depth")
    forward = [(i, i + 1) for i in range(count - 1)]
    backward = [(target, source) for source, target in forward]
    return lax.ppermute(up, "depth", forward), lax.ppermute(down, "depth", backward)


def call(kernel, outs, scratch, inputs, macs=0, waits=0):
    vmem, smem, anywhere = (
        pl.BlockSpec(memory_space=space) for space in (pltpu.VMEM, pltpu.SMEM, pl.ANY)
    )
    specs = [smem if x.dtype == jnp.int32 else vmem for x in inputs]
    specs[len(specs) - waits :] = [anywhere] * waits
    results = pl.pallas_call(
        kernel,
        out_shape=tuple(jax.ShapeDtypeStruct(shape, dtype) for shape, dtype in outs),
        in_specs=specs,
        out_specs=(vmem,) * len(outs),
        scratch_shapes=scratch,
        compiler_params=pltpu.CompilerParams(vmem_limit_bytes=VMEM_LIMIT),
        cost_estimate=pl.CostEstimate(
            flops=2 * macs, bytes_accessed=4 * 2**20, transcendentals=0
        ),
    )(*inputs)
    return results if len(results) > 1 else results[0]


def per_device(volume, kernels, partner, cotangent):
    _, rows, height, lanes = volume.shape
    pairs, tiles = height // 2, lanes // LANES
    cells = pairs * tiles
    groups, count = lax.axis_size("sample"), lax.axis_size("depth")
    depth = rows * count
    layers, taps, _ = kernels.shape
    bf16, f32 = jnp.bfloat16, jnp.float32
    row_macs = 3 * cells * WIDE * TILE
    size = rows * cells // groups
    packed_rows = taps * CH // CELLS
    wide = lambda *lead: pltpu.VMEM((*lead, cells, WIDE), bf16)
    index = lax.axis_index("depth").astype(jnp.int32).reshape(1)
    packed = kernels.reshape(layers, packed_rows, LANES)
    banded = ((layers, 3, WIDE, TILE), bf16)
    padded = pltpu.VMEM((layers, (taps + CELLS - 1) // CELLS * LANES, LANES), f32)
    rw = pltpu.VMEM((CELLS, taps * CH, LANES), f32)
    field = ((rows, cells, TILE), bf16)
    traded = [((groups, 2, size, TILE), bf16)] if size % tiles == 0 else []

    vol_own, cot_own, *pieces = call(
        functools.partial(tile_body, groups),
        [field, field, *traded],
        [pltpu.VMEM((2, rows, height * tiles, LANES), f32)],
        [volume[0], cotangent[0]],
    )
    if traded:
        (pieces,) = pieces
    else:
        pieces = jnp.stack([vol_own, cot_own]).reshape(2, groups, size, TILE).swapaxes(0, 1)
    spread = lax.all_to_all(pieces, "sample", split_axis=0, concat_axis=0, tiled=True)
    low, high = neighbours(vol_own, vol_own)
    chosen = call(
        choose_body,
        [((groups, 3, size, TILE), bf16)],
        [pltpu.SMEM((groups,), jnp.int32)],
        [partner, spread, low, high],
        waits=2,
    )
    joined = lax.all_to_all(chosen, "sample", split_axis=0, concat_axis=0, tiled=True)
    fwd = call(functools.partial(weights_body, taps), [banded], [padded], [packed], 2**28)
    hid_rows = rows + 2 * H_HIDDEN
    hid_own, sl1, xv_own = call(
        functools.partial(own_body, pairs, tiles),
        [
            ((hid_rows, cells, TILE), bf16),
            ((rows + 2 * H_G1, cells, TILE), f32),
            ((rows + 2, cells, WIDE), bf16),
        ],
        [wide(3 * rows)],
        [low, vol_own, high, fwd],
        hid_rows * row_macs,
    )
    vol, cot_other = call(
        split_body,
        [((2, groups, size, TILE), bf16), ((groups, size, TILE), bf16)],
        [],
        [joined, hid_own],
        waits=1,
    )
    vol, cot_other = vol.reshape(2, rows, cells, TILE), cot_other.reshape(rows, cells, TILE)

    low, high = neighbours(vol, vol)
    g3, g3_up, g3_down, sl2, xb_own, xs_own = call(
        functools.partial(forward_body, depth, pairs, tiles),
        [
            ((2, rows, cells, TILE), bf16),
            ((2, H_G3, cells, TILE), bf16),
            ((2, H_G3, cells, TILE), bf16),
            ((2, rows + 2 * H_TWO, cells, TILE), f32),
            ((rows + 2, cells, WIDE), bf16),
            ((rows + 2, cells, WIDE), bf16),
        ],
        [
            wide(2, 3 * rows),
            pltpu.VMEM((2, hid_rows, cells, TILE), bf16),
            wide(2, hid_rows),
            wide(2, rows + 2),
        ],
        [index, low, vol, high, hid_own, cot_own, cot_other, fwd],
        (2 * hid_rows + 2 * (rows + 4) + 2 * rows) * row_macs,
    )

    low, high = neighbours(g3_up, g3_down)
    bwd, terms_three = call(
        functools.partial(between_body, taps),
        [banded, ((packed_rows, LANES), bf16)],
        [padded, padded, rw],
        [packed, xs_own, g3],
        rows * row_macs,
    )
    xg2_own, terms = call(
        functools.partial(own_back_body, depth, pairs, tiles),
        [
            ((rows + 2 * H_G2, cells, WIDE), bf16),
            ((count, 2, packed_rows, LANES), bf16),
        ],
        [wide(rows + 2 * H_G3), rw],
        [index, low, g3, high, sl2, xb_own, terms_three, bwd],
        (2 * rows + 4) * row_macs,
    )
    later = lax.all_to_all(terms, "depth", split_axis=0, concat_axis=0, tiled=True)
    xg1, terms = call(
        functools.partial(back_body, depth, pairs, tiles),
        [((rows + 2 * H_G1, cells, WIDE), bf16), ((count, packed_rows, LANES), bf16)],
        [wide(rows + 2 * H_G3), wide(rows + 2 * H_G2), rw],
        [index, low, g3, high, sl1, sl2, xv_own, xg2_own, bwd],
        (4 * rows + 8) * row_macs,
    )
    first = lax.all_to_all(terms, "depth", split_axis=0, concat_axis=0, tiled=True)
    grad_volume = call(
        functools.partial(last_body, pairs, tiles),
        [((rows, height, lanes), bf16)],
        [pltpu.VMEM((rows, height * tiles, LANES), f32)],
        [xg1, bwd],
        rows * row_macs,
    )
    total = call(total_body, [((layers, packed_rows, LANES), f32)], [], [first, later])
    return (grad_volume[None], total.reshape(1, *kernels.shape))


def solution(mesh):
    in_specs = (P("sample", "depth", None, None), P(), P(), P("sample", "depth", None, None))
    out_specs = (P("sample", "depth", None, None), P("sample", None, None, None))
    return jax.shard_map(
        per_device, mesh=mesh, in_specs=in_specs, out_specs=out_specs, check_vma=False
    )
```

```python
import functools

import jax
import jax.numpy as jnp
from jax import lax
from jax.experimental import pallas as pl
from jax.experimental.pallas import tpu as pltpu
from jax.sharding import PartitionSpec as P

CH = 32
OWN_SHARE = 0.6
PARTNER_SHARE = 0.4
LANES = 128
CELLS = LANES // CH
TILE = 2 * LANES
WIDE = 3 * TILE
VMEM_LIMIT = 40 * 2**20

SLOTS = (
    [(1 + h, 1 + w) for h in range(2) for w in range(CELLS)]
    + [(0, 1 + w) for w in range(CELLS)]
    + [(3, 1 + w) for w in range(CELLS)]
    + [(1, 5), (0, 0), (0, 5), (1, 0)]
    + [(2, 5), (3, 0), (3, 5), (2, 0)]
)
SLOT_OF = {cell: at for at, cell in enumerate(SLOTS)}

H_HIDDEN, H_TWO, H_G3, H_G2, H_G1 = 3, 2, 3, 2, 1


def chunks_of(rows):
    count = max(1, (rows + 2) // 5)
    base, extra = divmod(rows, count)
    start, result = 0, []
    for index in range(count):
        size = base + (index < extra)
        result.append((start, size))
        start += size
    return result


def sigmoid(v):
    return 0.5 + 0.5 * jnp.tanh(0.5 * v)


def spread_group(x, group):
    cell = lax.broadcasted_iota(jnp.int32, x.shape, 1) // CH
    x = jnp.where(cell == group, x, 0.0)
    x = x + pltpu.roll(x, CH, 1)
    return x + pltpu.roll(x, 2 * CH, 1)


def fill_weights(taps, kr_ref, t_ref, kf, kb=None):
    cell = lax.broadcasted_iota(jnp.int32, (CH, LANES), 1) // CH
    layers, rows = kr_ref.shape[:2]
    source = kf if kb is None else kb
    if kb is not None:
        eye = jnp.where(
            lax.broadcasted_iota(jnp.int32, (CH, LANES), 0)
            == lax.broadcasted_iota(jnp.int32, (CH, LANES), 1),
            1.0,
            0.0,
        ).astype(jnp.bfloat16)
    for layer in range(layers):
        packed = kr_ref[layer].astype(jnp.float32)
        for q in range(CELLS):
            kf[layer, pl.ds(q, rows, stride=CELLS), :] = spread_group(packed, q)
        if kb is not None:
            kf[layer, taps * CH :, :] = jnp.zeros_like(kf[layer, taps * CH :, :])
            turned = lax.dot_general(
                eye,
                kf[layer].astype(jnp.bfloat16),
                (((1,), (1,)), ((), ())),
                preferred_element_type=jnp.float32,
            )
            for tap in range(taps):
                at, lane = taps - 1 - tap, tap // CELLS * LANES
                kb[layer, at * CH : (at + 1) * CH, :] = spread_group(
                    turned[:, lane : lane + LANES], tap % CELLS
                )

    zero = jnp.zeros((CH, LANES), jnp.bfloat16)
    for layer in range(layers):
        for a in range(3):
            bands = {}
            for b in range(3):
                first = (a * 9 + b * 3) * CH
                values = [
                    source[layer, first + c * CH : first + (c + 1) * CH, :] for c in range(3)
                ]
                for ww in range(CELLS + 2):
                    band = jnp.zeros((CH, LANES), jnp.float32)
                    for c in range(3):
                        if 0 <= ww - c < CELLS:
                            band = jnp.where(cell == ww - c, values[c], band)
                    bands[b, ww] = band.astype(jnp.bfloat16)
            for at, (hh, ww) in enumerate(SLOTS):
                for h in range(2):
                    t_ref[
                        layer, a, at * CH : (at + 1) * CH, h * LANES : (h + 1) * LANES
                    ] = bands.get((hh - h, ww), zero)


def edge_masks(tiles):
    shape = (1, tiles, TILE)
    cell = lax.broadcasted_iota(jnp.int32, shape, 2) % LANES // CH
    row = lax.broadcasted_iota(jnp.int32, shape, 1)
    from_before = (cell == CELLS - 1) & (row > 0)
    from_after = (cell == 0) & (row < tiles - 1)
    return tuple(
        jnp.where(mask, 1.0, 0.0).astype(jnp.bfloat16) for mask in (from_before, from_after)
    )


def expand(x, out_ref, lead, pairs, tiles, masks):
    x = x.reshape(pairs, tiles, TILE)
    edge = pltpu.roll(x, 1, 1) * masks[0] + pltpu.roll(x, tiles - 1, 1) * masks[1]
    e0, e1 = edge[..., :LANES], edge[..., LANES:]
    r0, r1 = pltpu.roll(e0, LANES // 2, 2), pltpu.roll(e1, LANES // 2, 2)
    zero = jnp.zeros((1, tiles, LANES), x.dtype)
    low = jnp.concatenate([zero, x[:-1, :, LANES:]], 0)
    high = jnp.concatenate([x[1:, :, :LANES], zero], 0)
    e0 = e0 + jnp.concatenate([zero, r1[:-1]], 0)
    e1 = e1 + jnp.concatenate([r0[1:], zero], 0)
    flat = lambda v: v.reshape(pairs * tiles, v.shape[-1])
    out_ref[(*lead, slice(None), slice(0, TILE))] = flat(x)
    out_ref[(*lead, slice(None), slice(TILE, TILE + LANES))] = flat(low)
    out_ref[(*lead, slice(None), slice(TILE + LANES, 2 * TILE))] = flat(high)
    out_ref[(*lead, slice(None), slice(2 * TILE, 2 * TILE + LANES))] = flat(e0)
    out_ref[(*lead, slice(None), slice(2 * TILE + LANES, WIDE))] = flat(e1)


def conv_rows(x_ref, lead, start, rows, t_ref, layer):
    total = None
    for a in range(3):
        block = x_ref[(*lead, pl.ds(start + a, rows))].reshape(-1, WIDE)
        part = jnp.dot(block, t_ref[layer, a], preferred_element_type=jnp.float32)
        total = part if total is None else total + part
    return total


def slope_of(pre, gate):
    return gate * (1.0 + pre * (1.0 - gate))


def rounded(v):
    return v.astype(jnp.bfloat16)


def inside(v, row, depth):
    return jnp.where((row >= 0) & (row < depth), v, 0.0)


def widen(parts, lead, x_ref, x_lead, grow):
    base = 0
    for part in parts:
        rows = part.shape[len(lead)]
        for d in range(rows):
            grow(part[(*lead, d)], x_ref, (*x_lead, base + d))
        base += rows


def layer_one(xv, lead, out_ref, t_ref, slopes_ref=None):
    rows, cells = out_ref.shape[len(lead)], out_ref.shape[-2]
    for start, count in chunks_of(rows):
        pre = conv_rows(xv, lead, start, count, t_ref, 0)
        gate = sigmoid(pre)
        value = (pre * gate).astype(jnp.bfloat16).reshape(count, cells, TILE)
        out_ref[(*lead, pl.ds(start, count))] = value
        if slopes_ref is not None:
            slope = slope_of(pre, gate).reshape(count, cells, TILE)
            for d in range(count):
                to = start + d - (H_HIDDEN - H_G1)
                if 0 <= to < slopes_ref.shape[0]:
                    slopes_ref[to] = slope[d]


def tiled_rows(source, d, scratch, at):
    _, height, lanes = source.shape
    tiles = lanes // LANES
    for t in range(tiles):
        piece = source[d, :, t * LANES : (t + 1) * LANES].astype(jnp.float32)
        scratch[at, t * height : (t + 1) * height, :] = piece
    for h in range(height):
        piece = scratch[at, pl.ds(h, tiles, stride=height), :].astype(jnp.bfloat16)
        yield h // 2 * tiles, slice(h % 2 * LANES, (h % 2 + 1) * LANES), piece


def pieces_body(vol_hbm, cot_hbm, out, vol, cot, scratch, sems):
    size = out.shape[2]
    fields = ((vol_hbm, vol), (cot_hbm, cot))
    copies = [pltpu.make_async_copy(*pair, sems.at[at]) for at, pair in enumerate(fields)]
    for copy in copies:
        copy.start()
    rows = vol.shape[0]
    for at, (_, source) in enumerate(fields):
        copies[at].wait()
        for d in range(rows):
            for row, side, piece in tiled_rows(source, d, scratch, at * rows + d):
                flat = d * (out.shape[0] * size // rows) + row
                to = flat % size
                out[flat // size, at, to : to + piece.shape[0], side] = piece


def own_body(
    taps, pairs, tiles,
    kr_ref, low_hbm, mid_hbm, high_hbm, cot_hbm,
    t_ref, hid, sl1, xv_own, cot_own,
    kf, xv, raw, field, scratch, sems,
):
    rows = cot_hbm.shape[0]
    parts = (low_hbm, mid_hbm, high_hbm, cot_hbm)
    copies = [
        pltpu.make_async_copy(part, raw.at[at], sems.at[at]) for at, part in enumerate(parts)
    ]
    for copy in copies:
        copy.start()
    fill_weights(taps, kr_ref, t_ref, kf)
    grow = functools.partial(expand, pairs=pairs, tiles=tiles, masks=edge_masks(tiles))
    for copy in copies:
        copy.wait()
    for at in range(4):
        for d in range(rows):
            for row, side, piece in tiled_rows(raw.at[at], d, scratch, at * rows + d):
                if at < 3:
                    field[at * rows + d, row : row + tiles, side] = piece
                else:
                    cot_own[d, row : row + tiles, side] = piece
    widen((field,), (), xv, (), grow)
    layer_one(xv, (), hid, t_ref, sl1)
    xv_own[...] = xv[rows - 1 : 2 * rows + 1]


def forward_body(
    depth, pairs, tiles,
    idx, low, mid, high, hid_own, cot_own, cot_other, t_ref,
    g3, g3_up, g3_down, sl2, xb_own, xs_own,
    xv, hid, xb, xs,
):
    rows = mid.shape[1]
    cells = pairs * tiles
    first = idx[0] * rows
    grow = functools.partial(expand, pairs=pairs, tiles=tiles, masks=edge_masks(tiles))

    for crop in range(2):
        widen((low, mid, high), (crop,), xv, (crop,), grow)
        layer_one(xv, (crop,), hid, t_ref)

    for d in range(rows + 2 * H_HIDDEN):
        own = hid_own[d].astype(jnp.float32)
        partner, other = hid[0, d].astype(jnp.float32), hid[1, d].astype(jnp.float32)
        row = first + d - H_HIDDEN
        for j, (a, b) in enumerate(((own, partner), (other, own))):
            mixed = OWN_SHARE * a + PARTNER_SHARE * b
            grow(rounded(inside(mixed, row, depth)), xb, (j, d))

    def middle(j, cot):
        for start, count in chunks_of(rows + 2 * H_TWO):
            pre = conv_rows(xb, (j,), start, count, t_ref, 1)
            gate = sigmoid(pre)
            value = (pre * gate).reshape(count, cells, TILE)
            slope = slope_of(pre, gate).reshape(count, cells, TILE)
            for d in range(count):
                sl2[j, start + d] = slope[d]
                to = start + d - (H_TWO - 1)
                if 0 <= to < rows + 2:
                    grow(rounded(inside(value[d], first + to - 1, depth)), xs, (j, to))
        for start, count in chunks_of(rows):
            pre = conv_rows(xs, (j,), start, count, t_ref, 2)
            slope = slope_of(pre, sigmoid(pre)).reshape(count, cells, TILE)
            for d in range(count):
                at = start + d
                grad = rounded(cot[at].astype(jnp.float32) * slope[d])
                g3[j, at] = grad
                if at >= rows - H_G3:
                    g3_up[j, at - (rows - H_G3)] = grad
                if at < H_G3:
                    g3_down[j, at] = grad

    middle(0, cot_own)
    middle(1, cot_other)
    xb_own[...] = xb[0, H_HIDDEN - 1 : H_HIDDEN + rows + 1]
    xs_own[...] = xs[0]


def kernel_terms(values, gradient, rw):
    rows = gradient.shape[0]
    gradient = gradient.reshape(-1, TILE)
    for a in range(3):
        block = values[a : a + rows].reshape(-1, WIDE)
        terms = lax.dot_general(
            block, gradient, (((0,), (0,)), ((), ())), preferred_element_type=jnp.float32
        )
        for b in range(3):
            for c in range(3):
                at = (a * 9 + b * 3 + c) * CH
                for w in range(CELLS):
                    s0, s1 = SLOT_OF[b, w + c] * CH, SLOT_OF[b + 1, w + c] * CH
                    rw[w, at : at + CH] = (
                        terms[s0 : s0 + CH, :LANES] + terms[s1 : s1 + CH, LANES:]
                    )
    count = rw.shape[1] // CELLS
    cell = lax.broadcasted_iota(jnp.int32, (count, LANES), 1) // CH
    dense = jnp.zeros((count, LANES), jnp.float32)
    for q in range(CELLS):
        part = None
        for w in range(CELLS):
            piece = rw[w, pl.ds(q, count, stride=CELLS), :]
            if q != w:
                piece = pltpu.roll(piece, (q - w) % CELLS * CH, 1)
            part = piece if part is None else part + piece
        dense = jnp.where(cell == q, part, dense)
    return dense.astype(jnp.bfloat16)


def between_body(taps, kr_ref, xs_own, g3, t_ref, terms, kf, kb, rw):
    fill_weights(taps, kr_ref, t_ref, kf, kb)
    terms[...] = kernel_terms(xs_own[...], g3[0], rw)


def back_two(j, x_ref, sl2, x2_ref, t_ref, first, depth, grow):
    rows, cells = x2_ref.shape[-3:-1]
    for start, count in chunks_of(rows):
        back = conv_rows(x_ref, (), start, count, t_ref, 2).reshape(count, cells, TILE)
        for d in range(count):
            at = start + d
            grad = inside(back[d] * sl2[j, at], first + at - H_G2, depth)
            grow(rounded(grad), x2_ref, (at,))


def back_body(
    depth, pairs, tiles,
    idx, low, mid, high, sl1, sl2, xv_own, xb_own, t_ref,
    xg1, terms,
    xg3, xg2, rw,
):
    rows = mid.shape[1]
    cells = pairs * tiles
    first = idx[0] * rows
    grow = functools.partial(expand, pairs=pairs, tiles=tiles, masks=edge_masks(tiles))
    for j in range(2):
        widen((low, mid, high), (j,), xg3.at[j], (), grow)
        back_two(j, xg3.at[j], sl2, xg2.at[j], t_ref, first, depth, grow)
    for start, count in chunks_of(rows + 2 * H_G1):
        own, other = (
            rounded(conv_rows(xg2, (j,), start, count, t_ref, 1)).astype(jnp.float32)
            for j in range(2)
        )
        mixed = (OWN_SHARE * own + PARTNER_SHARE * other).reshape(count, cells, TILE)
        for d in range(count):
            at = start + d
            grad = inside(mixed[d] * sl1[at], first + at - H_G1, depth)
            grow(rounded(grad), xg1, (at,))
    terms[1] = kernel_terms(xb_own[...], xg2[0, H_G2 : H_G2 + rows, :, :TILE], rw)
    terms[0] = kernel_terms(xv_own[...], xg1[H_G1 : H_G1 + rows, :, :TILE], rw)


def last_body(pairs, tiles, xg1, t_ref, gv, scratch):
    rows, height, _ = gv.shape
    cells = pairs * tiles
    for start, count in chunks_of(rows):
        back = conv_rows(xg1, (), start, count, t_ref, 0).reshape(count, cells, TILE)
        for d in range(count):
            for h in range(height):
                row, side = h // 2 * tiles, slice(h % 2 * LANES, (h % 2 + 1) * LANES)
                scratch[start + d, pl.ds(h, tiles, stride=height), :] = back[
                    d, row : row + tiles, side
                ]
            for t in range(tiles):
                gv[start + d, :, t * LANES : (t + 1) * LANES] = scratch[
                    start + d, t * height : (t + 1) * height, :
                ].astype(jnp.bfloat16)


def total_body(own, near, far, farther, three, out):
    for layer in range(own.shape[0]):
        one, two, three_, four = (
            part[layer].astype(jnp.float32) for part in (own, near, far, farther)
        )
        out[layer] = (one + two) + (three_ + four)
    out[own.shape[0]] = three[...].astype(jnp.float32)


def neighbours(up, down):
    count = lax.axis_size("depth")
    forward = [(i, i + 1) for i in range(count - 1)]
    backward = [(target, source) for source, target in forward]
    return lax.ppermute(up, "depth", forward), lax.ppermute(down, "depth", backward)


def call(kernel, outs, scratch, inputs, macs=0, far=()):
    vmem, smem, anywhere = (
        pl.BlockSpec(memory_space=space) for space in (pltpu.VMEM, pltpu.SMEM, pl.ANY)
    )
    specs = [
        anywhere if at in far else smem if x.dtype == jnp.int32 else vmem
        for at, x in enumerate(inputs)
    ]
    results = pl.pallas_call(
        kernel,
        out_shape=tuple(jax.ShapeDtypeStruct(shape, dtype) for shape, dtype in outs),
        in_specs=specs,
        out_specs=(vmem,) * len(outs),
        scratch_shapes=scratch,
        compiler_params=pltpu.CompilerParams(vmem_limit_bytes=VMEM_LIMIT),
        cost_estimate=pl.CostEstimate(
            flops=2 * macs, bytes_accessed=4 * 2**20, transcendentals=0
        ),
    )(*inputs)
    return results if len(results) > 1 else results[0]


def per_device(volume, kernels, partner, cotangent):
    _, rows, height, lanes = volume.shape
    pairs, tiles = height // 2, lanes // LANES
    cells = pairs * tiles
    groups, count = lax.axis_size("sample"), lax.axis_size("depth")
    depth = rows * count
    layers, taps, _ = kernels.shape
    bf16, f32 = jnp.bfloat16, jnp.float32
    row_macs = 3 * cells * WIDE * TILE
    size = rows * cells // groups
    packed_rows = taps * CH // CELLS
    wide = lambda *lead: pltpu.VMEM((*lead, cells, WIDE), bf16)
    index = lax.axis_index("depth").astype(jnp.int32).reshape(1)
    packed = kernels.reshape(layers, packed_rows, LANES)
    banded = ((layers, 3, WIDE, TILE), bf16)
    padded = pltpu.VMEM((layers, (taps + CELLS - 1) // CELLS * LANES, LANES), f32)
    rw = pltpu.VMEM((CELLS, taps * CH, LANES), f32)
    raw_rows = pltpu.VMEM((rows, height, lanes), bf16)
    volume, cotangent = volume[0], cotangent[0]

    if size % tiles == 0:
        pieces = call(
            pieces_body,
            [((groups, 2, size, TILE), bf16)],
            [
                raw_rows,
                raw_rows,
                pltpu.VMEM((2 * rows, height * tiles, LANES), f32),
                pltpu.SemaphoreType.DMA((2,)),
            ],
            [volume, cotangent],
            far=(0, 1),
        )
    else:
        split = jnp.stack([volume, cotangent]).reshape(2, rows, pairs, 2, tiles, LANES)
        pieces = split.transpose(0, 1, 2, 4, 3, 5).reshape(2, groups, size, TILE).swapaxes(0, 1)
    spread = lax.all_to_all(pieces, "sample", split_axis=0, concat_axis=0, tiled=True)
    low, high = neighbours(volume, volume)
    spread, low, high = lax.optimization_barrier((spread, low, high))

    ids = jnp.arange(groups, dtype=jnp.int32)
    inverse = jnp.sum(jnp.where(partner[:, None] == ids[None, :], ids[:, None], 0), axis=0)
    wanted = jnp.stack([2 * partner, 2 * inverse, 2 * inverse + 1], axis=1)
    chosen = jnp.take(spread.reshape(2 * groups, -1, TILE), wanted, axis=0)
    joined = lax.all_to_all(chosen, "sample", split_axis=0, concat_axis=0, tiled=True)
    others = jnp.swapaxes(joined, 0, 1).reshape(3, rows, cells, TILE)
    vol, cot_other = others[:2], others[2]
    vol_low, vol_high = neighbours(vol, vol)
    hid_rows = rows + 2 * H_HIDDEN
    fwd, hid_own, sl1, xv_own, cot_own = call(
        functools.partial(own_body, taps, pairs, tiles),
        [
            banded,
            ((hid_rows, cells, TILE), bf16),
            ((rows + 2 * H_G1, cells, TILE), f32),
            ((rows + 2, cells, WIDE), bf16),
            ((rows, cells, TILE), bf16),
        ],
        [
            padded,
            wide(3 * rows),
            pltpu.VMEM((4, rows, height, lanes), bf16),
            pltpu.VMEM((3 * rows, cells, TILE), bf16),
            pltpu.VMEM((4 * rows, height * tiles, LANES), f32),
            pltpu.SemaphoreType.DMA((4,)),
        ],
        [packed, low, volume, high, cotangent],
        hid_rows * row_macs,
        far=(1, 2, 3, 4),
    )

    g3, g3_up, g3_down, sl2, xb_own, xs_own = call(
        functools.partial(forward_body, depth, pairs, tiles),
        [
            ((2, rows, cells, TILE), bf16),
            ((2, H_G3, cells, TILE), bf16),
            ((2, H_G3, cells, TILE), bf16),
            ((2, rows + 2 * H_TWO, cells, TILE), f32),
            ((rows + 2, cells, WIDE), bf16),
            ((rows + 2, cells, WIDE), bf16),
        ],
        [
            wide(2, 3 * rows),
            pltpu.VMEM((2, hid_rows, cells, TILE), bf16),
            wide(2, hid_rows),
            wide(2, rows + 2),
        ],
        [index, vol_low, vol, vol_high, hid_own, cot_own, cot_other, fwd],
        (2 * hid_rows + 2 * (rows + 4) + 2 * rows) * row_macs,
    )

    low, high = neighbours(g3_up, g3_down)
    bwd, three = call(
        functools.partial(between_body, taps),
        [banded, ((packed_rows, LANES), bf16)],
        [padded, padded, rw],
        [packed, xs_own, g3],
        rows * row_macs,
    )
    three = lax.psum(three, "depth")
    xg1, terms = call(
        functools.partial(back_body, depth, pairs, tiles),
        [((rows + 2 * H_G1, cells, WIDE), bf16), ((2, packed_rows, LANES), bf16)],
        [wide(2, rows + 2 * H_G3), wide(2, rows + 2 * H_G2), rw],
        [index, low, g3, high, sl1, sl2, xv_own, xb_own, bwd],
        (6 * rows + 12) * row_macs,
    )
    every = [
        lax.ppermute(terms, "depth", [(i, i ^ hop) for i in range(count)])
        for hop in range(1, count)
    ]
    grad_volume = call(
        functools.partial(last_body, pairs, tiles),
        [((rows, height, lanes), bf16)],
        [pltpu.VMEM((rows, height * tiles, LANES), f32)],
        [xg1, bwd],
        rows * row_macs,
    )
    total = call(
        total_body, [((layers, packed_rows, LANES), f32)], [], [terms, *every, three]
    )
    return (grad_volume[None], total.reshape(1, *kernels.shape))


def solution(mesh):
    in_specs = (P("sample", "depth", None, None), P(), P(), P("sample", "depth", None, None))
    out_specs = (P("sample", "depth", None, None), P("sample", None, None, None))
    return jax.shard_map(
        per_device, mesh=mesh, in_specs=in_specs, out_specs=out_specs, check_vma=False
    )
```

```python
import functools

import jax
import jax.numpy as jnp
from jax import lax
from jax.experimental import pallas as pl
from jax.experimental.pallas import tpu as pltpu
from jax.sharding import PartitionSpec as P

CH = 32
OWN_SHARE = 0.6
PARTNER_SHARE = 0.4
LANES = 128
CELLS = LANES // CH
TILE = 2 * LANES
WIDE = 3 * TILE
VMEM_LIMIT = 40 * 2**20

SLOTS = (
    [(1 + h, 1 + w) for h in range(2) for w in range(CELLS)]
    + [(0, 1 + w) for w in range(CELLS)]
    + [(3, 1 + w) for w in range(CELLS)]
    + [(1, 5), (0, 0), (0, 5), (1, 0)]
    + [(2, 5), (3, 0), (3, 5), (2, 0)]
)
SLOT_OF = {cell: at for at, cell in enumerate(SLOTS)}

H_HIDDEN, H_TWO, H_G3, H_G2, H_G1 = 3, 2, 3, 2, 1


def chunks_of(rows):
    count = max(1, (rows + 2) // 5)
    base, extra = divmod(rows, count)
    start, result = 0, []
    for index in range(count):
        size = base + (index < extra)
        result.append((start, size))
        start += size
    return result


def sigmoid(v):
    return 0.5 + 0.5 * jnp.tanh(0.5 * v)


def spread_group(x, group):
    cell = lax.broadcasted_iota(jnp.int32, x.shape, 1) // CH
    x = jnp.where(cell == group, x, 0.0)
    x = x + pltpu.roll(x, CH, 1)
    return x + pltpu.roll(x, 2 * CH, 1)


def taps_body(taps, kr_ref, fwd_ref, bwd_ref, scratch):
    layers, rows = kr_ref.shape[:2]
    eye = jnp.where(
        lax.broadcasted_iota(jnp.int32, (CH, LANES), 0)
        == lax.broadcasted_iota(jnp.int32, (CH, LANES), 1),
        1.0,
        0.0,
    ).astype(jnp.bfloat16)
    for layer in range(layers):
        packed = kr_ref[layer].astype(jnp.float32)
        for q in range(CELLS):
            scratch[layer, pl.ds(q, rows, stride=CELLS), :] = spread_group(packed, q)
        scratch[layer, taps * CH :, :] = jnp.zeros_like(scratch[layer, taps * CH :, :])
        spread = scratch[layer].astype(jnp.bfloat16)
        fwd_ref[layer] = spread[: taps * CH]
        turned = lax.dot_general(
            eye, spread, (((1,), (1,)), ((), ())), preferred_element_type=jnp.float32
        )
        for tap in range(taps):
            at, lane = taps - 1 - tap, tap // CELLS * LANES
            bwd_ref[layer, at * CH : (at + 1) * CH, :] = spread_group(
                turned[:, lane : lane + LANES], tap % CELLS
            ).astype(jnp.bfloat16)


def fill_weights(taps_ref, t_ref):
    cell = lax.broadcasted_iota(jnp.int32, (CH, LANES), 1) // CH
    zero = jnp.zeros((CH, LANES), jnp.bfloat16)
    for layer in range(t_ref.shape[0]):
        for a in range(3):
            bands = {}
            for b in range(3):
                first = (a * 9 + b * 3) * CH
                values = [taps_ref[layer, first + c * CH : first + (c + 1) * CH, :] for c in range(3)]
                for ww in range(CELLS + 2):
                    band = zero
                    for c in range(3):
                        if 0 <= ww - c < CELLS:
                            band = jnp.where(cell == ww - c, values[c], band)
                    bands[b, ww] = band
            for at, (hh, ww) in enumerate(SLOTS):
                for h in range(2):
                    t_ref[
                        layer, a, at * CH : (at + 1) * CH, h * LANES : (h + 1) * LANES
                    ] = bands.get((hh - h, ww), zero)


def edge_masks(tiles):
    shape = (1, tiles, TILE)
    cell = lax.broadcasted_iota(jnp.int32, shape, 2) % LANES // CH
    row = lax.broadcasted_iota(jnp.int32, shape, 1)
    from_before = (cell == CELLS - 1) & (row > 0)
    from_after = (cell == 0) & (row < tiles - 1)
    return tuple(
        jnp.where(mask, 1.0, 0.0).astype(jnp.bfloat16) for mask in (from_before, from_after)
    )


def expand(x, out_ref, lead, pairs, tiles, masks):
    x = x.reshape(pairs, tiles, TILE)
    edge = pltpu.roll(x, 1, 1) * masks[0] + pltpu.roll(x, tiles - 1, 1) * masks[1]
    e0, e1 = edge[..., :LANES], edge[..., LANES:]
    r0, r1 = pltpu.roll(e0, LANES // 2, 2), pltpu.roll(e1, LANES // 2, 2)
    zero = jnp.zeros((1, tiles, LANES), x.dtype)
    low = jnp.concatenate([zero, x[:-1, :, LANES:]], 0)
    high = jnp.concatenate([x[1:, :, :LANES], zero], 0)
    e0 = e0 + jnp.concatenate([zero, r1[:-1]], 0)
    e1 = e1 + jnp.concatenate([r0[1:], zero], 0)
    flat = lambda v: v.reshape(pairs * tiles, v.shape[-1])
    out_ref[(*lead, slice(None), slice(0, TILE))] = flat(x)
    out_ref[(*lead, slice(None), slice(TILE, TILE + LANES))] = flat(low)
    out_ref[(*lead, slice(None), slice(TILE + LANES, 2 * TILE))] = flat(high)
    out_ref[(*lead, slice(None), slice(2 * TILE, 2 * TILE + LANES))] = flat(e0)
    out_ref[(*lead, slice(None), slice(2 * TILE + LANES, WIDE))] = flat(e1)


def conv_rows(x_ref, lead, start, rows, t_ref, layer):
    total = None
    for a in range(3):
        block = x_ref[(*lead, pl.ds(start + a, rows))].reshape(-1, WIDE)
        part = jnp.dot(block, t_ref[layer, a], preferred_element_type=jnp.float32)
        total = part if total is None else total + part
    return total


def slope_of(pre, gate):
    return gate * (1.0 + pre * (1.0 - gate))


def rounded(v):
    return v.astype(jnp.bfloat16)


def inside(v, row, depth):
    return jnp.where((row >= 0) & (row < depth), v, 0.0)


def widen(parts, lead, x_ref, x_lead, grow):
    base = 0
    for part in parts:
        rows = part.shape[len(lead)]
        for d in range(rows):
            grow(part[(*lead, d)], x_ref, (*x_lead, base + d))
        base += rows


def layer_one(xv, lead, out_ref, t_ref, slopes_ref=None):
    rows, cells = out_ref.shape[len(lead)], out_ref.shape[-2]
    for start, count in chunks_of(rows):
        pre = conv_rows(xv, lead, start, count, t_ref, 0)
        gate = sigmoid(pre)
        value = (pre * gate).astype(jnp.bfloat16).reshape(count, cells, TILE)
        out_ref[(*lead, pl.ds(start, count))] = value
        if slopes_ref is not None:
            slope = slope_of(pre, gate).reshape(count, cells, TILE)
            for d in range(count):
                to = start + d - (H_HIDDEN - H_G1)
                if 0 <= to < slopes_ref.shape[0]:
                    slopes_ref[to] = slope[d]


def tiled_rows(source, d, scratch, at):
    _, height, lanes = source.shape
    tiles = lanes // LANES
    for t in range(tiles):
        piece = source[d, :, t * LANES : (t + 1) * LANES].astype(jnp.float32)
        scratch[at, t * height : (t + 1) * height, :] = piece
    for h in range(height):
        piece = scratch[at, pl.ds(h, tiles, stride=height), :].astype(jnp.bfloat16)
        yield h // 2 * tiles, slice(h % 2 * LANES, (h % 2 + 1) * LANES), piece


def pieces_body(vol_hbm, cot_hbm, out, vol, cot, scratch, sems):
    size = out.shape[2]
    fields = ((vol_hbm, vol), (cot_hbm, cot))
    copies = [pltpu.make_async_copy(*pair, sems.at[at]) for at, pair in enumerate(fields)]
    for copy in copies:
        copy.start()
    rows = vol.shape[0]
    for at, (_, source) in enumerate(fields):
        copies[at].wait()
        for d in range(rows):
            for row, side, piece in tiled_rows(source, d, scratch, at * rows + d):
                flat = d * (out.shape[0] * size // rows) + row
                to = flat % size
                out[flat // size, at, to : to + piece.shape[0], side] = piece


def own_body(
    pairs, tiles,
    taps_ref, low_hbm, mid_hbm, high_hbm, cot_hbm,
    t_ref, hid, sl1, xv_own, cot_own,
    xv, raw, field, scratch, sems,
):
    rows = cot_hbm.shape[0]
    parts = (low_hbm, mid_hbm, high_hbm, cot_hbm)
    copies = [
        pltpu.make_async_copy(part, raw.at[at], sems.at[at]) for at, part in enumerate(parts)
    ]
    for copy in copies:
        copy.start()
    fill_weights(taps_ref, t_ref)
    grow = functools.partial(expand, pairs=pairs, tiles=tiles, masks=edge_masks(tiles))
    for copy in copies:
        copy.wait()
    for at in range(4):
        for d in range(rows):
            for row, side, piece in tiled_rows(raw.at[at], d, scratch, at * rows + d):
                if at < 3:
                    field[at * rows + d, row : row + tiles, side] = piece
                else:
                    cot_own[d, row : row + tiles, side] = piece
    widen((field,), (), xv, (), grow)
    layer_one(xv, (), hid, t_ref, sl1)
    xv_own[...] = xv[rows - 1 : 2 * rows + 1]


def forward_body(
    depth, pairs, tiles,
    idx, low, mid, high, hid_own, cot_own, cot_other, t_ref,
    g3, g3_up, g3_down, sl2, xb_own, xs_own,
    xv, hid, xb, xs,
):
    rows = mid.shape[1]
    cells = pairs * tiles
    first = idx[0] * rows
    grow = functools.partial(expand, pairs=pairs, tiles=tiles, masks=edge_masks(tiles))

    for crop in range(2):
        widen((low, mid, high), (crop,), xv, (crop,), grow)
        layer_one(xv, (crop,), hid, t_ref)

    for d in range(rows + 2 * H_HIDDEN):
        own = hid_own[d].astype(jnp.float32)
        partner, other = hid[0, d].astype(jnp.float32), hid[1, d].astype(jnp.float32)
        row = first + d - H_HIDDEN
        for j, (a, b) in enumerate(((own, partner), (other, own))):
            mixed = OWN_SHARE * a + PARTNER_SHARE * b
            grow(rounded(inside(mixed, row, depth)), xb, (j, d))

    def middle(j, cot):
        for start, count in chunks_of(rows + 2 * H_TWO):
            pre = conv_rows(xb, (j,), start, count, t_ref, 1)
            gate = sigmoid(pre)
            value = (pre * gate).reshape(count, cells, TILE)
            slope = slope_of(pre, gate).reshape(count, cells, TILE)
            for d in range(count):
                sl2[j, start + d] = slope[d]
                to = start + d - (H_TWO - 1)
                if 0 <= to < rows + 2:
                    grow(rounded(inside(value[d], first + to - 1, depth)), xs, (j, to))
        for start, count in chunks_of(rows):
            pre = conv_rows(xs, (j,), start, count, t_ref, 2)
            slope = slope_of(pre, sigmoid(pre)).reshape(count, cells, TILE)
            for d in range(count):
                at = start + d
                grad = rounded(cot[at].astype(jnp.float32) * slope[d])
                g3[j, at] = grad
                if at >= rows - H_G3:
                    g3_up[j, at - (rows - H_G3)] = grad
                if at < H_G3:
                    g3_down[j, at] = grad

    middle(0, cot_own)
    middle(1, cot_other)
    xb_own[...] = xb[0, H_HIDDEN - 1 : H_HIDDEN + rows + 1]
    xs_own[...] = xs[0]


def kernel_terms(values, gradient, rw):
    rows = gradient.shape[0]
    gradient = gradient.reshape(-1, TILE)
    for a in range(3):
        block = values[a : a + rows].reshape(-1, WIDE)
        terms = lax.dot_general(
            block, gradient, (((0,), (0,)), ((), ())), preferred_element_type=jnp.float32
        )
        for b in range(3):
            for c in range(3):
                at = (a * 9 + b * 3 + c) * CH
                for w in range(CELLS):
                    s0, s1 = SLOT_OF[b, w + c] * CH, SLOT_OF[b + 1, w + c] * CH
                    rw[w, at : at + CH] = (
                        terms[s0 : s0 + CH, :LANES] + terms[s1 : s1 + CH, LANES:]
                    )
    count = rw.shape[1] // CELLS
    cell = lax.broadcasted_iota(jnp.int32, (count, LANES), 1) // CH
    dense = jnp.zeros((count, LANES), jnp.float32)
    for q in range(CELLS):
        part = None
        for w in range(CELLS):
            piece = rw[w, pl.ds(q, count, stride=CELLS), :]
            if q != w:
                piece = pltpu.roll(piece, (q - w) % CELLS * CH, 1)
            part = piece if part is None else part + piece
        dense = jnp.where(cell == q, part, dense)
    return dense


def between_body(taps_ref, xs_own, g3, t_ref, terms, rw):
    fill_weights(taps_ref, t_ref)
    terms[...] = kernel_terms(xs_own[...], g3[0], rw)


def back_two(j, x_ref, sl2, x2_ref, t_ref, first, depth, grow):
    rows, cells = x2_ref.shape[-3:-1]
    for start, count in chunks_of(rows):
        back = conv_rows(x_ref, (), start, count, t_ref, 2).reshape(count, cells, TILE)
        for d in range(count):
            at = start + d
            grad = inside(back[d] * sl2[j, at], first + at - H_G2, depth)
            grow(rounded(grad), x2_ref, (at,))


def back_body(
    depth, pairs, tiles,
    idx, low, mid, high, sl1, sl2, xv_own, xb_own, three, t_ref,
    xg1, *refs,
):
    *shares, xg3, xg2, rw, terms = refs
    rows = mid.shape[1]
    cells = pairs * tiles
    first = idx[0] * rows
    grow = functools.partial(expand, pairs=pairs, tiles=tiles, masks=edge_masks(tiles))
    for j in range(2):
        widen((low, mid, high), (j,), xg3.at[j], (), grow)
        back_two(j, xg3.at[j], sl2, xg2.at[j], t_ref, first, depth, grow)
    for start, count in chunks_of(rows + 2 * H_G1):
        own, other = (
            rounded(conv_rows(xg2, (j,), start, count, t_ref, 1)).astype(jnp.float32)
            for j in range(2)
        )
        mixed = (OWN_SHARE * own + PARTNER_SHARE * other).reshape(count, cells, TILE)
        for d in range(count):
            at = start + d
            grad = inside(mixed[d] * sl1[at], first + at - H_G1, depth)
            grow(rounded(grad), xg1, (at,))
    one = kernel_terms(xv_own[...], xg1[H_G1 : H_G1 + rows, :, :TILE], rw)
    two = kernel_terms(xb_own[...], xg2[0, H_G2 : H_G2 + rows, :, :TILE], rw)
    size = one.shape[0]
    for layer, part in enumerate((one, two, three[...])):
        terms[layer * size : (layer + 1) * size] = part
    terms[3 * size :] = jnp.zeros_like(terms[3 * size :])
    share = shares[0].shape[0]
    for hop, out in enumerate(shares):
        at = pl.multiple_of((idx[0] ^ hop) * share, 16)
        out[...] = terms[pl.ds(at, share)].astype(jnp.bfloat16)


def last_body(pairs, tiles, xg1, t_ref, gv, scratch):
    rows, height, _ = gv.shape
    cells = pairs * tiles
    for start, count in chunks_of(rows):
        back = conv_rows(xg1, (), start, count, t_ref, 0).reshape(count, cells, TILE)
        for d in range(count):
            for h in range(height):
                row, side = h // 2 * tiles, slice(h % 2 * LANES, (h % 2 + 1) * LANES)
                scratch[start + d, pl.ds(h, tiles, stride=height), :] = back[
                    d, row : row + tiles, side
                ]
            for t in range(tiles):
                gv[start + d, :, t * LANES : (t + 1) * LANES] = scratch[
                    start + d, t * height : (t + 1) * height, :
                ].astype(jnp.bfloat16)


def tree_sum(parts):
    parts = [part.astype(jnp.float32) for part in parts]
    while len(parts) > 1:
        parts = [a + b for a, b in zip(parts[::2], parts[1::2])]
    return parts[0]


def share_body(*refs):
    *parts, out = refs
    out[...] = tree_sum([part[...] for part in parts]).astype(out.dtype)


def total_body(idx, *refs):
    *parts, out, whole = refs
    share = parts[0].shape[0]
    for hop, part in enumerate(parts):
        at = pl.multiple_of((idx[0] ^ hop) * share, 16)
        whole[pl.ds(at, share)] = part[...].astype(jnp.float32)
    out[...] = whole[: out.shape[0]]


def swapped(values, hop):
    count = lax.axis_size("depth")
    return lax.ppermute(values, "depth", [(i, i ^ hop) for i in range(count)])


def neighbours(up, down):
    count = lax.axis_size("depth")
    forward = [(i, i + 1) for i in range(count - 1)]
    backward = [(target, source) for source, target in forward]
    return lax.ppermute(up, "depth", forward), lax.ppermute(down, "depth", backward)


def call(kernel, outs, scratch, inputs, macs=0, far=()):
    vmem, smem, anywhere = (
        pl.BlockSpec(memory_space=space) for space in (pltpu.VMEM, pltpu.SMEM, pl.ANY)
    )
    specs = [
        anywhere if at in far else smem if x.dtype == jnp.int32 else vmem
        for at, x in enumerate(inputs)
    ]
    results = pl.pallas_call(
        kernel,
        out_shape=tuple(jax.ShapeDtypeStruct(shape, dtype) for shape, dtype in outs),
        in_specs=specs,
        out_specs=(vmem,) * len(outs),
        scratch_shapes=scratch,
        compiler_params=pltpu.CompilerParams(vmem_limit_bytes=VMEM_LIMIT),
        cost_estimate=pl.CostEstimate(
            flops=2 * macs, bytes_accessed=4 * 2**20, transcendentals=0
        ),
    )(*inputs)
    return results if len(results) > 1 else results[0]


def per_device(volume, kernels, partner, cotangent):
    _, rows, height, lanes = volume.shape
    pairs, tiles = height // 2, lanes // LANES
    cells = pairs * tiles
    groups, count = lax.axis_size("sample"), lax.axis_size("depth")
    depth = rows * count
    layers, taps, _ = kernels.shape
    bf16, f32 = jnp.bfloat16, jnp.float32
    row_macs = 3 * cells * WIDE * TILE
    size = rows * cells // groups
    packed_rows = taps * CH // CELLS
    wide = lambda *lead: pltpu.VMEM((*lead, cells, WIDE), bf16)
    index = lax.axis_index("depth").astype(jnp.int32).reshape(1)
    packed = kernels.reshape(layers, packed_rows, LANES)
    banded = ((layers, 3, WIDE, TILE), bf16)
    padded = pltpu.VMEM((layers, (taps + CELLS - 1) // CELLS * LANES, LANES), f32)
    spread_taps = ((layers, taps * CH, LANES), bf16)
    rw = pltpu.VMEM((CELLS, taps * CH, LANES), f32)
    raw_rows = pltpu.VMEM((rows, height, lanes), bf16)
    volume, cotangent = volume[0], cotangent[0]

    if size % tiles == 0:
        pieces = call(
            pieces_body,
            [((groups, 2, size, TILE), bf16)],
            [
                raw_rows,
                raw_rows,
                pltpu.VMEM((2 * rows, height * tiles, LANES), f32),
                pltpu.SemaphoreType.DMA((2,)),
            ],
            [volume, cotangent],
            far=(0, 1),
        )
    else:
        split = jnp.stack([volume, cotangent]).reshape(2, rows, pairs, 2, tiles, LANES)
        pieces = split.transpose(0, 1, 2, 4, 3, 5).reshape(2, groups, size, TILE).swapaxes(0, 1)
    spread = lax.all_to_all(pieces, "sample", split_axis=0, concat_axis=0, tiled=True)
    fwd_taps, bwd_taps = call(
        functools.partial(taps_body, taps), [spread_taps, spread_taps], [padded], [packed], 2**28
    )
    spread, fwd_taps, bwd_taps = lax.optimization_barrier((spread, fwd_taps, bwd_taps))

    ids = jnp.arange(groups, dtype=jnp.int32)
    inverse = jnp.sum(jnp.where(partner[:, None] == ids[None, :], ids[:, None], 0), axis=0)
    wanted = jnp.stack([2 * partner, 2 * inverse, 2 * inverse + 1], axis=1)
    chosen = jnp.take(spread.reshape(2 * groups, -1, TILE), wanted, axis=0)
    chosen, volume = lax.optimization_barrier((chosen, volume))
    joined = lax.all_to_all(chosen, "sample", split_axis=0, concat_axis=0, tiled=True)
    low, high = neighbours(volume, volume)
    joined, low, high = lax.optimization_barrier((joined, low, high))
    others = jnp.swapaxes(joined, 0, 1).reshape(3, rows, cells, TILE)
    vol, cot_other = others[:2], others[2]
    vol_low, vol_high = neighbours(vol, vol)
    hid_rows = rows + 2 * H_HIDDEN
    fwd, hid_own, sl1, xv_own, cot_own = call(
        functools.partial(own_body, pairs, tiles),
        [
            banded,
            ((hid_rows, cells, TILE), bf16),
            ((rows + 2 * H_G1, cells, TILE), f32),
            ((rows + 2, cells, WIDE), bf16),
            ((rows, cells, TILE), bf16),
        ],
        [
            wide(3 * rows),
            pltpu.VMEM((4, rows, height, lanes), bf16),
            pltpu.VMEM((3 * rows, cells, TILE), bf16),
            pltpu.VMEM((4 * rows, height * tiles, LANES), f32),
            pltpu.SemaphoreType.DMA((4,)),
        ],
        [fwd_taps, low, volume, high, cotangent],
        hid_rows * row_macs,
        far=(1, 2, 3, 4),
    )

    g3, g3_up, g3_down, sl2, xb_own, xs_own = call(
        functools.partial(forward_body, depth, pairs, tiles),
        [
            ((2, rows, cells, TILE), bf16),
            ((2, H_G3, cells, TILE), bf16),
            ((2, H_G3, cells, TILE), bf16),
            ((2, rows + 2 * H_TWO, cells, TILE), f32),
            ((rows + 2, cells, WIDE), bf16),
            ((rows + 2, cells, WIDE), bf16),
        ],
        [
            wide(2, 3 * rows),
            pltpu.VMEM((2, hid_rows, cells, TILE), bf16),
            wide(2, hid_rows),
            wide(2, rows + 2),
        ],
        [index, vol_low, vol, vol_high, hid_own, cot_own, cot_other, fwd],
        (2 * hid_rows + 2 * (rows + 4) + 2 * rows) * row_macs,
    )

    low, high = neighbours(g3_up, g3_down)
    bwd, three = call(
        between_body,
        [banded, ((packed_rows, LANES), f32)],
        [rw],
        [bwd_taps, xs_own, g3],
        rows * row_macs,
    )
    share = -(-layers * packed_rows // (16 * count)) * 16
    xg1, *shares = call(
        functools.partial(back_body, depth, pairs, tiles),
        [((rows + 2 * H_G1, cells, WIDE), bf16), *[((share, LANES), bf16)] * count],
        [
            wide(2, rows + 2 * H_G3),
            wide(2, rows + 2 * H_G2),
            rw,
            pltpu.VMEM((count * share, LANES), f32),
        ],
        [index, low, g3, high, sl1, sl2, xv_own, xb_own, three, bwd],
        (6 * rows + 12) * row_macs,
    )
    got = [swapped(shares[hop], hop) for hop in range(1, count)]
    grad_volume = call(
        functools.partial(last_body, pairs, tiles),
        [((rows, height, lanes), bf16)],
        [pltpu.VMEM((rows, height * tiles, LANES), f32)],
        [xg1, bwd],
        rows * row_macs,
    )
    summed = call(share_body, [((share, LANES), bf16)], [], [shares[0], *got])
    every = [summed, *(swapped(summed, hop) for hop in range(1, count))]
    total = call(
        total_body,
        [((layers * packed_rows, LANES), f32)],
        [pltpu.VMEM((count * share, LANES), f32)],
        [index, *every],
    )
    return (grad_volume[None], total.reshape(1, *kernels.shape))


def solution(mesh):
    in_specs = (P("sample", "depth", None, None), P(), P(), P("sample", "depth", None, None))
    out_specs = (P("sample", "depth", None, None), P("sample", None, None, None))
    return jax.shard_map(
        per_device, mesh=mesh, in_specs=in_specs, out_specs=out_specs, check_vma=False
    )
```

```python
import functools

import jax
import jax.numpy as jnp
from jax import lax
from jax.experimental import pallas as pl
from jax.experimental.pallas import tpu as pltpu
from jax.sharding import PartitionSpec as P

CH = 32
OWN_SHARE = 0.6
PARTNER_SHARE = 0.4
LANES = 128
CELLS = LANES // CH
TILE = 2 * LANES
WIDE = 3 * TILE
VMEM_LIMIT = 40 * 2**20

SLOTS = (
    [(1 + h, 1 + w) for h in range(2) for w in range(CELLS)]
    + [(0, 1 + w) for w in range(CELLS)]
    + [(3, 1 + w) for w in range(CELLS)]
    + [(1, 5), (0, 0), (0, 5), (1, 0)]
    + [(2, 5), (3, 0), (3, 5), (2, 0)]
)
SLOT_OF = {cell: at for at, cell in enumerate(SLOTS)}

H_HIDDEN, H_TWO, H_G3, H_G2, H_G1 = 3, 2, 3, 2, 1


def chunks_of(rows):
    count = max(1, (rows + 2) // 5)
    base, extra = divmod(rows, count)
    start, result = 0, []
    for index in range(count):
        size = base + (index < extra)
        result.append((start, size))
        start += size
    return result


def sigmoid(v):
    return 0.5 + 0.5 * jnp.tanh(0.5 * v)


def spread_group(x, group):
    cell = lax.broadcasted_iota(jnp.int32, x.shape, 1) // CH
    x = jnp.where(cell == group, x, 0.0)
    x = x + pltpu.roll(x, CH, 1)
    return x + pltpu.roll(x, 2 * CH, 1)


def taps_body(taps, kr_ref, fwd_ref, bwd_ref, scratch):
    layers, rows = kr_ref.shape[:2]
    part = scratch.shape[1] // CELLS // CH
    for layer in range(layers):
        packed = kr_ref[layer].astype(jnp.float32)
        for q in range(CELLS):
            scratch[layer, pl.ds(q, rows, stride=CELLS), :] = spread_group(packed, q)
        scratch[layer, taps * CH :, :] = jnp.zeros_like(scratch[layer, taps * CH :, :])
        fwd_ref[layer] = scratch[layer, : taps * CH].astype(jnp.bfloat16)
        cell = lax.broadcasted_iota(jnp.int32, (part * CH, LANES), 1) // CH
        compact = jnp.zeros((part * CH, LANES), jnp.float32)
        for group in range(CELLS):
            at = group * part * CH
            compact = jnp.where(cell == group, scratch[layer, at : at + part * CH, :], compact)
        room = -(-part // CELLS) * LANES - part * CH
        turned = jnp.concatenate([compact, jnp.zeros((room, LANES), jnp.float32)], 0).T
        for tap in range(taps):
            group, index = divmod(tap, part)
            at, lane = taps - 1 - tap, index // CELLS * LANES
            bwd_ref[layer, at * CH : (at + 1) * CH, :] = spread_group(
                turned[group * CH : (group + 1) * CH, lane : lane + LANES], index % CELLS
            ).astype(jnp.bfloat16)


def fill_weights(taps_ref, t_ref):
    cell = lax.broadcasted_iota(jnp.int32, (CH, LANES), 1) // CH
    zero = jnp.zeros((CH, LANES), jnp.bfloat16)
    for layer in range(t_ref.shape[0]):
        for a in range(3):
            bands = {}
            for b in range(3):
                first = (a * 9 + b * 3) * CH
                values = [taps_ref[layer, first + c * CH : first + (c + 1) * CH, :] for c in range(3)]
                for ww in range(CELLS + 2):
                    band = zero
                    for c in range(3):
                        if 0 <= ww - c < CELLS:
                            band = jnp.where(cell == ww - c, values[c], band)
                    bands[b, ww] = band
            for at, (hh, ww) in enumerate(SLOTS):
                for h in range(2):
                    t_ref[
                        layer, a, at * CH : (at + 1) * CH, h * LANES : (h + 1) * LANES
                    ] = bands.get((hh - h, ww), zero)


def edge_masks(tiles):
    shape = (1, tiles, TILE)
    cell = lax.broadcasted_iota(jnp.int32, shape, 2) % LANES // CH
    row = lax.broadcasted_iota(jnp.int32, shape, 1)
    from_before = (cell == CELLS - 1) & (row > 0)
    from_after = (cell == 0) & (row < tiles - 1)
    return tuple(
        jnp.where(mask, 1.0, 0.0).astype(jnp.bfloat16) for mask in (from_before, from_after)
    )


def expand(x, out_ref, lead, pairs, tiles, masks):
    x = x.reshape(pairs, tiles, TILE)
    edge = pltpu.roll(x, 1, 1) * masks[0] + pltpu.roll(x, tiles - 1, 1) * masks[1]
    e0, e1 = edge[..., :LANES], edge[..., LANES:]
    r0, r1 = pltpu.roll(e0, LANES // 2, 2), pltpu.roll(e1, LANES // 2, 2)
    zero = jnp.zeros((1, tiles, LANES), x.dtype)
    low = jnp.concatenate([zero, x[:-1, :, LANES:]], 0)
    high = jnp.concatenate([x[1:, :, :LANES], zero], 0)
    e0 = e0 + jnp.concatenate([zero, r1[:-1]], 0)
    e1 = e1 + jnp.concatenate([r0[1:], zero], 0)
    flat = lambda v: v.reshape(pairs * tiles, v.shape[-1])
    out_ref[(*lead, slice(None), slice(0, TILE))] = flat(x)
    out_ref[(*lead, slice(None), slice(TILE, TILE + LANES))] = flat(low)
    out_ref[(*lead, slice(None), slice(TILE + LANES, 2 * TILE))] = flat(high)
    out_ref[(*lead, slice(None), slice(2 * TILE, 2 * TILE + LANES))] = flat(e0)
    out_ref[(*lead, slice(None), slice(2 * TILE + LANES, WIDE))] = flat(e1)


def conv_rows(x_ref, lead, start, rows, t_ref, layer):
    total = None
    for a in range(3):
        block = x_ref[(*lead, pl.ds(start + a, rows))].reshape(-1, WIDE)
        part = jnp.dot(block, t_ref[layer, a], preferred_element_type=jnp.float32)
        total = part if total is None else total + part
    return total


def slope_of(pre, gate):
    return gate * (1.0 + pre * (1.0 - gate))


def rounded(v):
    return v.astype(jnp.bfloat16)


def inside(v, row, depth):
    return jnp.where((row >= 0) & (row < depth), v, 0.0)


def either(flag, a, b):
    low = lambda *at: jnp.where(flag, a[at], b[at])
    high = lambda *at: jnp.where(flag, b[at], a[at])
    return low, high


def widen(idx, near, own, far, lead, x_ref, x_lead, grow):
    low, high = either(idx[0] % 2 == 1, near, far)
    halo, rows = near.shape[len(lead)], own.shape[len(lead)]
    for base, part, count in (
        (0, low, halo),
        (halo, lambda *at: own[at], rows),
        (halo + rows, high, halo),
    ):
        for d in range(count):
            grow(part(*lead, d), x_ref, (*x_lead, base + d))


def layer_one(xv, lead, out_ref, t_ref, slopes_ref=None):
    rows, cells = out_ref.shape[len(lead)], out_ref.shape[-2]
    for start, count in chunks_of(rows):
        pre = conv_rows(xv, lead, start, count, t_ref, 0)
        gate = sigmoid(pre)
        value = (pre * gate).astype(jnp.bfloat16).reshape(count, cells, TILE)
        out_ref[(*lead, pl.ds(start, count))] = value
        if slopes_ref is not None:
            slope = slope_of(pre, gate).reshape(count, cells, TILE)
            for d in range(count):
                to = start + d - (H_HIDDEN - H_G1)
                if 0 <= to < slopes_ref.shape[0]:
                    slopes_ref[to] = slope[d]


def tiled_rows(load, height, tiles, scratch, at):
    for t in range(tiles):
        scratch[at, t * height : (t + 1) * height, :] = load(t).astype(jnp.float32)
    for h in range(height):
        piece = scratch[at, pl.ds(h, tiles, stride=height), :].astype(jnp.bfloat16)
        yield h // 2 * tiles, slice(h % 2 * LANES, (h % 2 + 1) * LANES), piece


def lanes_of(t):
    return slice(t * LANES, (t + 1) * LANES)


def select_body(crops, idx, partner, near, far, out, scratch):
    own = idx[1]
    inverse = jnp.int32(0)
    for crop in range(partner.shape[0]):
        inverse = jnp.where(partner[crop] == own, crop, inverse)
    rows, height, lanes = near.shape[1:]
    tiles = lanes // LANES
    for to, crop in enumerate((partner[own], inverse)[-crops:]):
        hop = crop ^ own
        swapped, at = hop % 2 == 1, hop // 2
        for d in range(rows):

            def load(t, d=d):
                place = (at, d, slice(None), lanes_of(t))
                return jnp.where(swapped, far[place], near[place])

            for row, side, piece in tiled_rows(load, height, tiles, scratch, to * rows + d):
                out[to, d, row : row + tiles, side] = piece


def own_body(
    pairs, tiles,
    idx, taps_ref, near_hbm, mid_hbm, far_hbm, cot_hbm,
    t_ref, hid, sl1, xv_own, cot_own,
    xv, raw, field, scratch, sems,
):
    rows, height, _ = cot_hbm.shape
    parts = (near_hbm, mid_hbm, far_hbm, cot_hbm)
    copies = [
        pltpu.make_async_copy(part, raw.at[at], sems.at[at]) for at, part in enumerate(parts)
    ]
    for copy in copies:
        copy.start()
    fill_weights(taps_ref, t_ref)
    grow = functools.partial(expand, pairs=pairs, tiles=tiles, masks=edge_masks(tiles))
    for copy in copies:
        copy.wait()
    for at in range(4):
        for d in range(rows):
            load = lambda t, at=at, d=d: raw[at, d, :, lanes_of(t)]
            for row, side, piece in tiled_rows(load, height, tiles, scratch, at * rows + d):
                if at < 3:
                    field[at, d, row : row + tiles, side] = piece
                else:
                    cot_own[d, row : row + tiles, side] = piece
    widen(idx, field.at[0], field.at[1], field.at[2], (), xv, (), grow)
    layer_one(xv, (), hid, t_ref, sl1)
    xv_own[...] = xv[rows - 1 : 2 * rows + 1]


def forward_body(
    depth, pairs, tiles,
    idx, near, mid, far, hid_own, cot_own, cot_other, t_ref,
    g3, g3_near, g3_far, sl2, xb_own, xs_own,
    xv, hid, xb, xs,
):
    rows = mid.shape[1]
    cells = pairs * tiles
    first = idx[0] * rows
    grow = functools.partial(expand, pairs=pairs, tiles=tiles, masks=edge_masks(tiles))

    for crop in range(2):
        widen(idx, near, mid, far, (crop,), xv, (crop,), grow)
        layer_one(xv, (crop,), hid, t_ref)

    for d in range(rows + 2 * H_HIDDEN):
        own = hid_own[d].astype(jnp.float32)
        partner, other = hid[0, d].astype(jnp.float32), hid[1, d].astype(jnp.float32)
        row = first + d - H_HIDDEN
        for j, (a, b) in enumerate(((own, partner), (other, own))):
            mixed = OWN_SHARE * a + PARTNER_SHARE * b
            grow(rounded(inside(mixed, row, depth)), xb, (j, d))

    def middle(j, cot):
        for start, count in chunks_of(rows + 2 * H_TWO):
            pre = conv_rows(xb, (j,), start, count, t_ref, 1)
            gate = sigmoid(pre)
            value = (pre * gate).reshape(count, cells, TILE)
            slope = slope_of(pre, gate).reshape(count, cells, TILE)
            for d in range(count):
                sl2[j, start + d] = slope[d]
                to = start + d - (H_TWO - 1)
                if 0 <= to < rows + 2:
                    grow(rounded(inside(value[d], first + to - 1, depth)), xs, (j, to))
        for start, count in chunks_of(rows):
            pre = conv_rows(xs, (j,), start, count, t_ref, 2)
            slope = slope_of(pre, sigmoid(pre)).reshape(count, cells, TILE)
            for d in range(count):
                at = start + d
                grad = rounded(cot[at].astype(jnp.float32) * slope[d])
                g3[j, at] = grad

    middle(0, cot_own)
    middle(1, cot_other.at[0])
    odd = idx[0] % 2 == 1
    for j in range(2):
        for d in range(H_G3):
            up, down = g3[j, rows - H_G3 + d], g3[j, d]
            g3_near[j, d] = jnp.where(odd, down, up)
            g3_far[j, d] = jnp.where(odd, up, down)
    xb_own[...] = xb[0, H_HIDDEN - 1 : H_HIDDEN + rows + 1]
    xs_own[...] = xs[0]


def kernel_terms(values, gradient, rw):
    rows = gradient.shape[0]
    gradient = gradient.reshape(-1, TILE)
    for a in range(3):
        block = values[a : a + rows].reshape(-1, WIDE)
        terms = lax.dot_general(
            block, gradient, (((0,), (0,)), ((), ())), preferred_element_type=jnp.float32
        )
        for b in range(3):
            for c in range(3):
                at = (a * 9 + b * 3 + c) * CH
                for w in range(CELLS):
                    s0, s1 = SLOT_OF[b, w + c] * CH, SLOT_OF[b + 1, w + c] * CH
                    rw[w, at : at + CH] = (
                        terms[s0 : s0 + CH, :LANES] + terms[s1 : s1 + CH, LANES:]
                    )
    count = rw.shape[1] // CELLS
    cell = lax.broadcasted_iota(jnp.int32, (count, LANES), 1) // CH
    dense = jnp.zeros((count, LANES), jnp.float32)
    for q in range(CELLS):
        part = None
        for w in range(CELLS):
            piece = rw[w, pl.ds(q, count, stride=CELLS), :]
            if q != w:
                piece = pltpu.roll(piece, (q - w) % CELLS * CH, 1)
            part = piece if part is None else part + piece
        dense = jnp.where(cell == q, part, dense)
    return dense


def between_body(taps_ref, xs_own, g3, t_ref, terms, rw):
    fill_weights(taps_ref, t_ref)
    terms[...] = kernel_terms(xs_own[...], g3[0], rw)


def back_two(j, x_ref, sl2, x2_ref, t_ref, first, depth, grow):
    rows, cells = x2_ref.shape[-3:-1]
    for start, count in chunks_of(rows):
        back = conv_rows(x_ref, (), start, count, t_ref, 2).reshape(count, cells, TILE)
        for d in range(count):
            at = start + d
            grad = inside(back[d] * sl2[j, at], first + at - H_G2, depth)
            grow(rounded(grad), x2_ref, (at,))


def back_body(
    depth, pairs, tiles,
    idx, near, mid, far, sl1, sl2, xv_own, xb_own, three, t_ref,
    xg1, *refs,
):
    *shares, xg3, xg2, rw, terms = refs
    rows = mid.shape[1]
    cells = pairs * tiles
    first = idx[0] * rows
    grow = functools.partial(expand, pairs=pairs, tiles=tiles, masks=edge_masks(tiles))
    for j in range(2):
        widen(idx, near, mid, far, (j,), xg3.at[j], (), grow)
        back_two(j, xg3.at[j], sl2, xg2.at[j], t_ref, first, depth, grow)
    for start, count in chunks_of(rows + 2 * H_G1):
        own, other = (
            rounded(conv_rows(xg2, (j,), start, count, t_ref, 1)).astype(jnp.float32)
            for j in range(2)
        )
        mixed = (OWN_SHARE * own + PARTNER_SHARE * other).reshape(count, cells, TILE)
        for d in range(count):
            at = start + d
            grad = inside(mixed[d] * sl1[at], first + at - H_G1, depth)
            grow(rounded(grad), xg1, (at,))
    one = kernel_terms(xv_own[...], xg1[H_G1 : H_G1 + rows, :, :TILE], rw)
    two = kernel_terms(xb_own[...], xg2[0, H_G2 : H_G2 + rows, :, :TILE], rw)
    size = one.shape[0]
    for layer, part in enumerate((one, two, three[...])):
        terms[layer * size : (layer + 1) * size] = part
    terms[3 * size :] = jnp.zeros_like(terms[3 * size :])
    share = shares[0].shape[0]
    for hop, out in enumerate(shares):
        at = pl.multiple_of((idx[0] ^ hop) * share, 16)
        out[...] = terms[pl.ds(at, share)].astype(jnp.bfloat16)


def last_body(pairs, tiles, xg1, t_ref, gv, scratch):
    rows, height, _ = gv.shape
    cells = pairs * tiles
    for start, count in chunks_of(rows):
        back = conv_rows(xg1, (), start, count, t_ref, 0).reshape(count, cells, TILE)
        for d in range(count):
            for h in range(height):
                row, side = h // 2 * tiles, slice(h % 2 * LANES, (h % 2 + 1) * LANES)
                scratch[start + d, pl.ds(h, tiles, stride=height), :] = back[
                    d, row : row + tiles, side
                ]
            for t in range(tiles):
                gv[start + d, :, t * LANES : (t + 1) * LANES] = scratch[
                    start + d, t * height : (t + 1) * height, :
                ].astype(jnp.bfloat16)


def tree_sum(parts):
    parts = [part.astype(jnp.float32) for part in parts]
    while len(parts) > 1:
        parts = [a + b for a, b in zip(parts[::2], parts[1::2])]
    return parts[0]


def share_body(*refs):
    *parts, out = refs
    out[...] = tree_sum([part[...] for part in parts]).astype(out.dtype)


def total_body(idx, *refs):
    *parts, out, whole = refs
    share = parts[0].shape[0]
    for hop, part in enumerate(parts):
        at = pl.multiple_of((idx[0] ^ hop) * share, 16)
        whole[pl.ds(at, share)] = part[...].astype(jnp.float32)
    out[...] = whole[: out.shape[0]]


def swapped(values, hop):
    count = lax.axis_size("depth")
    return lax.ppermute(values, "depth", [(i, i ^ hop) for i in range(count)])


def neighbours(near, far):
    count = lax.axis_size("depth")
    result = []
    for values, first in ((near, 0), (far, 1)):
        lower = range(first, count - 1, 2)
        pairs = [(i, i + 1) for i in lower] + [(i + 1, i) for i in lower]
        result.append(lax.ppermute(values, "depth", pairs))
    return result


def gathered(values):
    groups = lax.axis_size("sample")
    swap = lambda x, hop: lax.ppermute(x, "sample", [(i, i ^ hop) for i in range(groups)])
    near = jnp.stack([values, *(swap(values, hop) for hop in range(2, groups, 2))])
    return near, swap(near, 1)


def traded(volume, cotangent, partner, tiles):
    groups = lax.axis_size("sample")
    rows, height, _ = volume.shape
    split = jnp.stack([volume, cotangent]).reshape(2, rows, height // 2, 2, tiles, LANES)
    split = split.transpose(0, 1, 2, 4, 3, 5).reshape(2, groups, -1, TILE)
    pieces = split.swapaxes(0, 1)
    spread = lax.all_to_all(pieces, "sample", split_axis=0, concat_axis=0, tiled=True)
    ids = jnp.arange(groups, dtype=jnp.int32)
    inverse = jnp.sum(jnp.where(partner[:, None] == ids[None, :], ids[:, None], 0), axis=0)
    wanted = jnp.stack([2 * partner, 2 * inverse, 2 * inverse + 1], axis=1)
    chosen = jnp.take(spread.reshape(2 * groups, -1, TILE), wanted, axis=0)
    joined = lax.all_to_all(chosen, "sample", split_axis=0, concat_axis=0, tiled=True)
    others = jnp.swapaxes(joined, 0, 1).reshape(3, rows, -1, TILE)
    return others[:2], others[2:]


def call(kernel, outs, scratch, inputs, macs=0, far=()):
    vmem, smem, anywhere = (
        pl.BlockSpec(memory_space=space) for space in (pltpu.VMEM, pltpu.SMEM, pl.ANY)
    )
    specs = [
        anywhere if at in far else smem if x.dtype == jnp.int32 else vmem
        for at, x in enumerate(inputs)
    ]
    results = pl.pallas_call(
        kernel,
        out_shape=tuple(jax.ShapeDtypeStruct(shape, dtype) for shape, dtype in outs),
        in_specs=specs,
        out_specs=(vmem,) * len(outs),
        scratch_shapes=scratch,
        compiler_params=pltpu.CompilerParams(vmem_limit_bytes=VMEM_LIMIT),
        cost_estimate=pl.CostEstimate(
            flops=2 * macs, bytes_accessed=4 * 2**20, transcendentals=0
        ),
    )(*inputs)
    return results if len(results) > 1 else results[0]


def per_device(volume, kernels, partner, cotangent):
    volume, cotangent = volume[0], cotangent[0]
    rows, height, lanes = volume.shape
    pairs, tiles = height // 2, lanes // LANES
    cells = pairs * tiles
    groups, count = lax.axis_size("sample"), lax.axis_size("depth")
    depth = rows * count
    layers, taps, width = kernels.shape
    bf16, f32 = jnp.bfloat16, jnp.float32
    row_macs = 3 * cells * WIDE * TILE
    packed_rows = taps * CH // CELLS
    wide = lambda *lead: pltpu.VMEM((*lead, cells, WIDE), bf16)
    field = lambda *lead: ((*lead, cells, TILE), bf16)
    raw_tiles = lambda n: pltpu.VMEM((n, height * tiles, LANES), f32)
    index = jnp.stack([lax.axis_index("depth"), lax.axis_index("sample")]).astype(jnp.int32)
    packed = kernels.reshape(layers, packed_rows, LANES)
    banded = ((layers, 3, WIDE, TILE), bf16)
    spread_taps = ((layers, taps * CH, LANES), bf16)
    rw = pltpu.VMEM((CELLS, taps * CH, LANES), f32)

    if groups in (2, 4, 8):
        crops = gathered(volume)
        vol = call(
            functools.partial(select_body, 2),
            [field(2, rows)],
            [raw_tiles(2 * rows)],
            [index, partner, *crops],
        )
    else:
        vol, cot_other = traded(volume, cotangent, partner, tiles)
    near, far = neighbours(volume, volume)
    vol_near, vol_far = neighbours(vol, vol)
    fwd_taps, bwd_taps = call(
        functools.partial(taps_body, taps),
        [spread_taps, spread_taps],
        [pltpu.VMEM((layers, -(-taps // CELLS) * LANES, LANES), f32)],
        [packed],
        2**28,
    )
    if groups in (2, 4, 8):
        crops = gathered(cotangent)
        cot_other = call(
            functools.partial(select_body, 1),
            [field(1, rows)],
            [raw_tiles(rows)],
            [index, partner, *crops],
        )
    hid_rows = rows + 2 * H_HIDDEN
    fwd, hid_own, sl1, xv_own, cot_own = call(
        functools.partial(own_body, pairs, tiles),
        [
            banded,
            field(hid_rows),
            ((rows + 2 * H_G1, cells, TILE), f32),
            ((rows + 2, cells, WIDE), bf16),
            field(rows),
        ],
        [
            wide(3 * rows),
            pltpu.VMEM((4, rows, height, lanes), bf16),
            pltpu.VMEM((3, rows, cells, TILE), bf16),
            raw_tiles(4 * rows),
            pltpu.SemaphoreType.DMA((4,)),
        ],
        [index, fwd_taps, near, volume, far, cotangent],
        hid_rows * row_macs,
        far=(2, 3, 4, 5),
    )

    g3, g3_near, g3_far, sl2, xb_own, xs_own = call(
        functools.partial(forward_body, depth, pairs, tiles),
        [
            field(2, rows),
            field(2, H_G3),
            field(2, H_G3),
            ((2, rows + 2 * H_TWO, cells, TILE), f32),
            ((rows + 2, cells, WIDE), bf16),
            ((rows + 2, cells, WIDE), bf16),
        ],
        [
            wide(2, 3 * rows),
            pltpu.VMEM((2, hid_rows, cells, TILE), bf16),
            wide(2, hid_rows),
            wide(2, rows + 2),
        ],
        [index, vol_near, vol, vol_far, hid_own, cot_own, cot_other, fwd],
        (2 * hid_rows + 2 * (rows + 4) + 2 * rows) * row_macs,
    )

    near, far = neighbours(g3_near, g3_far)
    bwd, three = call(
        between_body,
        [banded, ((packed_rows, LANES), f32)],
        [rw],
        [bwd_taps, xs_own, g3],
        rows * row_macs,
    )
    share = -(-layers * packed_rows // (16 * count)) * 16
    xg1, *shares = call(
        functools.partial(back_body, depth, pairs, tiles),
        [((rows + 2 * H_G1, cells, WIDE), bf16), *[((share, LANES), bf16)] * count],
        [
            wide(2, rows + 2 * H_G3),
            wide(2, rows + 2 * H_G2),
            rw,
            pltpu.VMEM((count * share, LANES), f32),
        ],
        [index, near, g3, far, sl1, sl2, xv_own, xb_own, three, bwd],
        (6 * rows + 12) * row_macs,
    )
    got = [swapped(shares[hop], hop) for hop in range(1, count)]
    grad_volume = call(
        functools.partial(last_body, pairs, tiles),
        [((rows, height, lanes), bf16)],
        [raw_tiles(rows)],
        [xg1, bwd],
        rows * row_macs,
    )
    summed = call(share_body, [((share, LANES), bf16)], [], [shares[0], *got])
    every = [summed, *(swapped(summed, hop) for hop in range(1, count))]
    total = call(
        total_body,
        [((layers * packed_rows, LANES), f32)],
        [pltpu.VMEM((count * share, LANES), f32)],
        [index, *every],
    )
    return (grad_volume[None], total.reshape(1, layers, taps, width))


def solution(mesh):
    in_specs = (P("sample", "depth", None, None), P(), P(), P("sample", "depth", None, None))
    out_specs = (P("sample", "depth", None, None), P("sample", None, None, None))
    return jax.shard_map(
        per_device, mesh=mesh, in_specs=in_specs, out_specs=out_specs, check_vma=False
    )
```

```python
import functools

import jax
import jax.numpy as jnp
from jax import lax
from jax.experimental import pallas as pl
from jax.experimental.pallas import tpu as pltpu
from jax.sharding import PartitionSpec as P

CH = 32
OWN_SHARE = 0.6
PARTNER_SHARE = 0.4
LANES = 128
CELLS = LANES // CH
TILE = 2 * LANES
WIDE = 3 * TILE
VMEM_LIMIT = 40 * 2**20

SLOTS = (
    [(1 + h, 1 + w) for h in range(2) for w in range(CELLS)]
    + [(0, 1 + w) for w in range(CELLS)]
    + [(3, 1 + w) for w in range(CELLS)]
    + [(1, 5), (0, 0), (0, 5), (1, 0)]
    + [(2, 5), (3, 0), (3, 5), (2, 0)]
)
SLOT_OF = {cell: at for at, cell in enumerate(SLOTS)}

H_HIDDEN, H_TWO, H_G3, H_G2, H_G1 = 3, 2, 3, 2, 1


def chunks_of(rows):
    count = max(1, (rows + 2) // 5)
    base, extra = divmod(rows, count)
    start, result = 0, []
    for index in range(count):
        size = base + (index < extra)
        result.append((start, size))
        start += size
    return result


def sigmoid(v):
    return 0.5 + 0.5 * jnp.tanh(0.5 * v)


def lanes_of(t):
    return slice(t * LANES, (t + 1) * LANES)


def taps_body(taps, kr_ref, fwd_ref, bwd_ref, scratch):
    layers, rows = kr_ref.shape[:2]
    part = scratch.shape[1] // CELLS // CH
    shape = (LANES, CELLS * LANES)
    lane = lax.broadcasted_iota(jnp.int32, shape, 1)
    chosen = lax.broadcasted_iota(jnp.int32, shape, 0) == lane // LANES * CH + lane % CH
    spread = jnp.where(chosen, 1.0, 0.0).astype(jnp.bfloat16)
    for layer in range(layers):
        groups = jnp.dot(kr_ref[layer], spread, preferred_element_type=jnp.float32)
        for q in range(CELLS):
            scratch[layer, pl.ds(q, rows, stride=CELLS), :] = groups[:, lanes_of(q)]
        scratch[layer, taps * CH :, :] = jnp.zeros_like(scratch[layer, taps * CH :, :])
        fwd_ref[layer] = scratch[layer, : taps * CH].astype(jnp.bfloat16)
        cell = lax.broadcasted_iota(jnp.int32, (part * CH, LANES), 1) // CH
        compact = jnp.zeros((part * CH, LANES), jnp.float32)
        for group in range(CELLS):
            at = group * part * CH
            compact = jnp.where(cell == group, scratch[layer, at : at + part * CH, :], compact)
        room = -(-part // CELLS) * LANES - part * CH
        turned = jnp.concatenate([compact, jnp.zeros((room, LANES), jnp.float32)], 0).T
        stacked = jnp.concatenate(
            [turned[:, lanes_of(t)] for t in range(turned.shape[1] // LANES)], 0
        ).astype(jnp.bfloat16)
        groups = jnp.dot(stacked, spread, preferred_element_type=jnp.float32)
        for tap in range(taps):
            group, index = divmod(tap, part)
            at, row = taps - 1 - tap, index // CELLS * LANES + group * CH
            bwd_ref[layer, at * CH : (at + 1) * CH, :] = groups[
                row : row + CH, lanes_of(index % CELLS)
            ].astype(jnp.bfloat16)


def fill_weights(taps_ref, t_ref):
    cell = lax.broadcasted_iota(jnp.int32, (CH, LANES), 1) // CH
    zero = jnp.zeros((CH, LANES), jnp.bfloat16)
    for layer in range(t_ref.shape[0]):
        for a in range(3):
            bands = {}
            for b in range(3):
                first = (a * 9 + b * 3) * CH
                values = [taps_ref[layer, first + c * CH : first + (c + 1) * CH, :] for c in range(3)]
                for ww in range(CELLS + 2):
                    band = zero
                    for c in range(3):
                        if 0 <= ww - c < CELLS:
                            band = jnp.where(cell == ww - c, values[c], band)
                    bands[b, ww] = band
            for at, (hh, ww) in enumerate(SLOTS):
                for h in range(2):
                    t_ref[
                        layer, a, at * CH : (at + 1) * CH, h * LANES : (h + 1) * LANES
                    ] = bands.get((hh - h, ww), zero)


def edge_masks(tiles):
    shape = (1, tiles, TILE)
    cell = lax.broadcasted_iota(jnp.int32, shape, 2) % LANES // CH
    row = lax.broadcasted_iota(jnp.int32, shape, 1)
    from_before = (cell == CELLS - 1) & (row > 0)
    from_after = (cell == 0) & (row < tiles - 1)
    return tuple(
        jnp.where(mask, 1.0, 0.0).astype(jnp.bfloat16) for mask in (from_before, from_after)
    )


def expand(x, out_ref, lead, pairs, tiles, masks):
    x = x.reshape(pairs, tiles, TILE)
    edge = pltpu.roll(x, 1, 1) * masks[0] + pltpu.roll(x, tiles - 1, 1) * masks[1]
    e0, e1 = edge[..., :LANES], edge[..., LANES:]
    r0, r1 = pltpu.roll(e0, LANES // 2, 2), pltpu.roll(e1, LANES // 2, 2)
    zero = jnp.zeros((1, tiles, LANES), x.dtype)
    low = jnp.concatenate([zero, x[:-1, :, LANES:]], 0)
    high = jnp.concatenate([x[1:, :, :LANES], zero], 0)
    e0 = e0 + jnp.concatenate([zero, r1[:-1]], 0)
    e1 = e1 + jnp.concatenate([r0[1:], zero], 0)
    flat = lambda v: v.reshape(pairs * tiles, v.shape[-1])
    out_ref[(*lead, slice(None), slice(0, TILE))] = flat(x)
    out_ref[(*lead, slice(None), slice(TILE, TILE + LANES))] = flat(low)
    out_ref[(*lead, slice(None), slice(TILE + LANES, 2 * TILE))] = flat(high)
    out_ref[(*lead, slice(None), slice(2 * TILE, 2 * TILE + LANES))] = flat(e0)
    out_ref[(*lead, slice(None), slice(2 * TILE + LANES, WIDE))] = flat(e1)


def conv_rows(x_ref, lead, start, rows, t_ref, layer):
    blocks = [x_ref[(*lead, pl.ds(start + a, rows))].reshape(-1, WIDE) for a in range(3)]
    return jnp.dot(
        jnp.concatenate(blocks, axis=1),
        t_ref[layer].reshape(3 * WIDE, TILE),
        preferred_element_type=jnp.float32,
    )


def slope_of(pre, gate):
    return gate * (1.0 + pre * (1.0 - gate))


def rounded(v):
    return v.astype(jnp.bfloat16)


def inside(v, row, depth):
    return jnp.where((row >= 0) & (row < depth), v, 0.0)


def either(flag, a, b):
    low = lambda *at: jnp.where(flag, a[at], b[at])
    high = lambda *at: jnp.where(flag, b[at], a[at])
    return low, high


def widen(near, own, far, lead, x_ref, x_lead, grow):
    low, high = either(lax.axis_index("depth") % 2 == 1, near, far)
    halo, rows = near.shape[len(lead)], own.shape[len(lead)]
    for base, part, count in (
        (0, low, halo),
        (halo, lambda *at: own[at], rows),
        (halo + rows, high, halo),
    ):
        for d in range(count):
            grow(part(*lead, d), x_ref, (*x_lead, base + d))


def layer_one(xv, lead, out_ref, t_ref, slopes_ref=None):
    rows, cells = out_ref.shape[len(lead)], out_ref.shape[-2]
    for start, count in chunks_of(rows):
        pre = conv_rows(xv, lead, start, count, t_ref, 0)
        gate = sigmoid(pre)
        value = (pre * gate).astype(jnp.bfloat16).reshape(count, cells, TILE)
        out_ref[(*lead, pl.ds(start, count))] = value
        if slopes_ref is not None:
            slope = slope_of(pre, gate).reshape(count, cells, TILE)
            for d in range(count):
                to = start + d - (H_HIDDEN - H_G1)
                if 0 <= to < slopes_ref.shape[0]:
                    slopes_ref[to] = slope[d]


def tiled_rows(load, height, tiles, scratch, at):
    for t in range(tiles):
        scratch[at, t * height : (t + 1) * height, :] = load(t).astype(jnp.float32)
    for h in range(height):
        piece = scratch[at, pl.ds(h, tiles, stride=height), :].astype(jnp.bfloat16)
        yield h // 2 * tiles, slice(h % 2 * LANES, (h % 2 + 1) * LANES), piece


def select_body(hops, *refs):
    *crops, out, scratch = refs
    rows, height, lanes = crops[0].shape
    tiles = lanes // LANES
    for to in range(out.shape[0]):
        for hop, crop in enumerate(crops):

            @pl.when(hops[to] == hop)
            def _(to=to, crop=crop):
                for d in range(rows):
                    for t in range(tiles):
                        scratch[to, d, t * height : (t + 1) * height, :] = crop[
                            d, :, lanes_of(t)
                        ].astype(jnp.float32)

        for d in range(rows):
            for h in range(height):
                piece = scratch[to, d, pl.ds(h, tiles, stride=height), :].astype(jnp.bfloat16)
                row, side = h // 2 * tiles, lanes_of(h % 2)
                out[to, d, row : row + tiles, side] = piece


def own_body(
    pairs, tiles,
    taps_ref, near_hbm, mid_hbm, far_hbm, cot_hbm,
    t_ref, hid, sl1, xv_own, cot_own,
    xv, raw, field, scratch, sems,
):
    rows, height, _ = cot_hbm.shape
    parts = (near_hbm, mid_hbm, far_hbm, cot_hbm)
    copies = [
        pltpu.make_async_copy(part, raw.at[at], sems.at[at]) for at, part in enumerate(parts)
    ]
    for copy in copies:
        copy.start()
    fill_weights(taps_ref, t_ref)
    grow = functools.partial(expand, pairs=pairs, tiles=tiles, masks=edge_masks(tiles))
    for copy in copies:
        copy.wait()
    for at in range(4):
        for d in range(rows):
            load = lambda t, at=at, d=d: raw[at, d, :, lanes_of(t)]
            for row, side, piece in tiled_rows(load, height, tiles, scratch, at * rows + d):
                if at < 3:
                    field[at, d, row : row + tiles, side] = piece
                else:
                    cot_own[d, row : row + tiles, side] = piece
    widen(field.at[0], field.at[1], field.at[2], (), xv, (), grow)
    layer_one(xv, (), hid, t_ref, sl1)
    xv_own[...] = xv[rows - 1 : 2 * rows + 1]


def forward_body(
    depth, pairs, tiles,
    near, mid, far, hid_own, cot_own, cot_other, t_ref,
    g3, g3_near, g3_far, sl2, xb_own, xs_own,
    xv, hid, xb, xs,
):
    rows = mid.shape[1]
    cells = pairs * tiles
    first = lax.axis_index("depth") * rows
    grow = functools.partial(expand, pairs=pairs, tiles=tiles, masks=edge_masks(tiles))

    for crop in range(2):
        widen(near, mid, far, (crop,), xv, (crop,), grow)
        layer_one(xv, (crop,), hid, t_ref)

    for d in range(rows + 2 * H_HIDDEN):
        own = hid_own[d].astype(jnp.float32)
        partner, other = hid[0, d].astype(jnp.float32), hid[1, d].astype(jnp.float32)
        row = first + d - H_HIDDEN
        for j, (a, b) in enumerate(((own, partner), (other, own))):
            mixed = OWN_SHARE * a + PARTNER_SHARE * b
            grow(rounded(inside(mixed, row, depth)), xb, (j, d))

    def middle(j, cot):
        for start, count in chunks_of(rows + 2 * H_TWO):
            pre = conv_rows(xb, (j,), start, count, t_ref, 1)
            gate = sigmoid(pre)
            value = (pre * gate).reshape(count, cells, TILE)
            slope = slope_of(pre, gate).reshape(count, cells, TILE)
            for d in range(count):
                sl2[j, start + d] = slope[d]
                to = start + d - (H_TWO - 1)
                if 0 <= to < rows + 2:
                    grow(rounded(inside(value[d], first + to - 1, depth)), xs, (j, to))
        for start, count in chunks_of(rows):
            pre = conv_rows(xs, (j,), start, count, t_ref, 2)
            slope = slope_of(pre, sigmoid(pre)).reshape(count, cells, TILE)
            for d in range(count):
                at = start + d
                grad = rounded(cot[at].astype(jnp.float32) * slope[d])
                g3[j, at] = grad

    middle(0, cot_own)
    middle(1, cot_other.at[0])
    odd = lax.axis_index("depth") % 2 == 1
    for j in range(2):
        for d in range(H_G3):
            up, down = g3[j, rows - H_G3 + d], g3[j, d]
            g3_near[j, d] = jnp.where(odd, down, up)
            g3_far[j, d] = jnp.where(odd, up, down)
    xb_own[...] = xb[0, H_HIDDEN - 1 : H_HIDDEN + rows + 1]
    xs_own[...] = xs[0]


def kernel_terms(values, gradient, rw):
    rows = gradient.shape[0]
    gradient = gradient.reshape(-1, TILE)
    for a in range(3):
        block = values[a : a + rows].reshape(-1, WIDE)
        terms = lax.dot_general(
            block, gradient, (((0,), (0,)), ((), ())), preferred_element_type=jnp.float32
        )
        for b in range(3):
            for c in range(3):
                at = (a * 9 + b * 3 + c) * CH
                for w in range(CELLS):
                    s0, s1 = SLOT_OF[b, w + c] * CH, SLOT_OF[b + 1, w + c] * CH
                    rw[w, at : at + CH] = (
                        terms[s0 : s0 + CH, :LANES] + terms[s1 : s1 + CH, LANES:]
                    )
    count = rw.shape[1] // CELLS
    cell = lax.broadcasted_iota(jnp.int32, (count, LANES), 1) // CH
    dense = jnp.zeros((count, LANES), jnp.float32)
    for q in range(CELLS):
        part = None
        for w in range(CELLS):
            piece = rw[w, pl.ds(q, count, stride=CELLS), :]
            if q != w:
                piece = pltpu.roll(piece, (q - w) % CELLS * CH, 1)
            part = piece if part is None else part + piece
        dense = jnp.where(cell == q, part, dense)
    return dense


def between_body(taps_ref, xs_own, g3, t_ref, terms, rw):
    fill_weights(taps_ref, t_ref)
    terms[...] = kernel_terms(xs_own[...], g3[0], rw)


def back_two(j, x_ref, sl2, x2_ref, t_ref, first, depth, grow):
    rows, cells = x2_ref.shape[-3:-1]
    for start, count in chunks_of(rows):
        back = conv_rows(x_ref, (), start, count, t_ref, 2).reshape(count, cells, TILE)
        for d in range(count):
            at = start + d
            grad = inside(back[d] * sl2[j, at], first + at - H_G2, depth)
            grow(rounded(grad), x2_ref, (at,))


def back_body(
    depth, pairs, tiles,
    near, mid, far, sl1, sl2, xv_own, xb_own, three, t_ref,
    xg1, *refs,
):
    *shares, xg3, xg2, rw, terms = refs
    rows = mid.shape[1]
    cells = pairs * tiles
    first = lax.axis_index("depth") * rows
    grow = functools.partial(expand, pairs=pairs, tiles=tiles, masks=edge_masks(tiles))
    for j in range(2):
        widen(near, mid, far, (j,), xg3.at[j], (), grow)
        back_two(j, xg3.at[j], sl2, xg2.at[j], t_ref, first, depth, grow)
    for start, count in chunks_of(rows + 2 * H_G1):
        own, other = (
            rounded(conv_rows(xg2, (j,), start, count, t_ref, 1)).astype(jnp.float32)
            for j in range(2)
        )
        mixed = (OWN_SHARE * own + PARTNER_SHARE * other).reshape(count, cells, TILE)
        for d in range(count):
            at = start + d
            grad = inside(mixed[d] * sl1[at], first + at - H_G1, depth)
            grow(rounded(grad), xg1, (at,))
    one = kernel_terms(xv_own[...], xg1[H_G1 : H_G1 + rows, :, :TILE], rw)
    two = kernel_terms(xb_own[...], xg2[0, H_G2 : H_G2 + rows, :, :TILE], rw)
    size = one.shape[0]
    for layer, part in enumerate((one, two, three[...])):
        terms[layer * size : (layer + 1) * size] = part
    terms[3 * size :] = jnp.zeros_like(terms[3 * size :])
    share = shares[0].shape[0]
    for hop, out in enumerate(shares):
        at = pl.multiple_of((lax.axis_index("depth") ^ hop) * share, 16)
        out[...] = terms[pl.ds(at, share)].astype(jnp.bfloat16)


def last_body(pairs, tiles, xg1, t_ref, gv, scratch):
    rows, height, _ = gv.shape
    cells = pairs * tiles
    for start, count in chunks_of(rows):
        back = conv_rows(xg1, (), start, count, t_ref, 0).reshape(count, cells, TILE)
        for d in range(count):
            for h in range(height):
                row, side = h // 2 * tiles, slice(h % 2 * LANES, (h % 2 + 1) * LANES)
                scratch[start + d, pl.ds(h, tiles, stride=height), :] = back[
                    d, row : row + tiles, side
                ]
            for t in range(tiles):
                gv[start + d, :, t * LANES : (t + 1) * LANES] = scratch[
                    start + d, t * height : (t + 1) * height, :
                ].astype(jnp.bfloat16)


def tree_sum(parts):
    parts = [part.astype(jnp.float32) for part in parts]
    while len(parts) > 1:
        parts = [a + b for a, b in zip(parts[::2], parts[1::2])]
    return parts[0]


def share_body(*refs):
    *parts, out = refs
    out[...] = tree_sum([part[...] for part in parts]).astype(out.dtype)


def total_body(*refs):
    *parts, out, whole = refs
    share = parts[0].shape[0]
    for hop, part in enumerate(parts):
        at = pl.multiple_of((lax.axis_index("depth") ^ hop) * share, 16)
        whole[pl.ds(at, share)] = part[...].astype(jnp.float32)
    out[...] = whole[: out.shape[0]]


def swapped(values, hop):
    count = lax.axis_size("depth")
    return lax.ppermute(values, "depth", [(i, i ^ hop) for i in range(count)])


def neighbours(near, far):
    count = lax.axis_size("depth")
    result = []
    for values, first in ((near, 0), (far, 1)):
        lower = range(first, count - 1, 2)
        pairs = [(i, i + 1) for i in lower] + [(i + 1, i) for i in lower]
        result.append(lax.ppermute(values, "depth", pairs))
    return result


def over_sample(values, hop):
    groups = lax.axis_size("sample")
    return lax.ppermute(values, "sample", [(i, i ^ hop) for i in range(groups)])


def even_hops(values):
    return [over_sample(values, hop) for hop in range(2, lax.axis_size("sample"), 2)]


def all_hops(values, evens):
    evens = [values, *evens]
    return [crop for even in evens for crop in (even, over_sample(even, 1))]


def traded(volume, cotangent, partner, tiles):
    groups = lax.axis_size("sample")
    rows, height, _ = volume.shape
    split = jnp.stack([volume, cotangent]).reshape(2, rows, height // 2, 2, tiles, LANES)
    split = split.transpose(0, 1, 2, 4, 3, 5).reshape(2, groups, -1, TILE)
    pieces = split.swapaxes(0, 1)
    spread = lax.all_to_all(pieces, "sample", split_axis=0, concat_axis=0, tiled=True)
    ids = jnp.arange(groups, dtype=jnp.int32)
    inverse = jnp.sum(jnp.where(partner[:, None] == ids[None, :], ids[:, None], 0), axis=0)
    wanted = jnp.stack([2 * partner, 2 * inverse, 2 * inverse + 1], axis=1)
    chosen = jnp.take(spread.reshape(2 * groups, -1, TILE), wanted, axis=0)
    joined = lax.all_to_all(chosen, "sample", split_axis=0, concat_axis=0, tiled=True)
    others = jnp.swapaxes(joined, 0, 1).reshape(3, rows, -1, TILE)
    return others[:2], others[2:]


def call(kernel, outs, scratch, inputs, macs=0, far=()):
    vmem, smem, anywhere = (
        pl.BlockSpec(memory_space=space) for space in (pltpu.VMEM, pltpu.SMEM, pl.ANY)
    )
    specs = [
        anywhere if at in far else smem if x.dtype == jnp.int32 else vmem
        for at, x in enumerate(inputs)
    ]
    results = pl.pallas_call(
        kernel,
        out_shape=tuple(jax.ShapeDtypeStruct(shape, dtype) for shape, dtype in outs),
        in_specs=specs,
        out_specs=(vmem,) * len(outs),
        scratch_shapes=scratch,
        compiler_params=pltpu.CompilerParams(vmem_limit_bytes=VMEM_LIMIT),
        cost_estimate=pl.CostEstimate(
            flops=2 * macs, bytes_accessed=4 * 2**20, transcendentals=0
        ),
    )(*inputs)
    return results if len(results) > 1 else results[0]


def per_device(volume, kernels, partner, cotangent):
    volume, cotangent = volume[0], cotangent[0]
    rows, height, lanes = volume.shape
    pairs, tiles = height // 2, lanes // LANES
    cells = pairs * tiles
    groups, count = lax.axis_size("sample"), lax.axis_size("depth")
    depth = rows * count
    layers, taps, width = kernels.shape
    bf16, f32 = jnp.bfloat16, jnp.float32
    row_macs = 3 * cells * WIDE * TILE
    packed_rows = taps * CH // CELLS
    wide = lambda *lead: pltpu.VMEM((*lead, cells, WIDE), bf16)
    field = lambda *lead: ((*lead, cells, TILE), bf16)
    raw_tiles = lambda *lead: pltpu.VMEM((*lead, height * tiles, LANES), f32)
    packed = kernels.reshape(layers, packed_rows, LANES)
    banded = ((layers, 3, WIDE, TILE), bf16)
    spread_taps = ((layers, taps * CH, LANES), bf16)
    rw = pltpu.VMEM((CELLS, taps * CH, LANES), f32)

    direct = groups in (2, 4, 8)
    fwd_taps, bwd_taps = call(
        functools.partial(taps_body, taps),
        [spread_taps, spread_taps],
        [pltpu.VMEM((layers, -(-taps // CELLS) * LANES, LANES), f32)],
        [packed],
        2**28,
    )
    if direct:
        own = lax.axis_index("sample").astype(jnp.int32)
        ids = jnp.arange(groups, dtype=jnp.int32)
        partner_hop = jnp.sum(jnp.where(ids == own, partner, 0)) ^ own
        inverse_hop = jnp.sum(jnp.where(partner == own, ids, 0)) ^ own
        hops = jnp.stack([partner_hop, inverse_hop])
        evens = even_hops(volume)
        near, far = neighbours(volume, volume)
        evens, late = lax.optimization_barrier((evens, cotangent))
        crops = all_hops(volume, evens)
        crops, near, far, fwd_taps, bwd_taps, hops = lax.optimization_barrier(
            (crops, near, far, fwd_taps, bwd_taps, hops)
        )
        vol = call(select_body, [field(2, rows)], [raw_tiles(2, rows)], [hops, *crops])
        vol_near, vol_far = neighbours(vol, vol)
        evens, vol = lax.optimization_barrier((even_hops(late), vol))
        cot_other = call(
            select_body,
            [field(1, rows)],
            [raw_tiles(1, rows)],
            [inverse_hop.reshape(1), *all_hops(late, evens)],
        )
    else:
        near, far = neighbours(volume, volume)
        vol, cot_other = traded(volume, cotangent, partner, tiles)
        vol_near, vol_far = neighbours(vol, vol)
    hid_rows = rows + 2 * H_HIDDEN
    fwd, hid_own, sl1, xv_own, cot_own = call(
        functools.partial(own_body, pairs, tiles),
        [
            banded,
            field(hid_rows),
            ((rows + 2 * H_G1, cells, TILE), f32),
            ((rows + 2, cells, WIDE), bf16),
            field(rows),
        ],
        [
            wide(3 * rows),
            pltpu.VMEM((4, rows, height, lanes), bf16),
            pltpu.VMEM((3, rows, cells, TILE), bf16),
            raw_tiles(4 * rows),
            pltpu.SemaphoreType.DMA((4,)),
        ],
        [fwd_taps, near, volume, far, cotangent],
        hid_rows * row_macs,
        far=(1, 2, 3, 4),
    )

    g3, g3_near, g3_far, sl2, xb_own, xs_own = call(
        functools.partial(forward_body, depth, pairs, tiles),
        [
            field(2, rows),
            field(2, H_G3),
            field(2, H_G3),
            ((2, rows + 2 * H_TWO, cells, TILE), f32),
            ((rows + 2, cells, WIDE), bf16),
            ((rows + 2, cells, WIDE), bf16),
        ],
        [
            wide(2, 3 * rows),
            pltpu.VMEM((2, hid_rows, cells, TILE), bf16),
            wide(2, hid_rows),
            wide(2, rows + 2),
        ],
        [vol_near, vol, vol_far, hid_own, cot_own, cot_other, fwd],
        (2 * hid_rows + 2 * (rows + 4) + 2 * rows) * row_macs,
    )

    near, far = neighbours(g3_near, g3_far)
    bwd, three = call(
        between_body,
        [banded, ((packed_rows, LANES), f32)],
        [rw],
        [bwd_taps, xs_own, g3],
        rows * row_macs,
    )
    share = -(-layers * packed_rows // (16 * count)) * 16
    xg1, *shares = call(
        functools.partial(back_body, depth, pairs, tiles),
        [((rows + 2 * H_G1, cells, WIDE), bf16), *[((share, LANES), bf16)] * count],
        [
            wide(2, rows + 2 * H_G3),
            wide(2, rows + 2 * H_G2),
            rw,
            pltpu.VMEM((count * share, LANES), f32),
        ],
        [near, g3, far, sl1, sl2, xv_own, xb_own, three, bwd],
        (6 * rows + 12) * row_macs,
    )
    got = [swapped(shares[hop], hop) for hop in range(1, count)]
    grad_volume = call(
        functools.partial(last_body, pairs, tiles),
        [((rows, height, lanes), bf16)],
        [raw_tiles(rows)],
        [xg1, bwd],
        rows * row_macs,
    )
    summed = call(share_body, [((share, LANES), bf16)], [], [shares[0], *got])
    every = [summed, *(swapped(summed, hop) for hop in range(1, count))]
    total = call(
        total_body,
        [((layers * packed_rows, LANES), f32)],
        [pltpu.VMEM((count * share, LANES), f32)],
        [*every],
    )
    return (grad_volume[None], total.reshape(1, layers, taps, width))


def solution(mesh):
    in_specs = (P("sample", "depth", None, None), P(), P(), P("sample", "depth", None, None))
    out_specs = (P("sample", "depth", None, None), P("sample", None, None, None))
    return jax.shard_map(
        per_device, mesh=mesh, in_specs=in_specs, out_specs=out_specs, check_vma=False
    )
```

```python
import functools

import jax
import jax.numpy as jnp
from jax import lax
from jax.experimental import pallas as pl
from jax.experimental.pallas import tpu as pltpu
from jax.sharding import PartitionSpec as P

CH = 32
OWN_SHARE = 0.6
PARTNER_SHARE = 0.4
LANES = 128
CELLS = LANES // CH
TILE = 2 * LANES
WIDE = 3 * TILE
VMEM_LIMIT = 40 * 2**20

SLOTS = (
    [(1 + h, 1 + w) for h in range(2) for w in range(CELLS)]
    + [(0, 1 + w) for w in range(CELLS)]
    + [(3, 1 + w) for w in range(CELLS)]
    + [(1, 5), (0, 0), (0, 5), (1, 0)]
    + [(2, 5), (3, 0), (3, 5), (2, 0)]
)
SLOT_OF = {cell: at for at, cell in enumerate(SLOTS)}

H_HIDDEN, H_TWO, H_G3, H_G2, H_G1 = 3, 2, 3, 2, 1


def chunks_of(rows):
    count = max(1, (rows + 2) // 5)
    base, extra = divmod(rows, count)
    start, result = 0, []
    for index in range(count):
        size = base + (index < extra)
        result.append((start, size))
        start += size
    return result


def sigmoid(v):
    return 0.5 + 0.5 * jnp.tanh(0.5 * v)


def lanes_of(t):
    return slice(t * LANES, (t + 1) * LANES)


def taps_body(taps, kr_ref, fwd_ref, bwd_ref, scratch):
    layers, rows = kr_ref.shape[:2]
    part = scratch.shape[1] // CELLS // CH
    shape = (LANES, CELLS * LANES)
    lane = lax.broadcasted_iota(jnp.int32, shape, 1)
    chosen = lax.broadcasted_iota(jnp.int32, shape, 0) == lane // LANES * CH + lane % CH
    spread = jnp.where(chosen, 1.0, 0.0).astype(jnp.bfloat16)
    for layer in range(layers):
        groups = jnp.dot(kr_ref[layer], spread, preferred_element_type=jnp.float32)
        for q in range(CELLS):
            scratch[layer, pl.ds(q, rows, stride=CELLS), :] = groups[:, lanes_of(q)]
        scratch[layer, taps * CH :, :] = jnp.zeros_like(scratch[layer, taps * CH :, :])
        fwd_ref[layer] = scratch[layer, : taps * CH].astype(jnp.bfloat16)
        cell = lax.broadcasted_iota(jnp.int32, (part * CH, LANES), 1) // CH
        compact = jnp.zeros((part * CH, LANES), jnp.float32)
        for group in range(CELLS):
            at = group * part * CH
            compact = jnp.where(cell == group, scratch[layer, at : at + part * CH, :], compact)
        room = -(-part // CELLS) * LANES - part * CH
        turned = jnp.concatenate([compact, jnp.zeros((room, LANES), jnp.float32)], 0).T
        stacked = jnp.concatenate(
            [turned[:, lanes_of(t)] for t in range(turned.shape[1] // LANES)], 0
        ).astype(jnp.bfloat16)
        groups = jnp.dot(stacked, spread, preferred_element_type=jnp.float32)
        for tap in range(taps):
            group, index = divmod(tap, part)
            at, row = taps - 1 - tap, index // CELLS * LANES + group * CH
            bwd_ref[layer, at * CH : (at + 1) * CH, :] = groups[
                row : row + CH, lanes_of(index % CELLS)
            ].astype(jnp.bfloat16)


def fill_weights(taps_ref, t_ref):
    cell = lax.broadcasted_iota(jnp.int32, (CH, LANES), 1) // CH
    zero = jnp.zeros((CH, LANES), jnp.bfloat16)
    for layer in range(t_ref.shape[0]):
        for a in range(3):
            bands = {}
            for b in range(3):
                first = (a * 9 + b * 3) * CH
                values = [taps_ref[layer, first + c * CH : first + (c + 1) * CH, :] for c in range(3)]
                for ww in range(CELLS + 2):
                    band = zero
                    for c in range(3):
                        if 0 <= ww - c < CELLS:
                            band = jnp.where(cell == ww - c, values[c], band)
                    bands[b, ww] = band
            for at, (hh, ww) in enumerate(SLOTS):
                for h in range(2):
                    t_ref[
                        layer, a, at * CH : (at + 1) * CH, h * LANES : (h + 1) * LANES
                    ] = bands.get((hh - h, ww), zero)


def edge_masks(tiles):
    shape = (1, tiles, TILE)
    cell = lax.broadcasted_iota(jnp.int32, shape, 2) % LANES // CH
    row = lax.broadcasted_iota(jnp.int32, shape, 1)
    from_before = (cell == CELLS - 1) & (row > 0)
    from_after = (cell == 0) & (row < tiles - 1)
    return tuple(
        jnp.where(mask, 1.0, 0.0).astype(jnp.bfloat16) for mask in (from_before, from_after)
    )


def expand(x, out_ref, lead, pairs, tiles, masks):
    x = x.reshape(pairs, tiles, TILE)
    edge = pltpu.roll(x, 1, 1) * masks[0] + pltpu.roll(x, tiles - 1, 1) * masks[1]
    e0, e1 = edge[..., :LANES], edge[..., LANES:]
    r0, r1 = pltpu.roll(e0, LANES // 2, 2), pltpu.roll(e1, LANES // 2, 2)
    zero = jnp.zeros((1, tiles, LANES), x.dtype)
    low = jnp.concatenate([zero, x[:-1, :, LANES:]], 0)
    high = jnp.concatenate([x[1:, :, :LANES], zero], 0)
    e0 = e0 + jnp.concatenate([zero, r1[:-1]], 0)
    e1 = e1 + jnp.concatenate([r0[1:], zero], 0)
    flat = lambda v: v.reshape(pairs * tiles, v.shape[-1])
    out_ref[(*lead, slice(None), slice(0, TILE))] = flat(x)
    out_ref[(*lead, slice(None), slice(TILE, TILE + LANES))] = flat(low)
    out_ref[(*lead, slice(None), slice(TILE + LANES, 2 * TILE))] = flat(high)
    out_ref[(*lead, slice(None), slice(2 * TILE, 2 * TILE + LANES))] = flat(e0)
    out_ref[(*lead, slice(None), slice(2 * TILE + LANES, WIDE))] = flat(e1)


def conv_rows(x_ref, lead, start, rows, t_ref, layer):
    blocks = [x_ref[(*lead, pl.ds(start + a, rows))].reshape(-1, WIDE) for a in range(3)]
    return jnp.dot(
        jnp.concatenate(blocks, axis=1),
        t_ref[layer].reshape(3 * WIDE, TILE),
        preferred_element_type=jnp.float32,
    )


def slope_of(pre, gate):
    return gate * (1.0 + pre * (1.0 - gate))


def rounded(v):
    return v.astype(jnp.bfloat16)


def inside(v, row, depth):
    return jnp.where((row >= 0) & (row < depth), v, 0.0)


def either(flag, a, b):
    low = lambda *at: jnp.where(flag, a[at], b[at])
    high = lambda *at: jnp.where(flag, b[at], a[at])
    return low, high


def widen(near, own, far, lead, x_ref, x_lead, grow):
    low, high = either(lax.axis_index("depth") % 2 == 1, near, far)
    halo, rows = near.shape[len(lead)], own.shape[len(lead)]
    for base, part, count in (
        (0, low, halo),
        (halo, lambda *at: own[at], rows),
        (halo + rows, high, halo),
    ):
        for d in range(count):
            grow(part(*lead, d), x_ref, (*x_lead, base + d))


def layer_one(xv, lead, out_ref, t_ref, slopes_ref=None):
    rows, cells = out_ref.shape[len(lead)], out_ref.shape[-2]
    for start, count in chunks_of(rows):
        pre = conv_rows(xv, lead, start, count, t_ref, 0)
        gate = sigmoid(pre)
        value = (pre * gate).astype(jnp.bfloat16).reshape(count, cells, TILE)
        out_ref[(*lead, pl.ds(start, count))] = value
        if slopes_ref is not None:
            slope = slope_of(pre, gate).reshape(count, cells, TILE)
            for d in range(count):
                to = start + d - (H_HIDDEN - H_G1)
                if 0 <= to < slopes_ref.shape[0]:
                    slopes_ref[to] = slope[d]


def tiled_rows(load, height, tiles, scratch, at):
    for t in range(tiles):
        scratch[at, t * height : (t + 1) * height, :] = load(t).astype(jnp.float32)
    for h in range(height):
        piece = scratch[at, pl.ds(h, tiles, stride=height), :].astype(jnp.bfloat16)
        yield h // 2 * tiles, slice(h % 2 * LANES, (h % 2 + 1) * LANES), piece


def select_body(partner, both, *refs):
    *crops, out, scratch = refs
    own = lax.axis_index("sample")
    inverse = jnp.int32(0)
    for crop in range(partner.shape[0]):
        inverse = jnp.where(partner[crop] == own, crop, inverse)
    wanted = (partner[own], inverse)[2 - out.shape[0] :]
    _, rows, height, lanes = both.shape
    tiles = lanes // LANES
    mine = both.at[2 - out.shape[0]]
    for to, crop in enumerate(wanted):
        for hop, source in enumerate((mine, *crops)):

            @pl.when(crop ^ own == hop)
            def _(to=to, source=source):
                for d in range(rows):
                    for t in range(tiles):
                        scratch[to, d, t * height : (t + 1) * height, :] = source[
                            d, :, lanes_of(t)
                        ].astype(jnp.float32)

        for d in range(rows):
            for h in range(height):
                piece = scratch[to, d, pl.ds(h, tiles, stride=height), :].astype(jnp.bfloat16)
                row, side = h // 2 * tiles, lanes_of(h % 2)
                out[to, d, row : row + tiles, side] = piece


def own_body(
    pairs, tiles,
    taps_ref, near, both, far,
    t_ref, hid, sl1, xv_own, cot_own,
    xv, field, scratch,
):
    _, rows, height, _ = both.shape
    fill_weights(taps_ref, t_ref)
    grow = functools.partial(expand, pairs=pairs, tiles=tiles, masks=edge_masks(tiles))
    for at, part in enumerate((near, both.at[0], far, both.at[1])):
        for d in range(rows):
            load = lambda t, part=part, d=d: part[d, :, lanes_of(t)]
            for row, side, piece in tiled_rows(load, height, tiles, scratch, at * rows + d):
                if at < 3:
                    field[at, d, row : row + tiles, side] = piece
                else:
                    cot_own[d, row : row + tiles, side] = piece
    widen(field.at[0], field.at[1], field.at[2], (), xv, (), grow)
    layer_one(xv, (), hid, t_ref, sl1)
    xv_own[...] = xv[rows - 1 : 2 * rows + 1]


def forward_body(
    depth, pairs, tiles,
    near, mid, far, hid_own, cot_own, cot_other, t_ref,
    g3, g3_near, g3_far, sl2, xb_own, xs_own,
    xv, hid, xb, xs,
):
    rows = mid.shape[1]
    cells = pairs * tiles
    first = lax.axis_index("depth") * rows
    grow = functools.partial(expand, pairs=pairs, tiles=tiles, masks=edge_masks(tiles))

    for crop in range(2):
        widen(near, mid, far, (crop,), xv, (crop,), grow)
        layer_one(xv, (crop,), hid, t_ref)

    for d in range(rows + 2 * H_HIDDEN):
        own = hid_own[d].astype(jnp.float32)
        partner, other = hid[0, d].astype(jnp.float32), hid[1, d].astype(jnp.float32)
        row = first + d - H_HIDDEN
        for j, (a, b) in enumerate(((own, partner), (other, own))):
            mixed = OWN_SHARE * a + PARTNER_SHARE * b
            grow(rounded(inside(mixed, row, depth)), xb, (j, d))

    def middle(j, cot):
        for start, count in chunks_of(rows + 2 * H_TWO):
            pre = conv_rows(xb, (j,), start, count, t_ref, 1)
            gate = sigmoid(pre)
            value = (pre * gate).reshape(count, cells, TILE)
            slope = slope_of(pre, gate).reshape(count, cells, TILE)
            for d in range(count):
                sl2[j, start + d] = slope[d]
                to = start + d - (H_TWO - 1)
                if 0 <= to < rows + 2:
                    grow(rounded(inside(value[d], first + to - 1, depth)), xs, (j, to))
        for start, count in chunks_of(rows):
            pre = conv_rows(xs, (j,), start, count, t_ref, 2)
            slope = slope_of(pre, sigmoid(pre)).reshape(count, cells, TILE)
            for d in range(count):
                at = start + d
                grad = rounded(cot[at].astype(jnp.float32) * slope[d])
                g3[j, at] = grad

    middle(0, cot_own)
    middle(1, cot_other.at[0])
    odd = lax.axis_index("depth") % 2 == 1
    for j in range(2):
        for d in range(H_G3):
            up, down = g3[j, rows - H_G3 + d], g3[j, d]
            g3_near[j, d] = jnp.where(odd, down, up)
            g3_far[j, d] = jnp.where(odd, up, down)
    xb_own[...] = xb[0, H_HIDDEN - 1 : H_HIDDEN + rows + 1]
    xs_own[...] = xs[0]


def kernel_terms(values, gradient, rw):
    rows = gradient.shape[0]
    gradient = gradient.reshape(-1, TILE)
    for a in range(3):
        block = values[a : a + rows].reshape(-1, WIDE)
        terms = lax.dot_general(
            block, gradient, (((0,), (0,)), ((), ())), preferred_element_type=jnp.float32
        )
        for b in range(3):
            for c in range(3):
                at = (a * 9 + b * 3 + c) * CH
                for w in range(CELLS):
                    s0, s1 = SLOT_OF[b, w + c] * CH, SLOT_OF[b + 1, w + c] * CH
                    rw[w, at : at + CH] = (
                        terms[s0 : s0 + CH, :LANES] + terms[s1 : s1 + CH, LANES:]
                    )
    count = rw.shape[1] // CELLS
    cell = lax.broadcasted_iota(jnp.int32, (count, LANES), 1) // CH
    dense = jnp.zeros((count, LANES), jnp.float32)
    for q in range(CELLS):
        part = None
        for w in range(CELLS):
            piece = rw[w, pl.ds(q, count, stride=CELLS), :]
            if q != w:
                piece = pltpu.roll(piece, (q - w) % CELLS * CH, 1)
            part = piece if part is None else part + piece
        dense = jnp.where(cell == q, part, dense)
    return dense.astype(jnp.bfloat16)


def between_body(taps_ref, xs_own, g3, t_ref, terms, rw):
    fill_weights(taps_ref, t_ref)
    terms[...] = kernel_terms(xs_own[...], g3[0], rw)


def back_two(j, x_ref, sl2, x2_ref, t_ref, first, depth, grow):
    rows, cells = x2_ref.shape[-3:-1]
    for start, count in chunks_of(rows):
        back = conv_rows(x_ref, (), start, count, t_ref, 2).reshape(count, cells, TILE)
        for d in range(count):
            at = start + d
            grad = inside(back[d] * sl2[j, at], first + at - H_G2, depth)
            grow(rounded(grad), x2_ref, (at,))


def back_body(
    depth, pairs, tiles,
    near, mid, far, sl1, sl2, xv_own, xb_own, t_ref,
    xg1, terms,
    xg3, xg2, rw,
):
    rows = mid.shape[1]
    cells = pairs * tiles
    first = lax.axis_index("depth") * rows
    grow = functools.partial(expand, pairs=pairs, tiles=tiles, masks=edge_masks(tiles))
    for j in range(2):
        widen(near, mid, far, (j,), xg3.at[j], (), grow)
        back_two(j, xg3.at[j], sl2, xg2.at[j], t_ref, first, depth, grow)
    for start, count in chunks_of(rows + 2 * H_G1):
        own, other = (
            rounded(conv_rows(xg2, (j,), start, count, t_ref, 1)).astype(jnp.float32)
            for j in range(2)
        )
        mixed = (OWN_SHARE * own + PARTNER_SHARE * other).reshape(count, cells, TILE)
        for d in range(count):
            at = start + d
            grad = inside(mixed[d] * sl1[at], first + at - H_G1, depth)
            grow(rounded(grad), xg1, (at,))
    terms[0] = kernel_terms(xv_own[...], xg1[H_G1 : H_G1 + rows, :, :TILE], rw)
    terms[1] = kernel_terms(xb_own[...], xg2[0, H_G2 : H_G2 + rows, :, :TILE], rw)


def last_body(pairs, tiles, xg1, t_ref, gv, scratch):
    rows, height, _ = gv.shape
    cells = pairs * tiles
    for start, count in chunks_of(rows):
        back = conv_rows(xg1, (), start, count, t_ref, 0).reshape(count, cells, TILE)
        for d in range(count):
            for h in range(height):
                row, side = h // 2 * tiles, slice(h % 2 * LANES, (h % 2 + 1) * LANES)
                scratch[start + d, pl.ds(h, tiles, stride=height), :] = back[
                    d, row : row + tiles, side
                ]
            for t in range(tiles):
                gv[start + d, :, t * LANES : (t + 1) * LANES] = scratch[
                    start + d, t * height : (t + 1) * height, :
                ].astype(jnp.bfloat16)


def tree_sum(parts):
    parts = [part.astype(jnp.float32) for part in parts]
    while len(parts) > 1:
        parts = [a + b for a, b in zip(parts[::2], parts[1::2])]
    return parts[0]


def total_body(count, *refs):
    *parts, out = refs
    for layer in range(2):
        out[layer] = tree_sum([part[layer] for part in parts[:count]])
    out[2] = tree_sum([part[...] for part in parts[count:]])


def by_hop(values):
    count = lax.axis_size("depth")
    swap = lambda hop: lax.ppermute(values, "depth", [(i, i ^ hop) for i in range(count)])
    return [values, *(swap(hop) for hop in range(1, count))]


def neighbours(near, far):
    count = lax.axis_size("depth")
    result = []
    for values, first in ((near, 0), (far, 1)):
        lower = range(first, count - 1, 2)
        pairs = [(i, i + 1) for i in lower] + [(i + 1, i) for i in lower]
        result.append(lax.ppermute(values, "depth", pairs))
    return result


def over_sample(values, hop):
    groups = lax.axis_size("sample")
    return lax.ppermute(values, "sample", [(i, i ^ hop) for i in range(groups)])


def even_hops(values):
    return [over_sample(values, hop) for hop in range(2, lax.axis_size("sample"), 2)]


def all_hops(odd, evens):
    return [odd, *(crop for even in evens for crop in (even, over_sample(even, 1)))]


def traded(volume, cotangent, partner, tiles):
    groups = lax.axis_size("sample")
    rows, height, _ = volume.shape
    split = jnp.stack([volume, cotangent]).reshape(2, rows, height // 2, 2, tiles, LANES)
    split = split.transpose(0, 1, 2, 4, 3, 5).reshape(2, groups, -1, TILE)
    pieces = split.swapaxes(0, 1)
    spread = lax.all_to_all(pieces, "sample", split_axis=0, concat_axis=0, tiled=True)
    ids = jnp.arange(groups, dtype=jnp.int32)
    inverse = jnp.sum(jnp.where(partner[:, None] == ids[None, :], ids[:, None], 0), axis=0)
    wanted = jnp.stack([2 * partner, 2 * inverse, 2 * inverse + 1], axis=1)
    chosen = jnp.take(spread.reshape(2 * groups, -1, TILE), wanted, axis=0)
    joined = lax.all_to_all(chosen, "sample", split_axis=0, concat_axis=0, tiled=True)
    others = jnp.swapaxes(joined, 0, 1).reshape(3, rows, -1, TILE)
    return others[:2], others[2:]


def call(kernel, outs, scratch, inputs, macs=0, far=()):
    vmem, smem, anywhere = (
        pl.BlockSpec(memory_space=space) for space in (pltpu.VMEM, pltpu.SMEM, pl.ANY)
    )
    specs = [
        anywhere if at in far else smem if x.dtype == jnp.int32 else vmem
        for at, x in enumerate(inputs)
    ]
    results = pl.pallas_call(
        kernel,
        out_shape=tuple(jax.ShapeDtypeStruct(shape, dtype) for shape, dtype in outs),
        in_specs=specs,
        out_specs=(vmem,) * len(outs),
        scratch_shapes=scratch,
        compiler_params=pltpu.CompilerParams(vmem_limit_bytes=VMEM_LIMIT),
        cost_estimate=pl.CostEstimate(
            flops=2 * macs, bytes_accessed=2**22 if macs else 1, transcendentals=0
        ),
    )(*inputs)
    return results if len(results) > 1 else results[0]


def per_device(volume, kernels, partner, cotangent):
    volume, cotangent = volume[0], cotangent[0]
    rows, height, lanes = volume.shape
    pairs, tiles = height // 2, lanes // LANES
    cells = pairs * tiles
    groups, count = lax.axis_size("sample"), lax.axis_size("depth")
    depth = rows * count
    layers, taps, width = kernels.shape
    bf16, f32 = jnp.bfloat16, jnp.float32
    row_macs = 3 * cells * WIDE * TILE
    packed_rows = taps * CH // CELLS
    wide = lambda *lead: pltpu.VMEM((*lead, cells, WIDE), bf16)
    field = lambda *lead: ((*lead, cells, TILE), bf16)
    raw_tiles = lambda *lead: pltpu.VMEM((*lead, height * tiles, LANES), f32)
    banded = ((layers, 3, WIDE, TILE), bf16)
    spread_taps = ((layers, taps * CH, LANES), bf16)
    rw = pltpu.VMEM((CELLS, taps * CH, LANES), f32)

    direct = groups in (2, 4, 8)
    evens = even_hops(volume) if direct else []
    odd = over_sample(volume, 1) if direct else volume
    both = jnp.stack([volume, cotangent])
    packed = kernels.reshape(layers, packed_rows, LANES)
    ids = jnp.clip(partner, 0, groups - 1)
    fwd_taps, bwd_taps = call(
        functools.partial(taps_body, taps),
        [spread_taps, spread_taps],
        [pltpu.VMEM((layers, -(-taps // CELLS) * LANES, LANES), f32)],
        [packed],
        2**28,
    )
    evens, both, ids, fwd_taps, bwd_taps, edges, late = lax.optimization_barrier(
        (evens, both, ids, fwd_taps, bwd_taps, volume, cotangent)
    )
    near, far = neighbours(edges, edges)
    if direct:
        crops = all_hops(odd, evens)
        crops, near, far = lax.optimization_barrier((crops, near, far))
        vol = call(select_body, [field(2, rows)], [raw_tiles(2, rows)], [ids, both, *crops])
        vol_near, vol_far = neighbours(vol, vol)
        odd, evens = over_sample(late, 1), even_hops(late)
        evens, vol = lax.optimization_barrier((evens, vol))
        cot_other = call(
            select_body,
            [field(1, rows)],
            [raw_tiles(1, rows)],
            [ids, both, *all_hops(odd, evens)],
        )
    else:
        vol, cot_other = traded(volume, cotangent, partner, tiles)
        vol_near, vol_far = neighbours(vol, vol)
    hid_rows = rows + 2 * H_HIDDEN
    fwd, hid_own, sl1, xv_own, cot_own = call(
        functools.partial(own_body, pairs, tiles),
        [
            banded,
            field(hid_rows),
            ((rows + 2 * H_G1, cells, TILE), f32),
            ((rows + 2, cells, WIDE), bf16),
            field(rows),
        ],
        [wide(3 * rows), pltpu.VMEM((3, rows, cells, TILE), bf16), raw_tiles(4 * rows)],
        [fwd_taps, near, both, far],
        hid_rows * row_macs,
    )

    g3, g3_near, g3_far, sl2, xb_own, xs_own = call(
        functools.partial(forward_body, depth, pairs, tiles),
        [
            field(2, rows),
            field(2, H_G3),
            field(2, H_G3),
            ((2, rows + 2 * H_TWO, cells, TILE), f32),
            ((rows + 2, cells, WIDE), bf16),
            ((rows + 2, cells, WIDE), bf16),
        ],
        [
            wide(2, 3 * rows),
            pltpu.VMEM((2, hid_rows, cells, TILE), bf16),
            wide(2, hid_rows),
            wide(2, rows + 2),
        ],
        [vol_near, vol, vol_far, hid_own, cot_own, cot_other, fwd],
        (2 * hid_rows + 2 * (rows + 4) + 2 * rows) * row_macs,
    )

    near, far = neighbours(g3_near, g3_far)
    terms = ((packed_rows, LANES), bf16)
    bwd, three = call(
        between_body, [banded, terms], [rw], [bwd_taps, xs_own, g3], rows * row_macs
    )
    three = by_hop(three)
    xg1, others = call(
        functools.partial(back_body, depth, pairs, tiles),
        [((rows + 2 * H_G1, cells, WIDE), bf16), ((2, packed_rows, LANES), bf16)],
        [wide(2, rows + 2 * H_G3), wide(2, rows + 2 * H_G2), rw],
        [near, g3, far, sl1, sl2, xv_own, xb_own, bwd],
        (6 * rows + 12) * row_macs,
    )
    others, three = lax.optimization_barrier((others, three))
    others = by_hop(others)
    grad_volume = call(
        functools.partial(last_body, pairs, tiles),
        [((rows, height, lanes), bf16)],
        [raw_tiles(rows)],
        [xg1, bwd],
        rows * row_macs,
    )
    total = call(
        functools.partial(total_body, count),
        [((layers, packed_rows, LANES), f32)],
        [],
        [*others, *three],
    )
    return (grad_volume[None], total.reshape(1, layers, taps, width))


def solution(mesh):
    in_specs = (P("sample", "depth", None, None), P(), P(), P("sample", "depth", None, None))
    out_specs = (P("sample", "depth", None, None), P("sample", None, None, None))
    return jax.shard_map(
        per_device, mesh=mesh, in_specs=in_specs, out_specs=out_specs, check_vma=False
    )
```

```python
import functools

import jax
import jax.numpy as jnp
from jax import lax
from jax.experimental import pallas as pl
from jax.experimental.pallas import tpu as pltpu
from jax.sharding import PartitionSpec as P

CH = 32
OWN_SHARE = 0.6
PARTNER_SHARE = 0.4
LANES = 128
CELLS = LANES // CH
TILE = 2 * LANES
WIDE = 3 * TILE
VMEM_LIMIT = 40 * 2**20

SLOTS = (
    [(1 + h, 1 + w) for h in range(2) for w in range(CELLS)]
    + [(0, 1 + w) for w in range(CELLS)]
    + [(3, 1 + w) for w in range(CELLS)]
    + [(1, 5), (0, 0), (0, 5), (1, 0)]
    + [(2, 5), (3, 0), (3, 5), (2, 0)]
)
SLOT_OF = {cell: at for at, cell in enumerate(SLOTS)}

H_HIDDEN, H_TWO, H_G3, H_G2, H_G1 = 3, 2, 3, 2, 1


def chunks_of(rows):
    count = max(1, (rows + 2) // 5)
    base, extra = divmod(rows, count)
    start, result = 0, []
    for index in range(count):
        size = base + (index < extra)
        result.append((start, size))
        start += size
    return result


def sigmoid(v):
    return 0.5 + 0.5 * jnp.tanh(0.5 * v)


def lanes_of(t):
    return slice(t * LANES, (t + 1) * LANES)


def taps_body(taps, kr_ref, fwd_ref, bwd_ref, scratch):
    layers, rows = kr_ref.shape[:2]
    part = scratch.shape[1] // CELLS // CH
    shape = (LANES, CELLS * LANES)
    lane = lax.broadcasted_iota(jnp.int32, shape, 1)
    chosen = lax.broadcasted_iota(jnp.int32, shape, 0) == lane // LANES * CH + lane % CH
    spread = jnp.where(chosen, 1.0, 0.0).astype(jnp.bfloat16)
    for layer in range(layers):
        groups = jnp.dot(kr_ref[layer], spread, preferred_element_type=jnp.float32)
        for q in range(CELLS):
            scratch[layer, pl.ds(q, rows, stride=CELLS), :] = groups[:, lanes_of(q)]
        scratch[layer, taps * CH :, :] = jnp.zeros_like(scratch[layer, taps * CH :, :])
        fwd_ref[layer] = scratch[layer, : taps * CH].astype(jnp.bfloat16)
        cell = lax.broadcasted_iota(jnp.int32, (part * CH, LANES), 1) // CH
        compact = jnp.zeros((part * CH, LANES), jnp.float32)
        for group in range(CELLS):
            at = group * part * CH
            compact = jnp.where(cell == group, scratch[layer, at : at + part * CH, :], compact)
        room = -(-part // CELLS) * LANES - part * CH
        turned = jnp.concatenate([compact, jnp.zeros((room, LANES), jnp.float32)], 0).T
        stacked = jnp.concatenate(
            [turned[:, lanes_of(t)] for t in range(turned.shape[1] // LANES)], 0
        ).astype(jnp.bfloat16)
        groups = jnp.dot(stacked, spread, preferred_element_type=jnp.float32)
        for tap in range(taps):
            group, index = divmod(tap, part)
            at, row = taps - 1 - tap, index // CELLS * LANES + group * CH
            bwd_ref[layer, at * CH : (at + 1) * CH, :] = groups[
                row : row + CH, lanes_of(index % CELLS)
            ].astype(jnp.bfloat16)


def fill_weights(taps_ref, t_ref):
    cell = lax.broadcasted_iota(jnp.int32, (CH, LANES), 1) // CH
    zero = jnp.zeros((CH, LANES), jnp.bfloat16)
    for layer in range(t_ref.shape[0]):
        for a in range(3):
            bands = {}
            for b in range(3):
                first = (a * 9 + b * 3) * CH
                values = [taps_ref[layer, first + c * CH : first + (c + 1) * CH, :] for c in range(3)]
                for ww in range(CELLS + 2):
                    band = zero
                    for c in range(3):
                        if 0 <= ww - c < CELLS:
                            band = jnp.where(cell == ww - c, values[c], band)
                    bands[b, ww] = band
            for at, (hh, ww) in enumerate(SLOTS):
                for h in range(2):
                    t_ref[
                        layer, a, at * CH : (at + 1) * CH, h * LANES : (h + 1) * LANES
                    ] = bands.get((hh - h, ww), zero)


def edge_masks(tiles):
    shape = (1, tiles, TILE)
    cell = lax.broadcasted_iota(jnp.int32, shape, 2) % LANES // CH
    row = lax.broadcasted_iota(jnp.int32, shape, 1)
    from_before = (cell == CELLS - 1) & (row > 0)
    from_after = (cell == 0) & (row < tiles - 1)
    return tuple(
        jnp.where(mask, 1.0, 0.0).astype(jnp.bfloat16) for mask in (from_before, from_after)
    )


def expand(x, out_ref, lead, pairs, tiles, masks):
    x = x.reshape(pairs, tiles, TILE)
    edge = pltpu.roll(x, 1, 1) * masks[0] + pltpu.roll(x, tiles - 1, 1) * masks[1]
    e0, e1 = edge[..., :LANES], edge[..., LANES:]
    r0, r1 = pltpu.roll(e0, LANES // 2, 2), pltpu.roll(e1, LANES // 2, 2)
    zero = jnp.zeros((1, tiles, LANES), x.dtype)
    low = jnp.concatenate([zero, x[:-1, :, LANES:]], 0)
    high = jnp.concatenate([x[1:, :, :LANES], zero], 0)
    e0 = e0 + jnp.concatenate([zero, r1[:-1]], 0)
    e1 = e1 + jnp.concatenate([r0[1:], zero], 0)
    flat = lambda v: v.reshape(pairs * tiles, v.shape[-1])
    out_ref[(*lead, slice(None), slice(0, TILE))] = flat(x)
    out_ref[(*lead, slice(None), slice(TILE, TILE + LANES))] = flat(low)
    out_ref[(*lead, slice(None), slice(TILE + LANES, 2 * TILE))] = flat(high)
    out_ref[(*lead, slice(None), slice(2 * TILE, 2 * TILE + LANES))] = flat(e0)
    out_ref[(*lead, slice(None), slice(2 * TILE + LANES, WIDE))] = flat(e1)


def conv_rows(x_ref, lead, start, rows, t_ref, layer):
    blocks = [x_ref[(*lead, pl.ds(start + a, rows))].reshape(-1, WIDE) for a in range(3)]
    return jnp.dot(
        jnp.concatenate(blocks, axis=1),
        t_ref[layer].reshape(3 * WIDE, TILE),
        preferred_element_type=jnp.float32,
    )


def slope_of(pre, gate):
    return gate * (1.0 + pre * (1.0 - gate))


def rounded(v):
    return v.astype(jnp.bfloat16)


def inside(v, row, depth):
    return jnp.where((row >= 0) & (row < depth), v, 0.0)


def either(flag, a, b):
    low = lambda *at: jnp.where(flag, a[at], b[at])
    high = lambda *at: jnp.where(flag, b[at], a[at])
    return low, high


def widen(near, own, far, lead, x_ref, x_lead, grow):
    at, last = lax.axis_index("depth"), lax.axis_size("depth") - 1
    low, high = either(at % 2 == 1, near, far)
    halo, rows = near.shape[len(lead)], own.shape[len(lead)]
    for d in range(halo):
        row = low(*lead, d)
        if d == halo - 1:
            row = jnp.where(at > 0, row, jnp.zeros_like(row))
        grow(row, x_ref, (*x_lead, d))
    for d in range(rows):
        grow(own[(*lead, d)], x_ref, (*x_lead, halo + d))
    for d in range(halo):
        row = high(*lead, d)
        if d == 0:
            row = jnp.where(at < last, row, jnp.zeros_like(row))
        grow(row, x_ref, (*x_lead, halo + rows + d))


def layer_one(xv, lead, out_ref, t_ref, slopes_ref=None):
    rows, cells = out_ref.shape[len(lead)], out_ref.shape[-2]
    for start, count in chunks_of(rows):
        pre = conv_rows(xv, lead, start, count, t_ref, 0)
        gate = sigmoid(pre)
        value = (pre * gate).astype(jnp.bfloat16).reshape(count, cells, TILE)
        out_ref[(*lead, pl.ds(start, count))] = value
        if slopes_ref is not None:
            slope = slope_of(pre, gate).reshape(count, cells, TILE)
            for d in range(count):
                to = start + d - (H_HIDDEN - H_G1)
                if 0 <= to < slopes_ref.shape[0]:
                    slopes_ref[to] = slope[d]


def tiled_rows(load, height, tiles, scratch, at):
    for t in range(tiles):
        scratch[at, t * height : (t + 1) * height, :] = load(t).astype(jnp.float32)
    for h in range(height):
        piece = scratch[at, pl.ds(h, tiles, stride=height), :].astype(jnp.bfloat16)
        yield h // 2 * tiles, slice(h % 2 * LANES, (h % 2 + 1) * LANES), piece


def select_body(partner, both, *refs):
    *crops, out, scratch = refs
    own = lax.axis_index("sample")
    inverse = jnp.int32(0)
    for crop in range(partner.shape[0]):
        inverse = jnp.where(partner[crop] == own, crop, inverse)
    wanted = (partner[own], inverse)[2 - out.shape[0] :]
    _, rows, height, lanes = both.shape
    tiles = lanes // LANES
    mine = both.at[2 - out.shape[0]]
    for to, crop in enumerate(wanted):
        for hop, source in enumerate((mine, *crops)):

            @pl.when(crop ^ own == hop)
            def _(to=to, source=source):
                for d in range(rows):
                    for t in range(tiles):
                        scratch[to, d, t * height : (t + 1) * height, :] = source[
                            d, :, lanes_of(t)
                        ].astype(jnp.float32)

        for d in range(rows):
            for h in range(height):
                piece = scratch[to, d, pl.ds(h, tiles, stride=height), :].astype(jnp.bfloat16)
                row, side = h // 2 * tiles, lanes_of(h % 2)
                out[to, d, row : row + tiles, side] = piece


def own_body(
    pairs, tiles,
    taps_ref, near, both, far,
    t_ref, hid, sl1, xv_own, cot_own,
    xv, field, scratch,
):
    _, rows, height, _ = both.shape
    fill_weights(taps_ref, t_ref)
    grow = functools.partial(expand, pairs=pairs, tiles=tiles, masks=edge_masks(tiles))
    for at, part in enumerate((near, both.at[0], far, both.at[1])):
        for d in range(rows):
            load = lambda t, part=part, d=d: part[d, :, lanes_of(t)]
            for row, side, piece in tiled_rows(load, height, tiles, scratch, at * rows + d):
                if at < 3:
                    field[at, d, row : row + tiles, side] = piece
                else:
                    cot_own[d, row : row + tiles, side] = piece
    widen(field.at[0], field.at[1], field.at[2], (), xv, (), grow)
    layer_one(xv, (), hid, t_ref, sl1)
    xv_own[...] = xv[rows - 1 : 2 * rows + 1]


def forward_body(
    depth, pairs, tiles,
    near, mid, far, hid_own, cot_own, cot_other, t_ref,
    g3, g3_near, g3_far, sl2, xb_own, xs_own,
    xv, hid, xb, xs,
):
    rows = mid.shape[1]
    cells = pairs * tiles
    first = lax.axis_index("depth") * rows
    grow = functools.partial(expand, pairs=pairs, tiles=tiles, masks=edge_masks(tiles))

    for crop in range(2):
        widen(near, mid, far, (crop,), xv, (crop,), grow)
        layer_one(xv, (crop,), hid, t_ref)

    for d in range(rows + 2 * H_HIDDEN):
        own = hid_own[d].astype(jnp.float32)
        partner, other = hid[0, d].astype(jnp.float32), hid[1, d].astype(jnp.float32)
        row = first + d - H_HIDDEN
        for j, (a, b) in enumerate(((own, partner), (other, own))):
            mixed = OWN_SHARE * a + PARTNER_SHARE * b
            grow(rounded(inside(mixed, row, depth)), xb, (j, d))

    def middle(j, cot):
        for start, count in chunks_of(rows + 2 * H_TWO):
            pre = conv_rows(xb, (j,), start, count, t_ref, 1)
            gate = sigmoid(pre)
            value = (pre * gate).reshape(count, cells, TILE)
            slope = slope_of(pre, gate).reshape(count, cells, TILE)
            for d in range(count):
                sl2[j, start + d] = slope[d]
                to = start + d - (H_TWO - 1)
                if 0 <= to < rows + 2:
                    grow(rounded(inside(value[d], first + to - 1, depth)), xs, (j, to))
        for start, count in chunks_of(rows):
            pre = conv_rows(xs, (j,), start, count, t_ref, 2)
            slope = slope_of(pre, sigmoid(pre)).reshape(count, cells, TILE)
            for d in range(count):
                at = start + d
                grad = rounded(cot[at].astype(jnp.float32) * slope[d])
                g3[j, at] = grad

    middle(0, cot_own)
    middle(1, cot_other.at[0])
    odd = lax.axis_index("depth") % 2 == 1
    for j in range(2):
        for d in range(H_G3):
            up, down = g3[j, rows - H_G3 + d], g3[j, d]
            g3_near[j, d] = jnp.where(odd, down, up)
            g3_far[j, d] = jnp.where(odd, up, down)
    xb_own[...] = xb[0, H_HIDDEN - 1 : H_HIDDEN + rows + 1]
    xs_own[...] = xs[0]


def kernel_terms(values, gradient, rw):
    rows = gradient.shape[0]
    gradient = gradient.reshape(-1, TILE)
    for a in range(3):
        block = values[a : a + rows].reshape(-1, WIDE)
        terms = lax.dot_general(
            block, gradient, (((0,), (0,)), ((), ())), preferred_element_type=jnp.float32
        )
        for b in range(3):
            for c in range(3):
                at = (a * 9 + b * 3 + c) * CH
                for w in range(CELLS):
                    s0, s1 = SLOT_OF[b, w + c] * CH, SLOT_OF[b + 1, w + c] * CH
                    rw[w, at : at + CH] = (
                        terms[s0 : s0 + CH, :LANES] + terms[s1 : s1 + CH, LANES:]
                    )
    count = rw.shape[1] // CELLS
    cell = lax.broadcasted_iota(jnp.int32, (count, LANES), 1) // CH
    dense = jnp.zeros((count, LANES), jnp.float32)
    for q in range(CELLS):
        part = None
        for w in range(CELLS):
            piece = rw[w, pl.ds(q, count, stride=CELLS), :]
            if q != w:
                piece = pltpu.roll(piece, (q - w) % CELLS * CH, 1)
            part = piece if part is None else part + piece
        dense = jnp.where(cell == q, part, dense)
    return dense.astype(jnp.bfloat16)


def between_body(taps_ref, xs_own, g3, t_ref, terms, rw):
    fill_weights(taps_ref, t_ref)
    terms[...] = kernel_terms(xs_own[...], g3[0], rw)


def back_two(j, x_ref, sl2, x2_ref, t_ref, first, depth, grow):
    rows, cells = x2_ref.shape[-3:-1]
    for start, count in chunks_of(rows):
        back = conv_rows(x_ref, (), start, count, t_ref, 2).reshape(count, cells, TILE)
        for d in range(count):
            at = start + d
            grad = inside(back[d] * sl2[j, at], first + at - H_G2, depth)
            grow(rounded(grad), x2_ref, (at,))


def back_body(
    depth, pairs, tiles,
    near, mid, far, sl1, sl2, xv_own, xb_own, t_ref,
    xg1, terms,
    xg3, xg2, rw,
):
    rows = mid.shape[1]
    cells = pairs * tiles
    first = lax.axis_index("depth") * rows
    grow = functools.partial(expand, pairs=pairs, tiles=tiles, masks=edge_masks(tiles))
    for j in range(2):
        widen(near, mid, far, (j,), xg3.at[j], (), grow)
        back_two(j, xg3.at[j], sl2, xg2.at[j], t_ref, first, depth, grow)
    for start, count in chunks_of(rows + 2 * H_G1):
        own, other = (
            rounded(conv_rows(xg2, (j,), start, count, t_ref, 1)).astype(jnp.float32)
            for j in range(2)
        )
        mixed = (OWN_SHARE * own + PARTNER_SHARE * other).reshape(count, cells, TILE)
        for d in range(count):
            at = start + d
            grad = inside(mixed[d] * sl1[at], first + at - H_G1, depth)
            grow(rounded(grad), xg1, (at,))
    terms[0] = kernel_terms(xv_own[...], xg1[H_G1 : H_G1 + rows, :, :TILE], rw)
    terms[1] = kernel_terms(xb_own[...], xg2[0, H_G2 : H_G2 + rows, :, :TILE], rw)


def last_body(pairs, tiles, xg1, t_ref, gv, scratch):
    rows, height, _ = gv.shape
    cells = pairs * tiles
    for start, count in chunks_of(rows):
        back = conv_rows(xg1, (), start, count, t_ref, 0).reshape(count, cells, TILE)
        for d in range(count):
            for h in range(height):
                row, side = h // 2 * tiles, slice(h % 2 * LANES, (h % 2 + 1) * LANES)
                scratch[start + d, pl.ds(h, tiles, stride=height), :] = back[
                    d, row : row + tiles, side
                ]
            for t in range(tiles):
                gv[start + d, :, t * LANES : (t + 1) * LANES] = scratch[
                    start + d, t * height : (t + 1) * height, :
                ].astype(jnp.bfloat16)


def tree_sum(parts):
    parts = [part.astype(jnp.float32) for part in parts]
    while len(parts) > 1:
        parts = [a + b for a, b in zip(parts[::2], parts[1::2])]
    return parts[0]


def total_body(count, *refs):
    *parts, out = refs
    for layer in range(2):
        out[layer] = tree_sum([part[layer] for part in parts[:count]])
    out[2] = tree_sum([part[...] for part in parts[count:]])


def by_hop(values):
    count = lax.axis_size("depth")
    swap = lambda hop: lax.ppermute(values, "depth", [(i, i ^ hop) for i in range(count)])
    return [values, *(swap(hop) for hop in range(1, count))]


def neighbours(near, far):
    count = lax.axis_size("depth")
    result = []
    for values, first in ((near, 0), (far, 1)):
        partner = {}
        for i in range(first, count - 1, 2):
            partner[i], partner[i + 1] = i + 1, i
        pairs = [(i, partner.get(i, i)) for i in range(count)]
        result.append(lax.ppermute(values, "depth", pairs))
    return result


def over_sample(values, hop):
    groups = lax.axis_size("sample")
    return lax.ppermute(values, "sample", [(i, i ^ hop) for i in range(groups)])


def even_hops(values):
    return [over_sample(values, hop) for hop in range(2, lax.axis_size("sample"), 2)]


def all_hops(odd, evens):
    return [odd, *(crop for even in evens for crop in (even, over_sample(even, 1)))]


def traded(volume, cotangent, partner, tiles):
    groups = lax.axis_size("sample")
    rows, height, _ = volume.shape
    split = jnp.stack([volume, cotangent]).reshape(2, rows, height // 2, 2, tiles, LANES)
    split = split.transpose(0, 1, 2, 4, 3, 5).reshape(2, groups, -1, TILE)
    pieces = split.swapaxes(0, 1)
    spread = lax.all_to_all(pieces, "sample", split_axis=0, concat_axis=0, tiled=True)
    ids = jnp.arange(groups, dtype=jnp.int32)
    inverse = jnp.sum(jnp.where(partner[:, None] == ids[None, :], ids[:, None], 0), axis=0)
    wanted = jnp.stack([2 * partner, 2 * inverse, 2 * inverse + 1], axis=1)
    chosen = jnp.take(spread.reshape(2 * groups, -1, TILE), wanted, axis=0)
    joined = lax.all_to_all(chosen, "sample", split_axis=0, concat_axis=0, tiled=True)
    others = jnp.swapaxes(joined, 0, 1).reshape(3, rows, -1, TILE)
    return others[:2], others[2:]


def call(kernel, outs, scratch, inputs, macs=0, far=()):
    vmem, smem, anywhere = (
        pl.BlockSpec(memory_space=space) for space in (pltpu.VMEM, pltpu.SMEM, pl.ANY)
    )
    specs = [
        anywhere if at in far else smem if x.dtype == jnp.int32 else vmem
        for at, x in enumerate(inputs)
    ]
    results = pl.pallas_call(
        kernel,
        out_shape=tuple(jax.ShapeDtypeStruct(shape, dtype) for shape, dtype in outs),
        in_specs=specs,
        out_specs=(vmem,) * len(outs),
        scratch_shapes=scratch,
        compiler_params=pltpu.CompilerParams(vmem_limit_bytes=VMEM_LIMIT),
        cost_estimate=pl.CostEstimate(
            flops=2 * macs, bytes_accessed=2**22 if macs else 1, transcendentals=0
        ),
    )(*inputs)
    return results if len(results) > 1 else results[0]


def per_device(volume, kernels, partner, cotangent):
    volume, cotangent = volume[0], cotangent[0]
    rows, height, lanes = volume.shape
    pairs, tiles = height // 2, lanes // LANES
    cells = pairs * tiles
    groups, count = lax.axis_size("sample"), lax.axis_size("depth")
    depth = rows * count
    layers, taps, width = kernels.shape
    bf16, f32 = jnp.bfloat16, jnp.float32
    row_macs = 3 * cells * WIDE * TILE
    packed_rows = taps * CH // CELLS
    wide = lambda *lead: pltpu.VMEM((*lead, cells, WIDE), bf16)
    field = lambda *lead: ((*lead, cells, TILE), bf16)
    raw_tiles = lambda *lead: pltpu.VMEM((*lead, height * tiles, LANES), f32)
    banded = ((layers, 3, WIDE, TILE), bf16)
    spread_taps = ((layers, taps * CH, LANES), bf16)
    rw = pltpu.VMEM((CELLS, taps * CH, LANES), f32)

    direct = groups in (2, 4, 8)
    evens = even_hops(volume) if direct else []
    odd = over_sample(volume, 1) if direct else volume
    both = jnp.stack([volume, cotangent])
    packed = kernels.reshape(layers, packed_rows, LANES)
    ids = jnp.clip(partner, 0, groups - 1)
    fwd_taps, bwd_taps = call(
        functools.partial(taps_body, taps),
        [spread_taps, spread_taps],
        [pltpu.VMEM((layers, -(-taps // CELLS) * LANES, LANES), f32)],
        [packed],
        2**28,
    )
    evens, both, ids, fwd_taps, bwd_taps, edges, late = lax.optimization_barrier(
        (evens, both, ids, fwd_taps, bwd_taps, volume, cotangent)
    )
    near, far = neighbours(edges, edges)
    if direct:
        crops = all_hops(odd, evens)
        crops, near, far = lax.optimization_barrier((crops, near, far))
        vol = call(select_body, [field(2, rows)], [raw_tiles(2, rows)], [ids, both, *crops])
        vol_near, vol_far = neighbours(vol, vol)
        odd, evens = over_sample(late, 1), even_hops(late)
        evens, vol = lax.optimization_barrier((evens, vol))
        cot_other = call(
            select_body,
            [field(1, rows)],
            [raw_tiles(1, rows)],
            [ids, both, *all_hops(odd, evens)],
        )
    else:
        vol, cot_other = traded(volume, cotangent, partner, tiles)
        vol_near, vol_far = neighbours(vol, vol)
    hid_rows = rows + 2 * H_HIDDEN
    fwd, hid_own, sl1, xv_own, cot_own = call(
        functools.partial(own_body, pairs, tiles),
        [
            banded,
            field(hid_rows),
            ((rows + 2 * H_G1, cells, TILE), f32),
            ((rows + 2, cells, WIDE), bf16),
            field(rows),
        ],
        [wide(3 * rows), pltpu.VMEM((3, rows, cells, TILE), bf16), raw_tiles(4 * rows)],
        [fwd_taps, near, both, far],
        hid_rows * row_macs,
    )

    g3, g3_near, g3_far, sl2, xb_own, xs_own = call(
        functools.partial(forward_body, depth, pairs, tiles),
        [
            field(2, rows),
            field(2, H_G3),
            field(2, H_G3),
            ((2, rows + 2 * H_TWO, cells, TILE), f32),
            ((rows + 2, cells, WIDE), bf16),
            ((rows + 2, cells, WIDE), bf16),
        ],
        [
            wide(2, 3 * rows),
            pltpu.VMEM((2, hid_rows, cells, TILE), bf16),
            wide(2, hid_rows),
            wide(2, rows + 2),
        ],
        [vol_near, vol, vol_far, hid_own, cot_own, cot_other, fwd],
        (2 * hid_rows + 2 * (rows + 4) + 2 * rows) * row_macs,
    )

    near, far = neighbours(g3_near, g3_far)
    terms = ((packed_rows, LANES), bf16)
    bwd, three = call(
        between_body, [banded, terms], [rw], [bwd_taps, xs_own, g3], rows * row_macs
    )
    three = by_hop(three)
    xg1, others = call(
        functools.partial(back_body, depth, pairs, tiles),
        [((rows + 2 * H_G1, cells, WIDE), bf16), ((2, packed_rows, LANES), bf16)],
        [wide(2, rows + 2 * H_G3), wide(2, rows + 2 * H_G2), rw],
        [near, g3, far, sl1, sl2, xv_own, xb_own, bwd],
        (6 * rows + 12) * row_macs,
    )
    others, three = lax.optimization_barrier((others, three))
    others = by_hop(others)
    grad_volume = call(
        functools.partial(last_body, pairs, tiles),
        [((rows, height, lanes), bf16)],
        [raw_tiles(rows)],
        [xg1, bwd],
        rows * row_macs,
    )
    total = call(
        functools.partial(total_body, count),
        [((layers, packed_rows, LANES), f32)],
        [],
        [*others, *three],
    )
    return (grad_volume[None], total.reshape(1, layers, taps, width))


def solution(mesh):
    in_specs = (P("sample", "depth", None, None), P(), P(), P("sample", "depth", None, None))
    out_specs = (P("sample", "depth", None, None), P("sample", None, None, None))
    return jax.shard_map(
        per_device, mesh=mesh, in_specs=in_specs, out_specs=out_specs, check_vma=False
    )
```

```python
import functools

import jax
import jax.numpy as jnp
from jax import lax
from jax.experimental import pallas as pl
from jax.experimental.pallas import tpu as pltpu
from jax.sharding import PartitionSpec as P

CH = 32
OWN_SHARE = 0.6
PARTNER_SHARE = 0.4
LANES = 128
CELLS = LANES // CH
TILE = 2 * LANES
WIDE = 3 * TILE
VMEM_LIMIT = 40 * 2**20

SLOTS = (
    [(1 + h, 1 + w) for h in range(2) for w in range(CELLS)]
    + [(0, 1 + w) for w in range(CELLS)]
    + [(3, 1 + w) for w in range(CELLS)]
    + [(1, 5), (0, 0), (0, 5), (1, 0)]
    + [(2, 5), (3, 0), (3, 5), (2, 0)]
)
SLOT_OF = {cell: at for at, cell in enumerate(SLOTS)}

H_HIDDEN, H_TWO, H_G3, H_G2, H_G1 = 3, 2, 3, 2, 1


def chunks_of(rows):
    count = max(1, (rows + 2) // 5)
    base, extra = divmod(rows, count)
    start, result = 0, []
    for index in range(count):
        size = base + (index < extra)
        result.append((start, size))
        start += size
    return result


def sigmoid(v):
    return 0.5 + 0.5 * jnp.tanh(0.5 * v)


def lanes_of(t):
    return slice(t * LANES, (t + 1) * LANES)


def taps_body(taps, kr_ref, fwd_ref, bwd_ref, scratch):
    layers, rows = kr_ref.shape[:2]
    part = scratch.shape[1] // CELLS // CH
    shape = (LANES, CELLS * LANES)
    lane = lax.broadcasted_iota(jnp.int32, shape, 1)
    chosen = lax.broadcasted_iota(jnp.int32, shape, 0) == lane // LANES * CH + lane % CH
    spread = jnp.where(chosen, 1.0, 0.0).astype(jnp.bfloat16)
    for layer in range(layers):
        groups = jnp.dot(kr_ref[layer], spread, preferred_element_type=jnp.float32)
        for q in range(CELLS):
            scratch[layer, pl.ds(q, rows, stride=CELLS), :] = groups[:, lanes_of(q)]
        scratch[layer, taps * CH :, :] = jnp.zeros_like(scratch[layer, taps * CH :, :])
        fwd_ref[layer] = scratch[layer, : taps * CH].astype(jnp.bfloat16)
        cell = lax.broadcasted_iota(jnp.int32, (part * CH, LANES), 1) // CH
        compact = jnp.zeros((part * CH, LANES), jnp.float32)
        for group in range(CELLS):
            at = group * part * CH
            compact = jnp.where(cell == group, scratch[layer, at : at + part * CH, :], compact)
        room = -(-part // CELLS) * LANES - part * CH
        turned = jnp.concatenate([compact, jnp.zeros((room, LANES), jnp.float32)], 0).T
        stacked = jnp.concatenate(
            [turned[:, lanes_of(t)] for t in range(turned.shape[1] // LANES)], 0
        ).astype(jnp.bfloat16)
        groups = jnp.dot(stacked, spread, preferred_element_type=jnp.float32)
        for tap in range(taps):
            group, index = divmod(tap, part)
            at, row = taps - 1 - tap, index // CELLS * LANES + group * CH
            bwd_ref[layer, at * CH : (at + 1) * CH, :] = groups[
                row : row + CH, lanes_of(index % CELLS)
            ].astype(jnp.bfloat16)


def fill_weights(taps_ref, t_ref):
    cell = lax.broadcasted_iota(jnp.int32, (CH, LANES), 1) // CH
    zero = jnp.zeros((CH, LANES), jnp.bfloat16)
    for layer in range(t_ref.shape[0]):
        for a in range(3):
            bands = {}
            for b in range(3):
                first = (a * 9 + b * 3) * CH
                values = [taps_ref[layer, first + c * CH : first + (c + 1) * CH, :] for c in range(3)]
                for ww in range(CELLS + 2):
                    band = zero
                    for c in range(3):
                        if 0 <= ww - c < CELLS:
                            band = jnp.where(cell == ww - c, values[c], band)
                    bands[b, ww] = band
            for at, (hh, ww) in enumerate(SLOTS):
                for h in range(2):
                    t_ref[
                        layer, a, at * CH : (at + 1) * CH, h * LANES : (h + 1) * LANES
                    ] = bands.get((hh - h, ww), zero)


def edge_masks(tiles):
    shape = (1, tiles, TILE)
    cell = lax.broadcasted_iota(jnp.int32, shape, 2) % LANES // CH
    row = lax.broadcasted_iota(jnp.int32, shape, 1)
    from_before = (cell == CELLS - 1) & (row > 0)
    from_after = (cell == 0) & (row < tiles - 1)
    return tuple(
        jnp.where(mask, 1.0, 0.0).astype(jnp.bfloat16) for mask in (from_before, from_after)
    )


def expand(x, out_ref, lead, pairs, tiles, masks):
    x = x.reshape(pairs, tiles, TILE)
    edge = pltpu.roll(x, 1, 1) * masks[0] + pltpu.roll(x, tiles - 1, 1) * masks[1]
    e0, e1 = edge[..., :LANES], edge[..., LANES:]
    r0, r1 = pltpu.roll(e0, LANES // 2, 2), pltpu.roll(e1, LANES // 2, 2)
    zero = jnp.zeros((1, tiles, LANES), x.dtype)
    low = jnp.concatenate([zero, x[:-1, :, LANES:]], 0)
    high = jnp.concatenate([x[1:, :, :LANES], zero], 0)
    e0 = e0 + jnp.concatenate([zero, r1[:-1]], 0)
    e1 = e1 + jnp.concatenate([r0[1:], zero], 0)
    flat = lambda v: v.reshape(pairs * tiles, v.shape[-1])
    out_ref[(*lead, slice(None), slice(0, TILE))] = flat(x)
    out_ref[(*lead, slice(None), slice(TILE, TILE + LANES))] = flat(low)
    out_ref[(*lead, slice(None), slice(TILE + LANES, 2 * TILE))] = flat(high)
    out_ref[(*lead, slice(None), slice(2 * TILE, 2 * TILE + LANES))] = flat(e0)
    out_ref[(*lead, slice(None), slice(2 * TILE + LANES, WIDE))] = flat(e1)


def conv_rows(x_ref, lead, start, rows, t_ref, layer):
    blocks = [x_ref[(*lead, pl.ds(start + a, rows))].reshape(-1, WIDE) for a in range(3)]
    return jnp.dot(
        jnp.concatenate(blocks, axis=1),
        t_ref[layer].reshape(3 * WIDE, TILE),
        preferred_element_type=jnp.float32,
    )


def slope_of(pre, gate):
    return gate * (1.0 + pre * (1.0 - gate))


def rounded(v):
    return v.astype(jnp.bfloat16)


def inside(v, row, depth):
    return jnp.where((row >= 0) & (row < depth), v, 0.0)


def either(flag, a, b):
    low = lambda *at: jnp.where(flag, a[at], b[at])
    high = lambda *at: jnp.where(flag, b[at], a[at])
    return low, high


def widen(near, own, far, lead, x_ref, x_lead, grow):
    at, last = lax.axis_index("depth"), lax.axis_size("depth") - 1
    low, high = either(at % 2 == 1, near, far)
    halo, rows = near.shape[len(lead)], own.shape[len(lead)]
    for d in range(halo):
        row = low(*lead, d)
        if d == halo - 1:
            row = jnp.where(at > 0, row, jnp.zeros_like(row))
        grow(row, x_ref, (*x_lead, d))
    for d in range(rows):
        grow(own[(*lead, d)], x_ref, (*x_lead, halo + d))
    for d in range(halo):
        row = high(*lead, d)
        if d == 0:
            row = jnp.where(at < last, row, jnp.zeros_like(row))
        grow(row, x_ref, (*x_lead, halo + rows + d))


def layer_one(xv, lead, out_ref, t_ref, slopes_ref=None):
    rows, cells = out_ref.shape[len(lead)], out_ref.shape[-2]
    for start, count in chunks_of(rows):
        pre = conv_rows(xv, lead, start, count, t_ref, 0)
        gate = sigmoid(pre)
        value = (pre * gate).astype(jnp.bfloat16).reshape(count, cells, TILE)
        out_ref[(*lead, pl.ds(start, count))] = value
        if slopes_ref is not None:
            slope = slope_of(pre, gate).reshape(count, cells, TILE)
            for d in range(count):
                to = start + d - (H_HIDDEN - H_G1)
                if 0 <= to < slopes_ref.shape[0]:
                    slopes_ref[to] = slope[d]


def tiled_rows(load, height, tiles, scratch, at):
    for t in range(tiles):
        scratch[at, t * height : (t + 1) * height, :] = load(t).astype(jnp.float32)
    for h in range(height):
        piece = scratch[at, pl.ds(h, tiles, stride=height), :].astype(jnp.bfloat16)
        yield h // 2 * tiles, slice(h % 2 * LANES, (h % 2 + 1) * LANES), piece


def inverse_of(partner, own):
    inverse = jnp.int32(0)
    for crop in range(partner.shape[0]):
        inverse = jnp.where(partner[crop] == own, crop, inverse)
    return inverse


def tile_rows(source, out, scratch):
    rows, height, lanes = source.shape
    for d in range(rows):
        load = lambda t, d=d: source[d, :, lanes_of(t)]
        for row, side, piece in tiled_rows(load, height, lanes // LANES, scratch, d):
            out[d, row : row + piece.shape[0], side] = piece


def select_body(partner, both, *refs):
    *crops, out, scratch = refs
    own = lax.axis_index("sample")
    for to, crop in enumerate((partner[own], inverse_of(partner, own))):
        for hop, source in enumerate((both.at[0], *crops)):

            @pl.when(crop ^ own == hop)
            def _(to=to, source=source):
                tile_rows(source, out.at[to], scratch)


def cotangent_body(partner, crops, out, raw, scratch, sem):
    inverse = inverse_of(partner, lax.axis_index("sample"))
    copy = pltpu.make_async_copy(crops.at[inverse], raw, sem)
    copy.start()
    copy.wait()
    tile_rows(raw, out, scratch)


def own_body(
    pairs, tiles,
    taps_ref, near, both, far,
    t_ref, hid, sl1, xv_own, cot_own,
    xv, field, scratch,
):
    _, rows, height, _ = both.shape
    fill_weights(taps_ref, t_ref)
    grow = functools.partial(expand, pairs=pairs, tiles=tiles, masks=edge_masks(tiles))
    for at, part in enumerate((near, both.at[0], far, both.at[1])):
        for d in range(rows):
            load = lambda t, part=part, d=d: part[d, :, lanes_of(t)]
            for row, side, piece in tiled_rows(load, height, tiles, scratch, at * rows + d):
                if at < 3:
                    field[at, d, row : row + tiles, side] = piece
                else:
                    cot_own[d, row : row + tiles, side] = piece
    widen(field.at[0], field.at[1], field.at[2], (), xv, (), grow)
    layer_one(xv, (), hid, t_ref, sl1)
    xv_own[...] = xv[rows - 1 : 2 * rows + 1]


def forward_body(
    depth, pairs, tiles,
    near, mid, far, hid_own, cot_own, cot_other, t_ref,
    g3, g3_near, g3_far, sl2, xb_own, xs_own,
    xv, hid, xb, xs,
):
    rows = mid.shape[1]
    cells = pairs * tiles
    first = lax.axis_index("depth") * rows
    grow = functools.partial(expand, pairs=pairs, tiles=tiles, masks=edge_masks(tiles))

    for crop in range(2):
        widen(near, mid, far, (crop,), xv, (crop,), grow)
        layer_one(xv, (crop,), hid, t_ref)

    for d in range(rows + 2 * H_HIDDEN):
        own = hid_own[d].astype(jnp.float32)
        partner, other = hid[0, d].astype(jnp.float32), hid[1, d].astype(jnp.float32)
        row = first + d - H_HIDDEN
        for j, (a, b) in enumerate(((own, partner), (other, own))):
            mixed = OWN_SHARE * a + PARTNER_SHARE * b
            grow(rounded(inside(mixed, row, depth)), xb, (j, d))

    def middle(j, cot):
        for start, count in chunks_of(rows + 2 * H_TWO):
            pre = conv_rows(xb, (j,), start, count, t_ref, 1)
            gate = sigmoid(pre)
            value = (pre * gate).reshape(count, cells, TILE)
            slope = slope_of(pre, gate).reshape(count, cells, TILE)
            for d in range(count):
                sl2[j, start + d] = slope[d]
                to = start + d - (H_TWO - 1)
                if 0 <= to < rows + 2:
                    grow(rounded(inside(value[d], first + to - 1, depth)), xs, (j, to))
        for start, count in chunks_of(rows):
            pre = conv_rows(xs, (j,), start, count, t_ref, 2)
            slope = slope_of(pre, sigmoid(pre)).reshape(count, cells, TILE)
            for d in range(count):
                at = start + d
                grad = rounded(cot[at].astype(jnp.float32) * slope[d])
                g3[j, at] = grad

    middle(0, cot_own)
    middle(1, cot_other)
    odd = lax.axis_index("depth") % 2 == 1
    for j in range(2):
        for d in range(H_G3):
            up, down = g3[j, rows - H_G3 + d], g3[j, d]
            g3_near[j, d] = jnp.where(odd, down, up)
            g3_far[j, d] = jnp.where(odd, up, down)
    xb_own[...] = xb[0, H_HIDDEN - 1 : H_HIDDEN + rows + 1]
    xs_own[...] = xs[0]


def kernel_terms(values, gradient, rw):
    rows = gradient.shape[0]
    gradient = gradient.reshape(-1, TILE)
    for a in range(3):
        block = values[a : a + rows].reshape(-1, WIDE)
        terms = lax.dot_general(
            block, gradient, (((0,), (0,)), ((), ())), preferred_element_type=jnp.float32
        )
        for b in range(3):
            for c in range(3):
                at = (a * 9 + b * 3 + c) * CH
                for w in range(CELLS):
                    s0, s1 = SLOT_OF[b, w + c] * CH, SLOT_OF[b + 1, w + c] * CH
                    rw[w, at : at + CH] = (
                        terms[s0 : s0 + CH, :LANES] + terms[s1 : s1 + CH, LANES:]
                    )
    count = rw.shape[1] // CELLS
    cell = lax.broadcasted_iota(jnp.int32, (count, LANES), 1) // CH
    dense = jnp.zeros((count, LANES), jnp.float32)
    for q in range(CELLS):
        part = None
        for w in range(CELLS):
            piece = rw[w, pl.ds(q, count, stride=CELLS), :]
            if q != w:
                piece = pltpu.roll(piece, (q - w) % CELLS * CH, 1)
            part = piece if part is None else part + piece
        dense = jnp.where(cell == q, part, dense)
    return dense.astype(jnp.bfloat16)


def between_body(taps_ref, xs_own, g3, t_ref, terms, rw):
    fill_weights(taps_ref, t_ref)
    terms[...] = kernel_terms(xs_own[...], g3[0], rw)


def back_two(j, x_ref, sl2, x2_ref, t_ref, first, depth, grow):
    rows, cells = x2_ref.shape[-3:-1]
    for start, count in chunks_of(rows):
        back = conv_rows(x_ref, (), start, count, t_ref, 2).reshape(count, cells, TILE)
        for d in range(count):
            at = start + d
            grad = inside(back[d] * sl2[j, at], first + at - H_G2, depth)
            grow(rounded(grad), x2_ref, (at,))


def back_body(
    depth, pairs, tiles,
    near, mid, far, sl1, sl2, xv_own, xb_own, t_ref,
    xg1, terms,
    xg3, xg2, rw,
):
    rows = mid.shape[1]
    cells = pairs * tiles
    first = lax.axis_index("depth") * rows
    grow = functools.partial(expand, pairs=pairs, tiles=tiles, masks=edge_masks(tiles))
    for j in range(2):
        widen(near, mid, far, (j,), xg3.at[j], (), grow)
        back_two(j, xg3.at[j], sl2, xg2.at[j], t_ref, first, depth, grow)
    for start, count in chunks_of(rows + 2 * H_G1):
        own, other = (
            rounded(conv_rows(xg2, (j,), start, count, t_ref, 1)).astype(jnp.float32)
            for j in range(2)
        )
        mixed = (OWN_SHARE * own + PARTNER_SHARE * other).reshape(count, cells, TILE)
        for d in range(count):
            at = start + d
            grad = inside(mixed[d] * sl1[at], first + at - H_G1, depth)
            grow(rounded(grad), xg1, (at,))
    terms[0] = kernel_terms(xv_own[...], xg1[H_G1 : H_G1 + rows, :, :TILE], rw)
    terms[1] = kernel_terms(xb_own[...], xg2[0, H_G2 : H_G2 + rows, :, :TILE], rw)


def last_body(pairs, tiles, xg1, t_ref, gv, scratch):
    rows, height, _ = gv.shape
    cells = pairs * tiles
    for start, count in chunks_of(rows):
        back = conv_rows(xg1, (), start, count, t_ref, 0).reshape(count, cells, TILE)
        for d in range(count):
            for h in range(height):
                row, side = h // 2 * tiles, slice(h % 2 * LANES, (h % 2 + 1) * LANES)
                scratch[start + d, pl.ds(h, tiles, stride=height), :] = back[
                    d, row : row + tiles, side
                ]
            for t in range(tiles):
                gv[start + d, :, t * LANES : (t + 1) * LANES] = scratch[
                    start + d, t * height : (t + 1) * height, :
                ].astype(jnp.bfloat16)


def tree_sum(parts):
    parts = [part.astype(jnp.float32) for part in parts]
    while len(parts) > 1:
        parts = [a + b for a, b in zip(parts[::2], parts[1::2])]
    return parts[0]


def total_body(count, *refs):
    *parts, out = refs
    for layer in range(2):
        out[layer] = tree_sum([part[layer] for part in parts[:count]])
    out[2] = tree_sum([part[...] for part in parts[count:]])


def by_hop(values):
    count = lax.axis_size("depth")
    swap = lambda hop: lax.ppermute(values, "depth", [(i, i ^ hop) for i in range(count)])
    return [values, *(swap(hop) for hop in range(1, count))]


def neighbours(near, far):
    count = lax.axis_size("depth")
    result = []
    for values, first in ((near, 0), (far, 1)):
        partner = {}
        for i in range(first, count - 1, 2):
            partner[i], partner[i + 1] = i + 1, i
        pairs = [(i, partner.get(i, i)) for i in range(count)]
        result.append(lax.ppermute(values, "depth", pairs))
    return result


def over_sample(values, hop):
    groups = lax.axis_size("sample")
    return lax.ppermute(values, "sample", [(i, i ^ hop) for i in range(groups)])


def even_hops(values):
    return [over_sample(values, hop) for hop in range(2, lax.axis_size("sample"), 2)]


def all_hops(odd, evens):
    return [odd, *(crop for even in evens for crop in (even, over_sample(even, 1)))]


def traded(volume, partner, tiles):
    groups = lax.axis_size("sample")
    rows, height, _ = volume.shape
    split = volume.reshape(rows, height // 2, 2, tiles, LANES)
    pieces = split.transpose(0, 1, 3, 2, 4).reshape(groups, -1, TILE)
    spread = lax.all_to_all(pieces, "sample", split_axis=0, concat_axis=0, tiled=True)
    ids = jnp.arange(groups, dtype=jnp.int32)
    inverse = jnp.sum(jnp.where(partner[:, None] == ids[None, :], ids[:, None], 0), axis=0)
    chosen = jnp.take(spread, jnp.stack([partner, inverse], axis=1), axis=0)
    joined = lax.all_to_all(chosen, "sample", split_axis=0, concat_axis=0, tiled=True)
    return jnp.swapaxes(joined, 0, 1).reshape(2, rows, -1, TILE)


def call(kernel, outs, scratch, inputs, macs=0, far=(), limit=VMEM_LIMIT):
    vmem, smem, anywhere = (
        pl.BlockSpec(memory_space=space) for space in (pltpu.VMEM, pltpu.SMEM, pl.ANY)
    )
    specs = [
        anywhere if at in far else smem if x.dtype == jnp.int32 else vmem
        for at, x in enumerate(inputs)
    ]
    results = pl.pallas_call(
        kernel,
        out_shape=tuple(jax.ShapeDtypeStruct(shape, dtype) for shape, dtype in outs),
        in_specs=specs,
        out_specs=(vmem,) * len(outs),
        scratch_shapes=scratch,
        compiler_params=pltpu.CompilerParams(vmem_limit_bytes=limit),
        cost_estimate=pl.CostEstimate(
            flops=2 * macs, bytes_accessed=2**22 if macs else 1, transcendentals=0
        ),
    )(*inputs)
    return results if len(results) > 1 else results[0]


def per_device(volume, kernels, partner, cotangent):
    volume, cotangent = volume[0], cotangent[0]
    rows, height, lanes = volume.shape
    pairs, tiles = height // 2, lanes // LANES
    cells = pairs * tiles
    groups, count = lax.axis_size("sample"), lax.axis_size("depth")
    depth = rows * count
    layers, taps, width = kernels.shape
    bf16, f32 = jnp.bfloat16, jnp.float32
    row_macs = 3 * cells * WIDE * TILE
    packed_rows = taps * CH // CELLS
    wide = lambda *lead: pltpu.VMEM((*lead, cells, WIDE), bf16)
    field = lambda *lead: ((*lead, cells, TILE), bf16)
    raw_tiles = lambda *lead: pltpu.VMEM((*lead, height * tiles, LANES), f32)
    banded = ((layers, 3, WIDE, TILE), bf16)
    spread_taps = ((layers, taps * CH, LANES), bf16)
    rw = pltpu.VMEM((CELLS, taps * CH, LANES), f32)

    direct = groups in (2, 4, 8)
    cotangents = lax.all_gather(cotangent, "sample")
    evens = even_hops(volume) if direct else []
    odd = over_sample(volume, 1) if direct else volume
    both = jnp.stack([volume, cotangent])
    packed = kernels.reshape(layers, packed_rows, LANES)
    ids = jnp.clip(partner, 0, groups - 1)
    fwd_taps, bwd_taps = call(
        functools.partial(taps_body, taps),
        [spread_taps, spread_taps],
        [pltpu.VMEM((layers, -(-taps // CELLS) * LANES, LANES), f32)],
        [packed],
        2**28,
    )
    near, far = neighbours(volume, volume)
    evens, both, ids, fwd_taps, bwd_taps, near, far = lax.optimization_barrier(
        (evens, both, ids, fwd_taps, bwd_taps, near, far)
    )
    if direct:
        crops = all_hops(odd, evens)
        vol = call(
            select_body, [field(2, rows)], [raw_tiles(rows)], [ids, both, *crops]
        )
    else:
        vol = traded(volume, partner, tiles)
    vol_near, vol_far = neighbours(vol, vol)
    cot_other = call(
        cotangent_body,
        [field(rows)],
        [
            pltpu.VMEM((rows, height, lanes), bf16),
            raw_tiles(rows),
            pltpu.SemaphoreType.DMA,
        ],
        [ids, cotangents],
        far=(1,),
        limit=60 * 2**20,
    )
    hid_rows = rows + 2 * H_HIDDEN
    fwd, hid_own, sl1, xv_own, cot_own = call(
        functools.partial(own_body, pairs, tiles),
        [
            banded,
            field(hid_rows),
            ((rows + 2 * H_G1, cells, TILE), f32),
            ((rows + 2, cells, WIDE), bf16),
            field(rows),
        ],
        [wide(3 * rows), pltpu.VMEM((3, rows, cells, TILE), bf16), raw_tiles(4 * rows)],
        [fwd_taps, near, both, far],
        hid_rows * row_macs,
    )

    g3, g3_near, g3_far, sl2, xb_own, xs_own = call(
        functools.partial(forward_body, depth, pairs, tiles),
        [
            field(2, rows),
            field(2, H_G3),
            field(2, H_G3),
            ((2, rows + 2 * H_TWO, cells, TILE), f32),
            ((rows + 2, cells, WIDE), bf16),
            ((rows + 2, cells, WIDE), bf16),
        ],
        [
            wide(2, 3 * rows),
            pltpu.VMEM((2, hid_rows, cells, TILE), bf16),
            wide(2, hid_rows),
            wide(2, rows + 2),
        ],
        [vol_near, vol, vol_far, hid_own, cot_own, cot_other, fwd],
        (2 * hid_rows + 2 * (rows + 4) + 2 * rows) * row_macs,
    )

    near, far = neighbours(g3_near, g3_far)
    terms = ((packed_rows, LANES), bf16)
    bwd, three = call(
        between_body, [banded, terms], [rw], [bwd_taps, xs_own, g3], rows * row_macs
    )
    three = by_hop(three)
    xg1, others = call(
        functools.partial(back_body, depth, pairs, tiles),
        [((rows + 2 * H_G1, cells, WIDE), bf16), ((2, packed_rows, LANES), bf16)],
        [wide(2, rows + 2 * H_G3), wide(2, rows + 2 * H_G2), rw],
        [near, g3, far, sl1, sl2, xv_own, xb_own, bwd],
        (6 * rows + 12) * row_macs,
    )
    others, three = lax.optimization_barrier((others, three))
    others = by_hop(others)
    grad_volume = call(
        functools.partial(last_body, pairs, tiles),
        [((rows, height, lanes), bf16)],
        [raw_tiles(rows)],
        [xg1, bwd],
        rows * row_macs,
    )
    total = call(
        functools.partial(total_body, count),
        [((layers, packed_rows, LANES), f32)],
        [],
        [*others, *three],
    )
    return (grad_volume[None], total.reshape(1, layers, taps, width))


def solution(mesh):
    in_specs = (P("sample", "depth", None, None), P(), P(), P("sample", "depth", None, None))
    out_specs = (P("sample", "depth", None, None), P("sample", None, None, None))
    return jax.shard_map(
        per_device, mesh=mesh, in_specs=in_specs, out_specs=out_specs, check_vma=False
    )
```

```python
import functools

import jax
import jax.numpy as jnp
from jax import lax
from jax.experimental import pallas as pl
from jax.experimental.pallas import tpu as pltpu
from jax.sharding import PartitionSpec as P

CH = 32
OWN_SHARE = 0.6
PARTNER_SHARE = 0.4
LANES = 128
CELLS = LANES // CH
TILE = 2 * LANES
WIDE = 3 * TILE
VMEM_LIMIT = 40 * 2**20

SLOTS = (
    [(1 + h, 1 + w) for h in range(2) for w in range(CELLS)]
    + [(0, 1 + w) for w in range(CELLS)]
    + [(3, 1 + w) for w in range(CELLS)]
    + [(1, 5), (0, 0), (0, 5), (1, 0)]
    + [(2, 5), (3, 0), (3, 5), (2, 0)]
)
SLOT_OF = {cell: at for at, cell in enumerate(SLOTS)}

H_HIDDEN, H_TWO, H_G3, H_G2, H_G1 = 3, 2, 3, 2, 1


def chunks_of(rows):
    count = max(1, (rows + 2) // 5)
    base, extra = divmod(rows, count)
    start, result = 0, []
    for index in range(count):
        size = base + (index < extra)
        result.append((start, size))
        start += size
    return result


def sigmoid(v):
    return 0.5 + 0.5 * jnp.tanh(0.5 * v)


def lanes_of(t):
    return slice(t * LANES, (t + 1) * LANES)


def taps_body(taps, kr_ref, fwd_ref, bwd_ref, scratch):
    layers, rows = kr_ref.shape[:2]
    part = scratch.shape[1] // CELLS // CH
    shape = (LANES, CELLS * LANES)
    lane = lax.broadcasted_iota(jnp.int32, shape, 1)
    chosen = lax.broadcasted_iota(jnp.int32, shape, 0) == lane // LANES * CH + lane % CH
    spread = jnp.where(chosen, 1.0, 0.0).astype(jnp.bfloat16)
    for layer in range(layers):
        groups = jnp.dot(kr_ref[layer], spread, preferred_element_type=jnp.float32)
        for q in range(CELLS):
            scratch[layer, pl.ds(q, rows, stride=CELLS), :] = groups[:, lanes_of(q)]
        scratch[layer, taps * CH :, :] = jnp.zeros_like(scratch[layer, taps * CH :, :])
        fwd_ref[layer] = scratch[layer, : taps * CH].astype(jnp.bfloat16)
        cell = lax.broadcasted_iota(jnp.int32, (part * CH, LANES), 1) // CH
        compact = jnp.zeros((part * CH, LANES), jnp.float32)
        for group in range(CELLS):
            at = group * part * CH
            compact = jnp.where(cell == group, scratch[layer, at : at + part * CH, :], compact)
        room = -(-part // CELLS) * LANES - part * CH
        turned = jnp.concatenate([compact, jnp.zeros((room, LANES), jnp.float32)], 0).T
        stacked = jnp.concatenate(
            [turned[:, lanes_of(t)] for t in range(turned.shape[1] // LANES)], 0
        ).astype(jnp.bfloat16)
        groups = jnp.dot(stacked, spread, preferred_element_type=jnp.float32)
        for tap in range(taps):
            group, index = divmod(tap, part)
            at, row = taps - 1 - tap, index // CELLS * LANES + group * CH
            bwd_ref[layer, at * CH : (at + 1) * CH, :] = groups[
                row : row + CH, lanes_of(index % CELLS)
            ].astype(jnp.bfloat16)


def fill_weights(taps_ref, t_ref):
    cell = lax.broadcasted_iota(jnp.int32, (CH, LANES), 1) // CH
    zero = jnp.zeros((CH, LANES), jnp.bfloat16)
    for layer in range(t_ref.shape[0]):
        for a in range(3):
            bands = {}
            for b in range(3):
                first = (a * 9 + b * 3) * CH
                values = [taps_ref[layer, first + c * CH : first + (c + 1) * CH, :] for c in range(3)]
                for ww in range(CELLS + 2):
                    band = zero
                    for c in range(3):
                        if 0 <= ww - c < CELLS:
                            band = jnp.where(cell == ww - c, values[c], band)
                    bands[b, ww] = band
            for at, (hh, ww) in enumerate(SLOTS):
                for h in range(2):
                    t_ref[
                        layer, a, at * CH : (at + 1) * CH, h * LANES : (h + 1) * LANES
                    ] = bands.get((hh - h, ww), zero)


def edge_masks(tiles):
    shape = (1, tiles, TILE)
    cell = lax.broadcasted_iota(jnp.int32, shape, 2) % LANES // CH
    row = lax.broadcasted_iota(jnp.int32, shape, 1)
    from_before = (cell == CELLS - 1) & (row > 0)
    from_after = (cell == 0) & (row < tiles - 1)
    return tuple(
        jnp.where(mask, 1.0, 0.0).astype(jnp.bfloat16) for mask in (from_before, from_after)
    )


def expand(x, out_ref, lead, pairs, tiles, masks):
    x = x.reshape(pairs, tiles, TILE)
    edge = pltpu.roll(x, 1, 1) * masks[0] + pltpu.roll(x, tiles - 1, 1) * masks[1]
    e0, e1 = edge[..., :LANES], edge[..., LANES:]
    r0, r1 = pltpu.roll(e0, LANES // 2, 2), pltpu.roll(e1, LANES // 2, 2)
    zero = jnp.zeros((1, tiles, LANES), x.dtype)
    low = jnp.concatenate([zero, x[:-1, :, LANES:]], 0)
    high = jnp.concatenate([x[1:, :, :LANES], zero], 0)
    e0 = e0 + jnp.concatenate([zero, r1[:-1]], 0)
    e1 = e1 + jnp.concatenate([r0[1:], zero], 0)
    flat = lambda v: v.reshape(pairs * tiles, v.shape[-1])
    out_ref[(*lead, slice(None), slice(0, TILE))] = flat(x)
    out_ref[(*lead, slice(None), slice(TILE, TILE + LANES))] = flat(low)
    out_ref[(*lead, slice(None), slice(TILE + LANES, 2 * TILE))] = flat(high)
    out_ref[(*lead, slice(None), slice(2 * TILE, 2 * TILE + LANES))] = flat(e0)
    out_ref[(*lead, slice(None), slice(2 * TILE + LANES, WIDE))] = flat(e1)


def conv_rows(x_ref, lead, start, rows, t_ref, layer):
    blocks = [x_ref[(*lead, pl.ds(start + a, rows))].reshape(-1, WIDE) for a in range(3)]
    return jnp.dot(
        jnp.concatenate(blocks, axis=1),
        t_ref[layer].reshape(3 * WIDE, TILE),
        preferred_element_type=jnp.float32,
    )


def slope_of(pre, gate):
    return gate * (1.0 + pre * (1.0 - gate))


def rounded(v):
    return v.astype(jnp.bfloat16)


def inside(v, row, depth):
    return jnp.where((row >= 0) & (row < depth), v, 0.0)


def either(flag, a, b):
    low = lambda *at: jnp.where(flag, a[at], b[at])
    high = lambda *at: jnp.where(flag, b[at], a[at])
    return low, high


def widen(near, own, far, lead, x_ref, x_lead, grow):
    at, last = lax.axis_index("depth"), lax.axis_size("depth") - 1
    low, high = either(at % 2 == 1, near, far)
    halo, rows = near.shape[len(lead)], own.shape[len(lead)]
    for d in range(halo):
        row = low(*lead, d)
        if d == halo - 1:
            row = jnp.where(at > 0, row, jnp.zeros_like(row))
        grow(row, x_ref, (*x_lead, d))
    for d in range(rows):
        grow(own[(*lead, d)], x_ref, (*x_lead, halo + d))
    for d in range(halo):
        row = high(*lead, d)
        if d == 0:
            row = jnp.where(at < last, row, jnp.zeros_like(row))
        grow(row, x_ref, (*x_lead, halo + rows + d))


def layer_one(xv, lead, out_ref, t_ref, slopes_ref=None):
    rows, cells = out_ref.shape[len(lead)], out_ref.shape[-2]
    for start, count in chunks_of(rows):
        pre = conv_rows(xv, lead, start, count, t_ref, 0)
        gate = sigmoid(pre)
        value = (pre * gate).astype(jnp.bfloat16).reshape(count, cells, TILE)
        out_ref[(*lead, pl.ds(start, count))] = value
        if slopes_ref is not None:
            slope = slope_of(pre, gate).reshape(count, cells, TILE)
            for d in range(count):
                to = start + d - (H_HIDDEN - H_G1)
                if 0 <= to < slopes_ref.shape[0]:
                    slopes_ref[to] = slope[d]


def tiled_rows(load, height, tiles, scratch, at):
    for t in range(tiles):
        scratch[at, t * height : (t + 1) * height, :] = load(t).astype(jnp.float32)
    for h in range(height):
        piece = scratch[at, pl.ds(h, tiles, stride=height), :].astype(jnp.bfloat16)
        yield h // 2 * tiles, slice(h % 2 * LANES, (h % 2 + 1) * LANES), piece


def tile_field(source, out, scratch):
    rows, height, lanes = source.shape
    for d in range(rows):
        load = lambda t, d=d: source[d, :, lanes_of(t)]
        for row, side, piece in tiled_rows(load, height, lanes // LANES, scratch, d):
            out[d, row : row + piece.shape[0], side] = piece


def select_body(partner, *refs):
    *crops, vol, cot, scratch = refs
    own = lax.axis_index("sample")
    inverse = jnp.int32(0)
    for crop in range(partner.shape[0]):
        inverse = jnp.where(partner[crop] == own, crop, inverse)
    for hop, source in enumerate(crops):

        @pl.when(partner[own] ^ own == hop)
        def _(source=source):
            tile_field(source.at[0], vol.at[0], scratch)

        @pl.when(inverse ^ own == hop)
        def _(source=source):
            tile_field(source.at[0], vol.at[1], scratch)
            tile_field(source.at[1], cot, scratch)


def own_body(
    pairs, tiles,
    taps_ref, near, both, far,
    t_ref, hid, sl1, xv_own, cot_own,
    xv, field, scratch,
):
    _, rows, height, _ = both.shape
    fill_weights(taps_ref, t_ref)
    grow = functools.partial(expand, pairs=pairs, tiles=tiles, masks=edge_masks(tiles))
    for at, part in enumerate((near, both.at[0], far, both.at[1])):
        for d in range(rows):
            load = lambda t, part=part, d=d: part[d, :, lanes_of(t)]
            for row, side, piece in tiled_rows(load, height, tiles, scratch, at * rows + d):
                if at < 3:
                    field[at, d, row : row + tiles, side] = piece
                else:
                    cot_own[d, row : row + tiles, side] = piece
    widen(field.at[0], field.at[1], field.at[2], (), xv, (), grow)
    layer_one(xv, (), hid, t_ref, sl1)
    xv_own[...] = xv[rows - 1 : 2 * rows + 1]


def forward_body(
    depth, pairs, tiles,
    near, mid, far, hid_own, cot_own, cot_other, t_ref,
    g3, g3_near, g3_far, sl2, xb_own, xs_own,
    xv, hid, xb, xs,
):
    rows = mid.shape[1]
    cells = pairs * tiles
    first = lax.axis_index("depth") * rows
    grow = functools.partial(expand, pairs=pairs, tiles=tiles, masks=edge_masks(tiles))

    for crop in range(2):
        widen(near, mid, far, (crop,), xv, (crop,), grow)
        layer_one(xv, (crop,), hid, t_ref)

    for d in range(rows + 2 * H_HIDDEN):
        own = hid_own[d].astype(jnp.float32)
        partner, other = hid[0, d].astype(jnp.float32), hid[1, d].astype(jnp.float32)
        row = first + d - H_HIDDEN
        for j, (a, b) in enumerate(((own, partner), (other, own))):
            mixed = OWN_SHARE * a + PARTNER_SHARE * b
            grow(rounded(inside(mixed, row, depth)), xb, (j, d))

    def middle(j, cot):
        for start, count in chunks_of(rows + 2 * H_TWO):
            pre = conv_rows(xb, (j,), start, count, t_ref, 1)
            gate = sigmoid(pre)
            value = (pre * gate).reshape(count, cells, TILE)
            slope = slope_of(pre, gate).reshape(count, cells, TILE)
            for d in range(count):
                sl2[j, start + d] = slope[d]
                to = start + d - (H_TWO - 1)
                if 0 <= to < rows + 2:
                    grow(rounded(inside(value[d], first + to - 1, depth)), xs, (j, to))
        for start, count in chunks_of(rows):
            pre = conv_rows(xs, (j,), start, count, t_ref, 2)
            slope = slope_of(pre, sigmoid(pre)).reshape(count, cells, TILE)
            for d in range(count):
                at = start + d
                grad = rounded(cot[at].astype(jnp.float32) * slope[d])
                g3[j, at] = grad

    middle(0, cot_own)
    middle(1, cot_other)
    odd = lax.axis_index("depth") % 2 == 1
    for j in range(2):
        for d in range(H_G3):
            up, down = g3[j, rows - H_G3 + d], g3[j, d]
            g3_near[j, d] = jnp.where(odd, down, up)
            g3_far[j, d] = jnp.where(odd, up, down)
    xb_own[...] = xb[0, H_HIDDEN - 1 : H_HIDDEN + rows + 1]
    xs_own[...] = xs[0]


def kernel_terms(values, gradient, rw):
    rows = gradient.shape[0]
    gradient = gradient.reshape(-1, TILE)
    for a in range(3):
        block = values[a : a + rows].reshape(-1, WIDE)
        terms = lax.dot_general(
            block, gradient, (((0,), (0,)), ((), ())), preferred_element_type=jnp.float32
        )
        for b in range(3):
            for c in range(3):
                at = (a * 9 + b * 3 + c) * CH
                for w in range(CELLS):
                    s0, s1 = SLOT_OF[b, w + c] * CH, SLOT_OF[b + 1, w + c] * CH
                    rw[w, at : at + CH] = (
                        terms[s0 : s0 + CH, :LANES] + terms[s1 : s1 + CH, LANES:]
                    )
    count = rw.shape[1] // CELLS
    cell = lax.broadcasted_iota(jnp.int32, (count, LANES), 1) // CH
    dense = jnp.zeros((count, LANES), jnp.float32)
    for q in range(CELLS):
        part = None
        for w in range(CELLS):
            piece = rw[w, pl.ds(q, count, stride=CELLS), :]
            if q != w:
                piece = pltpu.roll(piece, (q - w) % CELLS * CH, 1)
            part = piece if part is None else part + piece
        dense = jnp.where(cell == q, part, dense)
    return dense.astype(jnp.bfloat16)


def between_body(taps_ref, xs_own, g3, t_ref, terms, rw):
    fill_weights(taps_ref, t_ref)
    terms[...] = kernel_terms(xs_own[...], g3[0], rw)


def back_two(j, x_ref, sl2, x2_ref, t_ref, first, depth, grow):
    rows, cells = x2_ref.shape[-3:-1]
    for start, count in chunks_of(rows):
        back = conv_rows(x_ref, (), start, count, t_ref, 2).reshape(count, cells, TILE)
        for d in range(count):
            at = start + d
            grad = inside(back[d] * sl2[j, at], first + at - H_G2, depth)
            grow(rounded(grad), x2_ref, (at,))


def back_body(
    depth, pairs, tiles,
    near, mid, far, sl1, sl2, xv_own, xb_own, t_ref,
    xg1, terms,
    xg3, xg2, rw,
):
    rows = mid.shape[1]
    cells = pairs * tiles
    first = lax.axis_index("depth") * rows
    grow = functools.partial(expand, pairs=pairs, tiles=tiles, masks=edge_masks(tiles))
    for j in range(2):
        widen(near, mid, far, (j,), xg3.at[j], (), grow)
        back_two(j, xg3.at[j], sl2, xg2.at[j], t_ref, first, depth, grow)
    for start, count in chunks_of(rows + 2 * H_G1):
        own, other = (
            rounded(conv_rows(xg2, (j,), start, count, t_ref, 1)).astype(jnp.float32)
            for j in range(2)
        )
        mixed = (OWN_SHARE * own + PARTNER_SHARE * other).reshape(count, cells, TILE)
        for d in range(count):
            at = start + d
            grad = inside(mixed[d] * sl1[at], first + at - H_G1, depth)
            grow(rounded(grad), xg1, (at,))
    terms[0] = kernel_terms(xv_own[...], xg1[H_G1 : H_G1 + rows, :, :TILE], rw)
    terms[1] = kernel_terms(xb_own[...], xg2[0, H_G2 : H_G2 + rows, :, :TILE], rw)


def last_body(pairs, tiles, xg1, t_ref, gv, scratch):
    rows, height, _ = gv.shape
    cells = pairs * tiles
    for start, count in chunks_of(rows):
        back = conv_rows(xg1, (), start, count, t_ref, 0).reshape(count, cells, TILE)
        for d in range(count):
            for h in range(height):
                row, side = h // 2 * tiles, slice(h % 2 * LANES, (h % 2 + 1) * LANES)
                scratch[start + d, pl.ds(h, tiles, stride=height), :] = back[
                    d, row : row + tiles, side
                ]
            for t in range(tiles):
                gv[start + d, :, t * LANES : (t + 1) * LANES] = scratch[
                    start + d, t * height : (t + 1) * height, :
                ].astype(jnp.bfloat16)


def tree_sum(parts):
    parts = [part.astype(jnp.float32) for part in parts]
    while len(parts) > 1:
        parts = [a + b for a, b in zip(parts[::2], parts[1::2])]
    return parts[0]


def total_body(count, *refs):
    *parts, out = refs
    for layer in range(2):
        out[layer] = tree_sum([part[layer] for part in parts[:count]])
    out[2] = tree_sum([part[...] for part in parts[count:]])


def by_hop(values):
    count = lax.axis_size("depth")
    swap = lambda hop: lax.ppermute(values, "depth", [(i, i ^ hop) for i in range(count)])
    return [values, *(swap(hop) for hop in range(1, count))]


def neighbours(near, far):
    count = lax.axis_size("depth")
    result = []
    for values, first in ((near, 0), (far, 1)):
        partner = {}
        for i in range(first, count - 1, 2):
            partner[i], partner[i + 1] = i + 1, i
        pairs = [(i, partner.get(i, i)) for i in range(count)]
        result.append(lax.ppermute(values, "depth", pairs))
    return result


def over_sample(values, hop):
    groups = lax.axis_size("sample")
    return lax.ppermute(values, "sample", [(i, i ^ hop) for i in range(groups)])


def even_hops(values):
    return [over_sample(values, hop) for hop in range(2, lax.axis_size("sample"), 2)]


def all_hops(odd, evens):
    return [odd, *(crop for even in evens for crop in (even, over_sample(even, 1)))]


def traded(volume, cotangent, partner, tiles):
    groups = lax.axis_size("sample")
    rows, height, _ = volume.shape
    split = jnp.stack([volume, cotangent]).reshape(2, rows, height // 2, 2, tiles, LANES)
    split = split.transpose(0, 1, 2, 4, 3, 5).reshape(2, groups, -1, TILE)
    pieces = split.swapaxes(0, 1)
    spread = lax.all_to_all(pieces, "sample", split_axis=0, concat_axis=0, tiled=True)
    ids = jnp.arange(groups, dtype=jnp.int32)
    inverse = jnp.sum(jnp.where(partner[:, None] == ids[None, :], ids[:, None], 0), axis=0)
    wanted = jnp.stack([2 * partner, 2 * inverse, 2 * inverse + 1], axis=1)
    chosen = jnp.take(spread.reshape(2 * groups, -1, TILE), wanted, axis=0)
    joined = lax.all_to_all(chosen, "sample", split_axis=0, concat_axis=0, tiled=True)
    others = jnp.swapaxes(joined, 0, 1).reshape(3, rows, -1, TILE)
    return others[:2], others[2]


def call(kernel, outs, scratch, inputs, macs=0, far=()):
    vmem, smem, anywhere = (
        pl.BlockSpec(memory_space=space) for space in (pltpu.VMEM, pltpu.SMEM, pl.ANY)
    )
    specs = [
        anywhere if at in far else smem if x.dtype == jnp.int32 else vmem
        for at, x in enumerate(inputs)
    ]
    results = pl.pallas_call(
        kernel,
        out_shape=tuple(jax.ShapeDtypeStruct(shape, dtype) for shape, dtype in outs),
        in_specs=specs,
        out_specs=(vmem,) * len(outs),
        scratch_shapes=scratch,
        compiler_params=pltpu.CompilerParams(vmem_limit_bytes=VMEM_LIMIT),
        cost_estimate=pl.CostEstimate(
            flops=2 * macs, bytes_accessed=2**22 if macs else 1, transcendentals=0
        ),
    )(*inputs)
    return results if len(results) > 1 else results[0]


def per_device(volume, kernels, partner, cotangent):
    volume, cotangent = volume[0], cotangent[0]
    rows, height, lanes = volume.shape
    pairs, tiles = height // 2, lanes // LANES
    cells = pairs * tiles
    groups, count = lax.axis_size("sample"), lax.axis_size("depth")
    depth = rows * count
    layers, taps, width = kernels.shape
    bf16, f32 = jnp.bfloat16, jnp.float32
    row_macs = 3 * cells * WIDE * TILE
    packed_rows = taps * CH // CELLS
    wide = lambda *lead: pltpu.VMEM((*lead, cells, WIDE), bf16)
    field = lambda *lead: ((*lead, cells, TILE), bf16)
    raw_tiles = lambda *lead: pltpu.VMEM((*lead, height * tiles, LANES), f32)
    banded = ((layers, 3, WIDE, TILE), bf16)
    spread_taps = ((layers, taps * CH, LANES), bf16)
    rw = pltpu.VMEM((CELLS, taps * CH, LANES), f32)

    direct = groups in (2, 4, 8)
    both, edges = lax.optimization_barrier((jnp.stack([volume, cotangent]), volume))
    evens = even_hops(both) if direct else []
    odd = over_sample(both, 1) if direct else both
    packed = kernels.reshape(layers, packed_rows, LANES)
    ids = jnp.clip(partner, 0, groups - 1)
    fwd_taps, bwd_taps = call(
        functools.partial(taps_body, taps),
        [spread_taps, spread_taps],
        [pltpu.VMEM((layers, -(-taps // CELLS) * LANES, LANES), f32)],
        [packed],
        2**28,
    )
    near, far = neighbours(edges, edges)
    evens, ids, fwd_taps, bwd_taps, near, far = lax.optimization_barrier(
        (evens, ids, fwd_taps, bwd_taps, near, far)
    )
    if direct:
        vol, cot_other = call(
            select_body,
            [field(2, rows), field(rows)],
            [raw_tiles(rows)],
            [ids, both, *all_hops(odd, evens)],
        )
    else:
        vol, cot_other = traded(volume, cotangent, partner, tiles)
    vol_near, vol_far = neighbours(vol, vol)
    hid_rows = rows + 2 * H_HIDDEN
    fwd, hid_own, sl1, xv_own, cot_own = call(
        functools.partial(own_body, pairs, tiles),
        [
            banded,
            field(hid_rows),
            ((rows + 2 * H_G1, cells, TILE), f32),
            ((rows + 2, cells, WIDE), bf16),
            field(rows),
        ],
        [wide(3 * rows), pltpu.VMEM((3, rows, cells, TILE), bf16), raw_tiles(4 * rows)],
        [fwd_taps, near, both, far],
        hid_rows * row_macs,
    )

    g3, g3_near, g3_far, sl2, xb_own, xs_own = call(
        functools.partial(forward_body, depth, pairs, tiles),
        [
            field(2, rows),
            field(2, H_G3),
            field(2, H_G3),
            ((2, rows + 2 * H_TWO, cells, TILE), f32),
            ((rows + 2, cells, WIDE), bf16),
            ((rows + 2, cells, WIDE), bf16),
        ],
        [
            wide(2, 3 * rows),
            pltpu.VMEM((2, hid_rows, cells, TILE), bf16),
            wide(2, hid_rows),
            wide(2, rows + 2),
        ],
        [vol_near, vol, vol_far, hid_own, cot_own, cot_other, fwd],
        (2 * hid_rows + 2 * (rows + 4) + 2 * rows) * row_macs,
    )

    near, far = neighbours(g3_near, g3_far)
    terms = ((packed_rows, LANES), bf16)
    bwd, three = call(
        between_body, [banded, terms], [rw], [bwd_taps, xs_own, g3], rows * row_macs
    )
    three = by_hop(three)
    xg1, others = call(
        functools.partial(back_body, depth, pairs, tiles),
        [((rows + 2 * H_G1, cells, WIDE), bf16), ((2, packed_rows, LANES), bf16)],
        [wide(2, rows + 2 * H_G3), wide(2, rows + 2 * H_G2), rw],
        [near, g3, far, sl1, sl2, xv_own, xb_own, bwd],
        (6 * rows + 12) * row_macs,
    )
    others, three = lax.optimization_barrier((others, three))
    others = by_hop(others)
    grad_volume = call(
        functools.partial(last_body, pairs, tiles),
        [((rows, height, lanes), bf16)],
        [raw_tiles(rows)],
        [xg1, bwd],
        rows * row_macs,
    )
    total = call(
        functools.partial(total_body, count),
        [((layers, packed_rows, LANES), f32)],
        [],
        [*others, *three],
    )
    return (grad_volume[None], total.reshape(1, layers, taps, width))


def solution(mesh):
    in_specs = (P("sample", "depth", None, None), P(), P(), P("sample", "depth", None, None))
    out_specs = (P("sample", "depth", None, None), P("sample", None, None, None))
    return jax.shard_map(
        per_device, mesh=mesh, in_specs=in_specs, out_specs=out_specs, check_vma=False
    )
```

```python
import functools

import jax
import jax.numpy as jnp
from jax import lax
from jax.experimental import pallas as pl
from jax.experimental.pallas import tpu as pltpu
from jax.sharding import PartitionSpec as P

CH = 32
OWN_SHARE = 0.6
PARTNER_SHARE = 0.4
LANES = 128
CELLS = LANES // CH
TILE = 2 * LANES
WIDE = 3 * TILE
VMEM_LIMIT = 40 * 2**20

SLOTS = (
    [(1 + h, 1 + w) for h in range(2) for w in range(CELLS)]
    + [(0, 1 + w) for w in range(CELLS)]
    + [(3, 1 + w) for w in range(CELLS)]
    + [(1, 5), (0, 0), (0, 5), (1, 0)]
    + [(2, 5), (3, 0), (3, 5), (2, 0)]
)
SLOT_OF = {cell: at for at, cell in enumerate(SLOTS)}

H_VOL, H_HIDDEN, H_TWO, H_G3, H_G2, H_G1 = 3, 2, 1, 2, 1, 1


def chunks_of(rows):
    count = max(1, (rows + 2) // 5)
    base, extra = divmod(rows, count)
    start, result = 0, []
    for index in range(count):
        size = base + (index < extra)
        result.append((start, size))
        start += size
    return result


def sigmoid(v):
    return 0.5 + 0.5 * jnp.tanh(0.5 * v)


def lanes_of(t):
    return slice(t * LANES, (t + 1) * LANES)


def taps_body(taps, kr_ref, fwd_ref, bwd_ref, scratch):
    layers, rows = kr_ref.shape[:2]
    part = scratch.shape[1] // CELLS // CH
    shape = (LANES, CELLS * LANES)
    lane = lax.broadcasted_iota(jnp.int32, shape, 1)
    chosen = lax.broadcasted_iota(jnp.int32, shape, 0) == lane // LANES * CH + lane % CH
    spread = jnp.where(chosen, 1.0, 0.0).astype(jnp.bfloat16)
    for layer in range(layers):
        groups = jnp.dot(kr_ref[layer], spread, preferred_element_type=jnp.float32)
        for q in range(CELLS):
            scratch[layer, pl.ds(q, rows, stride=CELLS), :] = groups[:, lanes_of(q)]
        scratch[layer, taps * CH :, :] = jnp.zeros_like(scratch[layer, taps * CH :, :])
        fwd_ref[layer] = scratch[layer, : taps * CH].astype(jnp.bfloat16)
        cell = lax.broadcasted_iota(jnp.int32, (part * CH, LANES), 1) // CH
        compact = jnp.zeros((part * CH, LANES), jnp.float32)
        for group in range(CELLS):
            at = group * part * CH
            compact = jnp.where(cell == group, scratch[layer, at : at + part * CH, :], compact)
        room = -(-part // CELLS) * LANES - part * CH
        turned = jnp.concatenate([compact, jnp.zeros((room, LANES), jnp.float32)], 0).T
        stacked = jnp.concatenate(
            [turned[:, lanes_of(t)] for t in range(turned.shape[1] // LANES)], 0
        ).astype(jnp.bfloat16)
        groups = jnp.dot(stacked, spread, preferred_element_type=jnp.float32)
        for tap in range(taps):
            group, index = divmod(tap, part)
            at, row = taps - 1 - tap, index // CELLS * LANES + group * CH
            bwd_ref[layer, at * CH : (at + 1) * CH, :] = groups[
                row : row + CH, lanes_of(index % CELLS)
            ].astype(jnp.bfloat16)


def fill_weights(taps_ref, t_ref):
    cell = lax.broadcasted_iota(jnp.int32, (CH, LANES), 1) // CH
    zero = jnp.zeros((CH, LANES), jnp.bfloat16)
    for layer in range(t_ref.shape[0]):
        for a in range(3):
            bands = {}
            for b in range(3):
                first = (a * 9 + b * 3) * CH
                values = [taps_ref[layer, first + c * CH : first + (c + 1) * CH, :] for c in range(3)]
                for ww in range(CELLS + 2):
                    band = zero
                    for c in range(3):
                        if 0 <= ww - c < CELLS:
                            band = jnp.where(cell == ww - c, values[c], band)
                    bands[b, ww] = band
            for at, (hh, ww) in enumerate(SLOTS):
                for h in range(2):
                    t_ref[
                        layer, a, at * CH : (at + 1) * CH, h * LANES : (h + 1) * LANES
                    ] = bands.get((hh - h, ww), zero)


def edge_masks(tiles):
    shape = (1, tiles, TILE)
    cell = lax.broadcasted_iota(jnp.int32, shape, 2) % LANES // CH
    row = lax.broadcasted_iota(jnp.int32, shape, 1)
    from_before = (cell == CELLS - 1) & (row > 0)
    from_after = (cell == 0) & (row < tiles - 1)
    return tuple(
        jnp.where(mask, 1.0, 0.0).astype(jnp.bfloat16) for mask in (from_before, from_after)
    )


def expand(x, out_ref, lead, pairs, tiles, masks):
    x = x.reshape(pairs, tiles, TILE)
    edge = pltpu.roll(x, 1, 1) * masks[0] + pltpu.roll(x, tiles - 1, 1) * masks[1]
    e0, e1 = edge[..., :LANES], edge[..., LANES:]
    r0, r1 = pltpu.roll(e0, LANES // 2, 2), pltpu.roll(e1, LANES // 2, 2)
    zero = jnp.zeros((1, tiles, LANES), x.dtype)
    low = jnp.concatenate([zero, x[:-1, :, LANES:]], 0)
    high = jnp.concatenate([x[1:, :, :LANES], zero], 0)
    e0 = e0 + jnp.concatenate([zero, r1[:-1]], 0)
    e1 = e1 + jnp.concatenate([r0[1:], zero], 0)
    flat = lambda v: v.reshape(pairs * tiles, v.shape[-1])
    out_ref[(*lead, slice(None), slice(0, TILE))] = flat(x)
    out_ref[(*lead, slice(None), slice(TILE, TILE + LANES))] = flat(low)
    out_ref[(*lead, slice(None), slice(TILE + LANES, 2 * TILE))] = flat(high)
    out_ref[(*lead, slice(None), slice(2 * TILE, 2 * TILE + LANES))] = flat(e0)
    out_ref[(*lead, slice(None), slice(2 * TILE + LANES, WIDE))] = flat(e1)


def conv_rows(x_ref, lead, start, rows, t_ref, layer):
    blocks = [x_ref[(*lead, pl.ds(start + a, rows))].reshape(-1, WIDE) for a in range(3)]
    return jnp.dot(
        jnp.concatenate(blocks, axis=1),
        t_ref[layer].reshape(3 * WIDE, TILE),
        preferred_element_type=jnp.float32,
    )


def slope_of(pre, gate):
    return gate * (1.0 + pre * (1.0 - gate))


def rounded(v):
    return v.astype(jnp.bfloat16)


def inside(v, row, depth):
    return jnp.where((row >= 0) & (row < depth), v, 0.0)


def either(flag, a, b):
    low = lambda *at: jnp.where(flag, a[at], b[at])
    high = lambda *at: jnp.where(flag, b[at], a[at])
    return low, high


def widen(near, own, far, lead, halo, x_ref, x_lead, grow):
    at, last = lax.axis_index("depth"), lax.axis_size("depth") - 1
    low, high = either(at % 2 == 1, near, far)
    held, rows = near.shape[len(lead)], own.shape[len(lead)]
    for d in range(halo):
        row = low(*lead, held - halo + d)
        if d == halo - 1:
            row = jnp.where(at > 0, row, jnp.zeros_like(row))
        grow(row, x_ref, (*x_lead, d))
    for d in range(rows):
        grow(own[(*lead, d)], x_ref, (*x_lead, halo + d))
    for d in range(halo):
        row = high(*lead, d)
        if d == 0:
            row = jnp.where(at < last, row, jnp.zeros_like(row))
        grow(row, x_ref, (*x_lead, halo + rows + d))


def edge_rows(values, near, far, halo):
    odd = lax.axis_index("depth") % 2 == 1
    rows = values.shape[0]
    for d in range(halo):
        up, down = values[rows - halo + d], values[d]
        near[d] = jnp.where(odd, down, up)
        far[d] = jnp.where(odd, up, down)


def layer_one(xv, lead, out_ref, t_ref, slopes_ref=None):
    rows, cells = out_ref.shape[len(lead)], out_ref.shape[-2]
    for start, count in chunks_of(rows):
        pre = conv_rows(xv, lead, start, count, t_ref, 0)
        gate = sigmoid(pre)
        value = (pre * gate).astype(jnp.bfloat16).reshape(count, cells, TILE)
        out_ref[(*lead, pl.ds(start, count))] = value
        if slopes_ref is not None:
            slope = slope_of(pre, gate).reshape(count, cells, TILE)
            for d in range(count):
                to = start + d - H_HIDDEN
                if 0 <= to < slopes_ref.shape[0]:
                    slopes_ref[to] = slope[d]


def tiled_rows(load, height, tiles, scratch, at):
    for t in range(tiles):
        scratch[at, t * height : (t + 1) * height, :] = load(t).astype(jnp.float32)
    for h in range(height):
        piece = scratch[at, pl.ds(h, tiles, stride=height), :].astype(jnp.bfloat16)
        yield h // 2 * tiles, slice(h % 2 * LANES, (h % 2 + 1) * LANES), piece


def select_body(partner, both, *refs):
    *crops, out, near, far, scratch = refs
    own = lax.axis_index("sample")
    inverse = jnp.int32(0)
    for crop in range(partner.shape[0]):
        inverse = jnp.where(partner[crop] == own, crop, inverse)
    wanted = (partner[own], inverse)[2 - out.shape[0] :]
    _, rows, height, lanes = both.shape
    tiles = lanes // LANES
    mine = both.at[2 - out.shape[0]]
    for to, crop in enumerate(wanted):
        for hop, source in enumerate((mine, *crops)):

            @pl.when(crop ^ own == hop)
            def _(to=to, source=source):
                for d in range(rows):
                    for t in range(tiles):
                        scratch[to, d, t * height : (t + 1) * height, :] = source[
                            d, :, lanes_of(t)
                        ].astype(jnp.float32)

        for d in range(rows):
            for h in range(height):
                piece = scratch[to, d, pl.ds(h, tiles, stride=height), :].astype(jnp.bfloat16)
                row, side = h // 2 * tiles, lanes_of(h % 2)
                out[to, d, row : row + tiles, side] = piece
        if near.shape[0] > 1:
            edge_rows(out.at[to], near.at[to], far.at[to], H_VOL)


def own_body(
    pairs, tiles,
    taps_ref, near, both, far,
    t_ref, hid, sl1, xv_own, cot_own,
    xv, field, scratch,
):
    _, rows, height, _ = both.shape
    fill_weights(taps_ref, t_ref)
    grow = functools.partial(expand, pairs=pairs, tiles=tiles, masks=edge_masks(tiles))
    for at, part in enumerate((near, both.at[0], far, both.at[1])):
        for d in range(rows):
            load = lambda t, part=part, d=d: part[d, :, lanes_of(t)]
            for row, side, piece in tiled_rows(load, height, tiles, scratch, at * rows + d):
                if at < 3:
                    field[at, d, row : row + tiles, side] = piece
                else:
                    cot_own[d, row : row + tiles, side] = piece
    widen(field.at[0], field.at[1], field.at[2], (), H_VOL, xv, (), grow)
    layer_one(xv, (), hid, t_ref, sl1)
    xv_own[...] = xv[H_VOL - 1 : H_VOL + rows + 1]


def forward_body(
    depth, pairs, tiles,
    near, mid, far, hid_own, cot_own, cot_other, t_ref,
    g3, g3_near, g3_far, sl2, xb_own, xs_own,
    xv, hid, xb, xs,
):
    rows = mid.shape[1]
    cells = pairs * tiles
    first = lax.axis_index("depth") * rows
    grow = functools.partial(expand, pairs=pairs, tiles=tiles, masks=edge_masks(tiles))

    for crop in range(2):
        widen(near, mid, far, (crop,), H_VOL, xv, (crop,), grow)
        layer_one(xv, (crop,), hid, t_ref)

    for d in range(rows + 2 * H_HIDDEN):
        own = hid_own[d].astype(jnp.float32)
        partner, other = hid[0, d].astype(jnp.float32), hid[1, d].astype(jnp.float32)
        row = first + d - H_HIDDEN
        for j, (a, b) in enumerate(((own, partner), (other, own))):
            mixed = OWN_SHARE * a + PARTNER_SHARE * b
            grow(rounded(inside(mixed, row, depth)), xb, (j, d))

    def middle(j, cot):
        for start, count in chunks_of(rows + 2 * H_TWO):
            pre = conv_rows(xb, (j,), start, count, t_ref, 1)
            gate = sigmoid(pre)
            value = (pre * gate).reshape(count, cells, TILE)
            slope = slope_of(pre, gate).reshape(count, cells, TILE)
            for d in range(count):
                sl2[j, start + d] = slope[d]
                to = start + d - (H_TWO - 1)
                if 0 <= to < rows + 2:
                    grow(rounded(inside(value[d], first + to - 1, depth)), xs, (j, to))
        for start, count in chunks_of(rows):
            pre = conv_rows(xs, (j,), start, count, t_ref, 2)
            slope = slope_of(pre, sigmoid(pre)).reshape(count, cells, TILE)
            for d in range(count):
                at = start + d
                grad = rounded(cot[at].astype(jnp.float32) * slope[d])
                g3[j, at] = grad

    middle(0, cot_own)
    middle(1, cot_other.at[0])
    for j in range(2):
        edge_rows(g3.at[j], g3_near.at[j], g3_far.at[j], H_G3)
    xb_own[...] = xb[0, H_HIDDEN - 1 : H_HIDDEN + rows + 1]
    xs_own[...] = xs[0]


def kernel_terms(values, gradient, rw):
    rows = gradient.shape[0]
    gradient = gradient.reshape(-1, TILE)
    for a in range(3):
        block = values[a : a + rows].reshape(-1, WIDE)
        terms = lax.dot_general(
            block, gradient, (((0,), (0,)), ((), ())), preferred_element_type=jnp.float32
        )
        for b in range(3):
            for c in range(3):
                at = (a * 9 + b * 3 + c) * CH
                for w in range(CELLS):
                    s0, s1 = SLOT_OF[b, w + c] * CH, SLOT_OF[b + 1, w + c] * CH
                    rw[w, at : at + CH] = (
                        terms[s0 : s0 + CH, :LANES] + terms[s1 : s1 + CH, LANES:]
                    )
    count = rw.shape[1] // CELLS
    cell = lax.broadcasted_iota(jnp.int32, (count, LANES), 1) // CH
    dense = jnp.zeros((count, LANES), jnp.float32)
    for q in range(CELLS):
        part = None
        for w in range(CELLS):
            piece = rw[w, pl.ds(q, count, stride=CELLS), :]
            if q != w:
                piece = pltpu.roll(piece, (q - w) % CELLS * CH, 1)
            part = piece if part is None else part + piece
        dense = jnp.where(cell == q, part, dense)
    return dense.astype(jnp.bfloat16)


def between_body(taps_ref, xs_own, g3, t_ref, terms, rw):
    fill_weights(taps_ref, t_ref)
    terms[...] = kernel_terms(xs_own[...], g3[0], rw)


def back_two(j, x_ref, sl2, x2_ref, t_ref, first, depth, grow):
    rows, cells = x2_ref.shape[-3:-1]
    for start, count in chunks_of(rows):
        back = conv_rows(x_ref, (), start, count, t_ref, 2).reshape(count, cells, TILE)
        for d in range(count):
            at = start + d
            grad = inside(back[d] * sl2[j, at], first + at - H_G2, depth)
            grow(rounded(grad), x2_ref, (at,))


def back_body(
    depth, pairs, tiles,
    near, mid, far, sl1, sl2, xv_own, xb_own, t_ref,
    g1, g1_near, g1_far, terms,
    xg3, xg2, rw,
):
    rows = mid.shape[1]
    cells = pairs * tiles
    first = lax.axis_index("depth") * rows
    grow = functools.partial(expand, pairs=pairs, tiles=tiles, masks=edge_masks(tiles))
    for j in range(2):
        widen(near, mid, far, (j,), H_G3, xg3.at[j], (), grow)
        back_two(j, xg3.at[j], sl2, xg2.at[j], t_ref, first, depth, grow)
    own, other = (
        rounded(conv_rows(xg2, (j,), 0, rows, t_ref, 1)).astype(jnp.float32) for j in range(2)
    )
    mixed = (OWN_SHARE * own + PARTNER_SHARE * other).reshape(rows, cells, TILE)
    g1[...] = rounded(mixed * sl1[...])
    edge_rows(g1, g1_near, g1_far, H_G1)
    terms[0] = kernel_terms(xv_own[...], g1[...], rw)
    terms[1] = kernel_terms(xb_own[...], xg2[0, H_G2 : H_G2 + rows, :, :TILE], rw)


def last_body(pairs, tiles, near, g1, far, t_ref, gv, scratch, xg1):
    rows, height, _ = gv.shape
    cells = pairs * tiles
    grow = functools.partial(expand, pairs=pairs, tiles=tiles, masks=edge_masks(tiles))
    widen(near, g1, far, (), H_G1, xg1, (), grow)
    for start, count in chunks_of(rows):
        back = conv_rows(xg1, (), start, count, t_ref, 0).reshape(count, cells, TILE)
        for d in range(count):
            for h in range(height):
                row, side = h // 2 * tiles, slice(h % 2 * LANES, (h % 2 + 1) * LANES)
                scratch[start + d, pl.ds(h, tiles, stride=height), :] = back[
                    d, row : row + tiles, side
                ]
            for t in range(tiles):
                gv[start + d, :, t * LANES : (t + 1) * LANES] = scratch[
                    start + d, t * height : (t + 1) * height, :
                ].astype(jnp.bfloat16)


def add_body(one, two, *refs):
    *three, out = refs
    add = lambda a, b: (a.astype(jnp.float32) + b.astype(jnp.float32)).astype(out.dtype)
    for layer in range(one.shape[0]):
        out[layer] = add(one[layer], two[layer])
    if three:
        out[one.shape[0]] = add(three[0][...], three[1][...])


def swapped(values, hop):
    count = lax.axis_size("depth")
    return lax.ppermute(values, "depth", [(i, i ^ hop) for i in range(count)])


def neighbours(near, far):
    count = lax.axis_size("depth")
    result = []
    for values, first in ((near, 0), (far, 1)):
        partner = {}
        for i in range(first, count - 1, 2):
            partner[i], partner[i + 1] = i + 1, i
        pairs = [(i, partner.get(i, i)) for i in range(count)]
        result.append(lax.ppermute(values, "depth", pairs))
    return result


def over_sample(values, hop):
    groups = lax.axis_size("sample")
    return lax.ppermute(values, "sample", [(i, i ^ hop) for i in range(groups)])


def even_hops(values):
    return [over_sample(values, hop) for hop in range(2, lax.axis_size("sample"), 2)]


def all_hops(odd, evens):
    return [odd, *(crop for even in evens for crop in (even, over_sample(even, 1)))]


def traded(volume, cotangent, partner, tiles):
    groups = lax.axis_size("sample")
    rows, height, _ = volume.shape
    split = jnp.stack([volume, cotangent]).reshape(2, rows, height // 2, 2, tiles, LANES)
    split = split.transpose(0, 1, 2, 4, 3, 5).reshape(2, groups, -1, TILE)
    pieces = split.swapaxes(0, 1)
    spread = lax.all_to_all(pieces, "sample", split_axis=0, concat_axis=0, tiled=True)
    ids = jnp.arange(groups, dtype=jnp.int32)
    inverse = jnp.sum(jnp.where(partner[:, None] == ids[None, :], ids[:, None], 0), axis=0)
    wanted = jnp.stack([2 * partner, 2 * inverse, 2 * inverse + 1], axis=1)
    chosen = jnp.take(spread.reshape(2 * groups, -1, TILE), wanted, axis=0)
    joined = lax.all_to_all(chosen, "sample", split_axis=0, concat_axis=0, tiled=True)
    others = jnp.swapaxes(joined, 0, 1).reshape(3, rows, -1, TILE)
    return others[:2], others[2:]


def call(kernel, outs, scratch, inputs, macs=0, far=()):
    vmem, smem, anywhere = (
        pl.BlockSpec(memory_space=space) for space in (pltpu.VMEM, pltpu.SMEM, pl.ANY)
    )
    specs = [
        anywhere if at in far else smem if x.dtype == jnp.int32 else vmem
        for at, x in enumerate(inputs)
    ]
    results = pl.pallas_call(
        kernel,
        out_shape=tuple(jax.ShapeDtypeStruct(shape, dtype) for shape, dtype in outs),
        in_specs=specs,
        out_specs=(vmem,) * len(outs),
        scratch_shapes=scratch,
        compiler_params=pltpu.CompilerParams(vmem_limit_bytes=VMEM_LIMIT),
        cost_estimate=pl.CostEstimate(
            flops=2 * macs, bytes_accessed=2**22 if macs else 1, transcendentals=0
        ),
    )(*inputs)
    return results if len(results) > 1 else results[0]


def per_device(volume, kernels, partner, cotangent):
    volume, cotangent = volume[0], cotangent[0]
    rows, height, lanes = volume.shape
    pairs, tiles = height // 2, lanes // LANES
    cells = pairs * tiles
    groups, count = lax.axis_size("sample"), lax.axis_size("depth")
    depth = rows * count
    layers, taps, width = kernels.shape
    bf16, f32 = jnp.bfloat16, jnp.float32
    row_macs = 3 * cells * WIDE * TILE
    packed_rows = taps * CH // CELLS
    wide = lambda *lead: pltpu.VMEM((*lead, cells, WIDE), bf16)
    field = lambda *lead: ((*lead, cells, TILE), bf16)
    raw_tiles = lambda *lead: pltpu.VMEM((*lead, height * tiles, LANES), f32)
    banded = ((layers, 3, WIDE, TILE), bf16)
    spread_taps = ((layers, taps * CH, LANES), bf16)
    rw = pltpu.VMEM((CELLS, taps * CH, LANES), f32)

    direct = groups in (2, 4, 8)
    evens = even_hops(volume) if direct else []
    both, edges = lax.optimization_barrier((jnp.stack([volume, cotangent]), volume))
    near, far = neighbours(edges, edges)
    packed = kernels.reshape(layers, packed_rows, LANES)
    ids = jnp.clip(partner, 0, groups - 1)
    fwd_taps, bwd_taps = call(
        functools.partial(taps_body, taps),
        [spread_taps, spread_taps],
        [pltpu.VMEM((layers, -(-taps // CELLS) * LANES, LANES), f32)],
        [packed],
        2**28,
    )
    evens, both, ids, fwd_taps, bwd_taps, own_crop, late = lax.optimization_barrier(
        (evens, both, ids, fwd_taps, bwd_taps, volume, cotangent)
    )
    edge = lambda n: ((n, H_VOL, cells, TILE), bf16)
    if direct:
        crops = all_hops(over_sample(own_crop, 1), evens)
        crops, near, far = lax.optimization_barrier((crops, near, far))
        vol, vol_near, vol_far = call(
            select_body,
            [field(2, rows), edge(2), edge(2)],
            [raw_tiles(2, rows)],
            [ids, both, *crops],
        )
        sides = neighbours(vol_near, vol_far)
        later, _ = lax.optimization_barrier((late, vol_near))
        evens, vol = lax.optimization_barrier((even_hops(late), vol))
        cot_other, *_ = call(
            select_body,
            [field(1, rows), edge(1), edge(1)],
            [raw_tiles(1, rows)],
            [ids, both, *all_hops(over_sample(later, 1), evens)],
        )
    else:
        vol, cot_other = traded(volume, cotangent, partner, tiles)
        sides = neighbours(vol, vol)
    hid_rows = rows + 2 * H_HIDDEN
    fwd, hid_own, sl1, xv_own, cot_own = call(
        functools.partial(own_body, pairs, tiles),
        [
            banded,
            field(hid_rows),
            ((rows, cells, TILE), f32),
            ((rows + 2, cells, WIDE), bf16),
            field(rows),
        ],
        [wide(rows + 2 * H_VOL), pltpu.VMEM((3, rows, cells, TILE), bf16), raw_tiles(4 * rows)],
        [fwd_taps, near, both, far],
        hid_rows * row_macs,
    )

    g3, g3_near, g3_far, sl2, xb_own, xs_own = call(
        functools.partial(forward_body, depth, pairs, tiles),
        [
            field(2, rows),
            field(2, H_G3),
            field(2, H_G3),
            ((2, rows + 2 * H_TWO, cells, TILE), f32),
            ((rows + 2, cells, WIDE), bf16),
            ((rows + 2, cells, WIDE), bf16),
        ],
        [
            wide(2, rows + 2 * H_VOL),
            pltpu.VMEM((2, hid_rows, cells, TILE), bf16),
            wide(2, hid_rows),
            wide(2, rows + 2),
        ],
        [sides[0], vol, sides[1], hid_own, cot_own, cot_other, fwd],
        (2 * hid_rows + 2 * (rows + 2) + 2 * rows) * row_macs,
    )

    near, far = neighbours(g3_near, g3_far)
    terms = ((packed_rows, LANES), bf16)
    bwd, three = call(
        between_body, [banded, terms], [rw], [bwd_taps, xs_own, g3], rows * row_macs
    )
    three_near = swapped(three, 1)
    edge = ((H_G1, cells, TILE), bf16)
    g1, g1_near, g1_far, others = call(
        functools.partial(back_body, depth, pairs, tiles),
        [field(rows), edge, edge, ((2, packed_rows, LANES), bf16)],
        [wide(2, rows + 2 * H_G3), wide(2, rows + 2 * H_G2), rw],
        [near, g3, far, sl1, sl2, xv_own, xb_own, bwd],
        (6 * rows + 4) * row_macs,
    )
    others, three_near = lax.optimization_barrier((others, three_near))
    every = ((layers, packed_rows, LANES), bf16)
    summed = call(add_body, [every], [], [others, swapped(others, 1), three, three_near])
    near, far = neighbours(g1_near, g1_far)
    grad_volume = call(
        functools.partial(last_body, pairs, tiles),
        [((rows, height, lanes), bf16)],
        [raw_tiles(rows), wide(rows + 2 * H_G1)],
        [near, g1, far, bwd],
        rows * row_macs,
    )
    hop = 2
    while hop < count:
        dtype = bf16 if 2 * hop < count else f32
        summed = call(
            add_body, [((layers, packed_rows, LANES), dtype)], [], [summed, swapped(summed, hop)]
        )
        hop *= 2
    total = summed.astype(f32)
    return (grad_volume[None], total.reshape(1, layers, taps, width))


def solution(mesh):
    in_specs = (P("sample", "depth", None, None), P(), P(), P("sample", "depth", None, None))
    out_specs = (P("sample", "depth", None, None), P("sample", None, None, None))
    return jax.shard_map(
        per_device, mesh=mesh, in_specs=in_specs, out_specs=out_specs, check_vma=False
    )
```

```python
import functools

import jax
import jax.numpy as jnp
from jax import lax
from jax.experimental import pallas as pl
from jax.experimental.pallas import tpu as pltpu
from jax.sharding import PartitionSpec as P

CH = 32
OWN_SHARE = 0.6
PARTNER_SHARE = 0.4
LANES = 128
CELLS = LANES // CH
TILE = 2 * LANES
WIDE = 3 * TILE
VMEM_LIMIT = 40 * 2**20

SLOTS = (
    [(1 + h, 1 + w) for h in range(2) for w in range(CELLS)]
    + [(0, 1 + w) for w in range(CELLS)]
    + [(3, 1 + w) for w in range(CELLS)]
    + [(1, 5), (0, 0), (0, 5), (1, 0)]
    + [(2, 5), (3, 0), (3, 5), (2, 0)]
)
SLOT_OF = {cell: at for at, cell in enumerate(SLOTS)}

H_VOL, H_HIDDEN, H_TWO, H_G3, H_G2, H_G1 = 3, 2, 1, 2, 1, 1


def chunks_of(rows):
    count = -(-rows // 3)
    base, extra = divmod(rows, count)
    start, result = 0, []
    for index in range(count):
        size = base + (index < extra)
        result.append((start, size))
        start += size
    return result


def sigmoid(v):
    return 0.5 + 0.5 * jnp.tanh(0.5 * v)


def lanes_of(t):
    return slice(t * LANES, (t + 1) * LANES)


def taps_body(taps, kr_ref, fwd_ref, bwd_ref, scratch):
    layers, _, width = kr_ref.shape
    part = scratch.shape[1] // CELLS // CH
    shape = (LANES, CELLS * LANES)
    lane = lax.broadcasted_iota(jnp.int32, shape, 1)
    chosen = lax.broadcasted_iota(jnp.int32, shape, 0) == lane // LANES * CH + lane % CH
    spread = jnp.where(chosen, 1.0, 0.0).astype(jnp.bfloat16)
    for layer in range(layers):
        for piece in range(width // LANES):
            groups = jnp.dot(
                kr_ref[layer, :, lanes_of(piece)], spread, preferred_element_type=jnp.float32
            )
            for q in range(CELLS):
                at = pl.ds(piece * CELLS + q, taps, stride=CH)
                scratch[layer, at, :] = groups[:, lanes_of(q)]
        scratch[layer, taps * CH :, :] = jnp.zeros_like(scratch[layer, taps * CH :, :])
        fwd_ref[layer] = scratch[layer, : taps * CH].astype(jnp.bfloat16)
        cell = lax.broadcasted_iota(jnp.int32, (part * CH, LANES), 1) // CH
        compact = jnp.zeros((part * CH, LANES), jnp.float32)
        for group in range(CELLS):
            at = group * part * CH
            compact = jnp.where(cell == group, scratch[layer, at : at + part * CH, :], compact)
        room = -(-part // CELLS) * LANES - part * CH
        turned = jnp.concatenate([compact, jnp.zeros((room, LANES), jnp.float32)], 0).T
        stacked = jnp.concatenate(
            [turned[:, lanes_of(t)] for t in range(turned.shape[1] // LANES)], 0
        ).astype(jnp.bfloat16)
        groups = jnp.dot(stacked, spread, preferred_element_type=jnp.float32)
        for tap in range(taps):
            group, index = divmod(tap, part)
            at, row = taps - 1 - tap, index // CELLS * LANES + group * CH
            bwd_ref[layer, at * CH : (at + 1) * CH, :] = groups[
                row : row + CH, lanes_of(index % CELLS)
            ].astype(jnp.bfloat16)


def fill_weights(taps_ref, t_ref):
    cell = lax.broadcasted_iota(jnp.int32, (CH, LANES), 1) // CH
    zero = jnp.zeros((CH, LANES), jnp.bfloat16)
    for layer in range(t_ref.shape[0]):
        for a in range(3):
            bands = {}
            for b in range(3):
                first = (a * 9 + b * 3) * CH
                values = [taps_ref[layer, first + c * CH : first + (c + 1) * CH, :] for c in range(3)]
                for ww in range(CELLS + 2):
                    band = zero
                    for c in range(3):
                        if 0 <= ww - c < CELLS:
                            band = jnp.where(cell == ww - c, values[c], band)
                    bands[b, ww] = band
            for at, (hh, ww) in enumerate(SLOTS):
                for h in range(2):
                    t_ref[
                        layer, a, at * CH : (at + 1) * CH, h * LANES : (h + 1) * LANES
                    ] = bands.get((hh - h, ww), zero)


def edge_masks(tiles):
    shape = (1, tiles, TILE)
    cell = lax.broadcasted_iota(jnp.int32, shape, 2) % LANES // CH
    row = lax.broadcasted_iota(jnp.int32, shape, 1)
    from_before = (cell == CELLS - 1) & (row > 0)
    from_after = (cell == 0) & (row < tiles - 1)
    return tuple(
        jnp.where(mask, 1.0, 0.0).astype(jnp.bfloat16) for mask in (from_before, from_after)
    )


def expand(x, out_ref, lead, pairs, tiles, masks):
    x = x.reshape(pairs, tiles, TILE)
    edge = pltpu.roll(x, 1, 1) * masks[0] + pltpu.roll(x, tiles - 1, 1) * masks[1]
    e0, e1 = edge[..., :LANES], edge[..., LANES:]
    r0, r1 = pltpu.roll(e0, LANES // 2, 2), pltpu.roll(e1, LANES // 2, 2)
    zero = jnp.zeros((1, tiles, LANES), x.dtype)
    low = jnp.concatenate([zero, x[:-1, :, LANES:]], 0)
    high = jnp.concatenate([x[1:, :, :LANES], zero], 0)
    e0 = e0 + jnp.concatenate([zero, r1[:-1]], 0)
    e1 = e1 + jnp.concatenate([r0[1:], zero], 0)
    flat = lambda v: v.reshape(pairs * tiles, v.shape[-1])
    out_ref[(*lead, slice(None), slice(0, TILE))] = flat(x)
    out_ref[(*lead, slice(None), slice(TILE, TILE + LANES))] = flat(low)
    out_ref[(*lead, slice(None), slice(TILE + LANES, 2 * TILE))] = flat(high)
    out_ref[(*lead, slice(None), slice(2 * TILE, 2 * TILE + LANES))] = flat(e0)
    out_ref[(*lead, slice(None), slice(2 * TILE + LANES, WIDE))] = flat(e1)


def conv_rows(x_ref, lead, start, rows, t_ref, layer):
    blocks = [x_ref[(*lead, pl.ds(start + a, rows))].reshape(-1, WIDE) for a in range(3)]
    return jnp.dot(
        jnp.concatenate(blocks, axis=1),
        t_ref[layer].reshape(3 * WIDE, TILE),
        preferred_element_type=jnp.float32,
    )


def slope_of(pre, gate):
    return gate * (1.0 + pre * (1.0 - gate))


def rounded(v):
    return v.astype(jnp.bfloat16)


def inside(v, row, depth):
    return jnp.where((row >= 0) & (row < depth), v, 0.0)


def either(flag, a, b):
    low = lambda *at: jnp.where(flag, a[at], b[at])
    high = lambda *at: jnp.where(flag, b[at], a[at])
    return low, high


def widen(near, own, far, lead, halo, x_ref, x_lead, grow):
    at, last = lax.axis_index("depth"), lax.axis_size("depth") - 1
    low, high = either(at % 2 == 1, near, far)
    held, rows = near.shape[len(lead)], own.shape[len(lead)]
    for d in range(halo):
        row = low(*lead, held - halo + d)
        if d == halo - 1:
            row = jnp.where(at > 0, row, jnp.zeros_like(row))
        grow(row, x_ref, (*x_lead, d))
    for d in range(rows):
        grow(own[(*lead, d)], x_ref, (*x_lead, halo + d))
    for d in range(halo):
        row = high(*lead, d)
        if d == 0:
            row = jnp.where(at < last, row, jnp.zeros_like(row))
        grow(row, x_ref, (*x_lead, halo + rows + d))


def edge_rows(values, near, far, halo):
    odd = lax.axis_index("depth") % 2 == 1
    rows = values.shape[0]
    for d in range(halo):
        up, down = values[rows - halo + d], values[d]
        near[d] = jnp.where(odd, down, up)
        far[d] = jnp.where(odd, up, down)


def layer_one(xv, lead, out_ref, t_ref, slopes_ref=None):
    rows, cells = out_ref.shape[len(lead)], out_ref.shape[-2]
    for start, count in chunks_of(rows):
        pre = conv_rows(xv, lead, start, count, t_ref, 0)
        gate = sigmoid(pre)
        value = (pre * gate).astype(jnp.bfloat16).reshape(count, cells, TILE)
        out_ref[(*lead, pl.ds(start, count))] = value
        if slopes_ref is not None:
            slope = slope_of(pre, gate).reshape(count, cells, TILE)
            for d in range(count):
                to = start + d - H_HIDDEN
                if 0 <= to < slopes_ref.shape[0]:
                    slopes_ref[to] = slope[d]


def tiled_rows(load, height, tiles, scratch, at):
    for t in range(tiles):
        scratch[at, t * height : (t + 1) * height, :] = load(t).astype(jnp.float32)
    for h in range(height):
        piece = scratch[at, pl.ds(h, tiles, stride=height), :].astype(jnp.bfloat16)
        yield h // 2 * tiles, slice(h % 2 * LANES, (h % 2 + 1) * LANES), piece


def select_body(hops, partner, both, *refs):
    crops, out, sides, scratch = refs[:hops], refs[hops], refs[hops + 1 : -1], refs[-1]
    own = lax.axis_index("sample")
    inverse = jnp.int32(0)
    for crop in range(partner.shape[0]):
        inverse = jnp.where(partner[crop] == own, crop, inverse)
    wanted = (partner[own], inverse)[2 - out.shape[0] :]
    _, rows, height, lanes = both.shape
    tiles = lanes // LANES
    mine = both.at[2 - out.shape[0]]
    for to, crop in enumerate(wanted):
        for hop, source in enumerate((mine, *crops)):

            @pl.when(crop ^ own == hop)
            def _(to=to, source=source):
                for d in range(rows):
                    for t in range(tiles):
                        scratch[to, d, t * height : (t + 1) * height, :] = source[
                            d, :, lanes_of(t)
                        ].astype(jnp.float32)

        for d in range(rows):
            for h in range(height):
                piece = scratch[to, d, pl.ds(h, tiles, stride=height), :].astype(jnp.bfloat16)
                row, side = h // 2 * tiles, lanes_of(h % 2)
                out[to, d, row : row + tiles, side] = piece
        if sides:
            edge_rows(out.at[to], *(side.at[to] for side in sides), H_VOL)


def own_body(
    pairs, tiles,
    taps_ref, near, both, far,
    t_ref, hid, sl1, xv_own, cot_own,
    xv, field, scratch,
):
    _, rows, height, _ = both.shape
    fill_weights(taps_ref, t_ref)
    grow = functools.partial(expand, pairs=pairs, tiles=tiles, masks=edge_masks(tiles))
    for at, part in enumerate((near, both.at[0], far, both.at[1])):
        for d in range(rows):
            load = lambda t, part=part, d=d: part[d, :, lanes_of(t)]
            for row, side, piece in tiled_rows(load, height, tiles, scratch, at * rows + d):
                if at < 3:
                    field[at, d, row : row + tiles, side] = piece
                else:
                    cot_own[d, row : row + tiles, side] = piece
    widen(field.at[0], field.at[1], field.at[2], (), H_VOL, xv, (), grow)
    layer_one(xv, (), hid, t_ref, sl1)
    xv_own[...] = xv[H_VOL - 1 : H_VOL + rows + 1]


def forward_body(
    depth, pairs, tiles,
    near, mid, far, hid_own, cot_own, cot_other, t_ref,
    g3, g3_near, g3_far, sl2, xb_own, xs_own,
    xv, hid, xb, xs,
):
    rows = mid.shape[1]
    cells = pairs * tiles
    first = lax.axis_index("depth") * rows
    grow = functools.partial(expand, pairs=pairs, tiles=tiles, masks=edge_masks(tiles))

    for crop in range(2):
        widen(near, mid, far, (crop,), H_VOL, xv, (crop,), grow)
        layer_one(xv, (crop,), hid, t_ref)

    for d in range(rows + 2 * H_HIDDEN):
        own = hid_own[d].astype(jnp.float32)
        partner, other = hid[0, d].astype(jnp.float32), hid[1, d].astype(jnp.float32)
        row = first + d - H_HIDDEN
        for j, (a, b) in enumerate(((own, partner), (other, own))):
            mixed = OWN_SHARE * a + PARTNER_SHARE * b
            grow(rounded(inside(mixed, row, depth)), xb, (j, d))

    def middle(j, cot):
        for start, count in chunks_of(rows + 2 * H_TWO):
            pre = conv_rows(xb, (j,), start, count, t_ref, 1)
            gate = sigmoid(pre)
            value = (pre * gate).reshape(count, cells, TILE)
            slope = slope_of(pre, gate).reshape(count, cells, TILE)
            for d in range(count):
                sl2[j, start + d] = slope[d]
                to = start + d - (H_TWO - 1)
                if 0 <= to < rows + 2:
                    grow(rounded(inside(value[d], first + to - 1, depth)), xs, (j, to))
        for start, count in chunks_of(rows):
            pre = conv_rows(xs, (j,), start, count, t_ref, 2)
            slope = slope_of(pre, sigmoid(pre)).reshape(count, cells, TILE)
            for d in range(count):
                at = start + d
                grad = rounded(cot[at].astype(jnp.float32) * slope[d])
                g3[j, at] = grad

    middle(0, cot_own)
    middle(1, cot_other.at[0])
    for j in range(2):
        edge_rows(g3.at[j], g3_near.at[j], g3_far.at[j], H_G3)
    xb_own[...] = xb[0, H_HIDDEN - 1 : H_HIDDEN + rows + 1]
    xs_own[...] = xs[0]


def kernel_terms(values, gradient, rw):
    rows = gradient.shape[0]
    gradient = gradient.reshape(-1, TILE)
    for a in range(3):
        block = values[a : a + rows].reshape(-1, WIDE)
        terms = lax.dot_general(
            block, gradient, (((0,), (0,)), ((), ())), preferred_element_type=jnp.float32
        )
        for b in range(3):
            for c in range(3):
                at = (a * 9 + b * 3 + c) * CH
                for w in range(CELLS):
                    s0, s1 = SLOT_OF[b, w + c] * CH, SLOT_OF[b + 1, w + c] * CH
                    rw[w, at : at + CH] = (
                        terms[s0 : s0 + CH, :LANES] + terms[s1 : s1 + CH, LANES:]
                    )
    count = rw.shape[1] // CELLS
    cell = lax.broadcasted_iota(jnp.int32, (count, LANES), 1) // CH
    dense = jnp.zeros((count, LANES), jnp.float32)
    for q in range(CELLS):
        part = None
        for w in range(CELLS):
            piece = rw[w, pl.ds(q, count, stride=CELLS), :]
            if q != w:
                piece = pltpu.roll(piece, (q - w) % CELLS * CH, 1)
            part = piece if part is None else part + piece
        dense = jnp.where(cell == q, part, dense)
    return dense.astype(jnp.bfloat16)


def between_body(taps_ref, xs_own, g3, t_ref, terms, rw):
    fill_weights(taps_ref, t_ref)
    terms[...] = kernel_terms(xs_own[...], g3[0], rw)


def back_two(j, x_ref, sl2, x2_ref, t_ref, first, depth, grow):
    rows, cells = x2_ref.shape[-3:-1]
    for start, count in chunks_of(rows):
        back = conv_rows(x_ref, (), start, count, t_ref, 2).reshape(count, cells, TILE)
        for d in range(count):
            at = start + d
            grad = inside(back[d] * sl2[j, at], first + at - H_G2, depth)
            grow(rounded(grad), x2_ref, (at,))


def back_body(
    depth, pairs, tiles,
    near, mid, far, sl1, sl2, xv_own, xb_own, t_ref,
    g1, g1_near, g1_far, terms,
    xg3, xg2, rw,
):
    rows = mid.shape[1]
    cells = pairs * tiles
    first = lax.axis_index("depth") * rows
    grow = functools.partial(expand, pairs=pairs, tiles=tiles, masks=edge_masks(tiles))
    for j in range(2):
        widen(near, mid, far, (j,), H_G3, xg3.at[j], (), grow)
        back_two(j, xg3.at[j], sl2, xg2.at[j], t_ref, first, depth, grow)
    own, other = (
        rounded(conv_rows(xg2, (j,), 0, rows, t_ref, 1)).astype(jnp.float32) for j in range(2)
    )
    mixed = (OWN_SHARE * own + PARTNER_SHARE * other).reshape(rows, cells, TILE)
    g1[...] = rounded(mixed * sl1[...])
    edge_rows(g1, g1_near, g1_far, H_G1)
    terms[0] = kernel_terms(xv_own[...], g1[...], rw)
    terms[1] = kernel_terms(xb_own[...], xg2[0, H_G2 : H_G2 + rows, :, :TILE], rw)


def last_body(pairs, tiles, near, g1, far, t_ref, gv, scratch, xg1):
    rows, height, _ = gv.shape
    cells = pairs * tiles
    grow = functools.partial(expand, pairs=pairs, tiles=tiles, masks=edge_masks(tiles))
    widen(near, g1, far, (), H_G1, xg1, (), grow)
    for start, count in chunks_of(rows):
        back = conv_rows(xg1, (), start, count, t_ref, 0).reshape(count, cells, TILE)
        for d in range(count):
            for h in range(height):
                row, side = h // 2 * tiles, slice(h % 2 * LANES, (h % 2 + 1) * LANES)
                scratch[start + d, pl.ds(h, tiles, stride=height), :] = back[
                    d, row : row + tiles, side
                ]
            for t in range(tiles):
                gv[start + d, :, t * LANES : (t + 1) * LANES] = scratch[
                    start + d, t * height : (t + 1) * height, :
                ].astype(jnp.bfloat16)


def add_body(one, two, *refs):
    *three, out = refs
    add = lambda a, b: (a.astype(jnp.float32) + b.astype(jnp.float32)).astype(out.dtype)
    for layer in range(one.shape[0]):
        out[layer] = add(one[layer], two[layer])
    if three:
        out[one.shape[0]] = add(three[0][...], three[1][...])


def swapped(values, hop):
    count = lax.axis_size("depth")
    return lax.ppermute(values, "depth", [(i, i ^ hop) for i in range(count)])


def neighbours(near, far):
    count = lax.axis_size("depth")
    result = []
    for values, first in ((near, 0), (far, 1)):
        partner = {}
        for i in range(first, count - 1, 2):
            partner[i], partner[i + 1] = i + 1, i
        pairs = [(i, partner.get(i, i)) for i in range(count)]
        result.append(lax.ppermute(values, "depth", pairs))
    return result


def over_sample(values, hop):
    groups = lax.axis_size("sample")
    return lax.ppermute(values, "sample", [(i, i ^ hop) for i in range(groups)])


def even_hops(values):
    return [over_sample(values, hop) for hop in range(2, lax.axis_size("sample"), 2)]


def all_hops(odd, evens):
    return [odd, *(crop for even in evens for crop in (even, over_sample(even, 1)))]


def traded(volume, cotangent, partner, tiles):
    groups = lax.axis_size("sample")
    rows, height, _ = volume.shape
    split = jnp.stack([volume, cotangent]).reshape(2, rows, height // 2, 2, tiles, LANES)
    split = split.transpose(0, 1, 2, 4, 3, 5).reshape(2, groups, -1, TILE)
    pieces = split.swapaxes(0, 1)
    spread = lax.all_to_all(pieces, "sample", split_axis=0, concat_axis=0, tiled=True)
    ids = jnp.arange(groups, dtype=jnp.int32)
    inverse = jnp.sum(jnp.where(partner[:, None] == ids[None, :], ids[:, None], 0), axis=0)
    wanted = jnp.stack([2 * partner, 2 * inverse, 2 * inverse + 1], axis=1)
    chosen = jnp.take(spread.reshape(2 * groups, -1, TILE), wanted, axis=0)
    joined = lax.all_to_all(chosen, "sample", split_axis=0, concat_axis=0, tiled=True)
    others = jnp.swapaxes(joined, 0, 1).reshape(3, rows, -1, TILE)
    return others[:2], others[2:]


def call(kernel, outs, scratch, inputs, macs=0, far=()):
    vmem, smem, anywhere = (
        pl.BlockSpec(memory_space=space) for space in (pltpu.VMEM, pltpu.SMEM, pl.ANY)
    )
    specs = [
        anywhere if at in far else smem if x.dtype == jnp.int32 else vmem
        for at, x in enumerate(inputs)
    ]
    results = pl.pallas_call(
        kernel,
        out_shape=tuple(jax.ShapeDtypeStruct(shape, dtype) for shape, dtype in outs),
        in_specs=specs,
        out_specs=(vmem,) * len(outs),
        scratch_shapes=scratch,
        compiler_params=pltpu.CompilerParams(vmem_limit_bytes=VMEM_LIMIT),
        cost_estimate=pl.CostEstimate(
            flops=2 * macs, bytes_accessed=2**22 if macs else 1, transcendentals=0
        ),
    )(*inputs)
    return results if len(results) > 1 else results[0]


def per_device(volume, kernels, partner, cotangent):
    volume, cotangent = volume[0], cotangent[0]
    rows, height, lanes = volume.shape
    pairs, tiles = height // 2, lanes // LANES
    cells = pairs * tiles
    groups, count = lax.axis_size("sample"), lax.axis_size("depth")
    depth = rows * count
    layers, taps, width = kernels.shape
    bf16, f32 = jnp.bfloat16, jnp.float32
    row_macs = 3 * cells * WIDE * TILE
    packed_rows = taps * CH // CELLS
    wide = lambda *lead: pltpu.VMEM((*lead, cells, WIDE), bf16)
    field = lambda *lead: ((*lead, cells, TILE), bf16)
    raw_tiles = lambda *lead: pltpu.VMEM((*lead, height * tiles, LANES), f32)
    banded = ((layers, 3, WIDE, TILE), bf16)
    spread_taps = ((layers, taps * CH, LANES), bf16)
    rw = pltpu.VMEM((CELLS, taps * CH, LANES), f32)

    direct = groups in (2, 4, 8)
    evens = even_hops(volume) if direct else []
    both, edges = lax.optimization_barrier((jnp.stack([volume, cotangent]), volume))
    near, far = neighbours(edges, edges)
    ids = jnp.clip(partner, 0, groups - 1)
    fwd_taps, bwd_taps = call(
        functools.partial(taps_body, taps),
        [spread_taps, spread_taps],
        [pltpu.VMEM((layers, -(-taps // CELLS) * LANES, LANES), f32)],
        [kernels],
        2**28,
    )
    evens, both, ids, fwd_taps, bwd_taps, own_crop, late = lax.optimization_barrier(
        (evens, both, ids, fwd_taps, bwd_taps, volume, cotangent)
    )
    edge = ((2, H_VOL, cells, TILE), bf16)
    if direct:
        crops = all_hops(over_sample(own_crop, 1), evens)
        crops, near, far = lax.optimization_barrier((crops, near, far))
        vol, vol_near, vol_far = call(
            functools.partial(select_body, groups - 1),
            [field(2, rows), edge, edge],
            [raw_tiles(2, rows)],
            [ids, both, *crops],
        )
        sides = neighbours(vol_near, vol_far)
        later, _ = lax.optimization_barrier((late, vol_near))
        evens, vol = lax.optimization_barrier((even_hops(late), vol))
        cot_other = call(
            functools.partial(select_body, groups - 1),
            [field(1, rows)],
            [raw_tiles(1, rows)],
            [ids, both, *all_hops(over_sample(later, 1), evens)],
        )
    else:
        vol, cot_other = traded(volume, cotangent, partner, tiles)
        sides = neighbours(vol, vol)
    hid_rows = rows + 2 * H_HIDDEN
    fwd, hid_own, sl1, xv_own, cot_own = call(
        functools.partial(own_body, pairs, tiles),
        [
            banded,
            field(hid_rows),
            ((rows, cells, TILE), f32),
            ((rows + 2, cells, WIDE), bf16),
            field(rows),
        ],
        [wide(rows + 2 * H_VOL), pltpu.VMEM((3, rows, cells, TILE), bf16), raw_tiles(4 * rows)],
        [fwd_taps, near, both, far],
        hid_rows * row_macs,
    )

    g3, g3_near, g3_far, sl2, xb_own, xs_own = call(
        functools.partial(forward_body, depth, pairs, tiles),
        [
            field(2, rows),
            field(2, H_G3),
            field(2, H_G3),
            ((2, rows + 2 * H_TWO, cells, TILE), f32),
            ((rows + 2, cells, WIDE), bf16),
            ((rows + 2, cells, WIDE), bf16),
        ],
        [
            wide(2, rows + 2 * H_VOL),
            pltpu.VMEM((2, hid_rows, cells, TILE), bf16),
            wide(2, hid_rows),
            wide(2, rows + 2),
        ],
        [sides[0], vol, sides[1], hid_own, cot_own, cot_other, fwd],
        (2 * hid_rows + 2 * (rows + 2) + 2 * rows) * row_macs,
    )

    near, far = neighbours(g3_near, g3_far)
    terms = ((packed_rows, LANES), bf16)
    bwd, three = call(
        between_body, [banded, terms], [rw], [bwd_taps, xs_own, g3], rows * row_macs
    )
    three_near = swapped(three, 1)
    edge = ((H_G1, cells, TILE), bf16)
    g1, g1_near, g1_far, others = call(
        functools.partial(back_body, depth, pairs, tiles),
        [field(rows), edge, edge, ((2, packed_rows, LANES), bf16)],
        [wide(2, rows + 2 * H_G3), wide(2, rows + 2 * H_G2), rw],
        [near, g3, far, sl1, sl2, xv_own, xb_own, bwd],
        (6 * rows + 4) * row_macs,
    )
    others, three_near = lax.optimization_barrier((others, three_near))
    every = ((layers, packed_rows, LANES), bf16)
    others_near, near, far = lax.optimization_barrier(
        (swapped(others, 1), *neighbours(g1_near, g1_far))
    )
    summed = call(add_body, [every], [], [others, others_near, three, three_near])
    grad_volume = call(
        functools.partial(last_body, pairs, tiles),
        [((rows, height, lanes), bf16)],
        [raw_tiles(rows), wide(rows + 2 * H_G1)],
        [near, g1, far, bwd],
        rows * row_macs,
    )
    hop = 2
    while hop < count:
        dtype = bf16 if 2 * hop < count else f32
        summed = call(
            add_body, [((layers, packed_rows, LANES), dtype)], [], [summed, swapped(summed, hop)]
        )
        hop *= 2
    total = summed.astype(f32)
    return (grad_volume[None], total.reshape(1, layers, taps, width))


def solution(mesh):
    in_specs = (P("sample", "depth", None, None), P(), P(), P("sample", "depth", None, None))
    out_specs = (P("sample", "depth", None, None), P("sample", None, None, None))
    return jax.shard_map(
        per_device, mesh=mesh, in_specs=in_specs, out_specs=out_specs, check_vma=False
    )
```

```python
import functools

import jax
import jax.numpy as jnp
from jax import lax
from jax.experimental import pallas as pl
from jax.experimental.pallas import tpu as pltpu
from jax.sharding import PartitionSpec as P

CH = 32
OWN_SHARE = 0.6
PARTNER_SHARE = 0.4
LANES = 128
CELLS = LANES // CH
TILE = 2 * LANES
WIDE = 3 * TILE
VMEM_LIMIT = 40 * 2**20
FORWARD_ROWS, BACKWARD_ROWS = 2, 6

SLOTS = (
    [(1 + h, 1 + w) for h in range(2) for w in range(CELLS)]
    + [(0, 1 + w) for w in range(CELLS)]
    + [(3, 1 + w) for w in range(CELLS)]
    + [(1, 5), (0, 0), (0, 5), (1, 0)]
    + [(2, 5), (3, 0), (3, 5), (2, 0)]
)
SLOT_OF = {cell: at for at, cell in enumerate(SLOTS)}

H_VOL, H_HIDDEN, H_TWO, H_G3, H_G2, H_G1 = 3, 2, 1, 2, 1, 1


def chunks_of(rows, most):
    count = -(-rows // most)
    base, extra = divmod(rows, count)
    start, result = 0, []
    for index in range(count):
        size = base + (index < extra)
        result.append((start, size))
        start += size
    return result


def sigmoid(v):
    return 0.5 + 0.5 * jnp.tanh(0.5 * v)


def lanes_of(t):
    return slice(t * LANES, (t + 1) * LANES)


def taps_body(taps, kr_ref, fwd_ref, bwd_ref, scratch):
    layers, rows = kr_ref.shape[:2]
    part = scratch.shape[1] // CELLS // CH
    shape = (LANES, CELLS * LANES)
    lane = lax.broadcasted_iota(jnp.int32, shape, 1)
    chosen = lax.broadcasted_iota(jnp.int32, shape, 0) == lane // LANES * CH + lane % CH
    spread = jnp.where(chosen, 1.0, 0.0).astype(jnp.bfloat16)
    for layer in range(layers):
        groups = jnp.dot(kr_ref[layer], spread, preferred_element_type=jnp.float32)
        for q in range(CELLS):
            scratch[layer, pl.ds(q, rows, stride=CELLS), :] = groups[:, lanes_of(q)]
        scratch[layer, taps * CH :, :] = jnp.zeros_like(scratch[layer, taps * CH :, :])
        fwd_ref[layer] = scratch[layer, : taps * CH].astype(jnp.bfloat16)
        cell = lax.broadcasted_iota(jnp.int32, (part * CH, LANES), 1) // CH
        compact = jnp.zeros((part * CH, LANES), jnp.float32)
        for group in range(CELLS):
            at = group * part * CH
            compact = jnp.where(cell == group, scratch[layer, at : at + part * CH, :], compact)
        room = -(-part // CELLS) * LANES - part * CH
        turned = jnp.concatenate([compact, jnp.zeros((room, LANES), jnp.float32)], 0).T
        stacked = jnp.concatenate(
            [turned[:, lanes_of(t)] for t in range(turned.shape[1] // LANES)], 0
        ).astype(jnp.bfloat16)
        groups = jnp.dot(stacked, spread, preferred_element_type=jnp.float32)
        for tap in range(taps):
            group, index = divmod(tap, part)
            at, row = taps - 1 - tap, index // CELLS * LANES + group * CH
            bwd_ref[layer, at * CH : (at + 1) * CH, :] = groups[
                row : row + CH, lanes_of(index % CELLS)
            ].astype(jnp.bfloat16)


def fill_weights(taps_ref, t_ref):
    cell = lax.broadcasted_iota(jnp.int32, (CH, LANES), 1) // CH
    zero = jnp.zeros((CH, LANES), jnp.bfloat16)
    for layer in range(t_ref.shape[0]):
        for a in range(3):
            bands = {}
            for b in range(3):
                first = (a * 9 + b * 3) * CH
                values = [taps_ref[layer, first + c * CH : first + (c + 1) * CH, :] for c in range(3)]
                for ww in range(CELLS + 2):
                    band = zero
                    for c in range(3):
                        if 0 <= ww - c < CELLS:
                            band = jnp.where(cell == ww - c, values[c], band)
                    bands[b, ww] = band
            for at, (hh, ww) in enumerate(SLOTS):
                for h in range(2):
                    t_ref[
                        layer, a, at * CH : (at + 1) * CH, h * LANES : (h + 1) * LANES
                    ] = bands.get((hh - h, ww), zero)


def edge_masks(tiles):
    shape = (1, tiles, TILE)
    cell = lax.broadcasted_iota(jnp.int32, shape, 2) % LANES // CH
    row = lax.broadcasted_iota(jnp.int32, shape, 1)
    from_before = (cell == CELLS - 1) & (row > 0)
    from_after = (cell == 0) & (row < tiles - 1)
    return tuple(
        jnp.where(mask, 1.0, 0.0).astype(jnp.bfloat16) for mask in (from_before, from_after)
    )


def expand(x, out_ref, lead, pairs, tiles, masks):
    x = x.reshape(pairs, tiles, TILE)
    edge = pltpu.roll(x, 1, 1) * masks[0] + pltpu.roll(x, tiles - 1, 1) * masks[1]
    e0, e1 = edge[..., :LANES], edge[..., LANES:]
    r0, r1 = pltpu.roll(e0, LANES // 2, 2), pltpu.roll(e1, LANES // 2, 2)
    zero = jnp.zeros((1, tiles, LANES), x.dtype)
    low = jnp.concatenate([zero, x[:-1, :, LANES:]], 0)
    high = jnp.concatenate([x[1:, :, :LANES], zero], 0)
    e0 = e0 + jnp.concatenate([zero, r1[:-1]], 0)
    e1 = e1 + jnp.concatenate([r0[1:], zero], 0)
    flat = lambda v: v.reshape(pairs * tiles, v.shape[-1])
    out_ref[(*lead, slice(None), slice(0, TILE))] = flat(x)
    out_ref[(*lead, slice(None), slice(TILE, TILE + LANES))] = flat(low)
    out_ref[(*lead, slice(None), slice(TILE + LANES, 2 * TILE))] = flat(high)
    out_ref[(*lead, slice(None), slice(2 * TILE, 2 * TILE + LANES))] = flat(e0)
    out_ref[(*lead, slice(None), slice(2 * TILE + LANES, WIDE))] = flat(e1)


def conv_rows(x_ref, lead, start, rows, t_ref, layer):
    blocks = [x_ref[(*lead, pl.ds(start + a, rows))].reshape(-1, WIDE) for a in range(3)]
    return jnp.dot(
        jnp.concatenate(blocks, axis=1),
        t_ref[layer].reshape(3 * WIDE, TILE),
        preferred_element_type=jnp.float32,
    )


def slope_of(pre, gate):
    return gate * (1.0 + pre * (1.0 - gate))


def rounded(v):
    return v.astype(jnp.bfloat16)


def inside(v, row, depth):
    return jnp.where((row >= 0) & (row < depth), v, 0.0)


def either(flag, a, b):
    low = lambda *at: jnp.where(flag, a[at], b[at])
    high = lambda *at: jnp.where(flag, b[at], a[at])
    return low, high


def widen(near, own, far, lead, halo, x_ref, x_lead, grow):
    at, last = lax.axis_index("depth"), lax.axis_size("depth") - 1
    low, high = either(at % 2 == 1, near, far)
    held, rows = near.shape[len(lead)], own.shape[len(lead)]
    for d in range(halo):
        row = low(*lead, held - halo + d)
        if d == halo - 1:
            row = jnp.where(at > 0, row, jnp.zeros_like(row))
        grow(row, x_ref, (*x_lead, d))
    for d in range(rows):
        grow(own[(*lead, d)], x_ref, (*x_lead, halo + d))
    for d in range(halo):
        row = high(*lead, d)
        if d == 0:
            row = jnp.where(at < last, row, jnp.zeros_like(row))
        grow(row, x_ref, (*x_lead, halo + rows + d))


def edge_rows(values, near, far, halo):
    odd = lax.axis_index("depth") % 2 == 1
    rows = values.shape[0]
    for d in range(halo):
        up, down = values[rows - halo + d], values[d]
        near[d] = jnp.where(odd, down, up)
        far[d] = jnp.where(odd, up, down)


def layer_one(xv, lead, out_ref, t_ref, slopes_ref=None):
    rows, cells = out_ref.shape[len(lead)], out_ref.shape[-2]
    for start, count in chunks_of(rows, FORWARD_ROWS):
        pre = conv_rows(xv, lead, start, count, t_ref, 0)
        gate = sigmoid(pre)
        value = (pre * gate).astype(jnp.bfloat16).reshape(count, cells, TILE)
        out_ref[(*lead, pl.ds(start, count))] = value
        if slopes_ref is not None:
            slope = slope_of(pre, gate).reshape(count, cells, TILE)
            for d in range(count):
                to = start + d - H_HIDDEN
                if 0 <= to < slopes_ref.shape[0]:
                    slopes_ref[to] = slope[d]


def tiled_rows(load, height, tiles, scratch, at):
    for t in range(tiles):
        scratch[at, t * height : (t + 1) * height, :] = load(t).astype(jnp.float32)
    for h in range(height):
        piece = scratch[at, pl.ds(h, tiles, stride=height), :].astype(jnp.bfloat16)
        yield h // 2 * tiles, slice(h % 2 * LANES, (h % 2 + 1) * LANES), piece


def select_body(hops, partner, both, *refs):
    crops, out, sides, scratch = refs[:hops], refs[hops], refs[hops + 1 : -1], refs[-1]
    own = lax.axis_index("sample")
    inverse = jnp.int32(0)
    for crop in range(partner.shape[0]):
        inverse = jnp.where(partner[crop] == own, crop, inverse)
    wanted = (partner[own], inverse)[2 - out.shape[0] :]
    _, rows, height, lanes = both.shape
    tiles = lanes // LANES
    mine = both.at[2 - out.shape[0]]
    for to, crop in enumerate(wanted):
        for hop, source in enumerate((mine, *crops)):

            @pl.when(crop ^ own == hop)
            def _(to=to, source=source):
                for d in range(rows):
                    for t in range(tiles):
                        scratch[to, d, t * height : (t + 1) * height, :] = source[
                            d, :, lanes_of(t)
                        ].astype(jnp.float32)

        for d in range(rows):
            for h in range(height):
                piece = scratch[to, d, pl.ds(h, tiles, stride=height), :].astype(jnp.bfloat16)
                row, side = h // 2 * tiles, lanes_of(h % 2)
                out[to, d, row : row + tiles, side] = piece
        if sides:
            edge_rows(out.at[to], *(side.at[to] for side in sides), H_VOL)


def own_body(
    pairs, tiles,
    taps_ref, near, both, far,
    t_ref, hid, sl1, xv_own, cot_own,
    xv, field, scratch,
):
    _, rows, height, _ = both.shape
    fill_weights(taps_ref, t_ref)
    grow = functools.partial(expand, pairs=pairs, tiles=tiles, masks=edge_masks(tiles))
    for at, part in enumerate((near, both.at[0], far, both.at[1])):
        for d in range(rows):
            load = lambda t, part=part, d=d: part[d, :, lanes_of(t)]
            for row, side, piece in tiled_rows(load, height, tiles, scratch, at * rows + d):
                if at < 3:
                    field[at, d, row : row + tiles, side] = piece
                else:
                    cot_own[d, row : row + tiles, side] = piece
    widen(field.at[0], field.at[1], field.at[2], (), H_VOL, xv, (), grow)
    layer_one(xv, (), hid, t_ref, sl1)
    xv_own[...] = xv[H_VOL - 1 : H_VOL + rows + 1]


def forward_body(
    depth, pairs, tiles,
    near, mid, far, hid_own, cot_own, cot_other, t_ref,
    g3, g3_near, g3_far, sl2, xb_own, xs_own,
    xv, hid, xb, xs,
):
    rows = mid.shape[1]
    cells = pairs * tiles
    first = lax.axis_index("depth") * rows
    grow = functools.partial(expand, pairs=pairs, tiles=tiles, masks=edge_masks(tiles))

    for crop in range(2):
        widen(near, mid, far, (crop,), H_VOL, xv, (crop,), grow)
        layer_one(xv, (crop,), hid, t_ref)

    for d in range(rows + 2 * H_HIDDEN):
        own = hid_own[d].astype(jnp.float32)
        partner, other = hid[0, d].astype(jnp.float32), hid[1, d].astype(jnp.float32)
        row = first + d - H_HIDDEN
        for j, (a, b) in enumerate(((own, partner), (other, own))):
            mixed = OWN_SHARE * a + PARTNER_SHARE * b
            grow(rounded(inside(mixed, row, depth)), xb, (j, d))

    def middle(j, cot):
        for start, count in chunks_of(rows + 2 * H_TWO, FORWARD_ROWS):
            pre = conv_rows(xb, (j,), start, count, t_ref, 1)
            gate = sigmoid(pre)
            value = (pre * gate).reshape(count, cells, TILE)
            slope = slope_of(pre, gate).reshape(count, cells, TILE)
            for d in range(count):
                sl2[j, start + d] = slope[d]
                to = start + d - (H_TWO - 1)
                if 0 <= to < rows + 2:
                    grow(rounded(inside(value[d], first + to - 1, depth)), xs, (j, to))
        for start, count in chunks_of(rows, FORWARD_ROWS):
            pre = conv_rows(xs, (j,), start, count, t_ref, 2)
            slope = slope_of(pre, sigmoid(pre)).reshape(count, cells, TILE)
            for d in range(count):
                at = start + d
                grad = rounded(cot[at].astype(jnp.float32) * slope[d])
                g3[j, at] = grad

    middle(0, cot_own)
    middle(1, cot_other.at[0])
    for j in range(2):
        edge_rows(g3.at[j], g3_near.at[j], g3_far.at[j], H_G3)
    xb_own[...] = xb[0, H_HIDDEN - 1 : H_HIDDEN + rows + 1]
    xs_own[...] = xs[0]


def kernel_terms(values, gradient, rw):
    rows = gradient.shape[0]
    gradient = gradient.reshape(-1, TILE)
    for a in range(3):
        block = values[a : a + rows].reshape(-1, WIDE)
        terms = lax.dot_general(
            block, gradient, (((0,), (0,)), ((), ())), preferred_element_type=jnp.float32
        )
        for b in range(3):
            for c in range(3):
                at = (a * 9 + b * 3 + c) * CH
                for w in range(CELLS):
                    s0, s1 = SLOT_OF[b, w + c] * CH, SLOT_OF[b + 1, w + c] * CH
                    rw[w, at : at + CH] = (
                        terms[s0 : s0 + CH, :LANES] + terms[s1 : s1 + CH, LANES:]
                    )
    count = rw.shape[1] // CELLS
    cell = lax.broadcasted_iota(jnp.int32, (count, LANES), 1) // CH
    dense = jnp.zeros((count, LANES), jnp.float32)
    for q in range(CELLS):
        part = None
        for w in range(CELLS):
            piece = rw[w, pl.ds(q, count, stride=CELLS), :]
            if q != w:
                piece = pltpu.roll(piece, (q - w) % CELLS * CH, 1)
            part = piece if part is None else part + piece
        dense = jnp.where(cell == q, part, dense)
    return dense.astype(jnp.bfloat16)


def between_body(taps_ref, xs_own, g3, t_ref, terms, rw):
    fill_weights(taps_ref, t_ref)
    terms[...] = kernel_terms(xs_own[...], g3[0], rw)


def back_two(j, x_ref, sl2, x2_ref, t_ref, first, depth, grow):
    rows, cells = x2_ref.shape[-3:-1]
    for start, count in chunks_of(rows, BACKWARD_ROWS):
        back = conv_rows(x_ref, (), start, count, t_ref, 2).reshape(count, cells, TILE)
        for d in range(count):
            at = start + d
            grad = inside(back[d] * sl2[j, at], first + at - H_G2, depth)
            grow(rounded(grad), x2_ref, (at,))


def put_row(message, row):
    half = row.shape[0]
    message[message.shape[0] - 2 * half : message.shape[0] - half] = row[:, :LANES]
    message[message.shape[0] - half :] = row[:, LANES:]


def back_body(
    depth, pairs, tiles,
    near, mid, far, sl1, sl2, xv_own, xb_own, t_ref,
    g1, g1_far, message,
    xg3, xg2, rw, g1_near, terms,
):
    rows = mid.shape[1]
    cells = pairs * tiles
    first = lax.axis_index("depth") * rows
    grow = functools.partial(expand, pairs=pairs, tiles=tiles, masks=edge_masks(tiles))
    for j in range(2):
        widen(near, mid, far, (j,), H_G3, xg3.at[j], (), grow)
        back_two(j, xg3.at[j], sl2, xg2.at[j], t_ref, first, depth, grow)
    own, other = (
        rounded(conv_rows(xg2, (j,), 0, rows, t_ref, 1)).astype(jnp.float32) for j in range(2)
    )
    mixed = (OWN_SHARE * own + PARTNER_SHARE * other).reshape(rows, cells, TILE)
    g1[...] = rounded(mixed * sl1[...])
    edge_rows(g1, g1_near, g1_far, H_G1)
    size = terms.shape[0] // 2
    terms[:size] = kernel_terms(xv_own[...], g1[...], rw).astype(jnp.float32)
    two = kernel_terms(xb_own[...], xg2[0, H_G2 : H_G2 + rows, :, :TILE], rw)
    terms[size:] = two.astype(jnp.float32)
    message[: 2 * size] = terms[...].astype(jnp.bfloat16)
    put_row(message, g1_near[0])


def last_body(pairs, tiles, near, g1, far, t_ref, gv, scratch, xg1, sides):
    rows, height, _ = gv.shape
    cells = pairs * tiles
    grow = functools.partial(expand, pairs=pairs, tiles=tiles, masks=edge_masks(tiles))
    for at, message in enumerate((near, far)):
        first = message.shape[0] - 2 * cells
        sides[at, 0, :, :LANES] = message[first : first + cells]
        sides[at, 0, :, LANES:] = message[first + cells :]
    widen(sides.at[0], g1, sides.at[1], (), H_G1, xg1, (), grow)
    for start, count in chunks_of(rows, BACKWARD_ROWS):
        back = conv_rows(xg1, (), start, count, t_ref, 0).reshape(count, cells, TILE)
        for d in range(count):
            for h in range(height):
                row, side = h // 2 * tiles, slice(h % 2 * LANES, (h % 2 + 1) * LANES)
                scratch[start + d, pl.ds(h, tiles, stride=height), :] = back[
                    d, row : row + tiles, side
                ]
            for t in range(tiles):
                gv[start + d, :, t * LANES : (t + 1) * LANES] = scratch[
                    start + d, t * height : (t + 1) * height, :
                ].astype(jnp.bfloat16)


def add_body(own, near, three, three_near, g1_far, message, terms):
    add = lambda a, b: a.astype(jnp.float32) + b.astype(jnp.float32)
    size = three.shape[0]
    terms[: 2 * size] = add(own[: 2 * size], near[: 2 * size])
    terms[2 * size : 3 * size] = add(three[...], three_near[...])
    terms[3 * size :] = jnp.zeros_like(terms[3 * size :])
    message[: terms.shape[0]] = terms[...].astype(jnp.bfloat16)
    put_row(message, g1_far[0])


def total_body(one, two, out):
    rows = -(-out.shape[0] // 16) * 16
    total = one[:rows].astype(jnp.float32) + two[:rows].astype(jnp.float32)
    out[...] = total[: out.shape[0]].astype(out.dtype)


def swapped(values, hop):
    count = lax.axis_size("depth")
    return lax.ppermute(values, "depth", [(i, i ^ hop) for i in range(count)])


def neighbours(near, far):
    count = lax.axis_size("depth")
    result = []
    for values, first in ((near, 0), (far, 1)):
        partner = {}
        for i in range(first, count - 1, 2):
            partner[i], partner[i + 1] = i + 1, i
        pairs = [(i, partner.get(i, i)) for i in range(count)]
        result.append(lax.ppermute(values, "depth", pairs))
    return result


def over_sample(values, hop):
    groups = lax.axis_size("sample")
    return lax.ppermute(values, "sample", [(i, i ^ hop) for i in range(groups)])


def even_hops(values):
    return [over_sample(values, hop) for hop in range(2, lax.axis_size("sample"), 2)]


def all_hops(odd, evens):
    return [odd, *(crop for even in evens for crop in (even, over_sample(even, 1)))]


def traded(volume, cotangent, partner, tiles):
    groups = lax.axis_size("sample")
    rows, height, _ = volume.shape
    split = jnp.stack([volume, cotangent]).reshape(2, rows, height // 2, 2, tiles, LANES)
    split = split.transpose(0, 1, 2, 4, 3, 5).reshape(2, groups, -1, TILE)
    pieces = split.swapaxes(0, 1)
    spread = lax.all_to_all(pieces, "sample", split_axis=0, concat_axis=0, tiled=True)
    ids = jnp.arange(groups, dtype=jnp.int32)
    inverse = jnp.sum(jnp.where(partner[:, None] == ids[None, :], ids[:, None], 0), axis=0)
    wanted = jnp.stack([2 * partner, 2 * inverse, 2 * inverse + 1], axis=1)
    chosen = jnp.take(spread.reshape(2 * groups, -1, TILE), wanted, axis=0)
    joined = lax.all_to_all(chosen, "sample", split_axis=0, concat_axis=0, tiled=True)
    others = jnp.swapaxes(joined, 0, 1).reshape(3, rows, -1, TILE)
    return others[:2], others[2:]


def call(kernel, outs, scratch, inputs, macs=0, far=()):
    vmem, smem, anywhere = (
        pl.BlockSpec(memory_space=space) for space in (pltpu.VMEM, pltpu.SMEM, pl.ANY)
    )
    specs = [
        anywhere if at in far else smem if x.dtype == jnp.int32 else vmem
        for at, x in enumerate(inputs)
    ]
    results = pl.pallas_call(
        kernel,
        out_shape=tuple(jax.ShapeDtypeStruct(shape, dtype) for shape, dtype in outs),
        in_specs=specs,
        out_specs=(vmem,) * len(outs),
        scratch_shapes=scratch,
        compiler_params=pltpu.CompilerParams(vmem_limit_bytes=VMEM_LIMIT),
        cost_estimate=pl.CostEstimate(
            flops=2 * macs, bytes_accessed=2**22 if macs else 1, transcendentals=0
        ),
    )(*inputs)
    return results if len(results) > 1 else results[0]


def per_device(volume, kernels, partner, cotangent):
    volume, cotangent = volume[0], cotangent[0]
    rows, height, lanes = volume.shape
    pairs, tiles = height // 2, lanes // LANES
    cells = pairs * tiles
    groups, count = lax.axis_size("sample"), lax.axis_size("depth")
    depth = rows * count
    layers, taps, width = kernels.shape
    bf16, f32 = jnp.bfloat16, jnp.float32
    row_macs = 3 * cells * WIDE * TILE
    packed_rows = taps * CH // CELLS
    wide = lambda *lead: pltpu.VMEM((*lead, cells, WIDE), bf16)
    field = lambda *lead: ((*lead, cells, TILE), bf16)
    raw_tiles = lambda *lead: pltpu.VMEM((*lead, height * tiles, LANES), f32)
    banded = ((layers, 3, WIDE, TILE), bf16)
    spread_taps = ((layers, taps * CH, LANES), bf16)
    rw = pltpu.VMEM((CELLS, taps * CH, LANES), f32)

    direct = groups in (2, 4, 8)
    evens = even_hops(volume) if direct else []
    both, edges = lax.optimization_barrier((jnp.stack([volume, cotangent]), volume))
    near, far = neighbours(edges, edges)
    packed = kernels.reshape(layers, packed_rows, LANES)
    ids = jnp.clip(partner, 0, groups - 1)
    fwd_taps, bwd_taps = call(
        functools.partial(taps_body, taps),
        [spread_taps, spread_taps],
        [pltpu.VMEM((layers, -(-taps // CELLS) * LANES, LANES), f32)],
        [packed],
        2**28,
    )
    evens, both, ids, fwd_taps, bwd_taps, own_crop, late = lax.optimization_barrier(
        (evens, both, ids, fwd_taps, bwd_taps, volume, cotangent)
    )
    edge = ((2, H_VOL, cells, TILE), bf16)
    if direct:
        crops = all_hops(over_sample(own_crop, 1), evens)
        crops, near, far = lax.optimization_barrier((crops, near, far))
        vol, vol_near, vol_far = call(
            functools.partial(select_body, groups - 1),
            [field(2, rows), edge, edge],
            [raw_tiles(2, rows)],
            [ids, both, *crops],
        )
        sides = neighbours(vol_near, vol_far)
        later, _ = lax.optimization_barrier((late, vol_near))
        evens, vol = lax.optimization_barrier((even_hops(late), vol))
        cot_other = call(
            functools.partial(select_body, groups - 1),
            [field(1, rows)],
            [raw_tiles(1, rows)],
            [ids, both, *all_hops(over_sample(later, 1), evens)],
        )
    else:
        vol, cot_other = traded(volume, cotangent, partner, tiles)
        sides = neighbours(vol, vol)
    hid_rows = rows + 2 * H_HIDDEN
    fwd, hid_own, sl1, xv_own, cot_own = call(
        functools.partial(own_body, pairs, tiles),
        [
            banded,
            field(hid_rows),
            ((rows, cells, TILE), f32),
            ((rows + 2, cells, WIDE), bf16),
            field(rows),
        ],
        [wide(rows + 2 * H_VOL), pltpu.VMEM((3, rows, cells, TILE), bf16), raw_tiles(4 * rows)],
        [fwd_taps, near, both, far],
        hid_rows * row_macs,
    )

    g3, g3_near, g3_far, sl2, xb_own, xs_own = call(
        functools.partial(forward_body, depth, pairs, tiles),
        [
            field(2, rows),
            field(2, H_G3),
            field(2, H_G3),
            ((2, rows + 2 * H_TWO, cells, TILE), f32),
            ((rows + 2, cells, WIDE), bf16),
            ((rows + 2, cells, WIDE), bf16),
        ],
        [
            wide(2, rows + 2 * H_VOL),
            pltpu.VMEM((2, hid_rows, cells, TILE), bf16),
            wide(2, hid_rows),
            wide(2, rows + 2),
        ],
        [sides[0], vol, sides[1], hid_own, cot_own, cot_other, fwd],
        (2 * hid_rows + 2 * (rows + 2) + 2 * rows) * row_macs,
    )

    near, far = neighbours(g3_near, g3_far)
    terms = ((packed_rows, LANES), bf16)
    bwd, three = call(
        between_body, [banded, terms], [rw], [bwd_taps, xs_own, g3], rows * row_macs
    )
    three_near = swapped(three, 1)
    short, long = 2 * packed_rows, -(-layers * packed_rows // 16) * 16
    message = lambda lines: ((lines + 2 * cells, LANES), bf16)
    g1, g1_far, own = call(
        functools.partial(back_body, depth, pairs, tiles),
        [field(rows), ((H_G1, cells, TILE), bf16), message(short)],
        [
            wide(2, rows + 2 * H_G3),
            wide(2, rows + 2 * H_G2),
            rw,
            pltpu.VMEM((H_G1, cells, TILE), bf16),
            pltpu.VMEM((short, LANES), f32),
        ],
        [near, g3, far, sl1, sl2, xv_own, xb_own, bwd],
        (6 * rows + 4) * row_macs,
    )
    own, three_near = lax.optimization_barrier((own, three_near))
    near = swapped(own, 1)
    summed = call(
        add_body,
        [message(long)],
        [pltpu.VMEM((long, LANES), f32)],
        [own, near, three, three_near, g1_far],
    )
    if count == 4:
        hops, far = [3], swapped(summed, 3)
        others = [far]
    else:
        hops, others = [2**i for i in range(1, count.bit_length() - 1)], []
        far = neighbours(summed, summed)[1]
    every = (layers * packed_rows, LANES)
    for at, hop in enumerate(hops):
        dtype = f32 if at == len(hops) - 1 else bf16
        part = others[at] if at < len(others) else swapped(summed, hop)
        summed = call(total_body, [(every, dtype)], [], [summed, part])
    grad_volume = call(
        functools.partial(last_body, pairs, tiles),
        [((rows, height, lanes), bf16)],
        [raw_tiles(rows), wide(rows + 2 * H_G1), pltpu.VMEM((2, H_G1, cells, TILE), bf16)],
        [near, g1, far, bwd],
        rows * row_macs,
    )
    total = summed[: layers * packed_rows].astype(f32)
    return (grad_volume[None], total.reshape(1, layers, taps, width))


def solution(mesh):
    in_specs = (P("sample", "depth", None, None), P(), P(), P("sample", "depth", None, None))
    out_specs = (P("sample", "depth", None, None), P("sample", None, None, None))
    return jax.shard_map(
        per_device, mesh=mesh, in_specs=in_specs, out_specs=out_specs, check_vma=False
    )
```

```python
import functools

import jax
import jax.numpy as jnp
from jax import lax
from jax.experimental import pallas as pl
from jax.experimental.pallas import tpu as pltpu
from jax.sharding import PartitionSpec as P

CH = 32
OWN_SHARE = 0.6
PARTNER_SHARE = 0.4
LANES = 128
CELLS = LANES // CH
TILE = 2 * LANES
WIDE = 3 * TILE
VMEM_LIMIT = 40 * 2**20
FORWARD_ROWS, BACKWARD_ROWS = 2, 6

SLOTS = (
    [(1 + h, 1 + w) for h in range(2) for w in range(CELLS)]
    + [(0, 1 + w) for w in range(CELLS)]
    + [(3, 1 + w) for w in range(CELLS)]
    + [(1, 5), (0, 0), (0, 5), (1, 0)]
    + [(2, 5), (3, 0), (3, 5), (2, 0)]
)
SLOT_OF = {cell: at for at, cell in enumerate(SLOTS)}

H_VOL, H_HIDDEN, H_TWO, H_G3, H_G2, H_G1 = 3, 2, 1, 2, 1, 1


def chunks_of(rows, most):
    count = -(-rows // most)
    base, extra = divmod(rows, count)
    start, result = 0, []
    for index in range(count):
        size = base + (index < extra)
        result.append((start, size))
        start += size
    return result


def sigmoid(v):
    return 0.5 + 0.5 * jnp.tanh(0.5 * v)


def lanes_of(t):
    return slice(t * LANES, (t + 1) * LANES)


def taps_body(taps, kr_ref, fwd_ref, bwd_ref, scratch):
    layers, rows = kr_ref.shape[:2]
    part = scratch.shape[1] // CELLS // CH
    shape = (LANES, CELLS * LANES)
    lane = lax.broadcasted_iota(jnp.int32, shape, 1)
    chosen = lax.broadcasted_iota(jnp.int32, shape, 0) == lane // LANES * CH + lane % CH
    spread = jnp.where(chosen, 1.0, 0.0).astype(jnp.bfloat16)
    for layer in range(layers):
        groups = jnp.dot(kr_ref[layer], spread, preferred_element_type=jnp.float32)
        for q in range(CELLS):
            scratch[layer, pl.ds(q, rows, stride=CELLS), :] = groups[:, lanes_of(q)]
        scratch[layer, taps * CH :, :] = jnp.zeros_like(scratch[layer, taps * CH :, :])
        fwd_ref[layer] = scratch[layer, : taps * CH].astype(jnp.bfloat16)
        cell = lax.broadcasted_iota(jnp.int32, (part * CH, LANES), 1) // CH
        compact = jnp.zeros((part * CH, LANES), jnp.float32)
        for group in range(CELLS):
            at = group * part * CH
            compact = jnp.where(cell == group, scratch[layer, at : at + part * CH, :], compact)
        room = -(-part // CELLS) * LANES - part * CH
        turned = jnp.concatenate([compact, jnp.zeros((room, LANES), jnp.float32)], 0).T
        stacked = jnp.concatenate(
            [turned[:, lanes_of(t)] for t in range(turned.shape[1] // LANES)], 0
        ).astype(jnp.bfloat16)
        groups = jnp.dot(stacked, spread, preferred_element_type=jnp.float32)
        for tap in range(taps):
            group, index = divmod(tap, part)
            at, row = taps - 1 - tap, index // CELLS * LANES + group * CH
            bwd_ref[layer, at * CH : (at + 1) * CH, :] = groups[
                row : row + CH, lanes_of(index % CELLS)
            ].astype(jnp.bfloat16)


def fill_weights(taps_ref, t_ref):
    cell = lax.broadcasted_iota(jnp.int32, (CH, LANES), 1) // CH
    zero = jnp.zeros((CH, LANES), jnp.bfloat16)
    for layer in range(t_ref.shape[0]):
        for a in range(3):
            bands = {}
            for b in range(3):
                first = (a * 9 + b * 3) * CH
                values = [taps_ref[layer, first + c * CH : first + (c + 1) * CH, :] for c in range(3)]
                for ww in range(CELLS + 2):
                    band = zero
                    for c in range(3):
                        if 0 <= ww - c < CELLS:
                            band = jnp.where(cell == ww - c, values[c], band)
                    bands[b, ww] = band
            for at, (hh, ww) in enumerate(SLOTS):
                for h in range(2):
                    t_ref[
                        layer, a, at * CH : (at + 1) * CH, h * LANES : (h + 1) * LANES
                    ] = bands.get((hh - h, ww), zero)


def edge_masks(tiles):
    shape = (1, tiles, TILE)
    cell = lax.broadcasted_iota(jnp.int32, shape, 2) % LANES // CH
    row = lax.broadcasted_iota(jnp.int32, shape, 1)
    from_before = (cell == CELLS - 1) & (row > 0)
    from_after = (cell == 0) & (row < tiles - 1)
    return tuple(
        jnp.where(mask, 1.0, 0.0).astype(jnp.bfloat16) for mask in (from_before, from_after)
    )


def expand(x, out_ref, lead, pairs, tiles, masks):
    x = x.reshape(pairs, tiles, TILE)
    edge = pltpu.roll(x, 1, 1) * masks[0] + pltpu.roll(x, tiles - 1, 1) * masks[1]
    e0, e1 = edge[..., :LANES], edge[..., LANES:]
    r0, r1 = pltpu.roll(e0, LANES // 2, 2), pltpu.roll(e1, LANES // 2, 2)
    zero = jnp.zeros((1, tiles, LANES), x.dtype)
    low = jnp.concatenate([zero, x[:-1, :, LANES:]], 0)
    high = jnp.concatenate([x[1:, :, :LANES], zero], 0)
    e0 = e0 + jnp.concatenate([zero, r1[:-1]], 0)
    e1 = e1 + jnp.concatenate([r0[1:], zero], 0)
    flat = lambda v: v.reshape(pairs * tiles, v.shape[-1])
    out_ref[(*lead, slice(None), slice(0, TILE))] = flat(x)
    out_ref[(*lead, slice(None), slice(TILE, TILE + LANES))] = flat(low)
    out_ref[(*lead, slice(None), slice(TILE + LANES, 2 * TILE))] = flat(high)
    out_ref[(*lead, slice(None), slice(2 * TILE, 2 * TILE + LANES))] = flat(e0)
    out_ref[(*lead, slice(None), slice(2 * TILE + LANES, WIDE))] = flat(e1)


def conv_rows(x_ref, lead, start, rows, t_ref, layer):
    blocks = [x_ref[(*lead, pl.ds(start + a, rows))].reshape(-1, WIDE) for a in range(3)]
    return jnp.dot(
        jnp.concatenate(blocks, axis=1),
        t_ref[layer].reshape(3 * WIDE, TILE),
        preferred_element_type=jnp.float32,
    )


def slope_of(pre, gate):
    return gate * (1.0 + pre * (1.0 - gate))


def rounded(v):
    return v.astype(jnp.bfloat16)


def inside(v, row, depth):
    return jnp.where((row >= 0) & (row < depth), v, 0.0)


def either(flag, a, b):
    low = lambda *at: jnp.where(flag, a[at], b[at])
    high = lambda *at: jnp.where(flag, b[at], a[at])
    return low, high


def widen(near, own, far, lead, halo, x_ref, x_lead, grow):
    at, last = lax.axis_index("depth"), lax.axis_size("depth") - 1
    low, high = either(at % 2 == 1, near, far)
    held, rows = near.shape[len(lead)], own.shape[len(lead)]
    for d in range(halo):
        row = low(*lead, held - halo + d)
        if d == halo - 1:
            row = jnp.where(at > 0, row, jnp.zeros_like(row))
        grow(row, x_ref, (*x_lead, d))
    for d in range(rows):
        grow(own[(*lead, d)], x_ref, (*x_lead, halo + d))
    for d in range(halo):
        row = high(*lead, d)
        if d == 0:
            row = jnp.where(at < last, row, jnp.zeros_like(row))
        grow(row, x_ref, (*x_lead, halo + rows + d))


def edge_rows(values, near, far, halo):
    odd = lax.axis_index("depth") % 2 == 1
    rows = values.shape[0]
    for d in range(halo):
        up, down = values[rows - halo + d], values[d]
        near[d] = jnp.where(odd, down, up)
        far[d] = jnp.where(odd, up, down)


def layer_one(xv, lead, out_ref, t_ref, slopes_ref=None):
    rows, cells = out_ref.shape[len(lead)], out_ref.shape[-2]
    for start, count in chunks_of(rows, FORWARD_ROWS):
        pre = conv_rows(xv, lead, start, count, t_ref, 0)
        gate = sigmoid(pre)
        value = (pre * gate).astype(jnp.bfloat16).reshape(count, cells, TILE)
        out_ref[(*lead, pl.ds(start, count))] = value
        if slopes_ref is not None:
            slope = slope_of(pre, gate).reshape(count, cells, TILE)
            for d in range(count):
                to = start + d - H_HIDDEN
                if 0 <= to < slopes_ref.shape[0]:
                    slopes_ref[to] = slope[d]


def tiled_rows(load, height, tiles, scratch, at):
    for t in range(tiles):
        scratch[at, t * height : (t + 1) * height, :] = load(t).astype(jnp.float32)
    for h in range(height):
        piece = scratch[at, pl.ds(h, tiles, stride=height), :].astype(jnp.bfloat16)
        yield h // 2 * tiles, slice(h % 2 * LANES, (h % 2 + 1) * LANES), piece


def wanted_by(partner, crop, count):
    inverse = jnp.int32(0)
    for other in range(partner.shape[0]):
        inverse = jnp.where(partner[other] == crop, other, inverse)
    return (partner[crop], inverse)[2 - count :]


def pick_body(partner, both, *refs):
    *evens, out = refs
    own = lax.axis_index("sample")
    count = out.shape[0]
    for to, crop in enumerate(wanted_by(partner, own ^ 1, count)):
        for at, source in enumerate((both.at[2 - count], *evens)):

            @pl.when(crop ^ own == 2 * at)
            def _(to=to, source=source):
                out[to] = source[...]


def select_body(hops, partner, both, *refs):
    evens, sent, out, sides, scratch = (
        refs[:hops], refs[hops], refs[hops + 1], refs[hops + 2 : -1], refs[-1]
    )
    own = lax.axis_index("sample")
    _, rows, height, lanes = both.shape
    count, tiles = out.shape[0], lanes // LANES

    def spread(to, source):
        for d in range(rows):
            for t in range(tiles):
                scratch[to, d, t * height : (t + 1) * height, :] = source[
                    d, :, lanes_of(t)
                ].astype(jnp.float32)

    for to, crop in enumerate(wanted_by(partner, own, count)):
        hop = crop ^ own
        for at, source in enumerate((both.at[2 - count], *evens)):
            pl.when(hop == 2 * at)(functools.partial(spread, to, source))
        pl.when(hop % 2 == 1)(functools.partial(spread, to, sent.at[to]))
        for d in range(rows):
            for h in range(height):
                piece = scratch[to, d, pl.ds(h, tiles, stride=height), :].astype(jnp.bfloat16)
                row, side = h // 2 * tiles, lanes_of(h % 2)
                out[to, d, row : row + tiles, side] = piece
        if sides:
            edge_rows(out.at[to], *(side.at[to] for side in sides), H_VOL)


def own_body(
    pairs, tiles,
    taps_ref, near, both, far,
    t_ref, hid, sl1, xv_own, cot_own,
    xv, field, scratch,
):
    _, rows, height, _ = both.shape
    fill_weights(taps_ref, t_ref)
    grow = functools.partial(expand, pairs=pairs, tiles=tiles, masks=edge_masks(tiles))
    for at, part in enumerate((near, both.at[0], far, both.at[1])):
        for d in range(rows):
            load = lambda t, part=part, d=d: part[d, :, lanes_of(t)]
            for row, side, piece in tiled_rows(load, height, tiles, scratch, at * rows + d):
                if at < 3:
                    field[at, d, row : row + tiles, side] = piece
                else:
                    cot_own[d, row : row + tiles, side] = piece
    widen(field.at[0], field.at[1], field.at[2], (), H_VOL, xv, (), grow)
    layer_one(xv, (), hid, t_ref, sl1)
    xv_own[...] = xv[H_VOL - 1 : H_VOL + rows + 1]


def forward_body(
    depth, pairs, tiles,
    far, mid, near, hid_own, cot_own, cot_other, t_ref,
    g3, g3_near, g3_far, sl2, xb_own, xs_own,
    xv, hid, xb, xs,
):
    rows = mid.shape[1]
    cells = pairs * tiles
    first = lax.axis_index("depth") * rows
    grow = functools.partial(expand, pairs=pairs, tiles=tiles, masks=edge_masks(tiles))

    for crop in range(2):
        widen(near, mid, far, (crop,), H_VOL, xv, (crop,), grow)
        layer_one(xv, (crop,), hid, t_ref)

    for d in range(rows + 2 * H_HIDDEN):
        own = hid_own[d].astype(jnp.float32)
        partner, other = hid[0, d].astype(jnp.float32), hid[1, d].astype(jnp.float32)
        row = first + d - H_HIDDEN
        for j, (a, b) in enumerate(((own, partner), (other, own))):
            mixed = OWN_SHARE * a + PARTNER_SHARE * b
            grow(rounded(inside(mixed, row, depth)), xb, (j, d))

    def middle(j, cot):
        for start, count in chunks_of(rows + 2 * H_TWO, FORWARD_ROWS):
            pre = conv_rows(xb, (j,), start, count, t_ref, 1)
            gate = sigmoid(pre)
            value = (pre * gate).reshape(count, cells, TILE)
            slope = slope_of(pre, gate).reshape(count, cells, TILE)
            for d in range(count):
                sl2[j, start + d] = slope[d]
                to = start + d - (H_TWO - 1)
                if 0 <= to < rows + 2:
                    grow(rounded(inside(value[d], first + to - 1, depth)), xs, (j, to))
        for start, count in chunks_of(rows, FORWARD_ROWS):
            pre = conv_rows(xs, (j,), start, count, t_ref, 2)
            slope = slope_of(pre, sigmoid(pre)).reshape(count, cells, TILE)
            for d in range(count):
                at = start + d
                grad = rounded(cot[at].astype(jnp.float32) * slope[d])
                g3[j, at] = grad

    middle(0, cot_own)
    middle(1, cot_other.at[0])
    for j in range(2):
        edge_rows(g3.at[j], g3_near.at[j], g3_far.at[j], H_G3)
    xb_own[...] = xb[0, H_HIDDEN - 1 : H_HIDDEN + rows + 1]
    xs_own[...] = xs[0]


def kernel_terms(values, gradient, rw):
    rows = gradient.shape[0]
    gradient = gradient.reshape(-1, TILE)
    for a in range(3):
        block = values[a : a + rows].reshape(-1, WIDE)
        terms = lax.dot_general(
            block, gradient, (((0,), (0,)), ((), ())), preferred_element_type=jnp.float32
        )
        for b in range(3):
            for c in range(3):
                at = (a * 9 + b * 3 + c) * CH
                for w in range(CELLS):
                    s0, s1 = SLOT_OF[b, w + c] * CH, SLOT_OF[b + 1, w + c] * CH
                    rw[w, at : at + CH] = (
                        terms[s0 : s0 + CH, :LANES] + terms[s1 : s1 + CH, LANES:]
                    )
    count = rw.shape[1] // CELLS
    cell = lax.broadcasted_iota(jnp.int32, (count, LANES), 1) // CH
    dense = jnp.zeros((count, LANES), jnp.float32)
    for q in range(CELLS):
        part = None
        for w in range(CELLS):
            piece = rw[w, pl.ds(q, count, stride=CELLS), :]
            if q != w:
                piece = pltpu.roll(piece, (q - w) % CELLS * CH, 1)
            part = piece if part is None else part + piece
        dense = jnp.where(cell == q, part, dense)
    return dense.astype(jnp.bfloat16)


def between_body(taps_ref, xs_own, g3, t_ref, terms, rw):
    fill_weights(taps_ref, t_ref)
    terms[...] = kernel_terms(xs_own[...], g3[0], rw)


def back_two(j, x_ref, sl2, x2_ref, t_ref, first, depth, grow):
    rows, cells = x2_ref.shape[-3:-1]
    for start, count in chunks_of(rows, BACKWARD_ROWS):
        back = conv_rows(x_ref, (), start, count, t_ref, 2).reshape(count, cells, TILE)
        for d in range(count):
            at = start + d
            grad = inside(back[d] * sl2[j, at], first + at - H_G2, depth)
            grow(rounded(grad), x2_ref, (at,))


def put_row(message, row):
    half = row.shape[0]
    message[message.shape[0] - 2 * half : message.shape[0] - half] = row[:, :LANES]
    message[message.shape[0] - half :] = row[:, LANES:]


def back_body(
    depth, pairs, tiles,
    far, mid, near, sl1, sl2, xv_own, xb_own, t_ref,
    g1, g1_far, message,
    xg3, xg2, rw, g1_near, terms,
):
    rows = mid.shape[1]
    cells = pairs * tiles
    first = lax.axis_index("depth") * rows
    grow = functools.partial(expand, pairs=pairs, tiles=tiles, masks=edge_masks(tiles))
    for j in range(2):
        widen(near, mid, far, (j,), H_G3, xg3.at[j], (), grow)
        back_two(j, xg3.at[j], sl2, xg2.at[j], t_ref, first, depth, grow)
    own, other = (
        rounded(conv_rows(xg2, (j,), 0, rows, t_ref, 1)).astype(jnp.float32) for j in range(2)
    )
    mixed = (OWN_SHARE * own + PARTNER_SHARE * other).reshape(rows, cells, TILE)
    g1[...] = rounded(mixed * sl1[...])
    edge_rows(g1, g1_near, g1_far, H_G1)
    size = terms.shape[0] // 2
    terms[:size] = kernel_terms(xv_own[...], g1[...], rw).astype(jnp.float32)
    two = kernel_terms(xb_own[...], xg2[0, H_G2 : H_G2 + rows, :, :TILE], rw)
    terms[size:] = two.astype(jnp.float32)
    message[: 2 * size] = terms[...].astype(jnp.bfloat16)
    put_row(message, g1_near[0])


def last_body(pairs, tiles, near, g1, far, t_ref, *refs):
    *parts, gv, total, scratch, xg1, sides = refs
    lines = -(-total.shape[0] // 16) * 16
    terms = [part[:lines].astype(jnp.float32) for part in parts]
    total[...] = functools.reduce(lambda a, b: a + b, terms)[: total.shape[0]]
    rows, height, _ = gv.shape
    cells = pairs * tiles
    grow = functools.partial(expand, pairs=pairs, tiles=tiles, masks=edge_masks(tiles))
    for at, message in enumerate((near, far)):
        first = message.shape[0] - 2 * cells
        sides[at, 0, :, :LANES] = message[first : first + cells]
        sides[at, 0, :, LANES:] = message[first + cells :]
    widen(sides.at[0], g1, sides.at[1], (), H_G1, xg1, (), grow)
    for start, count in chunks_of(rows, BACKWARD_ROWS):
        back = conv_rows(xg1, (), start, count, t_ref, 0).reshape(count, cells, TILE)
        for d in range(count):
            for h in range(height):
                row, side = h // 2 * tiles, slice(h % 2 * LANES, (h % 2 + 1) * LANES)
                scratch[start + d, pl.ds(h, tiles, stride=height), :] = back[
                    d, row : row + tiles, side
                ]
            for t in range(tiles):
                gv[start + d, :, t * LANES : (t + 1) * LANES] = scratch[
                    start + d, t * height : (t + 1) * height, :
                ].astype(jnp.bfloat16)


def add_body(own, near, three, three_near, g1_far, message, terms):
    add = lambda a, b: a.astype(jnp.float32) + b.astype(jnp.float32)
    size = three.shape[0]
    terms[: 2 * size] = add(own[: 2 * size], near[: 2 * size])
    terms[2 * size : 3 * size] = add(three[...], three_near[...])
    terms[3 * size :] = jnp.zeros_like(terms[3 * size :])
    message[: terms.shape[0]] = terms[...].astype(jnp.bfloat16)
    put_row(message, g1_far[0])


def total_body(one, two, out):
    rows = -(-out.shape[0] // 16) * 16
    total = one[:rows].astype(jnp.float32) + two[:rows].astype(jnp.float32)
    out[...] = total[: out.shape[0]].astype(out.dtype)


def swapped(values, hop):
    count = lax.axis_size("depth")
    return lax.ppermute(values, "depth", [(i, i ^ hop) for i in range(count)])


def neighbours(near, far):
    count = lax.axis_size("depth")
    result = []
    for values, first in ((near, 0), (far, 1)):
        partner = {}
        for i in range(first, count - 1, 2):
            partner[i], partner[i + 1] = i + 1, i
        pairs = [(i, partner.get(i, i)) for i in range(count)]
        result.append(lax.ppermute(values, "depth", pairs))
    return result


def over_sample(values, hop):
    groups = lax.axis_size("sample")
    return lax.ppermute(values, "sample", [(i, i ^ hop) for i in range(groups)])


def even_hops(values):
    return [over_sample(values, hop) for hop in range(2, lax.axis_size("sample"), 2)]


def traded(volume, cotangent, partner, tiles):
    groups = lax.axis_size("sample")
    rows, height, _ = volume.shape
    split = jnp.stack([volume, cotangent]).reshape(2, rows, height // 2, 2, tiles, LANES)
    split = split.transpose(0, 1, 2, 4, 3, 5).reshape(2, groups, -1, TILE)
    pieces = split.swapaxes(0, 1)
    spread = lax.all_to_all(pieces, "sample", split_axis=0, concat_axis=0, tiled=True)
    ids = jnp.arange(groups, dtype=jnp.int32)
    inverse = jnp.sum(jnp.where(partner[:, None] == ids[None, :], ids[:, None], 0), axis=0)
    wanted = jnp.stack([2 * partner, 2 * inverse, 2 * inverse + 1], axis=1)
    chosen = jnp.take(spread.reshape(2 * groups, -1, TILE), wanted, axis=0)
    joined = lax.all_to_all(chosen, "sample", split_axis=0, concat_axis=0, tiled=True)
    others = jnp.swapaxes(joined, 0, 1).reshape(3, rows, -1, TILE)
    return others[:2], others[2:]


def call(kernel, outs, scratch, inputs, macs=0, far=()):
    vmem, smem, anywhere = (
        pl.BlockSpec(memory_space=space) for space in (pltpu.VMEM, pltpu.SMEM, pl.ANY)
    )
    specs = [
        anywhere if at in far else smem if x.dtype == jnp.int32 else vmem
        for at, x in enumerate(inputs)
    ]
    results = pl.pallas_call(
        kernel,
        out_shape=tuple(jax.ShapeDtypeStruct(shape, dtype) for shape, dtype in outs),
        in_specs=specs,
        out_specs=(vmem,) * len(outs),
        scratch_shapes=scratch,
        compiler_params=pltpu.CompilerParams(vmem_limit_bytes=VMEM_LIMIT),
        cost_estimate=pl.CostEstimate(
            flops=2 * macs, bytes_accessed=2**22 if macs else 1, transcendentals=0
        ),
    )(*inputs)
    return results if len(results) > 1 else results[0]


def per_device(volume, kernels, partner, cotangent):
    volume, cotangent = volume[0], cotangent[0]
    rows, height, lanes = volume.shape
    pairs, tiles = height // 2, lanes // LANES
    cells = pairs * tiles
    groups, count = lax.axis_size("sample"), lax.axis_size("depth")
    depth = rows * count
    layers, taps, width = kernels.shape
    bf16, f32 = jnp.bfloat16, jnp.float32
    row_macs = 3 * cells * WIDE * TILE
    packed_rows = taps * CH // CELLS
    wide = lambda *lead: pltpu.VMEM((*lead, cells, WIDE), bf16)
    field = lambda *lead: ((*lead, cells, TILE), bf16)
    raw_tiles = lambda *lead: pltpu.VMEM((*lead, height * tiles, LANES), f32)
    banded = ((layers, 3, WIDE, TILE), bf16)
    spread_taps = ((layers, taps * CH, LANES), bf16)
    rw = pltpu.VMEM((CELLS, taps * CH, LANES), f32)

    direct = groups in (2, 4, 8)
    evens = even_hops(volume) if direct else []
    both, edges = lax.optimization_barrier((jnp.stack([volume, cotangent]), volume))
    near, far = neighbours(edges, edges)
    packed = kernels.reshape(layers, packed_rows, LANES)
    ids = jnp.clip(partner, 0, groups - 1)
    fwd_taps, bwd_taps = call(
        functools.partial(taps_body, taps),
        [spread_taps, spread_taps],
        [pltpu.VMEM((layers, -(-taps // CELLS) * LANES, LANES), f32)],
        [packed],
        2**28,
    )
    evens, both, ids, fwd_taps, bwd_taps, late, near, far = lax.optimization_barrier(
        (evens, both, ids, fwd_taps, bwd_taps, cotangent, near, far)
    )
    edge = ((2, H_VOL, cells, TILE), bf16)
    if direct:
        raw = lambda n: ((n, rows, height, lanes), bf16)
        give = call(pick_body, [raw(2)], [], [ids, both, *evens])
        give, late = lax.optimization_barrier((give, late))
        sent = over_sample(give, 1)
        vol, vol_near, vol_far = call(
            functools.partial(select_body, len(evens)),
            [field(2, rows), edge, edge],
            [raw_tiles(2, rows)],
            [ids, both, *evens, sent],
        )
        sides = neighbours(vol_near, vol_far)
        evens, vol = lax.optimization_barrier((even_hops(late), vol))
        give = call(pick_body, [raw(1)], [], [ids, both, *evens])
        cot_other = call(
            functools.partial(select_body, len(evens)),
            [field(1, rows)],
            [raw_tiles(1, rows)],
            [ids, both, *evens, over_sample(give, 1)],
        )
    else:
        vol, cot_other = traded(volume, cotangent, partner, tiles)
        sides = neighbours(vol, vol)
    hid_rows = rows + 2 * H_HIDDEN
    fwd, hid_own, sl1, xv_own, cot_own = call(
        functools.partial(own_body, pairs, tiles),
        [
            banded,
            field(hid_rows),
            ((rows, cells, TILE), f32),
            ((rows + 2, cells, WIDE), bf16),
            field(rows),
        ],
        [wide(rows + 2 * H_VOL), pltpu.VMEM((3, rows, cells, TILE), bf16), raw_tiles(4 * rows)],
        [fwd_taps, near, both, far],
        hid_rows * row_macs,
    )

    g3, g3_near, g3_far, sl2, xb_own, xs_own = call(
        functools.partial(forward_body, depth, pairs, tiles),
        [
            field(2, rows),
            field(2, H_G3),
            field(2, H_G3),
            ((2, rows + 2 * H_TWO, cells, TILE), f32),
            ((rows + 2, cells, WIDE), bf16),
            ((rows + 2, cells, WIDE), bf16),
        ],
        [
            wide(2, rows + 2 * H_VOL),
            pltpu.VMEM((2, hid_rows, cells, TILE), bf16),
            wide(2, hid_rows),
            wide(2, rows + 2),
        ],
        [sides[1], vol, sides[0], hid_own, cot_own, cot_other, fwd],
        (2 * hid_rows + 2 * (rows + 2) + 2 * rows) * row_macs,
    )

    near, far = neighbours(g3_near, g3_far)
    terms = ((packed_rows, LANES), bf16)
    bwd, three = call(
        between_body, [banded, terms], [rw], [bwd_taps, xs_own, g3], rows * row_macs
    )
    three, far, near = lax.optimization_barrier((three, far, near))
    three_near = swapped(three, 1)
    short, long = 2 * packed_rows, -(-layers * packed_rows // 16) * 16
    message = lambda lines: ((lines + 2 * cells, LANES), bf16)
    g1, g1_far, own = call(
        functools.partial(back_body, depth, pairs, tiles),
        [field(rows), ((H_G1, cells, TILE), bf16), message(short)],
        [
            wide(2, rows + 2 * H_G3),
            wide(2, rows + 2 * H_G2),
            rw,
            pltpu.VMEM((H_G1, cells, TILE), bf16),
            pltpu.VMEM((short, LANES), f32),
        ],
        [far, g3, near, sl1, sl2, xv_own, xb_own, bwd],
        (6 * rows + 4) * row_macs,
    )
    own, three_near = lax.optimization_barrier((own, three_near))
    near = swapped(own, 1)
    summed = call(
        add_body,
        [message(long)],
        [pltpu.VMEM((long, LANES), f32)],
        [own, near, three, three_near, g1_far],
    )
    if count == 4:
        far = swapped(summed, 3)
        parts = [summed, far]
    else:
        far, parts, hop = neighbours(summed, summed)[1], [summed], 2
        while hop < count:
            if len(parts) > 1:
                parts = [call(total_body, [((long, LANES), bf16)], [], parts)]
            parts.append(swapped(parts[0], hop))
            hop *= 2
    grad_volume, total = call(
        functools.partial(last_body, pairs, tiles),
        [((rows, height, lanes), bf16), ((layers * packed_rows, LANES), f32)],
        [raw_tiles(rows), wide(rows + 2 * H_G1), pltpu.VMEM((2, H_G1, cells, TILE), bf16)],
        [near, g1, far, bwd, *parts],
        rows * row_macs,
    )
    return (grad_volume[None], total.reshape(1, layers, taps, width))


def solution(mesh):
    in_specs = (P("sample", "depth", None, None), P(), P(), P("sample", "depth", None, None))
    out_specs = (P("sample", "depth", None, None), P("sample", None, None, None))
    return jax.shard_map(
        per_device, mesh=mesh, in_specs=in_specs, out_specs=out_specs, check_vma=False
    )
```

```python
import functools

import jax
import jax.numpy as jnp
from jax import lax
from jax.experimental import pallas as pl
from jax.experimental.pallas import tpu as pltpu
from jax.sharding import PartitionSpec as P

CH = 32
OWN_SHARE = 0.6
PARTNER_SHARE = 0.4
LANES = 128
CELLS = LANES // CH
TILE = 2 * LANES
WIDE = 3 * TILE
VMEM_LIMIT = 40 * 2**20
FORWARD_ROWS, BACKWARD_ROWS = 2, 6

SLOTS = (
    [(1 + h, 1 + w) for h in range(2) for w in range(CELLS)]
    + [(0, 1 + w) for w in range(CELLS)]
    + [(3, 1 + w) for w in range(CELLS)]
    + [(1, 5), (0, 0), (0, 5), (1, 0)]
    + [(2, 5), (3, 0), (3, 5), (2, 0)]
)
SLOT_OF = {cell: at for at, cell in enumerate(SLOTS)}

H_VOL, H_HIDDEN, H_TWO, H_G3, H_G2, H_G1 = 3, 2, 1, 2, 1, 1


def chunks_of(rows, most):
    count = -(-rows // most)
    base, extra = divmod(rows, count)
    start, result = 0, []
    for index in range(count):
        size = base + (index < extra)
        result.append((start, size))
        start += size
    return result


def sigmoid(v):
    return 0.5 + 0.5 * jnp.tanh(0.5 * v)


def lanes_of(t):
    return slice(t * LANES, (t + 1) * LANES)


def taps_body(taps, kr_ref, fwd_ref, bwd_ref, scratch):
    layers, rows = kr_ref.shape[:2]
    part = scratch.shape[1] // CELLS // CH
    shape = (LANES, CELLS * LANES)
    lane = lax.broadcasted_iota(jnp.int32, shape, 1)
    chosen = lax.broadcasted_iota(jnp.int32, shape, 0) == lane // LANES * CH + lane % CH
    spread = jnp.where(chosen, 1.0, 0.0).astype(jnp.bfloat16)
    for layer in range(layers):
        groups = jnp.dot(kr_ref[layer], spread, preferred_element_type=jnp.float32)
        for q in range(CELLS):
            scratch[layer, pl.ds(q, rows, stride=CELLS), :] = groups[:, lanes_of(q)]
        scratch[layer, taps * CH :, :] = jnp.zeros_like(scratch[layer, taps * CH :, :])
        fwd_ref[layer] = scratch[layer, : taps * CH].astype(jnp.bfloat16)
        cell = lax.broadcasted_iota(jnp.int32, (part * CH, LANES), 1) // CH
        compact = jnp.zeros((part * CH, LANES), jnp.float32)
        for group in range(CELLS):
            at = group * part * CH
            compact = jnp.where(cell == group, scratch[layer, at : at + part * CH, :], compact)
        room = -(-part // CELLS) * LANES - part * CH
        turned = jnp.concatenate([compact, jnp.zeros((room, LANES), jnp.float32)], 0).T
        stacked = jnp.concatenate(
            [turned[:, lanes_of(t)] for t in range(turned.shape[1] // LANES)], 0
        ).astype(jnp.bfloat16)
        groups = jnp.dot(stacked, spread, preferred_element_type=jnp.float32)
        for tap in range(taps):
            group, index = divmod(tap, part)
            at, row = taps - 1 - tap, index // CELLS * LANES + group * CH
            bwd_ref[layer, at * CH : (at + 1) * CH, :] = groups[
                row : row + CH, lanes_of(index % CELLS)
            ].astype(jnp.bfloat16)


def fill_weights(taps_ref, t_ref):
    cell = lax.broadcasted_iota(jnp.int32, (CH, LANES), 1) // CH
    zero = jnp.zeros((CH, LANES), jnp.bfloat16)
    for layer in range(t_ref.shape[0]):
        for a in range(3):
            bands = {}
            for b in range(3):
                first = (a * 9 + b * 3) * CH
                values = [taps_ref[layer, first + c * CH : first + (c + 1) * CH, :] for c in range(3)]
                for ww in range(CELLS + 2):
                    band = zero
                    for c in range(3):
                        if 0 <= ww - c < CELLS:
                            band = jnp.where(cell == ww - c, values[c], band)
                    bands[b, ww] = band
            for at, (hh, ww) in enumerate(SLOTS):
                for h in range(2):
                    t_ref[
                        layer, a, at * CH : (at + 1) * CH, h * LANES : (h + 1) * LANES
                    ] = bands.get((hh - h, ww), zero)


def edge_masks(tiles):
    shape = (1, tiles, TILE)
    cell = lax.broadcasted_iota(jnp.int32, shape, 2) % LANES // CH
    row = lax.broadcasted_iota(jnp.int32, shape, 1)
    from_before = (cell == CELLS - 1) & (row > 0)
    from_after = (cell == 0) & (row < tiles - 1)
    return tuple(
        jnp.where(mask, 1.0, 0.0).astype(jnp.bfloat16) for mask in (from_before, from_after)
    )


def expand(x, out_ref, lead, pairs, tiles, masks):
    x = x.reshape(pairs, tiles, TILE)
    edge = pltpu.roll(x, 1, 1) * masks[0] + pltpu.roll(x, tiles - 1, 1) * masks[1]
    e0, e1 = edge[..., :LANES], edge[..., LANES:]
    r0, r1 = pltpu.roll(e0, LANES // 2, 2), pltpu.roll(e1, LANES // 2, 2)
    zero = jnp.zeros((1, tiles, LANES), x.dtype)
    low = jnp.concatenate([zero, x[:-1, :, LANES:]], 0)
    high = jnp.concatenate([x[1:, :, :LANES], zero], 0)
    e0 = e0 + jnp.concatenate([zero, r1[:-1]], 0)
    e1 = e1 + jnp.concatenate([r0[1:], zero], 0)
    flat = lambda v: v.reshape(pairs * tiles, v.shape[-1])
    out_ref[(*lead, slice(None), slice(0, TILE))] = flat(x)
    out_ref[(*lead, slice(None), slice(TILE, TILE + LANES))] = flat(low)
    out_ref[(*lead, slice(None), slice(TILE + LANES, 2 * TILE))] = flat(high)
    out_ref[(*lead, slice(None), slice(2 * TILE, 2 * TILE + LANES))] = flat(e0)
    out_ref[(*lead, slice(None), slice(2 * TILE + LANES, WIDE))] = flat(e1)


def conv_rows(x_ref, lead, start, rows, t_ref, layer):
    blocks = [x_ref[(*lead, pl.ds(start + a, rows))].reshape(-1, WIDE) for a in range(3)]
    return jnp.dot(
        jnp.concatenate(blocks, axis=1),
        t_ref[layer].reshape(3 * WIDE, TILE),
        preferred_element_type=jnp.float32,
    )


def slope_of(pre, gate):
    return gate * (1.0 + pre * (1.0 - gate))


def rounded(v):
    return v.astype(jnp.bfloat16)


def inside(v, row, depth):
    return jnp.where((row >= 0) & (row < depth), v, 0.0)


def either(flag, a, b):
    low = lambda *at: jnp.where(flag, a[at], b[at])
    high = lambda *at: jnp.where(flag, b[at], a[at])
    return low, high


def widen(near, own, far, lead, halo, x_ref, x_lead, grow):
    at, last = lax.axis_index("depth"), lax.axis_size("depth") - 1
    low, high = either(at % 2 == 1, near, far)
    held, rows = near.shape[len(lead)], own.shape[len(lead)]
    for d in range(halo):
        row = low(*lead, held - halo + d)
        if d == halo - 1:
            row = jnp.where(at > 0, row, jnp.zeros_like(row))
        grow(row, x_ref, (*x_lead, d))
    for d in range(rows):
        grow(own[(*lead, d)], x_ref, (*x_lead, halo + d))
    for d in range(halo):
        row = high(*lead, d)
        if d == 0:
            row = jnp.where(at < last, row, jnp.zeros_like(row))
        grow(row, x_ref, (*x_lead, halo + rows + d))


def edge_rows(values, near, far, halo):
    odd = lax.axis_index("depth") % 2 == 1
    rows = values.shape[0]
    for d in range(halo):
        up, down = values[rows - halo + d], values[d]
        near[d] = jnp.where(odd, down, up)
        far[d] = jnp.where(odd, up, down)


def layer_one(xv, lead, out_ref, t_ref, slopes_ref=None):
    rows, cells = out_ref.shape[len(lead)], out_ref.shape[-2]
    for start, count in chunks_of(rows, FORWARD_ROWS):
        pre = conv_rows(xv, lead, start, count, t_ref, 0)
        gate = sigmoid(pre)
        value = (pre * gate).astype(jnp.bfloat16).reshape(count, cells, TILE)
        out_ref[(*lead, pl.ds(start, count))] = value
        if slopes_ref is not None:
            slope = slope_of(pre, gate).reshape(count, cells, TILE)
            for d in range(count):
                to = start + d - H_HIDDEN
                if 0 <= to < slopes_ref.shape[0]:
                    slopes_ref[to] = slope[d]


def tiled_rows(load, height, tiles, scratch, at):
    for t in range(tiles):
        scratch[at, t * height : (t + 1) * height, :] = load(t).astype(jnp.float32)
    for h in range(height):
        piece = scratch[at, pl.ds(h, tiles, stride=height), :].astype(jnp.bfloat16)
        yield h // 2 * tiles, slice(h % 2 * LANES, (h % 2 + 1) * LANES), piece


def wanted_by(partner, crop, count):
    inverse = jnp.int32(0)
    for other in range(partner.shape[0]):
        inverse = jnp.where(partner[other] == crop, other, inverse)
    return (partner[crop], inverse)[2 - count :]


def pick_body(partner, both, *refs):
    *evens, out = refs
    own = lax.axis_index("sample")
    count = out.shape[0]
    for to, crop in enumerate(wanted_by(partner, own ^ 1, count)):
        for at, source in enumerate((both.at[2 - count], *evens)):

            @pl.when(crop ^ own == 2 * at)
            def _(to=to, source=source):
                out[to] = source[...]


def select_body(hops, partner, both, *refs):
    held, refs = (both, *refs[: len(hops) - 1]), refs[len(hops) - 1 :]
    own = lax.axis_index("sample")
    _, rows, height, lanes = both.shape
    tiles = lanes // LANES
    picked = len(hops) * 2 == lax.axis_size("sample")
    if picked:
        sent, *refs = refs
    out, *sides, scratch = refs
    count = out.shape[0]

    def spread(to, source):
        for d in range(rows):
            for t in range(tiles):
                scratch[to, d, t * height : (t + 1) * height, :] = source[
                    d, :, lanes_of(t)
                ].astype(jnp.float32)

    for to, crop in enumerate(wanted_by(partner, own, count)):
        for hop, source in zip(hops, held):
            source = both.at[2 - count] if hop == 0 else source
            pl.when(crop ^ own == hop)(functools.partial(spread, to, source))
        if picked:
            pl.when((crop ^ own) % 2 == 1)(functools.partial(spread, to, sent.at[to]))
        for d in range(rows):
            for h in range(height):
                piece = scratch[to, d, pl.ds(h, tiles, stride=height), :].astype(jnp.bfloat16)
                row, side = h // 2 * tiles, lanes_of(h % 2)
                out[to, d, row : row + tiles, side] = piece
        if sides:
            edge_rows(out.at[to], *(side.at[to] for side in sides), H_VOL)


def own_body(
    pairs, tiles,
    taps_ref, near, both, far,
    t_ref, hid, sl1, xv_own, cot_own,
    xv, field, scratch,
):
    _, rows, height, _ = both.shape
    fill_weights(taps_ref, t_ref)
    grow = functools.partial(expand, pairs=pairs, tiles=tiles, masks=edge_masks(tiles))
    for at, part in enumerate((near, both.at[0], far, both.at[1])):
        for d in range(rows):
            load = lambda t, part=part, d=d: part[d, :, lanes_of(t)]
            for row, side, piece in tiled_rows(load, height, tiles, scratch, at * rows + d):
                if at < 3:
                    field[at, d, row : row + tiles, side] = piece
                else:
                    cot_own[d, row : row + tiles, side] = piece
    widen(field.at[0], field.at[1], field.at[2], (), H_VOL, xv, (), grow)
    layer_one(xv, (), hid, t_ref, sl1)
    xv_own[...] = xv[H_VOL - 1 : H_VOL + rows + 1]


def forward_body(
    depth, pairs, tiles,
    near, mid, far, hid_own, cot_own, cot_other, t_ref,
    g3, g3_near, g3_far, sl2, xb_own, xs_own,
    xv, hid, xb, xs,
):
    rows = mid.shape[1]
    cells = pairs * tiles
    first = lax.axis_index("depth") * rows
    grow = functools.partial(expand, pairs=pairs, tiles=tiles, masks=edge_masks(tiles))

    for crop in range(2):
        widen(near, mid, far, (crop,), H_VOL, xv, (crop,), grow)
        layer_one(xv, (crop,), hid, t_ref)

    for d in range(rows + 2 * H_HIDDEN):
        own = hid_own[d].astype(jnp.float32)
        partner, other = hid[0, d].astype(jnp.float32), hid[1, d].astype(jnp.float32)
        row = first + d - H_HIDDEN
        for j, (a, b) in enumerate(((own, partner), (other, own))):
            mixed = OWN_SHARE * a + PARTNER_SHARE * b
            grow(rounded(inside(mixed, row, depth)), xb, (j, d))

    def middle(j, cot):
        for start, count in chunks_of(rows + 2 * H_TWO, FORWARD_ROWS):
            pre = conv_rows(xb, (j,), start, count, t_ref, 1)
            gate = sigmoid(pre)
            value = (pre * gate).reshape(count, cells, TILE)
            slope = slope_of(pre, gate).reshape(count, cells, TILE)
            for d in range(count):
                sl2[j, start + d] = slope[d]
                to = start + d - (H_TWO - 1)
                if 0 <= to < rows + 2:
                    grow(rounded(inside(value[d], first + to - 1, depth)), xs, (j, to))
        for start, count in chunks_of(rows, FORWARD_ROWS):
            pre = conv_rows(xs, (j,), start, count, t_ref, 2)
            slope = slope_of(pre, sigmoid(pre)).reshape(count, cells, TILE)
            for d in range(count):
                at = start + d
                grad = rounded(cot[at].astype(jnp.float32) * slope[d])
                g3[j, at] = grad

    middle(0, cot_own)
    middle(1, cot_other.at[0])
    for j in range(2):
        edge_rows(g3.at[j], g3_near.at[j], g3_far.at[j], H_G3)
    xb_own[...] = xb[0, H_HIDDEN - 1 : H_HIDDEN + rows + 1]
    xs_own[...] = xs[0]


def kernel_terms(values, gradient, rw):
    rows = gradient.shape[0]
    gradient = gradient.reshape(-1, TILE)
    for a in range(3):
        block = values[a : a + rows].reshape(-1, WIDE)
        terms = lax.dot_general(
            block, gradient, (((0,), (0,)), ((), ())), preferred_element_type=jnp.float32
        )
        for b in range(3):
            for c in range(3):
                at = (a * 9 + b * 3 + c) * CH
                for w in range(CELLS):
                    s0, s1 = SLOT_OF[b, w + c] * CH, SLOT_OF[b + 1, w + c] * CH
                    rw[w, at : at + CH] = (
                        terms[s0 : s0 + CH, :LANES] + terms[s1 : s1 + CH, LANES:]
                    )
    count = rw.shape[1] // CELLS
    cell = lax.broadcasted_iota(jnp.int32, (count, LANES), 1) // CH
    dense = jnp.zeros((count, LANES), jnp.float32)
    for q in range(CELLS):
        part = None
        for w in range(CELLS):
            piece = rw[w, pl.ds(q, count, stride=CELLS), :]
            if q != w:
                piece = pltpu.roll(piece, (q - w) % CELLS * CH, 1)
            part = piece if part is None else part + piece
        dense = jnp.where(cell == q, part, dense)
    return dense.astype(jnp.bfloat16)


def between_body(taps_ref, xs_own, g3, t_ref, terms, rw):
    fill_weights(taps_ref, t_ref)
    terms[...] = kernel_terms(xs_own[...], g3[0], rw)


def back_two(j, x_ref, sl2, x2_ref, t_ref, first, depth, grow):
    rows, cells = x2_ref.shape[-3:-1]
    for start, count in chunks_of(rows, BACKWARD_ROWS):
        back = conv_rows(x_ref, (), start, count, t_ref, 2).reshape(count, cells, TILE)
        for d in range(count):
            at = start + d
            grad = inside(back[d] * sl2[j, at], first + at - H_G2, depth)
            grow(rounded(grad), x2_ref, (at,))


def put_row(message, row):
    half = row.shape[0]
    message[message.shape[0] - 2 * half : message.shape[0] - half] = row[:, :LANES]
    message[message.shape[0] - half :] = row[:, LANES:]


def back_body(
    depth, pairs, tiles,
    near, mid, far, sl1, sl2, xv_own, xb_own, t_ref,
    g1, g1_far, message,
    xg3, xg2, rw, g1_near, terms,
):
    rows = mid.shape[1]
    cells = pairs * tiles
    first = lax.axis_index("depth") * rows
    grow = functools.partial(expand, pairs=pairs, tiles=tiles, masks=edge_masks(tiles))
    for j in range(2):
        widen(near, mid, far, (j,), H_G3, xg3.at[j], (), grow)
        back_two(j, xg3.at[j], sl2, xg2.at[j], t_ref, first, depth, grow)
    own, other = (
        rounded(conv_rows(xg2, (j,), 0, rows, t_ref, 1)).astype(jnp.float32) for j in range(2)
    )
    mixed = (OWN_SHARE * own + PARTNER_SHARE * other).reshape(rows, cells, TILE)
    g1[...] = rounded(mixed * sl1[...])
    edge_rows(g1, g1_near, g1_far, H_G1)
    size = terms.shape[0] // 2
    terms[:size] = kernel_terms(xv_own[...], g1[...], rw).astype(jnp.float32)
    two = kernel_terms(xb_own[...], xg2[0, H_G2 : H_G2 + rows, :, :TILE], rw)
    terms[size:] = two.astype(jnp.float32)
    message[: 2 * size] = terms[...].astype(jnp.bfloat16)
    put_row(message, g1_near[0])


def last_body(pairs, tiles, near, g1, far, t_ref, *refs):
    *parts, gv, total, scratch, xg1, sides = refs
    lines = -(-total.shape[0] // 16) * 16
    terms = [part[:lines].astype(jnp.float32) for part in parts]
    total[...] = functools.reduce(lambda a, b: a + b, terms)[: total.shape[0]]
    rows, height, _ = gv.shape
    cells = pairs * tiles
    grow = functools.partial(expand, pairs=pairs, tiles=tiles, masks=edge_masks(tiles))
    for at, message in enumerate((near, far)):
        first = message.shape[0] - 2 * cells
        sides[at, 0, :, :LANES] = message[first : first + cells]
        sides[at, 0, :, LANES:] = message[first + cells :]
    widen(sides.at[0], g1, sides.at[1], (), H_G1, xg1, (), grow)
    for start, count in chunks_of(rows, BACKWARD_ROWS):
        back = conv_rows(xg1, (), start, count, t_ref, 0).reshape(count, cells, TILE)
        for d in range(count):
            for h in range(height):
                row, side = h // 2 * tiles, slice(h % 2 * LANES, (h % 2 + 1) * LANES)
                scratch[start + d, pl.ds(h, tiles, stride=height), :] = back[
                    d, row : row + tiles, side
                ]
            for t in range(tiles):
                gv[start + d, :, t * LANES : (t + 1) * LANES] = scratch[
                    start + d, t * height : (t + 1) * height, :
                ].astype(jnp.bfloat16)


def add_body(own, near, three, three_near, g1_far, message, terms):
    add = lambda a, b: a.astype(jnp.float32) + b.astype(jnp.float32)
    size = three.shape[0]
    terms[: 2 * size] = add(own[: 2 * size], near[: 2 * size])
    terms[2 * size : 3 * size] = add(three[...], three_near[...])
    terms[3 * size :] = jnp.zeros_like(terms[3 * size :])
    message[: terms.shape[0]] = terms[...].astype(jnp.bfloat16)
    put_row(message, g1_far[0])


def total_body(one, two, out):
    rows = -(-out.shape[0] // 16) * 16
    total = one[:rows].astype(jnp.float32) + two[:rows].astype(jnp.float32)
    out[...] = total[: out.shape[0]].astype(out.dtype)


def swapped(values, hop):
    count = lax.axis_size("depth")
    return lax.ppermute(values, "depth", [(i, i ^ hop) for i in range(count)])


def neighbours(near, far):
    count = lax.axis_size("depth")
    result = []
    for values, first in ((near, 0), (far, 1)):
        partner = {}
        for i in range(first, count - 1, 2):
            partner[i], partner[i + 1] = i + 1, i
        pairs = [(i, partner.get(i, i)) for i in range(count)]
        result.append(lax.ppermute(values, "depth", pairs))
    return result


def over_sample(values, hop):
    groups = lax.axis_size("sample")
    return lax.ppermute(values, "sample", [(i, i ^ hop) for i in range(groups)])


def even_hops(values):
    return [over_sample(values, hop) for hop in range(2, lax.axis_size("sample"), 2)]


def all_hops(odd, evens):
    return [odd, *(crop for even in evens for crop in (even, over_sample(even, 1)))]


def traded(volume, cotangent, partner, tiles):
    groups = lax.axis_size("sample")
    rows, height, _ = volume.shape
    split = jnp.stack([volume, cotangent]).reshape(2, rows, height // 2, 2, tiles, LANES)
    split = split.transpose(0, 1, 2, 4, 3, 5).reshape(2, groups, -1, TILE)
    pieces = split.swapaxes(0, 1)
    spread = lax.all_to_all(pieces, "sample", split_axis=0, concat_axis=0, tiled=True)
    ids = jnp.arange(groups, dtype=jnp.int32)
    inverse = jnp.sum(jnp.where(partner[:, None] == ids[None, :], ids[:, None], 0), axis=0)
    wanted = jnp.stack([2 * partner, 2 * inverse, 2 * inverse + 1], axis=1)
    chosen = jnp.take(spread.reshape(2 * groups, -1, TILE), wanted, axis=0)
    joined = lax.all_to_all(chosen, "sample", split_axis=0, concat_axis=0, tiled=True)
    others = jnp.swapaxes(joined, 0, 1).reshape(3, rows, -1, TILE)
    return others[:2], others[2:]


def call(kernel, outs, scratch, inputs, macs=0, far=()):
    vmem, smem, anywhere = (
        pl.BlockSpec(memory_space=space) for space in (pltpu.VMEM, pltpu.SMEM, pl.ANY)
    )
    specs = [
        anywhere if at in far else smem if x.dtype == jnp.int32 else vmem
        for at, x in enumerate(inputs)
    ]
    results = pl.pallas_call(
        kernel,
        out_shape=tuple(jax.ShapeDtypeStruct(shape, dtype) for shape, dtype in outs),
        in_specs=specs,
        out_specs=(vmem,) * len(outs),
        scratch_shapes=scratch,
        compiler_params=pltpu.CompilerParams(vmem_limit_bytes=VMEM_LIMIT),
        cost_estimate=pl.CostEstimate(
            flops=2 * macs, bytes_accessed=2**22 if macs else 1, transcendentals=0
        ),
    )(*inputs)
    return results if len(results) > 1 else results[0]


def per_device(volume, kernels, partner, cotangent):
    volume, cotangent = volume[0], cotangent[0]
    rows, height, lanes = volume.shape
    pairs, tiles = height // 2, lanes // LANES
    cells = pairs * tiles
    groups, count = lax.axis_size("sample"), lax.axis_size("depth")
    depth = rows * count
    layers, taps, width = kernels.shape
    bf16, f32 = jnp.bfloat16, jnp.float32
    row_macs = 3 * cells * WIDE * TILE
    packed_rows = taps * CH // CELLS
    wide = lambda *lead: pltpu.VMEM((*lead, cells, WIDE), bf16)
    field = lambda *lead: ((*lead, cells, TILE), bf16)
    raw_tiles = lambda *lead: pltpu.VMEM((*lead, height * tiles, LANES), f32)
    banded = ((layers, 3, WIDE, TILE), bf16)
    spread_taps = ((layers, taps * CH, LANES), bf16)
    rw = pltpu.VMEM((CELLS, taps * CH, LANES), f32)

    direct = groups in (2, 4, 8)
    evens = even_hops(volume) if direct else []
    both, edges = lax.optimization_barrier((jnp.stack([volume, cotangent]), volume))
    near, far = neighbours(edges, edges)
    packed = kernels.reshape(layers, packed_rows, LANES)
    ids = jnp.clip(partner, 0, groups - 1)
    fwd_taps, bwd_taps = call(
        functools.partial(taps_body, taps),
        [spread_taps, spread_taps],
        [pltpu.VMEM((layers, -(-taps // CELLS) * LANES, LANES), f32)],
        [packed],
        2**28,
    )
    evens, both, ids, fwd_taps, bwd_taps, own_crop, late = lax.optimization_barrier(
        (evens, both, ids, fwd_taps, bwd_taps, volume, cotangent)
    )
    edge = ((2, H_VOL, cells, TILE), bf16)
    if direct:
        crops = all_hops(over_sample(own_crop, 1), evens)
        crops, near, far = lax.optimization_barrier((crops, near, far))
        vol, vol_near, vol_far = call(
            functools.partial(select_body, tuple(range(groups))),
            [field(2, rows), edge, edge],
            [raw_tiles(2, rows)],
            [ids, both, *crops],
        )
        sides = neighbours(vol_near, vol_far)
        evens, vol = lax.optimization_barrier((even_hops(late), vol))
        give = call(pick_body, [((1, rows, height, lanes), bf16)], [], [ids, both, *evens])
        cot_other = call(
            functools.partial(select_body, tuple(range(0, groups, 2))),
            [field(1, rows)],
            [raw_tiles(1, rows)],
            [ids, both, *evens, over_sample(give, 1)],
        )
    else:
        vol, cot_other = traded(volume, cotangent, partner, tiles)
        sides = neighbours(vol, vol)
    hid_rows = rows + 2 * H_HIDDEN
    fwd, hid_own, sl1, xv_own, cot_own = call(
        functools.partial(own_body, pairs, tiles),
        [
            banded,
            field(hid_rows),
            ((rows, cells, TILE), f32),
            ((rows + 2, cells, WIDE), bf16),
            field(rows),
        ],
        [wide(rows + 2 * H_VOL), pltpu.VMEM((3, rows, cells, TILE), bf16), raw_tiles(4 * rows)],
        [fwd_taps, near, both, far],
        hid_rows * row_macs,
    )

    g3, g3_near, g3_far, sl2, xb_own, xs_own = call(
        functools.partial(forward_body, depth, pairs, tiles),
        [
            field(2, rows),
            field(2, H_G3),
            field(2, H_G3),
            ((2, rows + 2 * H_TWO, cells, TILE), f32),
            ((rows + 2, cells, WIDE), bf16),
            ((rows + 2, cells, WIDE), bf16),
        ],
        [
            wide(2, rows + 2 * H_VOL),
            pltpu.VMEM((2, hid_rows, cells, TILE), bf16),
            wide(2, hid_rows),
            wide(2, rows + 2),
        ],
        [sides[0], vol, sides[1], hid_own, cot_own, cot_other, fwd],
        (2 * hid_rows + 2 * (rows + 2) + 2 * rows) * row_macs,
    )

    near, far = neighbours(g3_near, g3_far)
    terms = ((packed_rows, LANES), bf16)
    bwd, three = call(
        between_body, [banded, terms], [rw], [bwd_taps, xs_own, g3], rows * row_macs
    )
    three_near = swapped(three, 1)
    short, long = 2 * packed_rows, -(-layers * packed_rows // 16) * 16
    message = lambda lines: ((lines + 2 * cells, LANES), bf16)
    g1, g1_far, own = call(
        functools.partial(back_body, depth, pairs, tiles),
        [field(rows), ((H_G1, cells, TILE), bf16), message(short)],
        [
            wide(2, rows + 2 * H_G3),
            wide(2, rows + 2 * H_G2),
            rw,
            pltpu.VMEM((H_G1, cells, TILE), bf16),
            pltpu.VMEM((short, LANES), f32),
        ],
        [near, g3, far, sl1, sl2, xv_own, xb_own, bwd],
        (6 * rows + 4) * row_macs,
    )
    own, three_near = lax.optimization_barrier((own, three_near))
    near = swapped(own, 1)
    summed = call(
        add_body,
        [message(long)],
        [pltpu.VMEM((long, LANES), f32)],
        [own, near, three, three_near, g1_far],
    )
    if count == 4:
        far = swapped(summed, 3)
        parts = [summed, far]
    else:
        far, parts, hop = neighbours(summed, summed)[1], [summed], 2
        while hop < count:
            if len(parts) > 1:
                parts = [call(total_body, [((long, LANES), bf16)], [], parts)]
            parts.append(swapped(parts[0], hop))
            hop *= 2
    grad_volume, total = call(
        functools.partial(last_body, pairs, tiles),
        [((rows, height, lanes), bf16), ((layers * packed_rows, LANES), f32)],
        [raw_tiles(rows), wide(rows + 2 * H_G1), pltpu.VMEM((2, H_G1, cells, TILE), bf16)],
        [near, g1, far, bwd, *parts],
        rows * row_macs,
    )
    return (grad_volume[None], total.reshape(1, layers, taps, width))


def solution(mesh):
    in_specs = (P("sample", "depth", None, None), P(), P(), P("sample", "depth", None, None))
    out_specs = (P("sample", "depth", None, None), P("sample", None, None, None))
    return jax.shard_map(
        per_device, mesh=mesh, in_specs=in_specs, out_specs=out_specs, check_vma=False
    )
```

```python
import functools

import jax
import jax.numpy as jnp
from jax import lax
from jax.experimental import pallas as pl
from jax.experimental.pallas import tpu as pltpu
from jax.sharding import PartitionSpec as P

CH = 32
OWN_SHARE = 0.6
PARTNER_SHARE = 0.4
LANES = 128
CELLS = LANES // CH
TILE = 2 * LANES
WIDE = 3 * TILE
VMEM_LIMIT = 40 * 2**20
FORWARD_ROWS, BACKWARD_ROWS = 2, 6

SLOTS = (
    [(1 + h, 1 + w) for h in range(2) for w in range(CELLS)]
    + [(0, 1 + w) for w in range(CELLS)]
    + [(3, 1 + w) for w in range(CELLS)]
    + [(1, 5), (0, 0), (0, 5), (1, 0)]
    + [(2, 5), (3, 0), (3, 5), (2, 0)]
)
SLOT_OF = {cell: at for at, cell in enumerate(SLOTS)}

H_VOL, H_HIDDEN, H_TWO, H_G3, H_G2, H_G1 = 3, 2, 1, 2, 1, 1


def chunks_of(rows, most):
    count = -(-rows // most)
    base, extra = divmod(rows, count)
    start, result = 0, []
    for index in range(count):
        size = base + (index < extra)
        result.append((start, size))
        start += size
    return result


def sigmoid(v):
    return 0.5 + 0.5 * jnp.tanh(0.5 * v)


def lanes_of(t):
    return slice(t * LANES, (t + 1) * LANES)


def taps_body(taps, kr_ref, fwd_ref, bwd_ref, scratch):
    layers, rows = kr_ref.shape[:2]
    part = scratch.shape[1] // CELLS // CH
    shape = (LANES, CELLS * LANES)
    lane = lax.broadcasted_iota(jnp.int32, shape, 1)
    chosen = lax.broadcasted_iota(jnp.int32, shape, 0) == lane // LANES * CH + lane % CH
    spread = jnp.where(chosen, 1.0, 0.0).astype(jnp.bfloat16)
    for layer in range(layers):
        groups = jnp.dot(kr_ref[layer], spread, preferred_element_type=jnp.float32)
        for q in range(CELLS):
            scratch[layer, pl.ds(q, rows, stride=CELLS), :] = groups[:, lanes_of(q)]
        scratch[layer, taps * CH :, :] = jnp.zeros_like(scratch[layer, taps * CH :, :])
        fwd_ref[layer] = scratch[layer, : taps * CH].astype(jnp.bfloat16)
        cell = lax.broadcasted_iota(jnp.int32, (part * CH, LANES), 1) // CH
        compact = jnp.zeros((part * CH, LANES), jnp.float32)
        for group in range(CELLS):
            at = group * part * CH
            compact = jnp.where(cell == group, scratch[layer, at : at + part * CH, :], compact)
        room = -(-part // CELLS) * LANES - part * CH
        turned = jnp.concatenate([compact, jnp.zeros((room, LANES), jnp.float32)], 0).T
        stacked = jnp.concatenate(
            [turned[:, lanes_of(t)] for t in range(turned.shape[1] // LANES)], 0
        ).astype(jnp.bfloat16)
        groups = jnp.dot(stacked, spread, preferred_element_type=jnp.float32)
        for tap in range(taps):
            group, index = divmod(tap, part)
            at, row = taps - 1 - tap, index // CELLS * LANES + group * CH
            bwd_ref[layer, at * CH : (at + 1) * CH, :] = groups[
                row : row + CH, lanes_of(index % CELLS)
            ].astype(jnp.bfloat16)


def fill_weights(taps_ref, t_ref):
    cell = lax.broadcasted_iota(jnp.int32, (CH, LANES), 1) // CH
    zero = jnp.zeros((CH, LANES), jnp.bfloat16)
    for layer in range(t_ref.shape[0]):
        for a in range(3):
            bands = {}
            for b in range(3):
                first = (a * 9 + b * 3) * CH
                values = [taps_ref[layer, first + c * CH : first + (c + 1) * CH, :] for c in range(3)]
                for ww in range(CELLS + 2):
                    band = zero
                    for c in range(3):
                        if 0 <= ww - c < CELLS:
                            band = jnp.where(cell == ww - c, values[c], band)
                    bands[b, ww] = band
            for at, (hh, ww) in enumerate(SLOTS):
                for h in range(2):
                    t_ref[
                        layer, a, at * CH : (at + 1) * CH, h * LANES : (h + 1) * LANES
                    ] = bands.get((hh - h, ww), zero)


def edge_masks(tiles):
    shape = (1, tiles, TILE)
    cell = lax.broadcasted_iota(jnp.int32, shape, 2) % LANES // CH
    row = lax.broadcasted_iota(jnp.int32, shape, 1)
    from_before = (cell == CELLS - 1) & (row > 0)
    from_after = (cell == 0) & (row < tiles - 1)
    return tuple(
        jnp.where(mask, 1.0, 0.0).astype(jnp.bfloat16) for mask in (from_before, from_after)
    )


def expand(x, out_ref, lead, pairs, tiles, masks):
    x = x.reshape(pairs, tiles, TILE)
    edge = pltpu.roll(x, 1, 1) * masks[0] + pltpu.roll(x, tiles - 1, 1) * masks[1]
    e0, e1 = edge[..., :LANES], edge[..., LANES:]
    r0, r1 = pltpu.roll(e0, LANES // 2, 2), pltpu.roll(e1, LANES // 2, 2)
    zero = jnp.zeros((1, tiles, LANES), x.dtype)
    low = jnp.concatenate([zero, x[:-1, :, LANES:]], 0)
    high = jnp.concatenate([x[1:, :, :LANES], zero], 0)
    e0 = e0 + jnp.concatenate([zero, r1[:-1]], 0)
    e1 = e1 + jnp.concatenate([r0[1:], zero], 0)
    flat = lambda v: v.reshape(pairs * tiles, v.shape[-1])
    out_ref[(*lead, slice(None), slice(0, TILE))] = flat(x)
    out_ref[(*lead, slice(None), slice(TILE, TILE + LANES))] = flat(low)
    out_ref[(*lead, slice(None), slice(TILE + LANES, 2 * TILE))] = flat(high)
    out_ref[(*lead, slice(None), slice(2 * TILE, 2 * TILE + LANES))] = flat(e0)
    out_ref[(*lead, slice(None), slice(2 * TILE + LANES, WIDE))] = flat(e1)


def conv_rows(x_ref, lead, start, rows, t_ref, layer):
    blocks = [x_ref[(*lead, pl.ds(start + a, rows))].reshape(-1, WIDE) for a in range(3)]
    return jnp.dot(
        jnp.concatenate(blocks, axis=1),
        t_ref[layer].reshape(3 * WIDE, TILE),
        preferred_element_type=jnp.float32,
    )


def slope_of(pre, gate):
    return gate * (1.0 + pre * (1.0 - gate))


def rounded(v):
    return v.astype(jnp.bfloat16)


def inside(v, row, depth):
    return jnp.where((row >= 0) & (row < depth), v, 0.0)


def either(flag, a, b):
    low = lambda *at: jnp.where(flag, a[at], b[at])
    high = lambda *at: jnp.where(flag, b[at], a[at])
    return low, high


def widen(near, own, far, lead, halo, x_ref, x_lead, grow):
    at, last = lax.axis_index("depth"), lax.axis_size("depth") - 1
    low, high = either(at % 2 == 1, near, far)
    held, rows = near.shape[len(lead)], own.shape[len(lead)]
    for d in range(halo):
        row = low(*lead, held - halo + d)
        if d == halo - 1:
            row = jnp.where(at > 0, row, jnp.zeros_like(row))
        grow(row, x_ref, (*x_lead, d))
    for d in range(rows):
        grow(own[(*lead, d)], x_ref, (*x_lead, halo + d))
    for d in range(halo):
        row = high(*lead, d)
        if d == 0:
            row = jnp.where(at < last, row, jnp.zeros_like(row))
        grow(row, x_ref, (*x_lead, halo + rows + d))


def edge_rows(values, near, far, halo):
    odd = lax.axis_index("depth") % 2 == 1
    rows = values.shape[0]
    for d in range(halo):
        up, down = values[rows - halo + d], values[d]
        near[d] = jnp.where(odd, down, up)
        far[d] = jnp.where(odd, up, down)


def layer_one(xv, lead, out_ref, t_ref, slopes_ref=None):
    rows, cells = out_ref.shape[len(lead)], out_ref.shape[-2]
    for start, count in chunks_of(rows, FORWARD_ROWS):
        pre = conv_rows(xv, lead, start, count, t_ref, 0)
        gate = sigmoid(pre)
        value = (pre * gate).astype(jnp.bfloat16).reshape(count, cells, TILE)
        out_ref[(*lead, pl.ds(start, count))] = value
        if slopes_ref is not None:
            slope = slope_of(pre, gate).reshape(count, cells, TILE)
            for d in range(count):
                to = start + d - H_HIDDEN
                if 0 <= to < slopes_ref.shape[0]:
                    slopes_ref[to] = slope[d]


def tiled_rows(load, height, tiles, scratch, at):
    for t in range(tiles):
        scratch[at, t * height : (t + 1) * height, :] = load(t).astype(jnp.float32)
    for h in range(height):
        piece = scratch[at, pl.ds(h, tiles, stride=height), :].astype(jnp.bfloat16)
        yield h // 2 * tiles, slice(h % 2 * LANES, (h % 2 + 1) * LANES), piece


def wanted_by(partner, crop, count):
    inverse = jnp.int32(0)
    for other in range(partner.shape[0]):
        inverse = jnp.where(partner[other] == crop, other, inverse)
    return (partner[crop], inverse)[2 - count :]


def pick_body(partner, both, *refs):
    *evens, out = refs
    own = lax.axis_index("sample")
    count = out.shape[0]
    for to, crop in enumerate(wanted_by(partner, own ^ 1, count)):
        for at, source in enumerate((both.at[2 - count], *evens)):

            @pl.when(crop ^ own == 2 * at)
            def _(to=to, source=source):
                out[to] = source[...]


def select_body(hops, partner, both, *refs):
    held, refs = (both, *refs[: len(hops) - 1]), refs[len(hops) - 1 :]
    own = lax.axis_index("sample")
    _, rows, height, lanes = both.shape
    tiles = lanes // LANES
    picked = len(hops) * 2 == lax.axis_size("sample")
    if picked:
        sent, *refs = refs
    out, *sides, scratch = refs
    count = out.shape[0]

    def spread(to, source):
        for d in range(rows):
            for t in range(tiles):
                scratch[to, d, t * height : (t + 1) * height, :] = source[
                    d, :, lanes_of(t)
                ].astype(jnp.float32)

    for to, crop in enumerate(wanted_by(partner, own, count)):
        for hop, source in zip(hops, held):
            source = both.at[2 - count] if hop == 0 else source
            pl.when(crop ^ own == hop)(functools.partial(spread, to, source))
        if picked:
            pl.when((crop ^ own) % 2 == 1)(functools.partial(spread, to, sent.at[to]))
        for d in range(rows):
            for h in range(height):
                piece = scratch[to, d, pl.ds(h, tiles, stride=height), :].astype(jnp.bfloat16)
                row, side = h // 2 * tiles, lanes_of(h % 2)
                out[to, d, row : row + tiles, side] = piece
        if sides:
            edge_rows(out.at[to], *(side.at[to] for side in sides), H_VOL)


def own_body(
    pairs, tiles,
    taps_ref, near, both, far,
    t_ref, hid, sl1, xv_own, cot_own,
    xv, field, scratch,
):
    _, rows, height, _ = both.shape
    fill_weights(taps_ref, t_ref)
    grow = functools.partial(expand, pairs=pairs, tiles=tiles, masks=edge_masks(tiles))
    for at, part in enumerate((near, both.at[0], far, both.at[1])):
        for d in range(rows):
            load = lambda t, part=part, d=d: part[d, :, lanes_of(t)]
            for row, side, piece in tiled_rows(load, height, tiles, scratch, at * rows + d):
                if at < 3:
                    field[at, d, row : row + tiles, side] = piece
                else:
                    cot_own[d, row : row + tiles, side] = piece
    widen(field.at[0], field.at[1], field.at[2], (), H_VOL, xv, (), grow)
    layer_one(xv, (), hid, t_ref, sl1)
    xv_own[...] = xv[H_VOL - 1 : H_VOL + rows + 1]


def forward_body(
    depth, pairs, tiles,
    near, mid, far, hid_own, cot_own, cot_other, t_ref,
    g3, g3_near, g3_far, sl2, xb_own, xs_own,
    xv, hid, xb, xs,
):
    rows = mid.shape[1]
    cells = pairs * tiles
    first = lax.axis_index("depth") * rows
    grow = functools.partial(expand, pairs=pairs, tiles=tiles, masks=edge_masks(tiles))

    for crop in range(2):
        widen(near, mid, far, (crop,), H_VOL, xv, (crop,), grow)
        layer_one(xv, (crop,), hid, t_ref)

    for d in range(rows + 2 * H_HIDDEN):
        own = hid_own[d].astype(jnp.float32)
        partner, other = hid[0, d].astype(jnp.float32), hid[1, d].astype(jnp.float32)
        row = first + d - H_HIDDEN
        for j, (a, b) in enumerate(((own, partner), (other, own))):
            mixed = OWN_SHARE * a + PARTNER_SHARE * b
            grow(rounded(inside(mixed, row, depth)), xb, (j, d))

    def middle(j, cot):
        for start, count in chunks_of(rows + 2 * H_TWO, FORWARD_ROWS):
            pre = conv_rows(xb, (j,), start, count, t_ref, 1)
            gate = sigmoid(pre)
            value = (pre * gate).reshape(count, cells, TILE)
            slope = slope_of(pre, gate).reshape(count, cells, TILE)
            for d in range(count):
                sl2[j, start + d] = slope[d]
                to = start + d - (H_TWO - 1)
                if 0 <= to < rows + 2:
                    grow(rounded(inside(value[d], first + to - 1, depth)), xs, (j, to))
        for start, count in chunks_of(rows, FORWARD_ROWS):
            pre = conv_rows(xs, (j,), start, count, t_ref, 2)
            slope = slope_of(pre, sigmoid(pre)).reshape(count, cells, TILE)
            for d in range(count):
                at = start + d
                grad = rounded(cot[at].astype(jnp.float32) * slope[d])
                g3[j, at] = grad

    middle(0, cot_own)
    middle(1, cot_other.at[0])
    for j in range(2):
        edge_rows(g3.at[j], g3_near.at[j], g3_far.at[j], H_G3)
    xb_own[...] = xb[0, H_HIDDEN - 1 : H_HIDDEN + rows + 1]
    xs_own[...] = xs[0]


def kernel_terms(values, gradient, rw):
    rows = gradient.shape[0]
    gradient = gradient.reshape(-1, TILE)
    for a in range(3):
        block = values[a : a + rows].reshape(-1, WIDE)
        terms = lax.dot_general(
            block, gradient, (((0,), (0,)), ((), ())), preferred_element_type=jnp.float32
        )
        for b in range(3):
            for c in range(3):
                at = (a * 9 + b * 3 + c) * CH
                for w in range(CELLS):
                    s0, s1 = SLOT_OF[b, w + c] * CH, SLOT_OF[b + 1, w + c] * CH
                    rw[w, at : at + CH] = (
                        terms[s0 : s0 + CH, :LANES] + terms[s1 : s1 + CH, LANES:]
                    )
    count = rw.shape[1] // CELLS
    cell = lax.broadcasted_iota(jnp.int32, (count, LANES), 1) // CH
    dense = jnp.zeros((count, LANES), jnp.float32)
    for q in range(CELLS):
        part = None
        for w in range(CELLS):
            piece = rw[w, pl.ds(q, count, stride=CELLS), :]
            if q != w:
                piece = pltpu.roll(piece, (q - w) % CELLS * CH, 1)
            part = piece if part is None else part + piece
        dense = jnp.where(cell == q, part, dense)
    return dense.astype(jnp.bfloat16)


def between_body(taps_ref, xs_own, g3, t_ref, terms, rw):
    fill_weights(taps_ref, t_ref)
    terms[...] = kernel_terms(xs_own[...], g3[0], rw)


def back_two(j, x_ref, sl2, x2_ref, t_ref, first, depth, grow):
    rows, cells = x2_ref.shape[-3:-1]
    for start, count in chunks_of(rows, BACKWARD_ROWS):
        back = conv_rows(x_ref, (), start, count, t_ref, 2).reshape(count, cells, TILE)
        for d in range(count):
            at = start + d
            grad = inside(back[d] * sl2[j, at], first + at - H_G2, depth)
            grow(rounded(grad), x2_ref, (at,))


def put_row(message, row):
    half = row.shape[0]
    message[message.shape[0] - 2 * half : message.shape[0] - half] = row[:, :LANES]
    message[message.shape[0] - half :] = row[:, LANES:]


def back_body(
    depth, pairs, tiles,
    near, mid, far, sl1, sl2, xv_own, xb_own, t_ref,
    g1, g1_far, message,
    xg3, xg2, rw, g1_near, terms,
):
    rows = mid.shape[1]
    cells = pairs * tiles
    first = lax.axis_index("depth") * rows
    grow = functools.partial(expand, pairs=pairs, tiles=tiles, masks=edge_masks(tiles))
    for j in range(2):
        widen(near, mid, far, (j,), H_G3, xg3.at[j], (), grow)
        back_two(j, xg3.at[j], sl2, xg2.at[j], t_ref, first, depth, grow)
    own, other = (
        rounded(conv_rows(xg2, (j,), 0, rows, t_ref, 1)).astype(jnp.float32) for j in range(2)
    )
    mixed = (OWN_SHARE * own + PARTNER_SHARE * other).reshape(rows, cells, TILE)
    g1[...] = rounded(mixed * sl1[...])
    edge_rows(g1, g1_near, g1_far, H_G1)
    size = terms.shape[0] // 2
    terms[:size] = kernel_terms(xv_own[...], g1[...], rw).astype(jnp.float32)
    two = kernel_terms(xb_own[...], xg2[0, H_G2 : H_G2 + rows, :, :TILE], rw)
    terms[size:] = two.astype(jnp.float32)
    message[: 2 * size] = terms[...].astype(jnp.bfloat16)
    put_row(message, g1_near[0])


def last_body(pairs, tiles, near, g1, far, t_ref, *refs):
    *parts, gv, total, scratch, xg1, sides = refs
    lines = near.shape[0] - 2 * g1.shape[1]
    half = len(parts) // 2
    add = lambda terms: functools.reduce(lambda a, b: a + b, terms)
    total[:lines] = add([part[:lines].astype(jnp.float32) for part in parts[:half]])
    total[lines:] = add([part[...].astype(jnp.float32) for part in parts[half:]])
    rows, height, _ = gv.shape
    cells = pairs * tiles
    grow = functools.partial(expand, pairs=pairs, tiles=tiles, masks=edge_masks(tiles))
    for at, message in enumerate((near, far)):
        first = message.shape[0] - 2 * cells
        sides[at, 0, :, :LANES] = message[first : first + cells]
        sides[at, 0, :, LANES:] = message[first + cells :]
    widen(sides.at[0], g1, sides.at[1], (), H_G1, xg1, (), grow)
    for start, count in chunks_of(rows, BACKWARD_ROWS):
        back = conv_rows(xg1, (), start, count, t_ref, 0).reshape(count, cells, TILE)
        for d in range(count):
            for h in range(height):
                row, side = h // 2 * tiles, slice(h % 2 * LANES, (h % 2 + 1) * LANES)
                scratch[start + d, pl.ds(h, tiles, stride=height), :] = back[
                    d, row : row + tiles, side
                ]
            for t in range(tiles):
                gv[start + d, :, t * LANES : (t + 1) * LANES] = scratch[
                    start + d, t * height : (t + 1) * height, :
                ].astype(jnp.bfloat16)


def add_body(one, two, out):
    out[...] = (one[...].astype(jnp.float32) + two[...].astype(jnp.float32)).astype(out.dtype)


def step_body(own, near, g1_far, message):
    lines = message.shape[0] - 2 * g1_far.shape[1]
    total = own[:lines].astype(jnp.float32) + near[:lines].astype(jnp.float32)
    message[:lines] = total.astype(message.dtype)
    put_row(message, g1_far[0])


def swapped(values, hop):
    count = lax.axis_size("depth")
    return lax.ppermute(values, "depth", [(i, i ^ hop) for i in range(count)])


def butterfly(values, hops):
    parts = [values]
    for hop in hops:
        if len(parts) > 1:
            parts = [call(add_body, [(values.shape, values.dtype)], [], parts)]
        parts.append(swapped(parts[0], hop))
    return parts


def neighbours(near, far):
    count = lax.axis_size("depth")
    result = []
    for values, first in ((near, 0), (far, 1)):
        partner = {}
        for i in range(first, count - 1, 2):
            partner[i], partner[i + 1] = i + 1, i
        pairs = [(i, partner.get(i, i)) for i in range(count)]
        result.append(lax.ppermute(values, "depth", pairs))
    return result


def over_sample(values, hop):
    groups = lax.axis_size("sample")
    return lax.ppermute(values, "sample", [(i, i ^ hop) for i in range(groups)])


def even_hops(values):
    return [over_sample(values, hop) for hop in range(2, lax.axis_size("sample"), 2)]


def all_hops(odd, evens):
    return [odd, *(crop for even in evens for crop in (even, over_sample(even, 1)))]


def traded(volume, cotangent, partner, tiles):
    groups = lax.axis_size("sample")
    rows, height, _ = volume.shape
    split = jnp.stack([volume, cotangent]).reshape(2, rows, height // 2, 2, tiles, LANES)
    split = split.transpose(0, 1, 2, 4, 3, 5).reshape(2, groups, -1, TILE)
    pieces = split.swapaxes(0, 1)
    spread = lax.all_to_all(pieces, "sample", split_axis=0, concat_axis=0, tiled=True)
    ids = jnp.arange(groups, dtype=jnp.int32)
    inverse = jnp.sum(jnp.where(partner[:, None] == ids[None, :], ids[:, None], 0), axis=0)
    wanted = jnp.stack([2 * partner, 2 * inverse, 2 * inverse + 1], axis=1)
    chosen = jnp.take(spread.reshape(2 * groups, -1, TILE), wanted, axis=0)
    joined = lax.all_to_all(chosen, "sample", split_axis=0, concat_axis=0, tiled=True)
    others = jnp.swapaxes(joined, 0, 1).reshape(3, rows, -1, TILE)
    return others[:2], others[2:]


def call(kernel, outs, scratch, inputs, macs=0, far=()):
    vmem, smem, anywhere = (
        pl.BlockSpec(memory_space=space) for space in (pltpu.VMEM, pltpu.SMEM, pl.ANY)
    )
    specs = [
        anywhere if at in far else smem if x.dtype == jnp.int32 else vmem
        for at, x in enumerate(inputs)
    ]
    results = pl.pallas_call(
        kernel,
        out_shape=tuple(jax.ShapeDtypeStruct(shape, dtype) for shape, dtype in outs),
        in_specs=specs,
        out_specs=(vmem,) * len(outs),
        scratch_shapes=scratch,
        compiler_params=pltpu.CompilerParams(vmem_limit_bytes=VMEM_LIMIT),
        cost_estimate=pl.CostEstimate(
            flops=2 * macs, bytes_accessed=2**22 if macs else 1, transcendentals=0
        ),
    )(*inputs)
    return results if len(results) > 1 else results[0]


def per_device(volume, kernels, partner, cotangent):
    volume, cotangent = volume[0], cotangent[0]
    rows, height, lanes = volume.shape
    pairs, tiles = height // 2, lanes // LANES
    cells = pairs * tiles
    groups, count = lax.axis_size("sample"), lax.axis_size("depth")
    depth = rows * count
    layers, taps, width = kernels.shape
    bf16, f32 = jnp.bfloat16, jnp.float32
    row_macs = 3 * cells * WIDE * TILE
    packed_rows = taps * CH // CELLS
    wide = lambda *lead: pltpu.VMEM((*lead, cells, WIDE), bf16)
    field = lambda *lead: ((*lead, cells, TILE), bf16)
    raw_tiles = lambda *lead: pltpu.VMEM((*lead, height * tiles, LANES), f32)
    banded = ((layers, 3, WIDE, TILE), bf16)
    spread_taps = ((layers, taps * CH, LANES), bf16)
    rw = pltpu.VMEM((CELLS, taps * CH, LANES), f32)

    direct = groups in (2, 4, 8)
    evens = even_hops(volume) if direct else []
    both, edges = lax.optimization_barrier((jnp.stack([volume, cotangent]), volume))
    near, far = neighbours(edges, edges)
    packed = kernels.reshape(layers, packed_rows, LANES)
    ids = jnp.clip(partner, 0, groups - 1)
    fwd_taps, bwd_taps = call(
        functools.partial(taps_body, taps),
        [spread_taps, spread_taps],
        [pltpu.VMEM((layers, -(-taps // CELLS) * LANES, LANES), f32)],
        [packed],
        2**28,
    )
    evens, both, ids, own_crop, late = lax.optimization_barrier(
        (evens, both, ids, volume, cotangent)
    )
    edge = ((2, H_VOL, cells, TILE), bf16)
    if direct:
        crops = all_hops(over_sample(own_crop, 1), evens)
        crops, near, far = lax.optimization_barrier((crops, near, far))
        vol, vol_near, vol_far = call(
            functools.partial(select_body, tuple(range(groups))),
            [field(2, rows), edge, edge],
            [raw_tiles(2, rows)],
            [ids, both, *crops],
        )
        sides = neighbours(vol_near, vol_far)
        evens, vol = lax.optimization_barrier((even_hops(late), vol))
        give = call(pick_body, [((1, rows, height, lanes), bf16)], [], [ids, both, *evens])
        cot_other = call(
            functools.partial(select_body, tuple(range(0, groups, 2))),
            [field(1, rows)],
            [raw_tiles(1, rows)],
            [ids, both, *evens, over_sample(give, 1)],
        )
    else:
        vol, cot_other = traded(volume, cotangent, partner, tiles)
        sides = neighbours(vol, vol)
    hid_rows = rows + 2 * H_HIDDEN
    fwd, hid_own, sl1, xv_own, cot_own = call(
        functools.partial(own_body, pairs, tiles),
        [
            banded,
            field(hid_rows),
            ((rows, cells, TILE), f32),
            ((rows + 2, cells, WIDE), bf16),
            field(rows),
        ],
        [wide(rows + 2 * H_VOL), pltpu.VMEM((3, rows, cells, TILE), bf16), raw_tiles(4 * rows)],
        [fwd_taps, near, both, far],
        hid_rows * row_macs,
    )

    g3, g3_near, g3_far, sl2, xb_own, xs_own = call(
        functools.partial(forward_body, depth, pairs, tiles),
        [
            field(2, rows),
            field(2, H_G3),
            field(2, H_G3),
            ((2, rows + 2 * H_TWO, cells, TILE), f32),
            ((rows + 2, cells, WIDE), bf16),
            ((rows + 2, cells, WIDE), bf16),
        ],
        [
            wide(2, rows + 2 * H_VOL),
            pltpu.VMEM((2, hid_rows, cells, TILE), bf16),
            wide(2, hid_rows),
            wide(2, rows + 2),
        ],
        [sides[0], vol, sides[1], hid_own, cot_own, cot_other, fwd],
        (2 * hid_rows + 2 * (rows + 2) + 2 * rows) * row_macs,
    )

    near, far = neighbours(g3_near, g3_far)
    terms = ((packed_rows, LANES), bf16)
    bwd, three = call(
        between_body, [banded, terms], [rw], [bwd_taps, xs_own, g3], rows * row_macs
    )
    hops = [3] if count == 4 else [2**i for i in range(1, count.bit_length() - 1)]
    three_near = swapped(three, 1)
    three_near, near, far = lax.optimization_barrier((three_near, near, far))
    three = call(add_body, [((packed_rows, LANES), bf16)], [], [three, three_near])
    three = butterfly(three, hops)
    lines = 2 * packed_rows
    message = ((lines + 2 * cells, LANES), bf16)
    g1, g1_far, own = call(
        functools.partial(back_body, depth, pairs, tiles),
        [field(rows), ((H_G1, cells, TILE), bf16), message],
        [
            wide(2, rows + 2 * H_G3),
            wide(2, rows + 2 * H_G2),
            rw,
            pltpu.VMEM((H_G1, cells, TILE), bf16),
            pltpu.VMEM((lines, LANES), f32),
        ],
        [near, g3, far, sl1, sl2, xv_own, xb_own, bwd],
        (6 * rows + 4) * row_macs,
    )
    own, three = lax.optimization_barrier((own, three))
    near = swapped(own, 1)
    summed = call(step_body, [message], [], [own, near, g1_far])
    others = butterfly(summed, hops)
    far = others[1] if hops == [3] else neighbours(summed, summed)[1]
    grad_volume, total = call(
        functools.partial(last_body, pairs, tiles),
        [((rows, height, lanes), bf16), ((layers * packed_rows, LANES), f32)],
        [raw_tiles(rows), wide(rows + 2 * H_G1), pltpu.VMEM((2, H_G1, cells, TILE), bf16)],
        [near, g1, far, bwd, *others, *three],
        rows * row_macs,
    )
    return (grad_volume[None], total.reshape(1, layers, taps, width))


def solution(mesh):
    in_specs = (P("sample", "depth", None, None), P(), P(), P("sample", "depth", None, None))
    out_specs = (P("sample", "depth", None, None), P("sample", None, None, None))
    return jax.shard_map(
        per_device, mesh=mesh, in_specs=in_specs, out_specs=out_specs, check_vma=False
    )
```

```python
import functools

import jax
import jax.numpy as jnp
from jax import lax
from jax.experimental import pallas as pl
from jax.experimental.pallas import tpu as pltpu
from jax.sharding import PartitionSpec as P

CH = 32
OWN_SHARE = 0.6
PARTNER_SHARE = 0.4
LANES = 128
CELLS = LANES // CH
TILE = 2 * LANES
WIDE = 3 * TILE
VMEM_LIMIT = 40 * 2**20
FORWARD_ROWS, BACKWARD_ROWS = 2, 6

SLOTS = (
    [(1 + h, 1 + w) for h in range(2) for w in range(CELLS)]
    + [(0, 1 + w) for w in range(CELLS)]
    + [(3, 1 + w) for w in range(CELLS)]
    + [(1, 5), (0, 0), (0, 5), (1, 0)]
    + [(2, 5), (3, 0), (3, 5), (2, 0)]
)
SLOT_OF = {cell: at for at, cell in enumerate(SLOTS)}

H_VOL, H_HIDDEN, H_TWO, H_G3, H_G2, H_G1 = 3, 2, 1, 2, 1, 1


def chunks_of(rows, most):
    count = -(-rows // most)
    base, extra = divmod(rows, count)
    start, result = 0, []
    for index in range(count):
        size = base + (index < extra)
        result.append((start, size))
        start += size
    return result


def sigmoid(v):
    return 0.5 + 0.5 * jnp.tanh(0.5 * v)


def lanes_of(t):
    return slice(t * LANES, (t + 1) * LANES)


def taps_body(taps, kr_ref, fwd_ref, bwd_ref, scratch):
    layers, rows = kr_ref.shape[:2]
    part = scratch.shape[1] // CELLS // CH
    shape = (LANES, CELLS * LANES)
    lane = lax.broadcasted_iota(jnp.int32, shape, 1)
    chosen = lax.broadcasted_iota(jnp.int32, shape, 0) == lane // LANES * CH + lane % CH
    spread = jnp.where(chosen, 1.0, 0.0).astype(jnp.bfloat16)
    for layer in range(layers):
        groups = jnp.dot(kr_ref[layer], spread, preferred_element_type=jnp.float32)
        for q in range(CELLS):
            scratch[layer, pl.ds(q, rows, stride=CELLS), :] = groups[:, lanes_of(q)]
        scratch[layer, taps * CH :, :] = jnp.zeros_like(scratch[layer, taps * CH :, :])
        fwd_ref[layer] = scratch[layer, : taps * CH].astype(jnp.bfloat16)
        cell = lax.broadcasted_iota(jnp.int32, (part * CH, LANES), 1) // CH
        compact = jnp.zeros((part * CH, LANES), jnp.float32)
        for group in range(CELLS):
            at = group * part * CH
            compact = jnp.where(cell == group, scratch[layer, at : at + part * CH, :], compact)
        room = -(-part // CELLS) * LANES - part * CH
        turned = jnp.concatenate([compact, jnp.zeros((room, LANES), jnp.float32)], 0).T
        stacked = jnp.concatenate(
            [turned[:, lanes_of(t)] for t in range(turned.shape[1] // LANES)], 0
        ).astype(jnp.bfloat16)
        groups = jnp.dot(stacked, spread, preferred_element_type=jnp.float32)
        for tap in range(taps):
            group, index = divmod(tap, part)
            at, row = taps - 1 - tap, index // CELLS * LANES + group * CH
            bwd_ref[layer, at * CH : (at + 1) * CH, :] = groups[
                row : row + CH, lanes_of(index % CELLS)
            ].astype(jnp.bfloat16)


def fill_weights(taps_ref, t_ref):
    cell = lax.broadcasted_iota(jnp.int32, (CH, LANES), 1) // CH
    zero = jnp.zeros((CH, LANES), jnp.bfloat16)
    for layer in range(t_ref.shape[0]):
        for a in range(3):
            bands = {}
            for b in range(3):
                first = (a * 9 + b * 3) * CH
                values = [taps_ref[layer, first + c * CH : first + (c + 1) * CH, :] for c in range(3)]
                for ww in range(CELLS + 2):
                    band = zero
                    for c in range(3):
                        if 0 <= ww - c < CELLS:
                            band = jnp.where(cell == ww - c, values[c], band)
                    bands[b, ww] = band
            for at, (hh, ww) in enumerate(SLOTS):
                for h in range(2):
                    t_ref[
                        layer, a, at * CH : (at + 1) * CH, h * LANES : (h + 1) * LANES
                    ] = bands.get((hh - h, ww), zero)


def edge_masks(tiles):
    shape = (1, tiles, TILE)
    cell = lax.broadcasted_iota(jnp.int32, shape, 2) % LANES // CH
    row = lax.broadcasted_iota(jnp.int32, shape, 1)
    from_before = (cell == CELLS - 1) & (row > 0)
    from_after = (cell == 0) & (row < tiles - 1)
    return tuple(
        jnp.where(mask, 1.0, 0.0).astype(jnp.bfloat16) for mask in (from_before, from_after)
    )


def expand(x, out_ref, lead, pairs, tiles, masks):
    x = x.reshape(pairs, tiles, TILE)
    edge = pltpu.roll(x, 1, 1) * masks[0] + pltpu.roll(x, tiles - 1, 1) * masks[1]
    e0, e1 = edge[..., :LANES], edge[..., LANES:]
    r0, r1 = pltpu.roll(e0, LANES // 2, 2), pltpu.roll(e1, LANES // 2, 2)
    zero = jnp.zeros((1, tiles, LANES), x.dtype)
    low = jnp.concatenate([zero, x[:-1, :, LANES:]], 0)
    high = jnp.concatenate([x[1:, :, :LANES], zero], 0)
    e0 = e0 + jnp.concatenate([zero, r1[:-1]], 0)
    e1 = e1 + jnp.concatenate([r0[1:], zero], 0)
    flat = lambda v: v.reshape(pairs * tiles, v.shape[-1])
    out_ref[(*lead, slice(None), slice(0, TILE))] = flat(x)
    out_ref[(*lead, slice(None), slice(TILE, TILE + LANES))] = flat(low)
    out_ref[(*lead, slice(None), slice(TILE + LANES, 2 * TILE))] = flat(high)
    out_ref[(*lead, slice(None), slice(2 * TILE, 2 * TILE + LANES))] = flat(e0)
    out_ref[(*lead, slice(None), slice(2 * TILE + LANES, WIDE))] = flat(e1)


def conv_rows(x_ref, lead, start, rows, t_ref, layer):
    blocks = [x_ref[(*lead, pl.ds(start + a, rows))].reshape(-1, WIDE) for a in range(3)]
    return jnp.dot(
        jnp.concatenate(blocks, axis=1),
        t_ref[layer].reshape(3 * WIDE, TILE),
        preferred_element_type=jnp.float32,
    )


def slope_of(pre, gate):
    return gate * (1.0 + pre * (1.0 - gate))


def rounded(v):
    return v.astype(jnp.bfloat16)


def inside(v, row, depth):
    return jnp.where((row >= 0) & (row < depth), v, 0.0)


def either(flag, a, b):
    low = lambda *at: jnp.where(flag, a[at], b[at])
    high = lambda *at: jnp.where(flag, b[at], a[at])
    return low, high


def widen(near, own, far, lead, halo, x_ref, x_lead, grow):
    at, last = lax.axis_index("depth"), lax.axis_size("depth") - 1
    low, high = either(at % 2 == 1, near, far)
    held, rows = near.shape[len(lead)], own.shape[len(lead)]
    for d in range(halo):
        row = low(*lead, held - halo + d)
        if d == halo - 1:
            row = jnp.where(at > 0, row, jnp.zeros_like(row))
        grow(row, x_ref, (*x_lead, d))
    for d in range(rows):
        grow(own[(*lead, d)], x_ref, (*x_lead, halo + d))
    for d in range(halo):
        row = high(*lead, d)
        if d == 0:
            row = jnp.where(at < last, row, jnp.zeros_like(row))
        grow(row, x_ref, (*x_lead, halo + rows + d))


def edge_rows(values, near, far, halo):
    odd = lax.axis_index("depth") % 2 == 1
    rows = values.shape[0]
    for d in range(halo):
        up, down = values[rows - halo + d], values[d]
        near[d] = jnp.where(odd, down, up)
        far[d] = jnp.where(odd, up, down)


def layer_one(xv, lead, out_ref, t_ref, slopes_ref=None):
    rows, cells = out_ref.shape[len(lead)], out_ref.shape[-2]
    for start, count in chunks_of(rows, FORWARD_ROWS):
        pre = conv_rows(xv, lead, start, count, t_ref, 0)
        gate = sigmoid(pre)
        value = (pre * gate).astype(jnp.bfloat16).reshape(count, cells, TILE)
        out_ref[(*lead, pl.ds(start, count))] = value
        if slopes_ref is not None:
            slope = slope_of(pre, gate).reshape(count, cells, TILE)
            for d in range(count):
                to = start + d - H_HIDDEN
                if 0 <= to < slopes_ref.shape[0]:
                    slopes_ref[to] = slope[d]


def tiled_rows(load, height, tiles, scratch, at):
    for t in range(tiles):
        scratch[at, t * height : (t + 1) * height, :] = load(t).astype(jnp.float32)
    for h in range(height):
        piece = scratch[at, pl.ds(h, tiles, stride=height), :].astype(jnp.bfloat16)
        yield h // 2 * tiles, slice(h % 2 * LANES, (h % 2 + 1) * LANES), piece


def wanted_by(partner, crop, count):
    inverse = jnp.int32(0)
    for other in range(partner.shape[0]):
        inverse = jnp.where(partner[other] == crop, other, inverse)
    return (partner[crop], inverse)[2 - count :]


def pick_body(partner, both, *refs):
    *evens, out = refs
    own = lax.axis_index("sample")
    count = out.shape[0]
    for to, crop in enumerate(wanted_by(partner, own ^ 1, count)):
        for at, source in enumerate((both.at[2 - count], *evens)):

            @pl.when(crop ^ own == 2 * at)
            def _(to=to, source=source):
                out[to] = source[...]


def select_body(hops, partner, both, *refs):
    held, refs = (both, *refs[: len(hops) - 1]), refs[len(hops) - 1 :]
    own = lax.axis_index("sample")
    _, rows, height, lanes = both.shape
    tiles = lanes // LANES
    picked = len(hops) * 2 == lax.axis_size("sample")
    if picked:
        sent, *refs = refs
    out, *sides, scratch = refs
    count = out.shape[0]

    def spread(to, source):
        for d in range(rows):
            for t in range(tiles):
                scratch[to, d, t * height : (t + 1) * height, :] = source[
                    d, :, lanes_of(t)
                ].astype(jnp.float32)

    for to, crop in enumerate(wanted_by(partner, own, count)):
        for hop, source in zip(hops, held):
            source = both.at[2 - count] if hop == 0 else source
            pl.when(crop ^ own == hop)(functools.partial(spread, to, source))
        if picked:
            pl.when((crop ^ own) % 2 == 1)(functools.partial(spread, to, sent.at[to]))
        for d in range(rows):
            for h in range(height):
                piece = scratch[to, d, pl.ds(h, tiles, stride=height), :].astype(jnp.bfloat16)
                row, side = h // 2 * tiles, lanes_of(h % 2)
                out[to, d, row : row + tiles, side] = piece
        if sides:
            edge_rows(out.at[to], *(side.at[to] for side in sides), H_VOL)


def own_body(
    pairs, tiles,
    taps_ref, near, both, far,
    t_ref, hid, sl1, xv_own, cot_own,
    xv, field, scratch,
):
    _, rows, height, _ = both.shape
    fill_weights(taps_ref, t_ref)
    grow = functools.partial(expand, pairs=pairs, tiles=tiles, masks=edge_masks(tiles))
    for at, part in enumerate((near, both.at[0], far, both.at[1])):
        for d in range(rows):
            load = lambda t, part=part, d=d: part[d, :, lanes_of(t)]
            for row, side, piece in tiled_rows(load, height, tiles, scratch, at * rows + d):
                if at < 3:
                    field[at, d, row : row + tiles, side] = piece
                else:
                    cot_own[d, row : row + tiles, side] = piece
    widen(field.at[0], field.at[1], field.at[2], (), H_VOL, xv, (), grow)
    layer_one(xv, (), hid, t_ref, sl1)
    xv_own[...] = xv[H_VOL - 1 : H_VOL + rows + 1]


def forward_body(
    depth, pairs, tiles,
    near, mid, far, hid_own, cot_own, cot_other, t_ref,
    g3, g3_near, g3_far, sl2, xb_own, xs_own,
    xv, hid, xb, xs,
):
    rows = mid.shape[1]
    cells = pairs * tiles
    first = lax.axis_index("depth") * rows
    grow = functools.partial(expand, pairs=pairs, tiles=tiles, masks=edge_masks(tiles))

    for crop in range(2):
        widen(near, mid, far, (crop,), H_VOL, xv, (crop,), grow)
        layer_one(xv, (crop,), hid, t_ref)

    for d in range(rows + 2 * H_HIDDEN):
        own = hid_own[d].astype(jnp.float32)
        partner, other = hid[0, d].astype(jnp.float32), hid[1, d].astype(jnp.float32)
        row = first + d - H_HIDDEN
        for j, (a, b) in enumerate(((own, partner), (other, own))):
            mixed = OWN_SHARE * a + PARTNER_SHARE * b
            grow(rounded(inside(mixed, row, depth)), xb, (j, d))

    def middle(j, cot):
        for start, count in chunks_of(rows + 2 * H_TWO, FORWARD_ROWS):
            pre = conv_rows(xb, (j,), start, count, t_ref, 1)
            gate = sigmoid(pre)
            value = (pre * gate).reshape(count, cells, TILE)
            slope = slope_of(pre, gate).reshape(count, cells, TILE)
            for d in range(count):
                sl2[j, start + d] = slope[d]
                to = start + d - (H_TWO - 1)
                if 0 <= to < rows + 2:
                    grow(rounded(inside(value[d], first + to - 1, depth)), xs, (j, to))
        for start, count in chunks_of(rows, FORWARD_ROWS):
            pre = conv_rows(xs, (j,), start, count, t_ref, 2)
            slope = slope_of(pre, sigmoid(pre)).reshape(count, cells, TILE)
            for d in range(count):
                at = start + d
                grad = rounded(cot[at].astype(jnp.float32) * slope[d])
                g3[j, at] = grad

    middle(0, cot_own)
    middle(1, cot_other.at[0])
    for j in range(2):
        edge_rows(g3.at[j], g3_near.at[j], g3_far.at[j], H_G3)
    xb_own[...] = xb[0, H_HIDDEN - 1 : H_HIDDEN + rows + 1]
    xs_own[...] = xs[0]


def kernel_terms(values, gradient, rw):
    rows = gradient.shape[0]
    gradient = gradient.reshape(-1, TILE)
    for a in range(3):
        block = values[a : a + rows].reshape(-1, WIDE)
        terms = lax.dot_general(
            block, gradient, (((0,), (0,)), ((), ())), preferred_element_type=jnp.float32
        )
        for b in range(3):
            for c in range(3):
                at = (a * 9 + b * 3 + c) * CH
                for w in range(CELLS):
                    s0, s1 = SLOT_OF[b, w + c] * CH, SLOT_OF[b + 1, w + c] * CH
                    rw[w, at : at + CH] = (
                        terms[s0 : s0 + CH, :LANES] + terms[s1 : s1 + CH, LANES:]
                    )
    count = rw.shape[1] // CELLS
    cell = lax.broadcasted_iota(jnp.int32, (count, LANES), 1) // CH
    dense = jnp.zeros((count, LANES), jnp.float32)
    for q in range(CELLS):
        part = None
        for w in range(CELLS):
            piece = rw[w, pl.ds(q, count, stride=CELLS), :]
            if q != w:
                piece = pltpu.roll(piece, (q - w) % CELLS * CH, 1)
            part = piece if part is None else part + piece
        dense = jnp.where(cell == q, part, dense)
    return dense.astype(jnp.bfloat16)


def between_body(taps_ref, xs_own, g3, t_ref, terms, rw):
    fill_weights(taps_ref, t_ref)
    terms[...] = kernel_terms(xs_own[...], g3[0], rw)


def back_two(j, x_ref, sl2, x2_ref, t_ref, first, depth, grow):
    rows, cells = x2_ref.shape[-3:-1]
    for start, count in chunks_of(rows, BACKWARD_ROWS):
        back = conv_rows(x_ref, (), start, count, t_ref, 2).reshape(count, cells, TILE)
        for d in range(count):
            at = start + d
            grad = inside(back[d] * sl2[j, at], first + at - H_G2, depth)
            grow(rounded(grad), x2_ref, (at,))


def put_row(message, row):
    half = row.shape[0]
    message[message.shape[0] - 2 * half : message.shape[0] - half] = row[:, :LANES]
    message[message.shape[0] - half :] = row[:, LANES:]


def back_body(
    depth, pairs, tiles,
    near, mid, far, sl1, sl2, xv_own, xb_own, t_ref,
    g1, g1_far, message,
    xg3, xg2, rw, g1_near, terms,
):
    rows = mid.shape[1]
    cells = pairs * tiles
    first = lax.axis_index("depth") * rows
    grow = functools.partial(expand, pairs=pairs, tiles=tiles, masks=edge_masks(tiles))
    for j in range(2):
        widen(near, mid, far, (j,), H_G3, xg3.at[j], (), grow)
        back_two(j, xg3.at[j], sl2, xg2.at[j], t_ref, first, depth, grow)
    own, other = (
        rounded(conv_rows(xg2, (j,), 0, rows, t_ref, 1)).astype(jnp.float32) for j in range(2)
    )
    mixed = (OWN_SHARE * own + PARTNER_SHARE * other).reshape(rows, cells, TILE)
    g1[...] = rounded(mixed * sl1[...])
    edge_rows(g1, g1_near, g1_far, H_G1)
    size = terms.shape[0] // 2
    terms[:size] = kernel_terms(xv_own[...], g1[...], rw).astype(jnp.float32)
    two = kernel_terms(xb_own[...], xg2[0, H_G2 : H_G2 + rows, :, :TILE], rw)
    terms[size:] = two.astype(jnp.float32)
    message[: 2 * size] = terms[...].astype(jnp.bfloat16)
    put_row(message, g1_near[0])


def last_body(pairs, tiles, near, g1, far, t_ref, *refs):
    *parts, gv, total, scratch, xg1, sides = refs
    lines = near.shape[0] - 2 * g1.shape[1]
    half = len(parts) // 2
    add = lambda terms: functools.reduce(lambda a, b: a + b, terms)
    total[:lines] = add([part[:lines].astype(jnp.float32) for part in parts[:half]])
    total[lines:] = add([part[...].astype(jnp.float32) for part in parts[half:]])
    rows, height, _ = gv.shape
    cells = pairs * tiles
    grow = functools.partial(expand, pairs=pairs, tiles=tiles, masks=edge_masks(tiles))
    for at, message in enumerate((near, far)):
        first = message.shape[0] - 2 * cells
        sides[at, 0, :, :LANES] = message[first : first + cells]
        sides[at, 0, :, LANES:] = message[first + cells :]
    widen(sides.at[0], g1, sides.at[1], (), H_G1, xg1, (), grow)
    for start, count in chunks_of(rows, BACKWARD_ROWS):
        back = conv_rows(xg1, (), start, count, t_ref, 0).reshape(count, cells, TILE)
        for d in range(count):
            for h in range(height):
                row, side = h // 2 * tiles, slice(h % 2 * LANES, (h % 2 + 1) * LANES)
                scratch[start + d, pl.ds(h, tiles, stride=height), :] = back[
                    d, row : row + tiles, side
                ]
            for t in range(tiles):
                gv[start + d, :, t * LANES : (t + 1) * LANES] = scratch[
                    start + d, t * height : (t + 1) * height, :
                ].astype(jnp.bfloat16)


def add_body(one, two, out):
    out[...] = (one[...].astype(jnp.float32) + two[...].astype(jnp.float32)).astype(out.dtype)


def step_body(own, near, g1_far, message):
    lines = message.shape[0] - 2 * g1_far.shape[1]
    total = own[:lines].astype(jnp.float32) + near[:lines].astype(jnp.float32)
    message[:lines] = total.astype(message.dtype)
    put_row(message, g1_far[0])


def swapped(values, hop):
    count = lax.axis_size("depth")
    return lax.ppermute(values, "depth", [(i, i ^ hop) for i in range(count)])


def butterfly(values, hops):
    parts = [values]
    for hop in hops:
        if len(parts) > 1:
            parts = [call(add_body, [(values.shape, values.dtype)], [], parts)]
        parts.append(swapped(parts[0], hop))
    return parts


def neighbours(near, far):
    count = lax.axis_size("depth")
    result = []
    for values, first in ((near, 0), (far, 1)):
        partner = {}
        for i in range(first, count - 1, 2):
            partner[i], partner[i + 1] = i + 1, i
        pairs = [(i, partner.get(i, i)) for i in range(count)]
        result.append(lax.ppermute(values, "depth", pairs))
    return result


def over_sample(values, hop):
    groups = lax.axis_size("sample")
    return lax.ppermute(values, "sample", [(i, i ^ hop) for i in range(groups)])


def even_hops(values):
    return [over_sample(values, hop) for hop in range(2, lax.axis_size("sample"), 2)]


def all_hops(odd, evens):
    return [odd, *(crop for even in evens for crop in (even, over_sample(even, 1)))]


def traded(volume, cotangent, partner, tiles):
    groups = lax.axis_size("sample")
    rows, height, _ = volume.shape
    split = jnp.stack([volume, cotangent]).reshape(2, rows, height // 2, 2, tiles, LANES)
    split = split.transpose(0, 1, 2, 4, 3, 5).reshape(2, groups, -1, TILE)
    pieces = split.swapaxes(0, 1)
    spread = lax.all_to_all(pieces, "sample", split_axis=0, concat_axis=0, tiled=True)
    ids = jnp.arange(groups, dtype=jnp.int32)
    inverse = jnp.sum(jnp.where(partner[:, None] == ids[None, :], ids[:, None], 0), axis=0)
    wanted = jnp.stack([2 * partner, 2 * inverse, 2 * inverse + 1], axis=1)
    chosen = jnp.take(spread.reshape(2 * groups, -1, TILE), wanted, axis=0)
    joined = lax.all_to_all(chosen, "sample", split_axis=0, concat_axis=0, tiled=True)
    others = jnp.swapaxes(joined, 0, 1).reshape(3, rows, -1, TILE)
    return others[:2], others[2:]


def call(kernel, outs, scratch, inputs, macs=0, far=()):
    vmem, smem, anywhere = (
        pl.BlockSpec(memory_space=space) for space in (pltpu.VMEM, pltpu.SMEM, pl.ANY)
    )
    specs = [
        anywhere if at in far else smem if x.dtype == jnp.int32 else vmem
        for at, x in enumerate(inputs)
    ]
    results = pl.pallas_call(
        kernel,
        out_shape=tuple(jax.ShapeDtypeStruct(shape, dtype) for shape, dtype in outs),
        in_specs=specs,
        out_specs=(vmem,) * len(outs),
        scratch_shapes=scratch,
        compiler_params=pltpu.CompilerParams(vmem_limit_bytes=VMEM_LIMIT),
        cost_estimate=pl.CostEstimate(
            flops=2 * macs, bytes_accessed=2**22 if macs else 1, transcendentals=0
        ),
    )(*inputs)
    return results if len(results) > 1 else results[0]


def per_device(volume, kernels, partner, cotangent):
    volume, cotangent = volume[0], cotangent[0]
    rows, height, lanes = volume.shape
    pairs, tiles = height // 2, lanes // LANES
    cells = pairs * tiles
    groups, count = lax.axis_size("sample"), lax.axis_size("depth")
    depth = rows * count
    layers, taps, width = kernels.shape
    bf16, f32 = jnp.bfloat16, jnp.float32
    row_macs = 3 * cells * WIDE * TILE
    packed_rows = taps * CH // CELLS
    wide = lambda *lead: pltpu.VMEM((*lead, cells, WIDE), bf16)
    field = lambda *lead: ((*lead, cells, TILE), bf16)
    raw_tiles = lambda *lead: pltpu.VMEM((*lead, height * tiles, LANES), f32)
    banded = ((layers, 3, WIDE, TILE), bf16)
    spread_taps = ((layers, taps * CH, LANES), bf16)
    rw = pltpu.VMEM((CELLS, taps * CH, LANES), f32)

    direct = groups in (2, 4, 8)
    evens = even_hops(volume) if direct else []
    both, edges = lax.optimization_barrier((jnp.stack([volume, cotangent]), volume))
    near, far = neighbours(edges, edges)
    packed = kernels.reshape(layers, packed_rows, LANES)
    ids = jnp.clip(partner, 0, groups - 1)
    fwd_taps, bwd_taps = call(
        functools.partial(taps_body, taps),
        [spread_taps, spread_taps],
        [pltpu.VMEM((layers, -(-taps // CELLS) * LANES, LANES), f32)],
        [packed],
        2**28,
    )
    evens, both, ids, fwd_taps, bwd_taps, own_crop, late = lax.optimization_barrier(
        (evens, both, ids, fwd_taps, bwd_taps, volume, cotangent)
    )
    edge = ((2, H_VOL, cells, TILE), bf16)
    if direct:
        crops = all_hops(over_sample(own_crop, 1), evens)
        crops, near, far = lax.optimization_barrier((crops, near, far))
        vol, vol_near, vol_far = call(
            functools.partial(select_body, tuple(range(groups))),
            [field(2, rows), edge, edge],
            [raw_tiles(2, rows)],
            [ids, both, *crops],
        )
        sides = neighbours(vol_near, vol_far)
        evens, vol = lax.optimization_barrier((even_hops(late), vol))
        give = call(pick_body, [((1, rows, height, lanes), bf16)], [], [ids, both, *evens])
        cot_other = call(
            functools.partial(select_body, tuple(range(0, groups, 2))),
            [field(1, rows)],
            [raw_tiles(1, rows)],
            [ids, both, *evens, over_sample(give, 1)],
        )
    else:
        vol, cot_other = traded(volume, cotangent, partner, tiles)
        sides = neighbours(vol, vol)
    hid_rows = rows + 2 * H_HIDDEN
    fwd, hid_own, sl1, xv_own, cot_own = call(
        functools.partial(own_body, pairs, tiles),
        [
            banded,
            field(hid_rows),
            ((rows, cells, TILE), f32),
            ((rows + 2, cells, WIDE), bf16),
            field(rows),
        ],
        [wide(rows + 2 * H_VOL), pltpu.VMEM((3, rows, cells, TILE), bf16), raw_tiles(4 * rows)],
        [fwd_taps, near, both, far],
        hid_rows * row_macs,
    )

    g3, g3_near, g3_far, sl2, xb_own, xs_own = call(
        functools.partial(forward_body, depth, pairs, tiles),
        [
            field(2, rows),
            field(2, H_G3),
            field(2, H_G3),
            ((2, rows + 2 * H_TWO, cells, TILE), f32),
            ((rows + 2, cells, WIDE), bf16),
            ((rows + 2, cells, WIDE), bf16),
        ],
        [
            wide(2, rows + 2 * H_VOL),
            pltpu.VMEM((2, hid_rows, cells, TILE), bf16),
            wide(2, hid_rows),
            wide(2, rows + 2),
        ],
        [sides[0], vol, sides[1], hid_own, cot_own, cot_other, fwd],
        (2 * hid_rows + 2 * (rows + 2) + 2 * rows) * row_macs,
    )

    near, far = neighbours(g3_near, g3_far)
    terms = ((packed_rows, LANES), bf16)
    bwd, three = call(
        between_body, [banded, terms], [rw], [bwd_taps, xs_own, g3], rows * row_macs
    )
    hops = [3] if count == 4 else [2**i for i in range(1, count.bit_length() - 1)]
    three_near = swapped(three, 1)
    lines = 2 * packed_rows
    message = ((lines + 2 * cells, LANES), bf16)
    g1, g1_far, own = call(
        functools.partial(back_body, depth, pairs, tiles),
        [field(rows), ((H_G1, cells, TILE), bf16), message],
        [
            wide(2, rows + 2 * H_G3),
            wide(2, rows + 2 * H_G2),
            rw,
            pltpu.VMEM((H_G1, cells, TILE), bf16),
            pltpu.VMEM((lines, LANES), f32),
        ],
        [near, g3, far, sl1, sl2, xv_own, xb_own, bwd],
        (6 * rows + 4) * row_macs,
    )
    own, three, three_near = lax.optimization_barrier((own, three, three_near))
    near = swapped(own, 1)
    three = call(add_body, [((packed_rows, LANES), bf16)], [], [three, three_near])
    near, three = lax.optimization_barrier((near, butterfly(three, hops)))
    summed = call(step_body, [message], [], [own, near, g1_far])
    others = butterfly(summed, hops)
    far = others[1] if hops == [3] else neighbours(summed, summed)[1]
    grad_volume, total = call(
        functools.partial(last_body, pairs, tiles),
        [((rows, height, lanes), bf16), ((layers * packed_rows, LANES), f32)],
        [raw_tiles(rows), wide(rows + 2 * H_G1), pltpu.VMEM((2, H_G1, cells, TILE), bf16)],
        [near, g1, far, bwd, *others, *three],
        rows * row_macs,
    )
    return (grad_volume[None], total.reshape(1, layers, taps, width))


def solution(mesh):
    in_specs = (P("sample", "depth", None, None), P(), P(), P("sample", "depth", None, None))
    out_specs = (P("sample", "depth", None, None), P("sample", None, None, None))
    return jax.shard_map(
        per_device, mesh=mesh, in_specs=in_specs, out_specs=out_specs, check_vma=False
    )
```

```python
import functools

import jax
import jax.numpy as jnp
from jax import lax
from jax.experimental import pallas as pl
from jax.experimental.pallas import tpu as pltpu
from jax.sharding import PartitionSpec as P

CH = 32
OWN_SHARE = 0.6
PARTNER_SHARE = 0.4
LANES = 128
CELLS = LANES // CH
TILE = 2 * LANES
WIDE = 3 * TILE
VMEM_LIMIT = 40 * 2**20
FORWARD_ROWS, BACKWARD_ROWS = 2, 3

SLOTS = (
    [(1 + h, 1 + w) for h in range(2) for w in range(CELLS)]
    + [(0, 1 + w) for w in range(CELLS)]
    + [(3, 1 + w) for w in range(CELLS)]
    + [(1, 5), (0, 0), (0, 5), (1, 0)]
    + [(2, 5), (3, 0), (3, 5), (2, 0)]
)
SLOT_OF = {cell: at for at, cell in enumerate(SLOTS)}

H_VOL, H_HIDDEN, H_TWO, H_G3, H_G2, H_G1 = 3, 2, 1, 2, 1, 1


def chunks_of(rows, most):
    count = -(-rows // most)
    base, extra = divmod(rows, count)
    start, result = 0, []
    for index in range(count):
        size = base + (index < extra)
        result.append((start, size))
        start += size
    return result


def sigmoid(v):
    return 0.5 + 0.5 * jnp.tanh(0.5 * v)


def lanes_of(t):
    return slice(t * LANES, (t + 1) * LANES)


def taps_body(taps, kr_ref, fwd_ref, bwd_ref, scratch):
    layers, rows = kr_ref.shape[:2]
    part = scratch.shape[1] // CELLS // CH
    shape = (LANES, CELLS * LANES)
    lane = lax.broadcasted_iota(jnp.int32, shape, 1)
    chosen = lax.broadcasted_iota(jnp.int32, shape, 0) == lane // LANES * CH + lane % CH
    spread = jnp.where(chosen, 1.0, 0.0).astype(jnp.bfloat16)
    for layer in range(layers):
        groups = jnp.dot(kr_ref[layer], spread, preferred_element_type=jnp.float32)
        for q in range(CELLS):
            scratch[layer, pl.ds(q, rows, stride=CELLS), :] = groups[:, lanes_of(q)]
        scratch[layer, taps * CH :, :] = jnp.zeros_like(scratch[layer, taps * CH :, :])
        fwd_ref[layer] = scratch[layer, : taps * CH].astype(jnp.bfloat16)
        cell = lax.broadcasted_iota(jnp.int32, (part * CH, LANES), 1) // CH
        compact = jnp.zeros((part * CH, LANES), jnp.float32)
        for group in range(CELLS):
            at = group * part * CH
            compact = jnp.where(cell == group, scratch[layer, at : at + part * CH, :], compact)
        room = -(-part // CELLS) * LANES - part * CH
        turned = jnp.concatenate([compact, jnp.zeros((room, LANES), jnp.float32)], 0).T
        stacked = jnp.concatenate(
            [turned[:, lanes_of(t)] for t in range(turned.shape[1] // LANES)], 0
        ).astype(jnp.bfloat16)
        groups = jnp.dot(stacked, spread, preferred_element_type=jnp.float32)
        for tap in range(taps):
            group, index = divmod(tap, part)
            at, row = taps - 1 - tap, index // CELLS * LANES + group * CH
            bwd_ref[layer, at * CH : (at + 1) * CH, :] = groups[
                row : row + CH, lanes_of(index % CELLS)
            ].astype(jnp.bfloat16)


def fill_weights(taps_ref, t_ref):
    cell = lax.broadcasted_iota(jnp.int32, (CH, LANES), 1) // CH
    zero = jnp.zeros((CH, LANES), jnp.bfloat16)
    for layer in range(t_ref.shape[0]):
        for a in range(3):
            bands = {}
            for b in range(3):
                first = (a * 9 + b * 3) * CH
                values = [taps_ref[layer, first + c * CH : first + (c + 1) * CH, :] for c in range(3)]
                for ww in range(CELLS + 2):
                    band = zero
                    for c in range(3):
                        if 0 <= ww - c < CELLS:
                            band = jnp.where(cell == ww - c, values[c], band)
                    bands[b, ww] = band
            for at, (hh, ww) in enumerate(SLOTS):
                for h in range(2):
                    t_ref[
                        layer, a, at * CH : (at + 1) * CH, h * LANES : (h + 1) * LANES
                    ] = bands.get((hh - h, ww), zero)


def edge_masks(tiles):
    shape = (1, tiles, TILE)
    cell = lax.broadcasted_iota(jnp.int32, shape, 2) % LANES // CH
    row = lax.broadcasted_iota(jnp.int32, shape, 1)
    from_before = (cell == CELLS - 1) & (row > 0)
    from_after = (cell == 0) & (row < tiles - 1)
    return tuple(
        jnp.where(mask, 1.0, 0.0).astype(jnp.bfloat16) for mask in (from_before, from_after)
    )


def expand(x, out_ref, lead, pairs, tiles, masks):
    x = x.reshape(pairs, tiles, TILE)
    edge = pltpu.roll(x, 1, 1) * masks[0] + pltpu.roll(x, tiles - 1, 1) * masks[1]
    e0, e1 = edge[..., :LANES], edge[..., LANES:]
    r0, r1 = pltpu.roll(e0, LANES // 2, 2), pltpu.roll(e1, LANES // 2, 2)
    zero = jnp.zeros((1, tiles, LANES), x.dtype)
    low = jnp.concatenate([zero, x[:-1, :, LANES:]], 0)
    high = jnp.concatenate([x[1:, :, :LANES], zero], 0)
    e0 = e0 + jnp.concatenate([zero, r1[:-1]], 0)
    e1 = e1 + jnp.concatenate([r0[1:], zero], 0)
    flat = lambda v: v.reshape(pairs * tiles, v.shape[-1])
    out_ref[(*lead, slice(None), slice(0, TILE))] = flat(x)
    out_ref[(*lead, slice(None), slice(TILE, TILE + LANES))] = flat(low)
    out_ref[(*lead, slice(None), slice(TILE + LANES, 2 * TILE))] = flat(high)
    out_ref[(*lead, slice(None), slice(2 * TILE, 2 * TILE + LANES))] = flat(e0)
    out_ref[(*lead, slice(None), slice(2 * TILE + LANES, WIDE))] = flat(e1)


def conv_rows(x_ref, lead, start, rows, t_ref, layer):
    blocks = [x_ref[(*lead, pl.ds(start + a, rows))].reshape(-1, WIDE) for a in range(3)]
    return jnp.dot(
        jnp.concatenate(blocks, axis=1),
        t_ref[layer].reshape(3 * WIDE, TILE),
        preferred_element_type=jnp.float32,
    )


def slope_of(pre, gate):
    return gate * (1.0 + pre * (1.0 - gate))


def rounded(v):
    return v.astype(jnp.bfloat16)


def inside(v, row, depth):
    return jnp.where((row >= 0) & (row < depth), v, 0.0)


def either(flag, a, b):
    low = lambda *at: jnp.where(flag, a[at], b[at])
    high = lambda *at: jnp.where(flag, b[at], a[at])
    return low, high


def widen(near, own, far, lead, halo, x_ref, x_lead, grow):
    at, last = lax.axis_index("depth"), lax.axis_size("depth") - 1
    low, high = either(at % 2 == 1, near, far)
    held, rows = near.shape[len(lead)], own.shape[len(lead)]
    for d in range(halo):
        row = low(*lead, held - halo + d)
        if d == halo - 1:
            row = jnp.where(at > 0, row, jnp.zeros_like(row))
        grow(row, x_ref, (*x_lead, d))
    for d in range(rows):
        grow(own[(*lead, d)], x_ref, (*x_lead, halo + d))
    for d in range(halo):
        row = high(*lead, d)
        if d == 0:
            row = jnp.where(at < last, row, jnp.zeros_like(row))
        grow(row, x_ref, (*x_lead, halo + rows + d))


def edge_rows(values, near, far, halo):
    odd = lax.axis_index("depth") % 2 == 1
    rows = values.shape[0]
    for d in range(halo):
        up, down = values[rows - halo + d], values[d]
        near[d] = jnp.where(odd, down, up)
        far[d] = jnp.where(odd, up, down)


def alternate(*crops):
    crops = list(crops)
    while crops:
        crops = [crop for crop in crops if next(crop, True) is None]


def layer_one(xv, lead, out_ref, t_ref, slopes_ref=None):
    rows, cells = out_ref.shape[len(lead)], out_ref.shape[-2]
    for start, count in chunks_of(rows, FORWARD_ROWS):
        pre = conv_rows(xv, lead, start, count, t_ref, 0)
        gate = sigmoid(pre)
        value = (pre * gate).astype(jnp.bfloat16).reshape(count, cells, TILE)
        out_ref[(*lead, pl.ds(start, count))] = value
        if slopes_ref is not None:
            slope = slope_of(pre, gate).reshape(count, cells, TILE)
            for d in range(count):
                to = start + d - H_HIDDEN
                if 0 <= to < slopes_ref.shape[0]:
                    slopes_ref[to] = slope[d]
        yield


def tiled_rows(load, height, tiles, scratch, at):
    for t in range(tiles):
        scratch[at, t * height : (t + 1) * height, :] = load(t).astype(jnp.float32)
    for h in range(height):
        piece = scratch[at, pl.ds(h, tiles, stride=height), :].astype(jnp.bfloat16)
        yield h // 2 * tiles, slice(h % 2 * LANES, (h % 2 + 1) * LANES), piece


def wanted_by(partner, crop, count):
    inverse = jnp.int32(0)
    for other in range(partner.shape[0]):
        inverse = jnp.where(partner[other] == crop, other, inverse)
    return (partner[crop], inverse)[2 - count :]


def pick_body(partner, both, *refs):
    *evens, out = refs
    own = lax.axis_index("sample")
    count = out.shape[0]
    for to, crop in enumerate(wanted_by(partner, own ^ 1, count)):
        for at, source in enumerate((both.at[2 - count], *evens)):

            @pl.when(crop ^ own == 2 * at)
            def _(to=to, source=source):
                out[to] = source[...]


def select_body(hops, partner, both, *refs):
    held, refs = (both, *refs[: len(hops) - 1]), refs[len(hops) - 1 :]
    own = lax.axis_index("sample")
    _, rows, height, lanes = both.shape
    tiles = lanes // LANES
    picked = len(hops) * 2 == lax.axis_size("sample")
    if picked:
        sent, *refs = refs
    out, *sides, scratch = refs
    count = out.shape[0]

    def spread(to, source):
        for d in range(rows):
            for t in range(tiles):
                scratch[to, d, t * height : (t + 1) * height, :] = source[
                    d, :, lanes_of(t)
                ].astype(jnp.float32)

    for to, crop in enumerate(wanted_by(partner, own, count)):
        for hop, source in zip(hops, held):
            source = both.at[2 - count] if hop == 0 else source
            pl.when(crop ^ own == hop)(functools.partial(spread, to, source))
        if picked:
            pl.when((crop ^ own) % 2 == 1)(functools.partial(spread, to, sent.at[to]))
        for d in range(rows):
            for h in range(height):
                piece = scratch[to, d, pl.ds(h, tiles, stride=height), :].astype(jnp.bfloat16)
                row, side = h // 2 * tiles, lanes_of(h % 2)
                out[to, d, row : row + tiles, side] = piece
        if sides:
            edge_rows(out.at[to], *(side.at[to] for side in sides), H_VOL)


def own_body(
    pairs, tiles,
    taps_ref, near, both, far,
    t_ref, hid, sl1, xv_own, cot_own,
    xv, field, scratch,
):
    _, rows, height, _ = both.shape
    fill_weights(taps_ref, t_ref)
    grow = functools.partial(expand, pairs=pairs, tiles=tiles, masks=edge_masks(tiles))
    for at, part in enumerate((near, both.at[0], far, both.at[1])):
        for d in range(rows):
            load = lambda t, part=part, d=d: part[d, :, lanes_of(t)]
            for row, side, piece in tiled_rows(load, height, tiles, scratch, at * rows + d):
                if at < 3:
                    field[at, d, row : row + tiles, side] = piece
                else:
                    cot_own[d, row : row + tiles, side] = piece
    widen(field.at[0], field.at[1], field.at[2], (), H_VOL, xv, (), grow)
    alternate(layer_one(xv, (), hid, t_ref, sl1))
    xv_own[...] = xv[H_VOL - 1 : H_VOL + rows + 1]


def forward_body(
    depth, pairs, tiles,
    near, mid, far, hid_own, cot_own, cot_other, t_ref,
    g3, g3_near, g3_far, sl2, xb_own, xs_own,
    xv, hid, xb, xs,
):
    rows = mid.shape[1]
    cells = pairs * tiles
    first = lax.axis_index("depth") * rows
    grow = functools.partial(expand, pairs=pairs, tiles=tiles, masks=edge_masks(tiles))

    for crop in range(2):
        widen(near, mid, far, (crop,), H_VOL, xv, (crop,), grow)
    alternate(*(layer_one(xv, (crop,), hid, t_ref) for crop in range(2)))

    for d in range(rows + 2 * H_HIDDEN):
        own = hid_own[d].astype(jnp.float32)
        partner, other = hid[0, d].astype(jnp.float32), hid[1, d].astype(jnp.float32)
        row = first + d - H_HIDDEN
        for j, (a, b) in enumerate(((own, partner), (other, own))):
            mixed = OWN_SHARE * a + PARTNER_SHARE * b
            grow(rounded(inside(mixed, row, depth)), xb, (j, d))

    def middle(j, cot):
        for start, count in chunks_of(rows + 2 * H_TWO, FORWARD_ROWS):
            pre = conv_rows(xb, (j,), start, count, t_ref, 1)
            gate = sigmoid(pre)
            value = (pre * gate).reshape(count, cells, TILE)
            slope = slope_of(pre, gate).reshape(count, cells, TILE)
            for d in range(count):
                sl2[j, start + d] = slope[d]
                to = start + d - (H_TWO - 1)
                if 0 <= to < rows + 2:
                    grow(rounded(inside(value[d], first + to - 1, depth)), xs, (j, to))
            yield
        for start, count in chunks_of(rows, FORWARD_ROWS):
            pre = conv_rows(xs, (j,), start, count, t_ref, 2)
            slope = slope_of(pre, sigmoid(pre)).reshape(count, cells, TILE)
            for d in range(count):
                at = start + d
                grad = rounded(cot[at].astype(jnp.float32) * slope[d])
                g3[j, at] = grad
            yield

    alternate(middle(0, cot_own), middle(1, cot_other.at[0]))
    for j in range(2):
        edge_rows(g3.at[j], g3_near.at[j], g3_far.at[j], H_G3)
    xb_own[...] = xb[0, H_HIDDEN - 1 : H_HIDDEN + rows + 1]
    xs_own[...] = xs[0]


def kernel_terms(values, gradient, rw):
    rows = gradient.shape[0]
    gradient = gradient.reshape(-1, TILE)
    for a in range(3):
        block = values[a : a + rows].reshape(-1, WIDE)
        terms = lax.dot_general(
            block, gradient, (((0,), (0,)), ((), ())), preferred_element_type=jnp.float32
        )
        for b in range(3):
            for c in range(3):
                at = (a * 9 + b * 3 + c) * CH
                for w in range(CELLS):
                    s0, s1 = SLOT_OF[b, w + c] * CH, SLOT_OF[b + 1, w + c] * CH
                    rw[w, at : at + CH] = (
                        terms[s0 : s0 + CH, :LANES] + terms[s1 : s1 + CH, LANES:]
                    )
    count = rw.shape[1] // CELLS
    cell = lax.broadcasted_iota(jnp.int32, (count, LANES), 1) // CH
    dense = jnp.zeros((count, LANES), jnp.float32)
    for q in range(CELLS):
        part = None
        for w in range(CELLS):
            piece = rw[w, pl.ds(q, count, stride=CELLS), :]
            if q != w:
                piece = pltpu.roll(piece, (q - w) % CELLS * CH, 1)
            part = piece if part is None else part + piece
        dense = jnp.where(cell == q, part, dense)
    return dense.astype(jnp.bfloat16)


def between_body(taps_ref, xs_own, g3, t_ref, terms, rw):
    fill_weights(taps_ref, t_ref)
    terms[...] = kernel_terms(xs_own[...], g3[0], rw)


def back_two(j, x_ref, sl2, x2_ref, t_ref, first, depth, grow):
    rows, cells = x2_ref.shape[-3:-1]
    for start, count in chunks_of(rows, BACKWARD_ROWS):
        back = conv_rows(x_ref, (), start, count, t_ref, 2).reshape(count, cells, TILE)
        for d in range(count):
            at = start + d
            grad = inside(back[d] * sl2[j, at], first + at - H_G2, depth)
            grow(rounded(grad), x2_ref, (at,))
        yield


def put_row(message, row):
    half = row.shape[0]
    message[message.shape[0] - 2 * half : message.shape[0] - half] = row[:, :LANES]
    message[message.shape[0] - half :] = row[:, LANES:]


def back_body(
    depth, pairs, tiles,
    near, mid, far, sl1, sl2, xv_own, xb_own, t_ref,
    g1, g1_far, message,
    xg3, xg2, rw, g1_near, terms,
):
    rows = mid.shape[1]
    cells = pairs * tiles
    first = lax.axis_index("depth") * rows
    grow = functools.partial(expand, pairs=pairs, tiles=tiles, masks=edge_masks(tiles))
    for j in range(2):
        widen(near, mid, far, (j,), H_G3, xg3.at[j], (), grow)
    alternate(
        *(back_two(j, xg3.at[j], sl2, xg2.at[j], t_ref, first, depth, grow) for j in range(2))
    )
    own, other = (
        rounded(conv_rows(xg2, (j,), 0, rows, t_ref, 1)).astype(jnp.float32) for j in range(2)
    )
    mixed = (OWN_SHARE * own + PARTNER_SHARE * other).reshape(rows, cells, TILE)
    g1[...] = rounded(mixed * sl1[...])
    edge_rows(g1, g1_near, g1_far, H_G1)
    size = terms.shape[0] // 2
    terms[:size] = kernel_terms(xv_own[...], g1[...], rw).astype(jnp.float32)
    two = kernel_terms(xb_own[...], xg2[0, H_G2 : H_G2 + rows, :, :TILE], rw)
    terms[size:] = two.astype(jnp.float32)
    message[: 2 * size] = terms[...].astype(jnp.bfloat16)
    put_row(message, g1_near[0])


def last_body(pairs, tiles, near, g1, far, t_ref, *refs):
    *parts, gv, total, scratch, xg1, sides = refs
    lines = -(-total.shape[0] // 16) * 16
    terms = [part[:lines].astype(jnp.float32) for part in parts]
    total[...] = functools.reduce(lambda a, b: a + b, terms)[: total.shape[0]]
    rows, height, _ = gv.shape
    cells = pairs * tiles
    grow = functools.partial(expand, pairs=pairs, tiles=tiles, masks=edge_masks(tiles))
    for at, message in enumerate((near, far)):
        first = message.shape[0] - 2 * cells
        sides[at, 0, :, :LANES] = message[first : first + cells]
        sides[at, 0, :, LANES:] = message[first + cells :]
    widen(sides.at[0], g1, sides.at[1], (), H_G1, xg1, (), grow)
    for start, count in chunks_of(rows, BACKWARD_ROWS):
        back = conv_rows(xg1, (), start, count, t_ref, 0).reshape(count, cells, TILE)
        for d in range(count):
            for h in range(height):
                row, side = h // 2 * tiles, slice(h % 2 * LANES, (h % 2 + 1) * LANES)
                scratch[start + d, pl.ds(h, tiles, stride=height), :] = back[
                    d, row : row + tiles, side
                ]
            for t in range(tiles):
                gv[start + d, :, t * LANES : (t + 1) * LANES] = scratch[
                    start + d, t * height : (t + 1) * height, :
                ].astype(jnp.bfloat16)


def add_body(own, near, three, three_near, g1_far, message, terms):
    add = lambda a, b: a.astype(jnp.float32) + b.astype(jnp.float32)
    size = three.shape[0]
    terms[: 2 * size] = add(own[: 2 * size], near[: 2 * size])
    terms[2 * size : 3 * size] = add(three[...], three_near[...])
    terms[3 * size :] = jnp.zeros_like(terms[3 * size :])
    message[: terms.shape[0]] = terms[...].astype(jnp.bfloat16)
    put_row(message, g1_far[0])


def total_body(one, two, out):
    rows = -(-out.shape[0] // 16) * 16
    total = one[:rows].astype(jnp.float32) + two[:rows].astype(jnp.float32)
    out[...] = total[: out.shape[0]].astype(out.dtype)


def swapped(values, hop):
    count = lax.axis_size("depth")
    return lax.ppermute(values, "depth", [(i, i ^ hop) for i in range(count)])


def neighbours(near, far):
    count = lax.axis_size("depth")
    result = []
    for values, first in ((near, 0), (far, 1)):
        partner = {}
        for i in range(first, count - 1, 2):
            partner[i], partner[i + 1] = i + 1, i
        pairs = [(i, partner.get(i, i)) for i in range(count)]
        result.append(lax.ppermute(values, "depth", pairs))
    return result


def over_sample(values, hop):
    groups = lax.axis_size("sample")
    return lax.ppermute(values, "sample", [(i, i ^ hop) for i in range(groups)])


def even_hops(values):
    return [over_sample(values, hop) for hop in range(2, lax.axis_size("sample"), 2)]


def all_hops(odd, evens):
    return [odd, *(crop for even in evens for crop in (even, over_sample(even, 1)))]


def traded(volume, cotangent, partner, tiles):
    groups = lax.axis_size("sample")
    rows, height, _ = volume.shape
    split = jnp.stack([volume, cotangent]).reshape(2, rows, height // 2, 2, tiles, LANES)
    split = split.transpose(0, 1, 2, 4, 3, 5).reshape(2, groups, -1, TILE)
    pieces = split.swapaxes(0, 1)
    spread = lax.all_to_all(pieces, "sample", split_axis=0, concat_axis=0, tiled=True)
    ids = jnp.arange(groups, dtype=jnp.int32)
    inverse = jnp.sum(jnp.where(partner[:, None] == ids[None, :], ids[:, None], 0), axis=0)
    wanted = jnp.stack([2 * partner, 2 * inverse, 2 * inverse + 1], axis=1)
    chosen = jnp.take(spread.reshape(2 * groups, -1, TILE), wanted, axis=0)
    joined = lax.all_to_all(chosen, "sample", split_axis=0, concat_axis=0, tiled=True)
    others = jnp.swapaxes(joined, 0, 1).reshape(3, rows, -1, TILE)
    return others[:2], others[2:]


def call(kernel, outs, scratch, inputs, macs=0, far=()):
    vmem, smem, anywhere = (
        pl.BlockSpec(memory_space=space) for space in (pltpu.VMEM, pltpu.SMEM, pl.ANY)
    )
    specs = [
        anywhere if at in far else smem if x.dtype == jnp.int32 else vmem
        for at, x in enumerate(inputs)
    ]
    results = pl.pallas_call(
        kernel,
        out_shape=tuple(jax.ShapeDtypeStruct(shape, dtype) for shape, dtype in outs),
        in_specs=specs,
        out_specs=(vmem,) * len(outs),
        scratch_shapes=scratch,
        compiler_params=pltpu.CompilerParams(vmem_limit_bytes=VMEM_LIMIT),
        cost_estimate=pl.CostEstimate(
            flops=2 * macs, bytes_accessed=2**22 if macs else 1, transcendentals=0
        ),
    )(*inputs)
    return results if len(results) > 1 else results[0]


def per_device(volume, kernels, partner, cotangent):
    volume, cotangent = volume[0], cotangent[0]
    rows, height, lanes = volume.shape
    pairs, tiles = height // 2, lanes // LANES
    cells = pairs * tiles
    groups, count = lax.axis_size("sample"), lax.axis_size("depth")
    depth = rows * count
    layers, taps, width = kernels.shape
    bf16, f32 = jnp.bfloat16, jnp.float32
    row_macs = 3 * cells * WIDE * TILE
    packed_rows = taps * CH // CELLS
    wide = lambda *lead: pltpu.VMEM((*lead, cells, WIDE), bf16)
    field = lambda *lead: ((*lead, cells, TILE), bf16)
    raw_tiles = lambda *lead: pltpu.VMEM((*lead, height * tiles, LANES), f32)
    banded = ((layers, 3, WIDE, TILE), bf16)
    spread_taps = ((layers, taps * CH, LANES), bf16)
    rw = pltpu.VMEM((CELLS, taps * CH, LANES), f32)

    direct = groups in (2, 4, 8)
    evens = even_hops(volume) if direct else []
    both, edges = lax.optimization_barrier((jnp.stack([volume, cotangent]), volume))
    near, far = neighbours(edges, edges)
    packed = kernels.reshape(layers, packed_rows, LANES)
    ids = jnp.clip(partner, 0, groups - 1)
    fwd_taps, bwd_taps = call(
        functools.partial(taps_body, taps),
        [spread_taps, spread_taps],
        [pltpu.VMEM((layers, -(-taps // CELLS) * LANES, LANES), f32)],
        [packed],
        2**28,
    )
    evens, both, ids, fwd_taps, bwd_taps, own_crop, late = lax.optimization_barrier(
        (evens, both, ids, fwd_taps, bwd_taps, volume, cotangent)
    )
    edge = ((2, H_VOL, cells, TILE), bf16)
    if direct:
        crops = all_hops(over_sample(own_crop, 1), evens)
        crops, near, far = lax.optimization_barrier((crops, near, far))
        vol, vol_near, vol_far = call(
            functools.partial(select_body, tuple(range(groups))),
            [field(2, rows), edge, edge],
            [raw_tiles(2, rows)],
            [ids, both, *crops],
        )
        sides = neighbours(vol_near, vol_far)
        evens, vol = lax.optimization_barrier((even_hops(late), vol))
        give = call(pick_body, [((1, rows, height, lanes), bf16)], [], [ids, both, *evens])
        cot_other = call(
            functools.partial(select_body, tuple(range(0, groups, 2))),
            [field(1, rows)],
            [raw_tiles(1, rows)],
            [ids, both, *evens, over_sample(give, 1)],
        )
    else:
        vol, cot_other = traded(volume, cotangent, partner, tiles)
        sides = neighbours(vol, vol)
    hid_rows = rows + 2 * H_HIDDEN
    fwd, hid_own, sl1, xv_own, cot_own = call(
        functools.partial(own_body, pairs, tiles),
        [
            banded,
            field(hid_rows),
            ((rows, cells, TILE), f32),
            ((rows + 2, cells, WIDE), bf16),
            field(rows),
        ],
        [wide(rows + 2 * H_VOL), pltpu.VMEM((3, rows, cells, TILE), bf16), raw_tiles(4 * rows)],
        [fwd_taps, near, both, far],
        hid_rows * row_macs,
    )

    g3, g3_near, g3_far, sl2, xb_own, xs_own = call(
        functools.partial(forward_body, depth, pairs, tiles),
        [
            field(2, rows),
            field(2, H_G3),
            field(2, H_G3),
            ((2, rows + 2 * H_TWO, cells, TILE), f32),
            ((rows + 2, cells, WIDE), bf16),
            ((rows + 2, cells, WIDE), bf16),
        ],
        [
            wide(2, rows + 2 * H_VOL),
            pltpu.VMEM((2, hid_rows, cells, TILE), bf16),
            wide(2, hid_rows),
            wide(2, rows + 2),
        ],
        [sides[0], vol, sides[1], hid_own, cot_own, cot_other, fwd],
        (2 * hid_rows + 2 * (rows + 2) + 2 * rows) * row_macs,
    )

    near, far = neighbours(g3_near, g3_far)
    terms = ((packed_rows, LANES), bf16)
    bwd, three = call(
        between_body, [banded, terms], [rw], [bwd_taps, xs_own, g3], rows * row_macs
    )
    three_near = swapped(three, 1)
    short, long = 2 * packed_rows, -(-layers * packed_rows // 16) * 16
    message = lambda lines: ((lines + 2 * cells, LANES), bf16)
    g1, g1_far, own = call(
        functools.partial(back_body, depth, pairs, tiles),
        [field(rows), ((H_G1, cells, TILE), bf16), message(short)],
        [
            wide(2, rows + 2 * H_G3),
            wide(2, rows + 2 * H_G2),
            rw,
            pltpu.VMEM((H_G1, cells, TILE), bf16),
            pltpu.VMEM((short, LANES), f32),
        ],
        [near, g3, far, sl1, sl2, xv_own, xb_own, bwd],
        (6 * rows + 4) * row_macs,
    )
    own, three_near = lax.optimization_barrier((own, three_near))
    near = swapped(own, 1)
    summed = call(
        add_body,
        [message(long)],
        [pltpu.VMEM((long, LANES), f32)],
        [own, near, three, three_near, g1_far],
    )
    if count == 4:
        far = swapped(summed, 3)
        parts = [summed, far]
    else:
        far, parts, hop = neighbours(summed, summed)[1], [summed], 2
        while hop < count:
            if len(parts) > 1:
                parts = [call(total_body, [((long, LANES), bf16)], [], parts)]
            parts.append(swapped(parts[0], hop))
            hop *= 2
    grad_volume, total = call(
        functools.partial(last_body, pairs, tiles),
        [((rows, height, lanes), bf16), ((layers * packed_rows, LANES), f32)],
        [raw_tiles(rows), wide(rows + 2 * H_G1), pltpu.VMEM((2, H_G1, cells, TILE), bf16)],
        [near, g1, far, bwd, *parts],
        rows * row_macs,
    )
    return (grad_volume[None], total.reshape(1, layers, taps, width))


def solution(mesh):
    in_specs = (P("sample", "depth", None, None), P(), P(), P("sample", "depth", None, None))
    out_specs = (P("sample", "depth", None, None), P("sample", None, None, None))
    return jax.shard_map(
        per_device, mesh=mesh, in_specs=in_specs, out_specs=out_specs, check_vma=False
    )
```

```python
import functools

import jax
import jax.numpy as jnp
from jax import lax
from jax.experimental import pallas as pl
from jax.experimental.pallas import tpu as pltpu
from jax.sharding import PartitionSpec as P

CH = 32
OWN_SHARE = 0.6
PARTNER_SHARE = 0.4
LANES = 128
CELLS = LANES // CH
TILE = 2 * LANES
WIDE = 3 * TILE
VMEM_LIMIT = 40 * 2**20
FORWARD_ROWS, BACKWARD_ROWS = 2, 6

SLOTS = (
    [(1 + h, 1 + w) for h in range(2) for w in range(CELLS)]
    + [(0, 1 + w) for w in range(CELLS)]
    + [(3, 1 + w) for w in range(CELLS)]
    + [(1, 5), (0, 0), (0, 5), (1, 0)]
    + [(2, 5), (3, 0), (3, 5), (2, 0)]
)
SLOT_OF = {cell: at for at, cell in enumerate(SLOTS)}

H_VOL, H_HIDDEN, H_TWO, H_G3, H_G2, H_G1 = 3, 2, 1, 2, 1, 1


def chunks_of(rows, most):
    count = -(-rows // most)
    base, extra = divmod(rows, count)
    start, result = 0, []
    for index in range(count):
        size = base + (index < extra)
        result.append((start, size))
        start += size
    return result


def sigmoid(v):
    return 0.5 + 0.5 * jnp.tanh(0.5 * v)


def lanes_of(t):
    return slice(t * LANES, (t + 1) * LANES)


def taps_body(taps, kr_ref, fwd_ref, bwd_ref, scratch):
    layers, rows = kr_ref.shape[:2]
    part = scratch.shape[1] // CELLS // CH
    shape = (LANES, CELLS * LANES)
    lane = lax.broadcasted_iota(jnp.int32, shape, 1)
    chosen = lax.broadcasted_iota(jnp.int32, shape, 0) == lane // LANES * CH + lane % CH
    spread = jnp.where(chosen, 1.0, 0.0).astype(jnp.bfloat16)
    for layer in range(layers):
        groups = jnp.dot(kr_ref[layer], spread, preferred_element_type=jnp.float32)
        for q in range(CELLS):
            scratch[layer, pl.ds(q, rows, stride=CELLS), :] = groups[:, lanes_of(q)]
        scratch[layer, taps * CH :, :] = jnp.zeros_like(scratch[layer, taps * CH :, :])
        fwd_ref[layer] = scratch[layer, : taps * CH].astype(jnp.bfloat16)
        cell = lax.broadcasted_iota(jnp.int32, (part * CH, LANES), 1) // CH
        compact = jnp.zeros((part * CH, LANES), jnp.float32)
        for group in range(CELLS):
            at = group * part * CH
            compact = jnp.where(cell == group, scratch[layer, at : at + part * CH, :], compact)
        room = -(-part // CELLS) * LANES - part * CH
        turned = jnp.concatenate([compact, jnp.zeros((room, LANES), jnp.float32)], 0).T
        stacked = jnp.concatenate(
            [turned[:, lanes_of(t)] for t in range(turned.shape[1] // LANES)], 0
        ).astype(jnp.bfloat16)
        groups = jnp.dot(stacked, spread, preferred_element_type=jnp.float32)
        for tap in range(taps):
            group, index = divmod(tap, part)
            at, row = taps - 1 - tap, index // CELLS * LANES + group * CH
            bwd_ref[layer, at * CH : (at + 1) * CH, :] = groups[
                row : row + CH, lanes_of(index % CELLS)
            ].astype(jnp.bfloat16)


def fill_weights(taps_ref, t_ref):
    cell = lax.broadcasted_iota(jnp.int32, (CH, LANES), 1) // CH
    zero = jnp.zeros((CH, LANES), jnp.bfloat16)
    for layer in range(t_ref.shape[0]):
        for a in range(3):
            bands = {}
            for b in range(3):
                first = (a * 9 + b * 3) * CH
                values = [taps_ref[layer, first + c * CH : first + (c + 1) * CH, :] for c in range(3)]
                for ww in range(CELLS + 2):
                    band = zero
                    for c in range(3):
                        if 0 <= ww - c < CELLS:
                            band = jnp.where(cell == ww - c, values[c], band)
                    bands[b, ww] = band
            for at, (hh, ww) in enumerate(SLOTS):
                for h in range(2):
                    t_ref[
                        layer, a, at * CH : (at + 1) * CH, h * LANES : (h + 1) * LANES
                    ] = bands.get((hh - h, ww), zero)


def edge_masks(tiles):
    shape = (1, tiles, TILE)
    cell = lax.broadcasted_iota(jnp.int32, shape, 2) % LANES // CH
    row = lax.broadcasted_iota(jnp.int32, shape, 1)
    from_before = (cell == CELLS - 1) & (row > 0)
    from_after = (cell == 0) & (row < tiles - 1)
    return tuple(
        jnp.where(mask, 1.0, 0.0).astype(jnp.bfloat16) for mask in (from_before, from_after)
    )


def expand(x, out_ref, lead, pairs, tiles, masks):
    x = x.reshape(pairs, tiles, TILE)
    edge = pltpu.roll(x, 1, 1) * masks[0] + pltpu.roll(x, tiles - 1, 1) * masks[1]
    e0, e1 = edge[..., :LANES], edge[..., LANES:]
    r0, r1 = pltpu.roll(e0, LANES // 2, 2), pltpu.roll(e1, LANES // 2, 2)
    zero = jnp.zeros((1, tiles, LANES), x.dtype)
    low = jnp.concatenate([zero, x[:-1, :, LANES:]], 0)
    high = jnp.concatenate([x[1:, :, :LANES], zero], 0)
    e0 = e0 + jnp.concatenate([zero, r1[:-1]], 0)
    e1 = e1 + jnp.concatenate([r0[1:], zero], 0)
    flat = lambda v: v.reshape(pairs * tiles, v.shape[-1])
    out_ref[(*lead, slice(None), slice(0, TILE))] = flat(x)
    out_ref[(*lead, slice(None), slice(TILE, TILE + LANES))] = flat(low)
    out_ref[(*lead, slice(None), slice(TILE + LANES, 2 * TILE))] = flat(high)
    out_ref[(*lead, slice(None), slice(2 * TILE, 2 * TILE + LANES))] = flat(e0)
    out_ref[(*lead, slice(None), slice(2 * TILE + LANES, WIDE))] = flat(e1)


def conv_rows(x_ref, lead, start, rows, t_ref, layer):
    blocks = [x_ref[(*lead, pl.ds(start + a, rows))].reshape(-1, WIDE) for a in range(3)]
    return jnp.dot(
        jnp.concatenate(blocks, axis=1),
        t_ref[layer].reshape(3 * WIDE, TILE),
        preferred_element_type=jnp.float32,
    )


def slope_of(pre, gate):
    return gate * (1.0 + pre * (1.0 - gate))


def rounded(v):
    return v.astype(jnp.bfloat16)


def inside(v, row, depth):
    return jnp.where((row >= 0) & (row < depth), v, 0.0)


def either(flag, a, b):
    low = lambda *at: jnp.where(flag, a[at], b[at])
    high = lambda *at: jnp.where(flag, b[at], a[at])
    return low, high


def widen(near, own, far, lead, halo, x_ref, x_lead, grow):
    at, last = lax.axis_index("depth"), lax.axis_size("depth") - 1
    low, high = either(at % 2 == 1, near, far)
    held, rows = near.shape[len(lead)], own.shape[len(lead)]
    for d in range(halo):
        row = low(*lead, held - halo + d)
        if d == halo - 1:
            row = jnp.where(at > 0, row, jnp.zeros_like(row))
        grow(row, x_ref, (*x_lead, d))
    for d in range(rows):
        grow(own[(*lead, d)], x_ref, (*x_lead, halo + d))
    for d in range(halo):
        row = high(*lead, d)
        if d == 0:
            row = jnp.where(at < last, row, jnp.zeros_like(row))
        grow(row, x_ref, (*x_lead, halo + rows + d))


def edge_rows(values, near, far, halo):
    odd = lax.axis_index("depth") % 2 == 1
    rows = values.shape[0]
    for d in range(halo):
        up, down = values[rows - halo + d], values[d]
        near[d] = jnp.where(odd, down, up)
        far[d] = jnp.where(odd, up, down)


def layer_one(xv, lead, out_ref, t_ref, slopes_ref=None):
    rows, cells = out_ref.shape[len(lead)], out_ref.shape[-2]
    for start, count in chunks_of(rows, FORWARD_ROWS):
        pre = conv_rows(xv, lead, start, count, t_ref, 0)
        gate = sigmoid(pre)
        value = (pre * gate).astype(jnp.bfloat16).reshape(count, cells, TILE)
        out_ref[(*lead, pl.ds(start, count))] = value
        if slopes_ref is not None:
            slope = slope_of(pre, gate).reshape(count, cells, TILE)
            for d in range(count):
                to = start + d - H_HIDDEN
                if 0 <= to < slopes_ref.shape[0]:
                    slopes_ref[to] = slope[d]


def tiled_rows(load, height, tiles, scratch, at):
    for t in range(tiles):
        scratch[at, t * height : (t + 1) * height, :] = load(t).astype(jnp.float32)
    for h in range(height):
        piece = scratch[at, pl.ds(h, tiles, stride=height), :].astype(jnp.bfloat16)
        yield h // 2 * tiles, slice(h % 2 * LANES, (h % 2 + 1) * LANES), piece


def wanted_by(partner, crop, count):
    inverse = jnp.int32(0)
    for other in range(partner.shape[0]):
        inverse = jnp.where(partner[other] == crop, other, inverse)
    return (partner[crop], inverse)[2 - count :]


def pick_body(partner, both, *refs):
    *evens, out = refs
    own = lax.axis_index("sample")
    count = out.shape[0]
    for to, crop in enumerate(wanted_by(partner, own ^ 1, count)):
        for at, source in enumerate((both.at[2 - count], *evens)):

            @pl.when(crop ^ own == 2 * at)
            def _(to=to, source=source):
                out[to] = source[...]


def select_body(hops, partner, both, *refs):
    held, refs = (both, *refs[: len(hops) - 1]), refs[len(hops) - 1 :]
    own = lax.axis_index("sample")
    _, rows, height, lanes = both.shape
    tiles = lanes // LANES
    picked = len(hops) * 2 == lax.axis_size("sample")
    if picked:
        sent, *refs = refs
    out, *sides, scratch = refs
    count = out.shape[0]

    def spread(to, source):
        for d in range(rows):
            for t in range(tiles):
                scratch[to, d, t * height : (t + 1) * height, :] = source[
                    d, :, lanes_of(t)
                ].astype(jnp.float32)

    for to, crop in enumerate(wanted_by(partner, own, count)):
        for hop, source in zip(hops, held):
            source = both.at[2 - count] if hop == 0 else source
            pl.when(crop ^ own == hop)(functools.partial(spread, to, source))
        if picked:
            pl.when((crop ^ own) % 2 == 1)(functools.partial(spread, to, sent.at[to]))
        for d in range(rows):
            for h in range(height):
                piece = scratch[to, d, pl.ds(h, tiles, stride=height), :].astype(jnp.bfloat16)
                row, side = h // 2 * tiles, lanes_of(h % 2)
                out[to, d, row : row + tiles, side] = piece
        if sides:
            edge_rows(out.at[to], *(side.at[to] for side in sides), H_VOL)


def own_body(
    pairs, tiles,
    taps_ref, near, both, far,
    t_ref, hid, sl1, xv_own, cot_own,
    xv, field, scratch,
):
    _, rows, height, _ = both.shape
    fill_weights(taps_ref, t_ref)
    grow = functools.partial(expand, pairs=pairs, tiles=tiles, masks=edge_masks(tiles))
    for at, part in enumerate((near, both.at[0], far, both.at[1])):
        for d in range(rows):
            load = lambda t, part=part, d=d: part[d, :, lanes_of(t)]
            for row, side, piece in tiled_rows(load, height, tiles, scratch, at * rows + d):
                if at < 3:
                    field[at, d, row : row + tiles, side] = piece
                else:
                    cot_own[d, row : row + tiles, side] = piece
    widen(field.at[0], field.at[1], field.at[2], (), H_VOL, xv, (), grow)
    layer_one(xv, (), hid, t_ref, sl1)
    xv_own[...] = xv[H_VOL - 1 : H_VOL + rows + 1]


def forward_body(
    depth, pairs, tiles,
    near, mid, far, hid_own, cot_own, cot_other, t_ref,
    g3, g3_near, g3_far, sl2, xb_own, xs_own,
    xv, hid, xb, xs,
):
    rows = mid.shape[1]
    cells = pairs * tiles
    first = lax.axis_index("depth") * rows
    grow = functools.partial(expand, pairs=pairs, tiles=tiles, masks=edge_masks(tiles))

    for crop in range(2):
        widen(near, mid, far, (crop,), H_VOL, xv, (crop,), grow)
        layer_one(xv, (crop,), hid, t_ref)

    for d in range(rows + 2 * H_HIDDEN):
        own = hid_own[d].astype(jnp.float32)
        partner, other = hid[0, d].astype(jnp.float32), hid[1, d].astype(jnp.float32)
        row = first + d - H_HIDDEN
        for j, (a, b) in enumerate(((own, partner), (other, own))):
            mixed = OWN_SHARE * a + PARTNER_SHARE * b
            grow(rounded(inside(mixed, row, depth)), xb, (j, d))

    def middle(j, cot):
        for start, count in chunks_of(rows + 2 * H_TWO, FORWARD_ROWS):
            pre = conv_rows(xb, (j,), start, count, t_ref, 1)
            gate = sigmoid(pre)
            value = (pre * gate).reshape(count, cells, TILE)
            slope = slope_of(pre, gate).reshape(count, cells, TILE)
            for d in range(count):
                sl2[j, start + d] = slope[d]
                to = start + d - (H_TWO - 1)
                if 0 <= to < rows + 2:
                    grow(rounded(inside(value[d], first + to - 1, depth)), xs, (j, to))
        for start, count in chunks_of(rows, FORWARD_ROWS):
            pre = conv_rows(xs, (j,), start, count, t_ref, 2)
            slope = slope_of(pre, sigmoid(pre)).reshape(count, cells, TILE)
            for d in range(count):
                at = start + d
                grad = rounded(cot[at].astype(jnp.float32) * slope[d])
                g3[j, at] = grad

    middle(0, cot_own)
    middle(1, cot_other.at[0])
    for j in range(2):
        edge_rows(g3.at[j], g3_near.at[j], g3_far.at[j], H_G3)
    xb_own[...] = xb[0, H_HIDDEN - 1 : H_HIDDEN + rows + 1]
    xs_own[...] = xs[0]


def kernel_terms(values, gradient, rw):
    rows = gradient.shape[0]
    gradient = gradient.reshape(-1, TILE)
    for a in range(3):
        block = values[a : a + rows].reshape(-1, WIDE)
        terms = lax.dot_general(
            block, gradient, (((0,), (0,)), ((), ())), preferred_element_type=jnp.float32
        )
        for b in range(3):
            for c in range(3):
                at = (a * 9 + b * 3 + c) * CH
                for w in range(CELLS):
                    s0, s1 = SLOT_OF[b, w + c] * CH, SLOT_OF[b + 1, w + c] * CH
                    rw[w, at : at + CH] = (
                        terms[s0 : s0 + CH, :LANES] + terms[s1 : s1 + CH, LANES:]
                    )
    count = rw.shape[1] // CELLS
    cell = lax.broadcasted_iota(jnp.int32, (count, LANES), 1) // CH
    dense = jnp.zeros((count, LANES), jnp.float32)
    for q in range(CELLS):
        part = None
        for w in range(CELLS):
            piece = rw[w, pl.ds(q, count, stride=CELLS), :]
            if q != w:
                piece = pltpu.roll(piece, (q - w) % CELLS * CH, 1)
            part = piece if part is None else part + piece
        dense = jnp.where(cell == q, part, dense)
    return dense.astype(jnp.bfloat16)


def between_body(taps_ref, xs_own, g3, t_ref, terms, rw):
    fill_weights(taps_ref, t_ref)
    terms[...] = kernel_terms(xs_own[...], g3[0], rw)


def back_two(j, x_ref, sl2, x2_ref, t_ref, first, depth, grow):
    rows, cells = x2_ref.shape[-3:-1]
    for start, count in chunks_of(rows, BACKWARD_ROWS):
        back = conv_rows(x_ref, (), start, count, t_ref, 2).reshape(count, cells, TILE)
        for d in range(count):
            at = start + d
            grad = inside(back[d] * sl2[j, at], first + at - H_G2, depth)
            grow(rounded(grad), x2_ref, (at,))


def put_row(message, row):
    half = row.shape[0]
    message[message.shape[0] - 2 * half : message.shape[0] - half] = row[:, :LANES]
    message[message.shape[0] - half :] = row[:, LANES:]


def back_body(
    depth, pairs, tiles,
    near, mid, far, sl1, sl2, xv_own, xb_own, t_ref,
    g1, g1_far, message,
    xg3, xg2, rw, g1_near, terms,
):
    rows = mid.shape[1]
    cells = pairs * tiles
    first = lax.axis_index("depth") * rows
    grow = functools.partial(expand, pairs=pairs, tiles=tiles, masks=edge_masks(tiles))
    for j in range(2):
        widen(near, mid, far, (j,), H_G3, xg3.at[j], (), grow)
        back_two(j, xg3.at[j], sl2, xg2.at[j], t_ref, first, depth, grow)
    own, other = (
        rounded(conv_rows(xg2, (j,), 0, rows, t_ref, 1)).astype(jnp.float32) for j in range(2)
    )
    mixed = (OWN_SHARE * own + PARTNER_SHARE * other).reshape(rows, cells, TILE)
    g1[...] = rounded(mixed * sl1[...])
    edge_rows(g1, g1_near, g1_far, H_G1)
    size = terms.shape[0] // 2
    terms[:size] = kernel_terms(xv_own[...], g1[...], rw).astype(jnp.float32)
    two = kernel_terms(xb_own[...], xg2[0, H_G2 : H_G2 + rows, :, :TILE], rw)
    terms[size:] = two.astype(jnp.float32)
    message[: 2 * size] = terms[...].astype(jnp.bfloat16)
    put_row(message, g1_near[0])


def last_body(pairs, tiles, near, g1, far, t_ref, *refs):
    *parts, gv, total, scratch, xg1, sides = refs
    lines = -(-total.shape[0] // 16) * 16
    terms = [part[:lines].astype(jnp.float32) for part in parts]
    total[...] = functools.reduce(lambda a, b: a + b, terms)[: total.shape[0]]
    rows, height, _ = gv.shape
    cells = pairs * tiles
    grow = functools.partial(expand, pairs=pairs, tiles=tiles, masks=edge_masks(tiles))
    for at, message in enumerate((near, far)):
        first = message.shape[0] - 2 * cells
        sides[at, 0, :, :LANES] = message[first : first + cells]
        sides[at, 0, :, LANES:] = message[first + cells :]
    widen(sides.at[0], g1, sides.at[1], (), H_G1, xg1, (), grow)
    for start, count in chunks_of(rows, BACKWARD_ROWS):
        back = conv_rows(xg1, (), start, count, t_ref, 0).reshape(count, cells, TILE)
        for d in range(count):
            for h in range(height):
                row, side = h // 2 * tiles, slice(h % 2 * LANES, (h % 2 + 1) * LANES)
                scratch[start + d, pl.ds(h, tiles, stride=height), :] = back[
                    d, row : row + tiles, side
                ]
            for t in range(tiles):
                gv[start + d, :, t * LANES : (t + 1) * LANES] = scratch[
                    start + d, t * height : (t + 1) * height, :
                ].astype(jnp.bfloat16)


def add_body(own, near, three, three_near, g1_far, message, terms):
    add = lambda a, b: a.astype(jnp.float32) + b.astype(jnp.float32)
    size = three.shape[0]
    terms[: 2 * size] = add(own[: 2 * size], near[: 2 * size])
    terms[2 * size : 3 * size] = add(three[...], three_near[...])
    terms[3 * size :] = jnp.zeros_like(terms[3 * size :])
    message[: terms.shape[0]] = terms[...].astype(jnp.bfloat16)
    put_row(message, g1_far[0])


def total_body(one, two, out):
    rows = -(-out.shape[0] // 16) * 16
    total = one[:rows].astype(jnp.float32) + two[:rows].astype(jnp.float32)
    out[...] = total[: out.shape[0]].astype(out.dtype)


def swapped(values, hop):
    count = lax.axis_size("depth")
    return lax.ppermute(values, "depth", [(i, i ^ hop) for i in range(count)])


def neighbours(near, far):
    count = lax.axis_size("depth")
    result = []
    for values, first in ((near, 0), (far, 1)):
        partner = {}
        for i in range(first, count - 1, 2):
            partner[i], partner[i + 1] = i + 1, i
        pairs = [(i, partner.get(i, i)) for i in range(count)]
        result.append(lax.ppermute(values, "depth", pairs))
    return result


def over_sample(values, hop):
    groups = lax.axis_size("sample")
    return lax.ppermute(values, "sample", [(i, i ^ hop) for i in range(groups)])


def even_hops(values):
    return [over_sample(values, hop) for hop in range(2, lax.axis_size("sample"), 2)]


def all_hops(odd, evens):
    return [odd, *(crop for even in evens for crop in (even, over_sample(even, 1)))]


def traded(volume, cotangent, partner, tiles):
    groups = lax.axis_size("sample")
    rows, height, _ = volume.shape
    split = jnp.stack([volume, cotangent]).reshape(2, rows, height // 2, 2, tiles, LANES)
    split = split.transpose(0, 1, 2, 4, 3, 5).reshape(2, groups, -1, TILE)
    pieces = split.swapaxes(0, 1)
    spread = lax.all_to_all(pieces, "sample", split_axis=0, concat_axis=0, tiled=True)
    ids = jnp.arange(groups, dtype=jnp.int32)
    inverse = jnp.sum(jnp.where(partner[:, None] == ids[None, :], ids[:, None], 0), axis=0)
    wanted = jnp.stack([2 * partner, 2 * inverse, 2 * inverse + 1], axis=1)
    chosen = jnp.take(spread.reshape(2 * groups, -1, TILE), wanted, axis=0)
    joined = lax.all_to_all(chosen, "sample", split_axis=0, concat_axis=0, tiled=True)
    others = jnp.swapaxes(joined, 0, 1).reshape(3, rows, -1, TILE)
    return others[:2], others[2:]


def call(kernel, outs, scratch, inputs, macs=0, far=()):
    vmem, smem, anywhere = (
        pl.BlockSpec(memory_space=space) for space in (pltpu.VMEM, pltpu.SMEM, pl.ANY)
    )
    specs = [
        anywhere if at in far else smem if x.dtype == jnp.int32 else vmem
        for at, x in enumerate(inputs)
    ]
    results = pl.pallas_call(
        kernel,
        out_shape=tuple(jax.ShapeDtypeStruct(shape, dtype) for shape, dtype in outs),
        in_specs=specs,
        out_specs=(vmem,) * len(outs),
        scratch_shapes=scratch,
        compiler_params=pltpu.CompilerParams(vmem_limit_bytes=VMEM_LIMIT),
        cost_estimate=pl.CostEstimate(
            flops=2 * macs, bytes_accessed=2**22 if macs else 1, transcendentals=0
        ),
    )(*inputs)
    return results if len(results) > 1 else results[0]


def per_device(volume, kernels, partner, cotangent):
    volume, cotangent = volume[0], cotangent[0]
    rows, height, lanes = volume.shape
    pairs, tiles = height // 2, lanes // LANES
    cells = pairs * tiles
    groups, count = lax.axis_size("sample"), lax.axis_size("depth")
    depth = rows * count
    layers, taps, width = kernels.shape
    bf16, f32 = jnp.bfloat16, jnp.float32
    row_macs = 3 * cells * WIDE * TILE
    packed_rows = taps * CH // CELLS
    wide = lambda *lead: pltpu.VMEM((*lead, cells, WIDE), bf16)
    field = lambda *lead: ((*lead, cells, TILE), bf16)
    raw_tiles = lambda *lead: pltpu.VMEM((*lead, height * tiles, LANES), f32)
    banded = ((layers, 3, WIDE, TILE), bf16)
    spread_taps = ((layers, taps * CH, LANES), bf16)
    rw = pltpu.VMEM((CELLS, taps * CH, LANES), f32)

    direct = groups in (2, 4, 8)
    evens = even_hops(volume) if direct else []
    both, edges = lax.optimization_barrier((jnp.stack([volume, cotangent]), volume))
    near, far = neighbours(edges, edges)
    packed = kernels.reshape(layers, packed_rows, LANES)
    ids = jnp.clip(partner, 0, groups - 1)
    fwd_taps, bwd_taps = call(
        functools.partial(taps_body, taps),
        [spread_taps, spread_taps],
        [pltpu.VMEM((layers, -(-taps // CELLS) * LANES, LANES), f32)],
        [packed],
        2**28,
    )
    evens, both, ids, fwd_taps, bwd_taps, own_crop, late = lax.optimization_barrier(
        (evens, both, ids, fwd_taps, bwd_taps, volume, cotangent)
    )
    edge = ((2, H_VOL, cells, TILE), bf16)
    if direct:
        crops = all_hops(over_sample(own_crop, 1), evens)
        crops, far = lax.optimization_barrier((crops, far))
        vol, vol_near, vol_far = call(
            functools.partial(select_body, tuple(range(groups))),
            [field(2, rows), edge, edge],
            [raw_tiles(2, rows)],
            [ids, both, *crops],
        )
        vol_near, vol_far, near = lax.optimization_barrier((vol_near, vol_far, near))
        sides = neighbours(vol_near, vol_far)
        evens, vol = lax.optimization_barrier((even_hops(late), vol))
        give = call(pick_body, [((1, rows, height, lanes), bf16)], [], [ids, both, *evens])
        cot_other = call(
            functools.partial(select_body, tuple(range(0, groups, 2))),
            [field(1, rows)],
            [raw_tiles(1, rows)],
            [ids, both, *evens, over_sample(give, 1)],
        )
    else:
        vol, cot_other = traded(volume, cotangent, partner, tiles)
        sides = neighbours(vol, vol)
    hid_rows = rows + 2 * H_HIDDEN
    fwd, hid_own, sl1, xv_own, cot_own = call(
        functools.partial(own_body, pairs, tiles),
        [
            banded,
            field(hid_rows),
            ((rows, cells, TILE), f32),
            ((rows + 2, cells, WIDE), bf16),
            field(rows),
        ],
        [wide(rows + 2 * H_VOL), pltpu.VMEM((3, rows, cells, TILE), bf16), raw_tiles(4 * rows)],
        [fwd_taps, near, both, far],
        hid_rows * row_macs,
    )

    g3, g3_near, g3_far, sl2, xb_own, xs_own = call(
        functools.partial(forward_body, depth, pairs, tiles),
        [
            field(2, rows),
            field(2, H_G3),
            field(2, H_G3),
            ((2, rows + 2 * H_TWO, cells, TILE), f32),
            ((rows + 2, cells, WIDE), bf16),
            ((rows + 2, cells, WIDE), bf16),
        ],
        [
            wide(2, rows + 2 * H_VOL),
            pltpu.VMEM((2, hid_rows, cells, TILE), bf16),
            wide(2, hid_rows),
            wide(2, rows + 2),
        ],
        [sides[0], vol, sides[1], hid_own, cot_own, cot_other, fwd],
        (2 * hid_rows + 2 * (rows + 2) + 2 * rows) * row_macs,
    )

    near, far = neighbours(g3_near, g3_far)
    terms = ((packed_rows, LANES), bf16)
    bwd, three = call(
        between_body, [banded, terms], [rw], [bwd_taps, xs_own, g3], rows * row_macs
    )
    three_near = swapped(three, 1)
    short, long = 2 * packed_rows, -(-layers * packed_rows // 16) * 16
    message = lambda lines: ((lines + 2 * cells, LANES), bf16)
    g1, g1_far, own = call(
        functools.partial(back_body, depth, pairs, tiles),
        [field(rows), ((H_G1, cells, TILE), bf16), message(short)],
        [
            wide(2, rows + 2 * H_G3),
            wide(2, rows + 2 * H_G2),
            rw,
            pltpu.VMEM((H_G1, cells, TILE), bf16),
            pltpu.VMEM((short, LANES), f32),
        ],
        [near, g3, far, sl1, sl2, xv_own, xb_own, bwd],
        (6 * rows + 4) * row_macs,
    )
    own, three_near = lax.optimization_barrier((own, three_near))
    near = swapped(own, 1)
    summed = call(
        add_body,
        [message(long)],
        [pltpu.VMEM((long, LANES), f32)],
        [own, near, three, three_near, g1_far],
    )
    if count == 4:
        far = swapped(summed, 3)
        parts = [summed, far]
    else:
        far, parts, hop = neighbours(summed, summed)[1], [summed], 2
        while hop < count:
            if len(parts) > 1:
                parts = [call(total_body, [((long, LANES), bf16)], [], parts)]
            parts.append(swapped(parts[0], hop))
            hop *= 2
    grad_volume, total = call(
        functools.partial(last_body, pairs, tiles),
        [((rows, height, lanes), bf16), ((layers * packed_rows, LANES), f32)],
        [raw_tiles(rows), wide(rows + 2 * H_G1), pltpu.VMEM((2, H_G1, cells, TILE), bf16)],
        [near, g1, far, bwd, *parts],
        rows * row_macs,
    )
    return (grad_volume[None], total.reshape(1, layers, taps, width))


def solution(mesh):
    in_specs = (P("sample", "depth", None, None), P(), P(), P("sample", "depth", None, None))
    out_specs = (P("sample", "depth", None, None), P("sample", None, None, None))
    return jax.shard_map(
        per_device, mesh=mesh, in_specs=in_specs, out_specs=out_specs, check_vma=False
    )
```

```python
import functools

import jax
import jax.numpy as jnp
from jax import lax
from jax.experimental import pallas as pl
from jax.experimental.pallas import tpu as pltpu
from jax.sharding import PartitionSpec as P

CH = 32
OWN_SHARE = 0.6
PARTNER_SHARE = 0.4
LANES = 128
CELLS = LANES // CH
TILE = 2 * LANES
WIDE = 3 * TILE
VMEM_LIMIT = 40 * 2**20
FORWARD_ROWS, BACKWARD_ROWS = 1, 6

SLOTS = (
    [(1 + h, 1 + w) for h in range(2) for w in range(CELLS)]
    + [(0, 1 + w) for w in range(CELLS)]
    + [(3, 1 + w) for w in range(CELLS)]
    + [(1, 5), (0, 0), (0, 5), (1, 0)]
    + [(2, 5), (3, 0), (3, 5), (2, 0)]
)
SLOT_OF = {cell: at for at, cell in enumerate(SLOTS)}

H_VOL, H_HIDDEN, H_TWO, H_G3, H_G2, H_G1 = 3, 2, 1, 2, 1, 1


def chunks_of(rows, most):
    count = -(-rows // most)
    base, extra = divmod(rows, count)
    start, result = 0, []
    for index in range(count):
        size = base + (index < extra)
        result.append((start, size))
        start += size
    return result


def sigmoid(v):
    return 0.5 + 0.5 * jnp.tanh(0.5 * v)


def lanes_of(t):
    return slice(t * LANES, (t + 1) * LANES)


def taps_body(taps, kr_ref, fwd_ref, bwd_ref, scratch):
    layers, rows = kr_ref.shape[:2]
    part = scratch.shape[1] // CELLS // CH
    shape = (LANES, CELLS * LANES)
    lane = lax.broadcasted_iota(jnp.int32, shape, 1)
    chosen = lax.broadcasted_iota(jnp.int32, shape, 0) == lane // LANES * CH + lane % CH
    spread = jnp.where(chosen, 1.0, 0.0).astype(jnp.bfloat16)
    for layer in range(layers):
        groups = jnp.dot(kr_ref[layer], spread, preferred_element_type=jnp.float32)
        for q in range(CELLS):
            scratch[layer, pl.ds(q, rows, stride=CELLS), :] = groups[:, lanes_of(q)]
        scratch[layer, taps * CH :, :] = jnp.zeros_like(scratch[layer, taps * CH :, :])
        fwd_ref[layer] = scratch[layer, : taps * CH].astype(jnp.bfloat16)
        cell = lax.broadcasted_iota(jnp.int32, (part * CH, LANES), 1) // CH
        compact = jnp.zeros((part * CH, LANES), jnp.float32)
        for group in range(CELLS):
            at = group * part * CH
            compact = jnp.where(cell == group, scratch[layer, at : at + part * CH, :], compact)
        room = -(-part // CELLS) * LANES - part * CH
        turned = jnp.concatenate([compact, jnp.zeros((room, LANES), jnp.float32)], 0).T
        stacked = jnp.concatenate(
            [turned[:, lanes_of(t)] for t in range(turned.shape[1] // LANES)], 0
        ).astype(jnp.bfloat16)
        groups = jnp.dot(stacked, spread, preferred_element_type=jnp.float32)
        for tap in range(taps):
            group, index = divmod(tap, part)
            at, row = taps - 1 - tap, index // CELLS * LANES + group * CH
            bwd_ref[layer, at * CH : (at + 1) * CH, :] = groups[
                row : row + CH, lanes_of(index % CELLS)
            ].astype(jnp.bfloat16)


def fill_weights(taps_ref, t_ref):
    cell = lax.broadcasted_iota(jnp.int32, (CH, LANES), 1) // CH
    zero = jnp.zeros((CH, LANES), jnp.bfloat16)
    for layer in range(t_ref.shape[0]):
        for a in range(3):
            bands = {}
            for b in range(3):
                first = (a * 9 + b * 3) * CH
                values = [taps_ref[layer, first + c * CH : first + (c + 1) * CH, :] for c in range(3)]
                for ww in range(CELLS + 2):
                    band = zero
                    for c in range(3):
                        if 0 <= ww - c < CELLS:
                            band = jnp.where(cell == ww - c, values[c], band)
                    bands[b, ww] = band
            for at, (hh, ww) in enumerate(SLOTS):
                for h in range(2):
                    t_ref[
                        layer, a, at * CH : (at + 1) * CH, h * LANES : (h + 1) * LANES
                    ] = bands.get((hh - h, ww), zero)


def edge_masks(tiles):
    shape = (1, tiles, TILE)
    cell = lax.broadcasted_iota(jnp.int32, shape, 2) % LANES // CH
    row = lax.broadcasted_iota(jnp.int32, shape, 1)
    from_before = (cell == CELLS - 1) & (row > 0)
    from_after = (cell == 0) & (row < tiles - 1)
    return tuple(
        jnp.where(mask, 1.0, 0.0).astype(jnp.bfloat16) for mask in (from_before, from_after)
    )


def expand(x, out_ref, lead, pairs, tiles, masks):
    x = x.reshape(pairs, tiles, TILE)
    edge = pltpu.roll(x, 1, 1) * masks[0] + pltpu.roll(x, tiles - 1, 1) * masks[1]
    e0, e1 = edge[..., :LANES], edge[..., LANES:]
    r0, r1 = pltpu.roll(e0, LANES // 2, 2), pltpu.roll(e1, LANES // 2, 2)
    zero = jnp.zeros((1, tiles, LANES), x.dtype)
    low = jnp.concatenate([zero, x[:-1, :, LANES:]], 0)
    high = jnp.concatenate([x[1:, :, :LANES], zero], 0)
    e0 = e0 + jnp.concatenate([zero, r1[:-1]], 0)
    e1 = e1 + jnp.concatenate([r0[1:], zero], 0)
    flat = lambda v: v.reshape(pairs * tiles, v.shape[-1])
    out_ref[(*lead, slice(None), slice(0, TILE))] = flat(x)
    out_ref[(*lead, slice(None), slice(TILE, TILE + LANES))] = flat(low)
    out_ref[(*lead, slice(None), slice(TILE + LANES, 2 * TILE))] = flat(high)
    out_ref[(*lead, slice(None), slice(2 * TILE, 2 * TILE + LANES))] = flat(e0)
    out_ref[(*lead, slice(None), slice(2 * TILE + LANES, WIDE))] = flat(e1)


def conv_rows(x_ref, lead, start, rows, t_ref, layer):
    blocks = [x_ref[(*lead, pl.ds(start + a, rows))].reshape(-1, WIDE) for a in range(3)]
    return jnp.dot(
        jnp.concatenate(blocks, axis=1),
        t_ref[layer].reshape(3 * WIDE, TILE),
        preferred_element_type=jnp.float32,
    )


def slope_of(pre, gate):
    return gate * (1.0 + pre * (1.0 - gate))


def rounded(v):
    return v.astype(jnp.bfloat16)


def inside(v, row, depth):
    return jnp.where((row >= 0) & (row < depth), v, 0.0)


def either(flag, a, b):
    low = lambda *at: jnp.where(flag, a[at], b[at])
    high = lambda *at: jnp.where(flag, b[at], a[at])
    return low, high


def widen(near, own, far, lead, halo, x_ref, x_lead, grow):
    at, last = lax.axis_index("depth"), lax.axis_size("depth") - 1
    low, high = either(at % 2 == 1, near, far)
    held, rows = near.shape[len(lead)], own.shape[len(lead)]
    for d in range(halo):
        row = low(*lead, held - halo + d)
        if d == halo - 1:
            row = jnp.where(at > 0, row, jnp.zeros_like(row))
        grow(row, x_ref, (*x_lead, d))
    for d in range(rows):
        grow(own[(*lead, d)], x_ref, (*x_lead, halo + d))
    for d in range(halo):
        row = high(*lead, d)
        if d == 0:
            row = jnp.where(at < last, row, jnp.zeros_like(row))
        grow(row, x_ref, (*x_lead, halo + rows + d))


def edge_rows(values, near, far, halo):
    odd = lax.axis_index("depth") % 2 == 1
    rows = values.shape[0]
    for d in range(halo):
        up, down = values[rows - halo + d], values[d]
        near[d] = jnp.where(odd, down, up)
        far[d] = jnp.where(odd, up, down)


def layer_one(xv, lead, out_ref, t_ref, slopes_ref=None):
    rows, cells = out_ref.shape[len(lead)], out_ref.shape[-2]
    for start, count in chunks_of(rows, FORWARD_ROWS):
        pre = conv_rows(xv, lead, start, count, t_ref, 0)
        gate = sigmoid(pre)
        value = (pre * gate).astype(jnp.bfloat16).reshape(count, cells, TILE)
        out_ref[(*lead, pl.ds(start, count))] = value
        if slopes_ref is not None:
            slope = slope_of(pre, gate).reshape(count, cells, TILE)
            for d in range(count):
                to = start + d - H_HIDDEN
                if 0 <= to < slopes_ref.shape[0]:
                    slopes_ref[to] = slope[d]


def tiled_rows(load, height, tiles, scratch, at):
    for t in range(tiles):
        scratch[at, t * height : (t + 1) * height, :] = load(t).astype(jnp.float32)
    for h in range(height):
        piece = scratch[at, pl.ds(h, tiles, stride=height), :].astype(jnp.bfloat16)
        yield h // 2 * tiles, slice(h % 2 * LANES, (h % 2 + 1) * LANES), piece


def wanted_by(partner, crop, count):
    inverse = jnp.int32(0)
    for other in range(partner.shape[0]):
        inverse = jnp.where(partner[other] == crop, other, inverse)
    return (partner[crop], inverse)[2 - count :]


def pick_body(partner, both, *refs):
    *evens, out = refs
    own = lax.axis_index("sample")
    count = out.shape[0]
    for to, crop in enumerate(wanted_by(partner, own ^ 1, count)):
        for at, source in enumerate((both.at[2 - count], *evens)):

            @pl.when(crop ^ own == 2 * at)
            def _(to=to, source=source):
                out[to] = source[...]


def select_body(hops, partner, both, *refs):
    held, refs = (both, *refs[: len(hops) - 1]), refs[len(hops) - 1 :]
    own = lax.axis_index("sample")
    _, rows, height, lanes = both.shape
    tiles = lanes // LANES
    picked = len(hops) * 2 == lax.axis_size("sample")
    if picked:
        sent, *refs = refs
    out, *sides, scratch = refs
    count = out.shape[0]

    def spread(to, source):
        for d in range(rows):
            for t in range(tiles):
                scratch[to, d, t * height : (t + 1) * height, :] = source[
                    d, :, lanes_of(t)
                ].astype(jnp.float32)

    for to, crop in enumerate(wanted_by(partner, own, count)):
        for hop, source in zip(hops, held):
            source = both.at[2 - count] if hop == 0 else source
            pl.when(crop ^ own == hop)(functools.partial(spread, to, source))
        if picked:
            pl.when((crop ^ own) % 2 == 1)(functools.partial(spread, to, sent.at[to]))
        for d in range(rows):
            for h in range(height):
                piece = scratch[to, d, pl.ds(h, tiles, stride=height), :].astype(jnp.bfloat16)
                row, side = h // 2 * tiles, lanes_of(h % 2)
                out[to, d, row : row + tiles, side] = piece
        if sides:
            edge_rows(out.at[to], *(side.at[to] for side in sides), H_VOL)


def own_body(
    pairs, tiles,
    taps_ref, near, both, far,
    t_ref, hid, sl1, xv_own, cot_own,
    xv, field, scratch,
):
    _, rows, height, _ = both.shape
    fill_weights(taps_ref, t_ref)
    grow = functools.partial(expand, pairs=pairs, tiles=tiles, masks=edge_masks(tiles))
    for at, part in enumerate((near, both.at[0], far, both.at[1])):
        for d in range(rows):
            load = lambda t, part=part, d=d: part[d, :, lanes_of(t)]
            for row, side, piece in tiled_rows(load, height, tiles, scratch, at * rows + d):
                if at < 3:
                    field[at, d, row : row + tiles, side] = piece
                else:
                    cot_own[d, row : row + tiles, side] = piece
    widen(field.at[0], field.at[1], field.at[2], (), H_VOL, xv, (), grow)
    layer_one(xv, (), hid, t_ref, sl1)
    xv_own[...] = xv[H_VOL - 1 : H_VOL + rows + 1]


def forward_body(
    depth, pairs, tiles,
    near, mid, far, hid_own, cot_own, cot_other, t_ref,
    g3, g3_near, g3_far, sl2, xb_own, xs_own,
    xv, hid, xb, xs,
):
    rows = mid.shape[1]
    cells = pairs * tiles
    first = lax.axis_index("depth") * rows
    grow = functools.partial(expand, pairs=pairs, tiles=tiles, masks=edge_masks(tiles))

    for crop in range(2):
        widen(near, mid, far, (crop,), H_VOL, xv, (crop,), grow)
        layer_one(xv, (crop,), hid, t_ref)

    for d in range(rows + 2 * H_HIDDEN):
        own = hid_own[d].astype(jnp.float32)
        partner, other = hid[0, d].astype(jnp.float32), hid[1, d].astype(jnp.float32)
        row = first + d - H_HIDDEN
        for j, (a, b) in enumerate(((own, partner), (other, own))):
            mixed = OWN_SHARE * a + PARTNER_SHARE * b
            grow(rounded(inside(mixed, row, depth)), xb, (j, d))

    def middle(j, cot):
        for start, count in chunks_of(rows + 2 * H_TWO, FORWARD_ROWS):
            pre = conv_rows(xb, (j,), start, count, t_ref, 1)
            gate = sigmoid(pre)
            value = (pre * gate).reshape(count, cells, TILE)
            slope = slope_of(pre, gate).reshape(count, cells, TILE)
            for d in range(count):
                sl2[j, start + d] = slope[d]
                to = start + d - (H_TWO - 1)
                if 0 <= to < rows + 2:
                    grow(rounded(inside(value[d], first + to - 1, depth)), xs, (j, to))
        for start, count in chunks_of(rows, FORWARD_ROWS):
            pre = conv_rows(xs, (j,), start, count, t_ref, 2)
            slope = slope_of(pre, sigmoid(pre)).reshape(count, cells, TILE)
            for d in range(count):
                at = start + d
                grad = rounded(cot[at].astype(jnp.float32) * slope[d])
                g3[j, at] = grad

    middle(0, cot_own)
    middle(1, cot_other.at[0])
    for j in range(2):
        edge_rows(g3.at[j], g3_near.at[j], g3_far.at[j], H_G3)
    xb_own[...] = xb[0, H_HIDDEN - 1 : H_HIDDEN + rows + 1]
    xs_own[...] = xs[0]


def kernel_terms(values, gradient, rw):
    rows = gradient.shape[0]
    gradient = gradient.reshape(-1, TILE)
    for a in range(3):
        block = values[a : a + rows].reshape(-1, WIDE)
        terms = lax.dot_general(
            block, gradient, (((0,), (0,)), ((), ())), preferred_element_type=jnp.float32
        )
        for b in range(3):
            for c in range(3):
                at = (a * 9 + b * 3 + c) * CH
                for w in range(CELLS):
                    s0, s1 = SLOT_OF[b, w + c] * CH, SLOT_OF[b + 1, w + c] * CH
                    rw[w, at : at + CH] = (
                        terms[s0 : s0 + CH, :LANES] + terms[s1 : s1 + CH, LANES:]
                    )
    count = rw.shape[1] // CELLS
    cell = lax.broadcasted_iota(jnp.int32, (count, LANES), 1) // CH
    dense = jnp.zeros((count, LANES), jnp.float32)
    for q in range(CELLS):
        part = None
        for w in range(CELLS):
            piece = rw[w, pl.ds(q, count, stride=CELLS), :]
            if q != w:
                piece = pltpu.roll(piece, (q - w) % CELLS * CH, 1)
            part = piece if part is None else part + piece
        dense = jnp.where(cell == q, part, dense)
    return dense.astype(jnp.bfloat16)


def between_body(taps_ref, xs_own, g3, t_ref, terms, rw):
    fill_weights(taps_ref, t_ref)
    terms[...] = kernel_terms(xs_own[...], g3[0], rw)


def back_two(j, x_ref, sl2, x2_ref, t_ref, first, depth, grow):
    rows, cells = x2_ref.shape[-3:-1]
    for start, count in chunks_of(rows, BACKWARD_ROWS):
        back = conv_rows(x_ref, (), start, count, t_ref, 2).reshape(count, cells, TILE)
        for d in range(count):
            at = start + d
            grad = inside(back[d] * sl2[j, at], first + at - H_G2, depth)
            grow(rounded(grad), x2_ref, (at,))


def put_row(message, row):
    half = row.shape[0]
    message[message.shape[0] - 2 * half : message.shape[0] - half] = row[:, :LANES]
    message[message.shape[0] - half :] = row[:, LANES:]


def back_body(
    depth, pairs, tiles,
    near, mid, far, sl1, sl2, xv_own, xb_own, t_ref,
    g1, g1_far, message,
    xg3, xg2, rw, g1_near, terms,
):
    rows = mid.shape[1]
    cells = pairs * tiles
    first = lax.axis_index("depth") * rows
    grow = functools.partial(expand, pairs=pairs, tiles=tiles, masks=edge_masks(tiles))
    for j in range(2):
        widen(near, mid, far, (j,), H_G3, xg3.at[j], (), grow)
        back_two(j, xg3.at[j], sl2, xg2.at[j], t_ref, first, depth, grow)
    own, other = (
        rounded(conv_rows(xg2, (j,), 0, rows, t_ref, 1)).astype(jnp.float32) for j in range(2)
    )
    mixed = (OWN_SHARE * own + PARTNER_SHARE * other).reshape(rows, cells, TILE)
    g1[...] = rounded(mixed * sl1[...])
    edge_rows(g1, g1_near, g1_far, H_G1)
    size = terms.shape[0] // 2
    terms[:size] = kernel_terms(xv_own[...], g1[...], rw).astype(jnp.float32)
    two = kernel_terms(xb_own[...], xg2[0, H_G2 : H_G2 + rows, :, :TILE], rw)
    terms[size:] = two.astype(jnp.float32)
    message[: 2 * size] = terms[...].astype(jnp.bfloat16)
    put_row(message, g1_near[0])


def last_body(pairs, tiles, near, g1, far, t_ref, *refs):
    *parts, gv, total, scratch, xg1, sides = refs
    lines = -(-total.shape[0] // 16) * 16
    terms = [part[:lines].astype(jnp.float32) for part in parts]
    total[...] = functools.reduce(lambda a, b: a + b, terms)[: total.shape[0]]
    rows, height, _ = gv.shape
    cells = pairs * tiles
    grow = functools.partial(expand, pairs=pairs, tiles=tiles, masks=edge_masks(tiles))
    for at, message in enumerate((near, far)):
        first = message.shape[0] - 2 * cells
        sides[at, 0, :, :LANES] = message[first : first + cells]
        sides[at, 0, :, LANES:] = message[first + cells :]
    widen(sides.at[0], g1, sides.at[1], (), H_G1, xg1, (), grow)
    for start, count in chunks_of(rows, BACKWARD_ROWS):
        back = conv_rows(xg1, (), start, count, t_ref, 0).reshape(count, cells, TILE)
        for d in range(count):
            for h in range(height):
                row, side = h // 2 * tiles, slice(h % 2 * LANES, (h % 2 + 1) * LANES)
                scratch[start + d, pl.ds(h, tiles, stride=height), :] = back[
                    d, row : row + tiles, side
                ]
            for t in range(tiles):
                gv[start + d, :, t * LANES : (t + 1) * LANES] = scratch[
                    start + d, t * height : (t + 1) * height, :
                ].astype(jnp.bfloat16)


def add_body(own, near, three, three_near, g1_far, message, terms):
    add = lambda a, b: a.astype(jnp.float32) + b.astype(jnp.float32)
    size = three.shape[0]
    terms[: 2 * size] = add(own[: 2 * size], near[: 2 * size])
    terms[2 * size : 3 * size] = add(three[...], three_near[...])
    terms[3 * size :] = jnp.zeros_like(terms[3 * size :])
    message[: terms.shape[0]] = terms[...].astype(jnp.bfloat16)
    put_row(message, g1_far[0])


def total_body(one, two, out):
    rows = -(-out.shape[0] // 16) * 16
    total = one[:rows].astype(jnp.float32) + two[:rows].astype(jnp.float32)
    out[...] = total[: out.shape[0]].astype(out.dtype)


def swapped(values, hop):
    count = lax.axis_size("depth")
    return lax.ppermute(values, "depth", [(i, i ^ hop) for i in range(count)])


def neighbours(near, far):
    count = lax.axis_size("depth")
    result = []
    for values, first in ((near, 0), (far, 1)):
        partner = {}
        for i in range(first, count - 1, 2):
            partner[i], partner[i + 1] = i + 1, i
        pairs = [(i, partner.get(i, i)) for i in range(count)]
        result.append(lax.ppermute(values, "depth", pairs))
    return result


def over_sample(values, hop):
    groups = lax.axis_size("sample")
    return lax.ppermute(values, "sample", [(i, i ^ hop) for i in range(groups)])


def even_hops(values):
    return [over_sample(values, hop) for hop in range(2, lax.axis_size("sample"), 2)]


def all_hops(odd, evens):
    return [odd, *(crop for even in evens for crop in (even, over_sample(even, 1)))]


def traded(volume, cotangent, partner, tiles):
    groups = lax.axis_size("sample")
    rows, height, _ = volume.shape
    split = jnp.stack([volume, cotangent]).reshape(2, rows, height // 2, 2, tiles, LANES)
    split = split.transpose(0, 1, 2, 4, 3, 5).reshape(2, groups, -1, TILE)
    pieces = split.swapaxes(0, 1)
    spread = lax.all_to_all(pieces, "sample", split_axis=0, concat_axis=0, tiled=True)
    ids = jnp.arange(groups, dtype=jnp.int32)
    inverse = jnp.sum(jnp.where(partner[:, None] == ids[None, :], ids[:, None], 0), axis=0)
    wanted = jnp.stack([2 * partner, 2 * inverse, 2 * inverse + 1], axis=1)
    chosen = jnp.take(spread.reshape(2 * groups, -1, TILE), wanted, axis=0)
    joined = lax.all_to_all(chosen, "sample", split_axis=0, concat_axis=0, tiled=True)
    others = jnp.swapaxes(joined, 0, 1).reshape(3, rows, -1, TILE)
    return others[:2], others[2:]


def call(kernel, outs, scratch, inputs, macs=0, far=()):
    vmem, smem, anywhere = (
        pl.BlockSpec(memory_space=space) for space in (pltpu.VMEM, pltpu.SMEM, pl.ANY)
    )
    specs = [
        anywhere if at in far else smem if x.dtype == jnp.int32 else vmem
        for at, x in enumerate(inputs)
    ]
    results = pl.pallas_call(
        kernel,
        out_shape=tuple(jax.ShapeDtypeStruct(shape, dtype) for shape, dtype in outs),
        in_specs=specs,
        out_specs=(vmem,) * len(outs),
        scratch_shapes=scratch,
        compiler_params=pltpu.CompilerParams(vmem_limit_bytes=VMEM_LIMIT),
        cost_estimate=pl.CostEstimate(
            flops=2 * macs, bytes_accessed=2**22 if macs else 1, transcendentals=0
        ),
    )(*inputs)
    return results if len(results) > 1 else results[0]


def per_device(volume, kernels, partner, cotangent):
    volume, cotangent = volume[0], cotangent[0]
    rows, height, lanes = volume.shape
    pairs, tiles = height // 2, lanes // LANES
    cells = pairs * tiles
    groups, count = lax.axis_size("sample"), lax.axis_size("depth")
    depth = rows * count
    layers, taps, width = kernels.shape
    bf16, f32 = jnp.bfloat16, jnp.float32
    row_macs = 3 * cells * WIDE * TILE
    packed_rows = taps * CH // CELLS
    wide = lambda *lead: pltpu.VMEM((*lead, cells, WIDE), bf16)
    field = lambda *lead: ((*lead, cells, TILE), bf16)
    raw_tiles = lambda *lead: pltpu.VMEM((*lead, height * tiles, LANES), f32)
    banded = ((layers, 3, WIDE, TILE), bf16)
    spread_taps = ((layers, taps * CH, LANES), bf16)
    rw = pltpu.VMEM((CELLS, taps * CH, LANES), f32)

    direct = groups in (2, 4, 8)
    evens = even_hops(volume) if direct else []
    both, edges = lax.optimization_barrier((jnp.stack([volume, cotangent]), volume))
    near, far = neighbours(edges, edges)
    packed = kernels.reshape(layers, packed_rows, LANES)
    ids = jnp.clip(partner, 0, groups - 1)
    fwd_taps, bwd_taps = call(
        functools.partial(taps_body, taps),
        [spread_taps, spread_taps],
        [pltpu.VMEM((layers, -(-taps // CELLS) * LANES, LANES), f32)],
        [packed],
        2**28,
    )
    evens, both, ids, fwd_taps, bwd_taps, own_crop, late = lax.optimization_barrier(
        (evens, both, ids, fwd_taps, bwd_taps, volume, cotangent)
    )
    edge = ((2, H_VOL, cells, TILE), bf16)
    if direct:
        crops = all_hops(over_sample(own_crop, 1), evens)
        crops, far = lax.optimization_barrier((crops, far))
        vol, vol_near, vol_far = call(
            functools.partial(select_body, tuple(range(groups))),
            [field(2, rows), edge, edge],
            [raw_tiles(2, rows)],
            [ids, both, *crops],
        )
        vol_near, vol_far, near = lax.optimization_barrier((vol_near, vol_far, near))
        sides = neighbours(vol_near, vol_far)
        evens, vol = lax.optimization_barrier((even_hops(late), vol))
        give = call(pick_body, [((1, rows, height, lanes), bf16)], [], [ids, both, *evens])
        cot_other = call(
            functools.partial(select_body, tuple(range(0, groups, 2))),
            [field(1, rows)],
            [raw_tiles(1, rows)],
            [ids, both, *evens, over_sample(give, 1)],
        )
    else:
        vol, cot_other = traded(volume, cotangent, partner, tiles)
        sides = neighbours(vol, vol)
    hid_rows = rows + 2 * H_HIDDEN
    fwd, hid_own, sl1, xv_own, cot_own = call(
        functools.partial(own_body, pairs, tiles),
        [
            banded,
            field(hid_rows),
            ((rows, cells, TILE), f32),
            ((rows + 2, cells, WIDE), bf16),
            field(rows),
        ],
        [wide(rows + 2 * H_VOL), pltpu.VMEM((3, rows, cells, TILE), bf16), raw_tiles(4 * rows)],
        [fwd_taps, near, both, far],
        hid_rows * row_macs,
    )

    g3, g3_near, g3_far, sl2, xb_own, xs_own = call(
        functools.partial(forward_body, depth, pairs, tiles),
        [
            field(2, rows),
            field(2, H_G3),
            field(2, H_G3),
            ((2, rows + 2 * H_TWO, cells, TILE), f32),
            ((rows + 2, cells, WIDE), bf16),
            ((rows + 2, cells, WIDE), bf16),
        ],
        [
            wide(2, rows + 2 * H_VOL),
            pltpu.VMEM((2, hid_rows, cells, TILE), bf16),
            wide(2, hid_rows),
            wide(2, rows + 2),
        ],
        [sides[0], vol, sides[1], hid_own, cot_own, cot_other, fwd],
        (2 * hid_rows + 2 * (rows + 2) + 2 * rows) * row_macs,
    )

    near, far = neighbours(g3_near, g3_far)
    terms = ((packed_rows, LANES), bf16)
    bwd, three = call(
        between_body, [banded, terms], [rw], [bwd_taps, xs_own, g3], rows * row_macs
    )
    three_near = swapped(three, 1)
    short, long = 2 * packed_rows, -(-layers * packed_rows // 16) * 16
    message = lambda lines: ((lines + 2 * cells, LANES), bf16)
    g1, g1_far, own = call(
        functools.partial(back_body, depth, pairs, tiles),
        [field(rows), ((H_G1, cells, TILE), bf16), message(short)],
        [
            wide(2, rows + 2 * H_G3),
            wide(2, rows + 2 * H_G2),
            rw,
            pltpu.VMEM((H_G1, cells, TILE), bf16),
            pltpu.VMEM((short, LANES), f32),
        ],
        [near, g3, far, sl1, sl2, xv_own, xb_own, bwd],
        (6 * rows + 4) * row_macs,
    )
    own, three_near = lax.optimization_barrier((own, three_near))
    near = swapped(own, 1)
    summed = call(
        add_body,
        [message(long)],
        [pltpu.VMEM((long, LANES), f32)],
        [own, near, three, three_near, g1_far],
    )
    if count == 4:
        far = swapped(summed, 3)
        parts = [summed, far]
    else:
        far, parts, hop = neighbours(summed, summed)[1], [summed], 2
        while hop < count:
            if len(parts) > 1:
                parts = [call(total_body, [((long, LANES), bf16)], [], parts)]
            parts.append(swapped(parts[0], hop))
            hop *= 2
    grad_volume, total = call(
        functools.partial(last_body, pairs, tiles),
        [((rows, height, lanes), bf16), ((layers * packed_rows, LANES), f32)],
        [raw_tiles(rows), wide(rows + 2 * H_G1), pltpu.VMEM((2, H_G1, cells, TILE), bf16)],
        [near, g1, far, bwd, *parts],
        rows * row_macs,
    )
    return (grad_volume[None], total.reshape(1, layers, taps, width))


def solution(mesh):
    in_specs = (P("sample", "depth", None, None), P(), P(), P("sample", "depth", None, None))
    out_specs = (P("sample", "depth", None, None), P("sample", None, None, None))
    return jax.shard_map(
        per_device, mesh=mesh, in_specs=in_specs, out_specs=out_specs, check_vma=False
    )
```

```python
import functools

import jax
import jax.numpy as jnp
from jax import lax
from jax.experimental import pallas as pl
from jax.experimental.pallas import tpu as pltpu
from jax.sharding import PartitionSpec as P

CH = 32
OWN_SHARE = 0.6
PARTNER_SHARE = 0.4
LANES = 128
CELLS = LANES // CH
TILE = 2 * LANES
WIDE = 3 * TILE
VMEM_LIMIT = 40 * 2**20
FORWARD_ROWS, BACKWARD_ROWS = 2, 6

SLOTS = (
    [(1 + h, 1 + w) for h in range(2) for w in range(CELLS)]
    + [(0, 1 + w) for w in range(CELLS)]
    + [(3, 1 + w) for w in range(CELLS)]
    + [(1, 5), (0, 0), (0, 5), (1, 0)]
    + [(2, 5), (3, 0), (3, 5), (2, 0)]
)
SLOT_OF = {cell: at for at, cell in enumerate(SLOTS)}

H_VOL, H_HIDDEN, H_TWO, H_G3, H_G2, H_G1 = 3, 2, 1, 2, 1, 1


def chunks_of(rows, most):
    count = -(-rows // most)
    base, extra = divmod(rows, count)
    start, result = 0, []
    for index in range(count):
        size = base + (index < extra)
        result.append((start, size))
        start += size
    return result


def sigmoid(v):
    return 0.5 + 0.5 * jnp.tanh(0.5 * v)


def lanes_of(t):
    return slice(t * LANES, (t + 1) * LANES)


def taps_body(taps, kr_ref, fwd_ref, bwd_ref, scratch):
    layers, rows = kr_ref.shape[:2]
    part = scratch.shape[1] // CELLS // CH
    shape = (LANES, CELLS * LANES)
    lane = lax.broadcasted_iota(jnp.int32, shape, 1)
    chosen = lax.broadcasted_iota(jnp.int32, shape, 0) == lane // LANES * CH + lane % CH
    spread = jnp.where(chosen, 1.0, 0.0).astype(jnp.bfloat16)
    for layer in range(layers):
        groups = jnp.dot(kr_ref[layer], spread, preferred_element_type=jnp.float32)
        for q in range(CELLS):
            scratch[layer, pl.ds(q, rows, stride=CELLS), :] = groups[:, lanes_of(q)]
        scratch[layer, taps * CH :, :] = jnp.zeros_like(scratch[layer, taps * CH :, :])
        fwd_ref[layer] = scratch[layer, : taps * CH].astype(jnp.bfloat16)
        cell = lax.broadcasted_iota(jnp.int32, (part * CH, LANES), 1) // CH
        compact = jnp.zeros((part * CH, LANES), jnp.float32)
        for group in range(CELLS):
            at = group * part * CH
            compact = jnp.where(cell == group, scratch[layer, at : at + part * CH, :], compact)
        room = -(-part // CELLS) * LANES - part * CH
        turned = jnp.concatenate([compact, jnp.zeros((room, LANES), jnp.float32)], 0).T
        stacked = jnp.concatenate(
            [turned[:, lanes_of(t)] for t in range(turned.shape[1] // LANES)], 0
        ).astype(jnp.bfloat16)
        groups = jnp.dot(stacked, spread, preferred_element_type=jnp.float32)
        for tap in range(taps):
            group, index = divmod(tap, part)
            at, row = taps - 1 - tap, index // CELLS * LANES + group * CH
            bwd_ref[layer, at * CH : (at + 1) * CH, :] = groups[
                row : row + CH, lanes_of(index % CELLS)
            ].astype(jnp.bfloat16)


def fill_weights(taps_ref, t_ref):
    cell = lax.broadcasted_iota(jnp.int32, (CH, LANES), 1) // CH
    zero = jnp.zeros((CH, LANES), jnp.bfloat16)
    for layer in range(t_ref.shape[0]):
        for a in range(3):
            bands = {}
            for b in range(3):
                first = (a * 9 + b * 3) * CH
                values = [taps_ref[layer, first + c * CH : first + (c + 1) * CH, :] for c in range(3)]
                for ww in range(CELLS + 2):
                    band = zero
                    for c in range(3):
                        if 0 <= ww - c < CELLS:
                            band = jnp.where(cell == ww - c, values[c], band)
                    bands[b, ww] = band
            for at, (hh, ww) in enumerate(SLOTS):
                for h in range(2):
                    t_ref[
                        layer, a, at * CH : (at + 1) * CH, h * LANES : (h + 1) * LANES
                    ] = bands.get((hh - h, ww), zero)


def edge_masks(tiles):
    shape = (1, tiles, TILE)
    cell = lax.broadcasted_iota(jnp.int32, shape, 2) % LANES // CH
    row = lax.broadcasted_iota(jnp.int32, shape, 1)
    from_before = (cell == CELLS - 1) & (row > 0)
    from_after = (cell == 0) & (row < tiles - 1)
    return tuple(
        jnp.where(mask, 1.0, 0.0).astype(jnp.bfloat16) for mask in (from_before, from_after)
    )


def expand(x, out_ref, lead, pairs, tiles, masks):
    x = x.reshape(pairs, tiles, TILE)
    edge = pltpu.roll(x, 1, 1) * masks[0] + pltpu.roll(x, tiles - 1, 1) * masks[1]
    e0, e1 = edge[..., :LANES], edge[..., LANES:]
    r0, r1 = pltpu.roll(e0, LANES // 2, 2), pltpu.roll(e1, LANES // 2, 2)
    zero = jnp.zeros((1, tiles, LANES), x.dtype)
    low = jnp.concatenate([zero, x[:-1, :, LANES:]], 0)
    high = jnp.concatenate([x[1:, :, :LANES], zero], 0)
    e0 = e0 + jnp.concatenate([zero, r1[:-1]], 0)
    e1 = e1 + jnp.concatenate([r0[1:], zero], 0)
    flat = lambda v: v.reshape(pairs * tiles, v.shape[-1])
    out_ref[(*lead, slice(None), slice(0, TILE))] = flat(x)
    out_ref[(*lead, slice(None), slice(TILE, TILE + LANES))] = flat(low)
    out_ref[(*lead, slice(None), slice(TILE + LANES, 2 * TILE))] = flat(high)
    out_ref[(*lead, slice(None), slice(2 * TILE, 2 * TILE + LANES))] = flat(e0)
    out_ref[(*lead, slice(None), slice(2 * TILE + LANES, WIDE))] = flat(e1)


def conv_rows(x_ref, lead, start, rows, t_ref, layer):
    blocks = [x_ref[(*lead, pl.ds(start + a, rows))].reshape(-1, WIDE) for a in range(3)]
    return jnp.dot(
        jnp.concatenate(blocks, axis=1),
        t_ref[layer].reshape(3 * WIDE, TILE),
        preferred_element_type=jnp.float32,
    )


def slope_of(pre, gate):
    return gate * (1.0 + pre * (1.0 - gate))


def rounded(v):
    return v.astype(jnp.bfloat16)


def inside(v, row, depth):
    return jnp.where((row >= 0) & (row < depth), v, 0.0)


def either(flag, a, b):
    low = lambda *at: jnp.where(flag, a[at], b[at])
    high = lambda *at: jnp.where(flag, b[at], a[at])
    return low, high


def widen(near, own, far, lead, halo, x_ref, x_lead, grow):
    at, last = lax.axis_index("depth"), lax.axis_size("depth") - 1
    low, high = either(at % 2 == 1, near, far)
    held, rows = near.shape[len(lead)], own.shape[len(lead)]
    for d in range(halo):
        row = low(*lead, held - halo + d)
        if d == halo - 1:
            row = jnp.where(at > 0, row, jnp.zeros_like(row))
        grow(row, x_ref, (*x_lead, d))
    for d in range(rows):
        grow(own[(*lead, d)], x_ref, (*x_lead, halo + d))
    for d in range(halo):
        row = high(*lead, d)
        if d == 0:
            row = jnp.where(at < last, row, jnp.zeros_like(row))
        grow(row, x_ref, (*x_lead, halo + rows + d))


def edge_rows(values, near, far, halo):
    odd = lax.axis_index("depth") % 2 == 1
    rows = values.shape[0]
    for d in range(halo):
        up, down = values[rows - halo + d], values[d]
        near[d] = jnp.where(odd, down, up)
        far[d] = jnp.where(odd, up, down)


def layer_one(xv, lead, out_ref, t_ref, slopes_ref=None):
    rows, cells = out_ref.shape[len(lead)], out_ref.shape[-2]
    for start, count in chunks_of(rows, FORWARD_ROWS):
        pre = conv_rows(xv, lead, start, count, t_ref, 0)
        gate = sigmoid(pre)
        value = (pre * gate).astype(jnp.bfloat16).reshape(count, cells, TILE)
        out_ref[(*lead, pl.ds(start, count))] = value
        if slopes_ref is not None:
            slope = slope_of(pre, gate).reshape(count, cells, TILE)
            for d in range(count):
                to = start + d - H_HIDDEN
                if 0 <= to < slopes_ref.shape[0]:
                    slopes_ref[to] = slope[d]


def tiled_rows(load, height, tiles, scratch, at):
    for t in range(tiles):
        scratch[at, t * height : (t + 1) * height, :] = load(t).astype(jnp.float32)
    for h in range(height):
        piece = scratch[at, pl.ds(h, tiles, stride=height), :].astype(jnp.bfloat16)
        yield h // 2 * tiles, slice(h % 2 * LANES, (h % 2 + 1) * LANES), piece


def wanted_by(partner, crop, count):
    inverse = jnp.int32(0)
    for other in range(partner.shape[0]):
        inverse = jnp.where(partner[other] == crop, other, inverse)
    return (partner[crop], inverse)[2 - count :]


def pick_body(partner, both, *refs):
    *evens, out = refs
    own = lax.axis_index("sample")
    count = out.shape[0]
    for to, crop in enumerate(wanted_by(partner, own ^ 1, count)):
        for at, source in enumerate((both.at[2 - count], *evens)):

            @pl.when(crop ^ own == 2 * at)
            def _(to=to, source=source):
                out[to] = source[...]


def select_body(hops, partner, both, *refs):
    held, refs = (both, *refs[: len(hops) - 1]), refs[len(hops) - 1 :]
    own = lax.axis_index("sample")
    _, rows, height, lanes = both.shape
    tiles = lanes // LANES
    picked = len(hops) * 2 == lax.axis_size("sample")
    if picked:
        sent, *refs = refs
    out, *sides, scratch = refs
    count = out.shape[0]

    def spread(to, source):
        for d in range(rows):
            for t in range(tiles):
                scratch[to, d, t * height : (t + 1) * height, :] = source[
                    d, :, lanes_of(t)
                ].astype(jnp.float32)

    for to, crop in enumerate(wanted_by(partner, own, count)):
        for hop, source in zip(hops, held):
            source = both.at[2 - count] if hop == 0 else source
            pl.when(crop ^ own == hop)(functools.partial(spread, to, source))
        if picked:
            pl.when((crop ^ own) % 2 == 1)(functools.partial(spread, to, sent.at[to]))
        for d in range(rows):
            for h in range(height):
                piece = scratch[to, d, pl.ds(h, tiles, stride=height), :].astype(jnp.bfloat16)
                row, side = h // 2 * tiles, lanes_of(h % 2)
                out[to, d, row : row + tiles, side] = piece
        if sides:
            edge_rows(out.at[to], *(side.at[to] for side in sides), H_VOL)


def own_body(
    pairs, tiles,
    taps_ref, near, both, far,
    t_ref, hid, sl1, xv_own, cot_own,
    xv, field, scratch,
):
    _, rows, height, _ = both.shape
    fill_weights(taps_ref, t_ref)
    grow = functools.partial(expand, pairs=pairs, tiles=tiles, masks=edge_masks(tiles))
    for at, part in enumerate((near, both.at[0], far, both.at[1])):
        for d in range(rows):
            load = lambda t, part=part, d=d: part[d, :, lanes_of(t)]
            for row, side, piece in tiled_rows(load, height, tiles, scratch, at * rows + d):
                if at < 3:
                    field[at, d, row : row + tiles, side] = piece
                else:
                    cot_own[d, row : row + tiles, side] = piece
    widen(field.at[0], field.at[1], field.at[2], (), H_VOL, xv, (), grow)
    layer_one(xv, (), hid, t_ref, sl1)
    xv_own[...] = xv[H_VOL - 1 : H_VOL + rows + 1]


def forward_body(
    depth, pairs, tiles,
    near, mid, far, hid_own, cot_own, cot_other, t_ref,
    g3, g3_near, g3_far, sl2, xb_own, xs_own,
    xv, hid, xb, xs,
):
    rows = mid.shape[1]
    cells = pairs * tiles
    first = lax.axis_index("depth") * rows
    grow = functools.partial(expand, pairs=pairs, tiles=tiles, masks=edge_masks(tiles))

    for crop in range(2):
        widen(near, mid, far, (crop,), H_VOL, xv, (crop,), grow)
        layer_one(xv, (crop,), hid, t_ref)

    for d in range(rows + 2 * H_HIDDEN):
        own = hid_own[d].astype(jnp.float32)
        partner, other = hid[0, d].astype(jnp.float32), hid[1, d].astype(jnp.float32)
        row = first + d - H_HIDDEN
        for j, (a, b) in enumerate(((own, partner), (other, own))):
            mixed = OWN_SHARE * a + PARTNER_SHARE * b
            grow(rounded(inside(mixed, row, depth)), xb, (j, d))

    def middle(j, cot):
        for start, count in chunks_of(rows + 2 * H_TWO, FORWARD_ROWS):
            pre = conv_rows(xb, (j,), start, count, t_ref, 1)
            gate = sigmoid(pre)
            value = (pre * gate).reshape(count, cells, TILE)
            slope = slope_of(pre, gate).reshape(count, cells, TILE)
            for d in range(count):
                sl2[j, start + d] = slope[d]
                to = start + d - (H_TWO - 1)
                if 0 <= to < rows + 2:
                    grow(rounded(inside(value[d], first + to - 1, depth)), xs, (j, to))
        for start, count in chunks_of(rows, FORWARD_ROWS):
            pre = conv_rows(xs, (j,), start, count, t_ref, 2)
            slope = slope_of(pre, sigmoid(pre)).reshape(count, cells, TILE)
            for d in range(count):
                at = start + d
                grad = rounded(cot[at].astype(jnp.float32) * slope[d])
                g3[j, at] = grad

    middle(0, cot_own)
    middle(1, cot_other.at[0])
    for j in range(2):
        edge_rows(g3.at[j], g3_near.at[j], g3_far.at[j], H_G3)
    xb_own[...] = xb[0, H_HIDDEN - 1 : H_HIDDEN + rows + 1]
    xs_own[...] = xs[0]


def kernel_terms(values, gradient, rw):
    rows = gradient.shape[0]
    gradient = gradient.reshape(-1, TILE)
    for a in range(3):
        block = values[a : a + rows].reshape(-1, WIDE)
        terms = lax.dot_general(
            block, gradient, (((0,), (0,)), ((), ())), preferred_element_type=jnp.float32
        )
        for b in range(3):
            for c in range(3):
                at = (a * 9 + b * 3 + c) * CH
                for w in range(CELLS):
                    s0, s1 = SLOT_OF[b, w + c] * CH, SLOT_OF[b + 1, w + c] * CH
                    rw[w, at : at + CH] = (
                        terms[s0 : s0 + CH, :LANES] + terms[s1 : s1 + CH, LANES:]
                    )
    count = rw.shape[1] // CELLS
    cell = lax.broadcasted_iota(jnp.int32, (count, LANES), 1) // CH
    dense = jnp.zeros((count, LANES), jnp.float32)
    for q in range(CELLS):
        part = None
        for w in range(CELLS):
            piece = rw[w, pl.ds(q, count, stride=CELLS), :]
            if q != w:
                piece = pltpu.roll(piece, (q - w) % CELLS * CH, 1)
            part = piece if part is None else part + piece
        dense = jnp.where(cell == q, part, dense)
    return dense.astype(jnp.bfloat16)


def between_body(taps_ref, xs_own, g3, t_ref, terms, rw):
    fill_weights(taps_ref, t_ref)
    terms[...] = kernel_terms(xs_own[...], g3[0], rw)


def back_two(j, x_ref, sl2, x2_ref, t_ref, first, depth, grow):
    rows, cells = x2_ref.shape[-3:-1]
    for start, count in chunks_of(rows, BACKWARD_ROWS):
        back = conv_rows(x_ref, (), start, count, t_ref, 2).reshape(count, cells, TILE)
        for d in range(count):
            at = start + d
            grad = inside(back[d] * sl2[j, at], first + at - H_G2, depth)
            grow(rounded(grad), x2_ref, (at,))


def put_row(message, row):
    half = row.shape[0]
    message[message.shape[0] - 2 * half : message.shape[0] - half] = row[:, :LANES]
    message[message.shape[0] - half :] = row[:, LANES:]


def back_body(
    depth, pairs, tiles,
    near, mid, far, sl1, sl2, xv_own, xb_own, t_ref,
    g1, g1_far, message,
    xg3, xg2, rw, g1_near, terms,
):
    rows = mid.shape[1]
    cells = pairs * tiles
    first = lax.axis_index("depth") * rows
    grow = functools.partial(expand, pairs=pairs, tiles=tiles, masks=edge_masks(tiles))
    for j in range(2):
        widen(near, mid, far, (j,), H_G3, xg3.at[j], (), grow)
        back_two(j, xg3.at[j], sl2, xg2.at[j], t_ref, first, depth, grow)
    own, other = (
        rounded(conv_rows(xg2, (j,), 0, rows, t_ref, 1)).astype(jnp.float32) for j in range(2)
    )
    mixed = (OWN_SHARE * own + PARTNER_SHARE * other).reshape(rows, cells, TILE)
    g1[...] = rounded(mixed * sl1[...])
    edge_rows(g1, g1_near, g1_far, H_G1)
    size = terms.shape[0] // 2
    terms[:size] = kernel_terms(xv_own[...], g1[...], rw).astype(jnp.float32)
    two = kernel_terms(xb_own[...], xg2[0, H_G2 : H_G2 + rows, :, :TILE], rw)
    terms[size:] = two.astype(jnp.float32)
    message[: 2 * size] = terms[...].astype(jnp.bfloat16)
    put_row(message, g1_near[0])


def last_body(pairs, tiles, near, g1, far, t_ref, *refs):
    *parts, gv, total, scratch, xg1, sides = refs
    lines = -(-total.shape[0] // 16) * 16
    terms = [part[:lines].astype(jnp.float32) for part in parts]
    total[...] = functools.reduce(lambda a, b: a + b, terms)[: total.shape[0]]
    rows, height, _ = gv.shape
    cells = pairs * tiles
    grow = functools.partial(expand, pairs=pairs, tiles=tiles, masks=edge_masks(tiles))
    for at, message in enumerate((near, far)):
        first = message.shape[0] - 2 * cells
        sides[at, 0, :, :LANES] = message[first : first + cells]
        sides[at, 0, :, LANES:] = message[first + cells :]
    widen(sides.at[0], g1, sides.at[1], (), H_G1, xg1, (), grow)
    for start, count in chunks_of(rows, BACKWARD_ROWS):
        back = conv_rows(xg1, (), start, count, t_ref, 0).reshape(count, cells, TILE)
        for d in range(count):
            for h in range(height):
                row, side = h // 2 * tiles, slice(h % 2 * LANES, (h % 2 + 1) * LANES)
                scratch[start + d, pl.ds(h, tiles, stride=height), :] = back[
                    d, row : row + tiles, side
                ]
            for t in range(tiles):
                gv[start + d, :, t * LANES : (t + 1) * LANES] = scratch[
                    start + d, t * height : (t + 1) * height, :
                ].astype(jnp.bfloat16)


def add_body(own, near, three, three_near, g1_far, message, terms):
    add = lambda a, b: a.astype(jnp.float32) + b.astype(jnp.float32)
    size = three.shape[0]
    terms[: 2 * size] = add(own[: 2 * size], near[: 2 * size])
    terms[2 * size : 3 * size] = add(three[...], three_near[...])
    terms[3 * size :] = jnp.zeros_like(terms[3 * size :])
    message[: terms.shape[0]] = terms[...].astype(jnp.bfloat16)
    put_row(message, g1_far[0])


def total_body(one, two, out):
    rows = -(-out.shape[0] // 16) * 16
    total = one[:rows].astype(jnp.float32) + two[:rows].astype(jnp.float32)
    out[...] = total[: out.shape[0]].astype(out.dtype)


def swapped(values, hop):
    count = lax.axis_size("depth")
    return lax.ppermute(values, "depth", [(i, i ^ hop) for i in range(count)])


def neighbours(near, far):
    count = lax.axis_size("depth")
    result = []
    for values, first in ((near, 0), (far, 1)):
        partner = {}
        for i in range(first, count - 1, 2):
            partner[i], partner[i + 1] = i + 1, i
        pairs = [(i, partner.get(i, i)) for i in range(count)]
        result.append(lax.ppermute(values, "depth", pairs))
    return result


def over_sample(values, hop):
    groups = lax.axis_size("sample")
    return lax.ppermute(values, "sample", [(i, i ^ hop) for i in range(groups)])


def even_hops(values):
    return [over_sample(values, hop) for hop in range(2, lax.axis_size("sample"), 2)]


def all_hops(odd, evens):
    return [odd, *(crop for even in evens for crop in (even, over_sample(even, 1)))]


def traded(volume, cotangent, partner, tiles):
    groups = lax.axis_size("sample")
    rows, height, _ = volume.shape
    split = jnp.stack([volume, cotangent]).reshape(2, rows, height // 2, 2, tiles, LANES)
    split = split.transpose(0, 1, 2, 4, 3, 5).reshape(2, groups, -1, TILE)
    pieces = split.swapaxes(0, 1)
    spread = lax.all_to_all(pieces, "sample", split_axis=0, concat_axis=0, tiled=True)
    ids = jnp.arange(groups, dtype=jnp.int32)
    inverse = jnp.sum(jnp.where(partner[:, None] == ids[None, :], ids[:, None], 0), axis=0)
    wanted = jnp.stack([2 * partner, 2 * inverse, 2 * inverse + 1], axis=1)
    chosen = jnp.take(spread.reshape(2 * groups, -1, TILE), wanted, axis=0)
    joined = lax.all_to_all(chosen, "sample", split_axis=0, concat_axis=0, tiled=True)
    others = jnp.swapaxes(joined, 0, 1).reshape(3, rows, -1, TILE)
    return others[:2], others[2:]


def call(kernel, outs, scratch, inputs, macs=0, far=()):
    vmem, smem, anywhere = (
        pl.BlockSpec(memory_space=space) for space in (pltpu.VMEM, pltpu.SMEM, pl.ANY)
    )
    specs = [
        anywhere if at in far else smem if x.dtype == jnp.int32 else vmem
        for at, x in enumerate(inputs)
    ]
    results = pl.pallas_call(
        kernel,
        out_shape=tuple(jax.ShapeDtypeStruct(shape, dtype) for shape, dtype in outs),
        in_specs=specs,
        out_specs=(vmem,) * len(outs),
        scratch_shapes=scratch,
        compiler_params=pltpu.CompilerParams(vmem_limit_bytes=VMEM_LIMIT),
        cost_estimate=pl.CostEstimate(
            flops=2 * macs, bytes_accessed=2**22 if macs else 1, transcendentals=0
        ),
    )(*inputs)
    return results if len(results) > 1 else results[0]


def per_device(volume, kernels, partner, cotangent):
    volume, cotangent = volume[0], cotangent[0]
    rows, height, lanes = volume.shape
    pairs, tiles = height // 2, lanes // LANES
    cells = pairs * tiles
    groups, count = lax.axis_size("sample"), lax.axis_size("depth")
    depth = rows * count
    layers, taps, width = kernels.shape
    bf16, f32 = jnp.bfloat16, jnp.float32
    row_macs = 3 * cells * WIDE * TILE
    packed_rows = taps * CH // CELLS
    wide = lambda *lead: pltpu.VMEM((*lead, cells, WIDE), bf16)
    field = lambda *lead: ((*lead, cells, TILE), bf16)
    raw_tiles = lambda *lead: pltpu.VMEM((*lead, height * tiles, LANES), f32)
    banded = ((layers, 3, WIDE, TILE), bf16)
    spread_taps = ((layers, taps * CH, LANES), bf16)
    rw = pltpu.VMEM((CELLS, taps * CH, LANES), f32)

    direct = groups in (2, 4, 8)
    evens = even_hops(volume) if direct else []
    both, edges = lax.optimization_barrier((jnp.stack([volume, cotangent]), volume))
    near, far = neighbours(edges, edges)
    packed = kernels.reshape(layers, packed_rows, LANES)
    ids = jnp.clip(partner, 0, groups - 1)
    fwd_taps, bwd_taps = call(
        functools.partial(taps_body, taps),
        [spread_taps, spread_taps],
        [pltpu.VMEM((layers, -(-taps // CELLS) * LANES, LANES), f32)],
        [packed],
        2**28,
    )
    evens, both, ids, fwd_taps, bwd_taps, own_crop, late = lax.optimization_barrier(
        (evens, both, ids, fwd_taps, bwd_taps, volume, cotangent)
    )
    edge = ((2, H_VOL, cells, TILE), bf16)
    if direct:
        crops = all_hops(over_sample(own_crop, 1), evens)
        crops, far = lax.optimization_barrier((crops, far))
        vol, vol_near, vol_far = call(
            functools.partial(select_body, tuple(range(groups))),
            [field(2, rows), edge, edge],
            [raw_tiles(2, rows)],
            [ids, both, *crops],
        )
        vol_near, vol_far, near = lax.optimization_barrier((vol_near, vol_far, near))
        sides = neighbours(vol_near, vol_far)
        evens, vol = lax.optimization_barrier((even_hops(late), vol))
        give = call(pick_body, [((1, rows, height, lanes), bf16)], [], [ids, both, *evens])
        cot_other = call(
            functools.partial(select_body, tuple(range(0, groups, 2))),
            [field(1, rows)],
            [raw_tiles(1, rows)],
            [ids, both, *evens, over_sample(give, 1)],
        )
    else:
        vol, cot_other = traded(volume, cotangent, partner, tiles)
        sides = neighbours(vol, vol)
    hid_rows = rows + 2 * H_HIDDEN
    fwd, hid_own, sl1, xv_own, cot_own = call(
        functools.partial(own_body, pairs, tiles),
        [
            banded,
            field(hid_rows),
            ((rows, cells, TILE), f32),
            ((rows + 2, cells, WIDE), bf16),
            field(rows),
        ],
        [wide(rows + 2 * H_VOL), pltpu.VMEM((3, rows, cells, TILE), bf16), raw_tiles(4 * rows)],
        [fwd_taps, near, both, far],
        hid_rows * row_macs,
    )

    g3, g3_near, g3_far, sl2, xb_own, xs_own = call(
        functools.partial(forward_body, depth, pairs, tiles),
        [
            field(2, rows),
            field(2, H_G3),
            field(2, H_G3),
            ((2, rows + 2 * H_TWO, cells, TILE), f32),
            ((rows + 2, cells, WIDE), bf16),
            ((rows + 2, cells, WIDE), bf16),
        ],
        [
            wide(2, rows + 2 * H_VOL),
            pltpu.VMEM((2, hid_rows, cells, TILE), bf16),
            wide(2, hid_rows),
            wide(2, rows + 2),
        ],
        [sides[0], vol, sides[1], hid_own, cot_own, cot_other, fwd],
        (2 * hid_rows + 2 * (rows + 2) + 2 * rows) * row_macs,
    )

    near, far = neighbours(g3_near, g3_far)
    terms = ((packed_rows, LANES), bf16)
    bwd, three = call(
        between_body, [banded, terms], [rw], [bwd_taps, xs_own, g3], rows * row_macs
    )
    short, long = 2 * packed_rows, -(-layers * packed_rows // 16) * 16
    message = lambda lines: ((lines + 2 * cells, LANES), bf16)
    g1, g1_far, own = call(
        functools.partial(back_body, depth, pairs, tiles),
        [field(rows), ((H_G1, cells, TILE), bf16), message(short)],
        [
            wide(2, rows + 2 * H_G3),
            wide(2, rows + 2 * H_G2),
            rw,
            pltpu.VMEM((H_G1, cells, TILE), bf16),
            pltpu.VMEM((short, LANES), f32),
        ],
        [near, g3, far, sl1, sl2, xv_own, xb_own, bwd],
        (6 * rows + 4) * row_macs,
    )
    own, three = lax.optimization_barrier((own, three))
    near, three_near = swapped(own, 1), swapped(three, 1)
    summed = call(
        add_body,
        [message(long)],
        [pltpu.VMEM((long, LANES), f32)],
        [own, near, three, three_near, g1_far],
    )
    if count == 4:
        far = swapped(summed, 3)
        parts = [summed, far]
    else:
        far, parts, hop = neighbours(summed, summed)[1], [summed], 2
        while hop < count:
            if len(parts) > 1:
                parts = [call(total_body, [((long, LANES), bf16)], [], parts)]
            parts.append(swapped(parts[0], hop))
            hop *= 2
    grad_volume, total = call(
        functools.partial(last_body, pairs, tiles),
        [((rows, height, lanes), bf16), ((layers * packed_rows, LANES), f32)],
        [raw_tiles(rows), wide(rows + 2 * H_G1), pltpu.VMEM((2, H_G1, cells, TILE), bf16)],
        [near, g1, far, bwd, *parts],
        rows * row_macs,
    )
    return (grad_volume[None], total.reshape(1, layers, taps, width))


def solution(mesh):
    in_specs = (P("sample", "depth", None, None), P(), P(), P("sample", "depth", None, None))
    out_specs = (P("sample", "depth", None, None), P("sample", None, None, None))
    return jax.shard_map(
        per_device, mesh=mesh, in_specs=in_specs, out_specs=out_specs, check_vma=False
    )
```
